128 devices in a mesh: head: 2 (over z_hi), blk: 64 (over z_lo, x, y, core).
Axes of the slice: x: 4, y: 4, z: 4 (z_hi: 2, z_lo: 2; z = z_hi * 2 + z_lo), core: 2. Of those that a mesh axis runs over, the one named last changes fastest.
Arguments:
- hidden_in: bfloat16 [16384, 2048], P(('head', 'blk')), may hold values from -6 to 6
- gain_attn: float32 [2048], replicated, may hold values from 0.1 to 1.9
- gain_ffn: float32 [2048], replicated, may hold values from 0.1 to 1.9
- w_query: bfloat16 [2048, 2048], P(('head', 'blk')), may hold values from -0.125 to 0.125
- w_key: bfloat16 [2048, 1024], P(('head', 'blk')), may hold values from -0.125 to 0.125
- w_value: bfloat16 [2048, 1024], P(('head', 'blk')), may hold values from -0.125 to 0.125
- w_out: bfloat16 [2048, 2048], P(('head', 'blk')), may hold values from -0.375 to 0.375
- w_gate: bfloat16 [2048, 8192], P(('head', 'blk')), may hold values from -0.125 to 0.125
- w_up: bfloat16 [2048, 8192], P(('head', 'blk')), may hold values from -0.125 to 0.125
- w_down: bfloat16 [8192, 2048], P(('head', 'blk')), may hold values from -0.0625 to 0.0625
- qkv_shrink: bfloat16 [2048, 384], replicated, may hold values from -0.125 to 0.125
- query_expand: bfloat16 [128, 2048], replicated, may hold values from -1.5 to 1.5
- key_expand: bfloat16 [128, 1024], replicated, may hold values from -1.5 to 1.5
- value_expand: bfloat16 [128, 1024], replicated, may hold values from -1.5 to 1.5
- out_shrink: bfloat16 [2048, 128], replicated, may hold values from -0.125 to 0.125
- out_expand: bfloat16 [128, 2048], replicated, may hold values from -1.5 to 1.5
- gateup_shrink: bfloat16 [2048, 256], replicated, may hold values from -0.125 to 0.125
- gate_expand: bfloat16 [128, 8192], replicated, may hold values from -1.5 to 1.5
- up_expand: bfloat16 [128, 8192], replicated, may hold values from -1.5 to 1.5
- down_shrink: bfloat16 [8192, 128], replicated, may hold values from -0.0625 to 0.0625
- down_expand: bfloat16 [128, 2048], replicated, may hold values from -1.5 to 1.5
- lengths: int32 [16], replicated, may hold values from 1 to 4096, 16384 in all
- adapter: int32 [16], replicated, may hold values from 0 to 7
- packed_pos: int32 [16384], replicated, may hold values from 0 to 16383, as said below
- cotangent: bfloat16 [16384, 2048], P(('head', 'blk')), may hold values from -6 to 6
Outputs:
- output: bfloat16 [16384, 2048], P(('head', 'blk'))
- grad_input: bfloat16 [16384, 2048], P(('head', 'blk'))
- grad_qkv_shrink: float32 [2048, 384], replicated
- grad_query_expand: float32 [128, 2048], replicated
- grad_key_expand: float32 [128, 1024], replicated
- grad_value_expand: float32 [128, 1024], replicated
- grad_out_shrink: float32 [2048, 128], replicated
- grad_out_expand: float32 [128, 2048], replicated
- grad_gateup_shrink: float32 [2048, 256], replicated
- grad_gate_expand: float32 [128, 8192], replicated
- grad_up_expand: float32 [128, 8192], replicated
- grad_down_shrink: float32 [8192, 128], replicated
- grad_down_expand: float32 [128, 2048], replicated
The draws below stay inside these ranges and needn't reach their ends.
Inputs may be any that keep to these rules, and one draw needn't show every extreme that they name: The lengths sum to 16384; sequence s takes the packed positions after those of sequences 0 to s - 1; the longest is exactly 4096. packed_pos is a permutation of 0 to 16383. Each half of an aligned block of 128 rows holds one aligned run of 64 packed positions, in shuffled order; the block of 128 rows held by the device at head index i and blk index j (rows (i * 64 + j) * 128 onward) holds runs number (2 i) * 64 + (j + r) % 64 and (2 i + 1) * 64 + (j + r) % 64, for one r per draw.
All inputs are finite; a program needn't handle non-finite values.
Results may differ from the reference program's by a relative error of at most 0.028.
Values may be sent and summed in bfloat16 or wider, within the bound.
No kernel may reach another device: no remote copies, remote signals or barrier semaphores. Data moves between devices by JAX's collectives and lax.ppermute only.
A program may use at most 448 MiB of HBM per device.

```python
import math
import jax
import jax.numpy as jnp
import numpy as np
from jax import lax

D = 2048
QUERY_HEADS = 8
KEY_VALUE_HEADS = 4
HEAD_SIZE = 256
FF = 8192
RANK = 16
ADAPTERS = 8
NSEQ = 16
TOK_DEV = 128
TOKEN_TOTAL = 16384
SEQ_MOST = 4096
QW = 2048
KW = 1024
N_HEAD = 2
N_BLK = 64


def draw_packed_pos(key, part):
    key = jax.random.fold_in(key, 7)
    rotate_key, shuffle_key = jax.random.split(key)
    span_rows = TOK_DEV // 2
    offset = jax.random.randint(rotate_key, (), 0, N_BLK)
    rows_all = jnp.arange(TOK_DEV * N_HEAD * N_BLK, dtype=jnp.int32)
    block_index = rows_all // TOK_DEV
    head_index = block_index // N_BLK
    blk_index = block_index % N_BLK
    within = rows_all % TOK_DEV
    half_index = within // span_rows
    place = within % span_rows
    span = (2 * head_index + half_index) * N_BLK + (blk_index + offset) % N_BLK
    scores = jax.random.randint(shuffle_key, (2 * N_HEAD * N_BLK, span_rows), 0, 1 << 20)
    scores = scores * span_rows + jnp.arange(span_rows, dtype=jnp.int32)[None, :]
    shuffles = jnp.argsort(scores, axis=1).astype(jnp.int32)
    return (span * span_rows + shuffles[span, place]).astype(jnp.int32)


def plant(drawn, rng, least, high):
    index_at = [jax.random.randint(jax.random.fold_in(rng, axis), (), 0, length) for axis, length in enumerate(drawn.shape)]
    longest = drawn.shape.index(max(drawn.shape))
    next_to = index_at[:longest] + [(index_at[longest] + 1) % drawn.shape[longest]] + index_at[longest + 1:]
    return drawn.at[tuple(index_at)].set(least).at[tuple(next_to)].set(high)


def block_levels(rng, dims, pieces, smallest, high):
    level = 1.0
    for axis_at, parts in pieces:
        heights = jax.random.uniform(jax.random.fold_in(jax.random.fold_in(rng, 6), axis_at), (parts,), jnp.float32, smallest / len(pieces), high / len(pieces))
        level = level * jnp.repeat(jnp.exp(heights), dims[axis_at] // parts).reshape((-1,) + (1,) * (len(dims) - 1 - axis_at))
    return level


def split_up(count, total, most, lean):
    loads = [(1 << 20) // math.isqrt(grade ** lean) + 1 for grade in range(2, count + 1)]
    rest, holding = total - most - (count - 1), [1] * (count - 1)
    while rest > 0:
        candidates = [i for i in range(count - 1) if holding[i] < most]
        mass, left = sum([loads[i] for i in candidates]), rest
        for i in candidates:
            addition = min(most - holding[i], max(1, left * loads[i] // mass), rest)
            holding[i] = holding[i] + addition
            rest = rest - addition
    return np.array([most] + holding)


def uneven_parts(key, amount, total, bound, skew):
    if amount == 2:
        one = jax.random.randint(key, (), max(1, total - bound), min(bound, total - 1) + 1)
        return jnp.stack([one, total - one])
    sizes = jnp.asarray(split_up(amount, total, bound, skew), jnp.int32)
    twos = (amount - 1) // 2
    donor, receiver = sizes[1:1 + 2 * twos:2], sizes[2:2 + 2 * twos:2]
    room = jnp.minimum(donor - 1, bound - receiver)
    moved = jax.random.randint(jax.random.fold_in(key, 1), (twos,), 0, 1 << 20) % (room + 1)
    sizes = sizes.at[1:1 + 2 * twos:2].set(donor - moved).at[2:2 + 2 * twos:2].set(receiver + moved)
    return sizes[jax.random.permutation(jax.random.fold_in(key, 2), amount)]


def scatter_about(own_key, extent, deviation, bound, pieces=(), held_as=jnp.bfloat16):
    factor_of = block_levels(own_key, extent, pieces, -0.22, 0.18) if pieces else 1.0
    entries = jax.random.normal(own_key, extent, jnp.float32) * deviation * factor_of
    return jnp.minimum(jnp.maximum(entries, -bound), bound).astype(held_as)


def setup_inputs(seed: int = 0) -> dict:
    seeds = jax.random.split(jax.random.key(seed), 26)
    return {
        "hidden_in": scatter_about(seeds[0], (TOKEN_TOTAL, D), 1.0, 6.0, ((0, 128),)),
        "gain_attn": jnp.clip(1.0 + 0.18 * jax.random.normal(seeds[1], (D,), jnp.float32), 0.1, 1.9),
        "gain_ffn": jnp.clip(1.0 + 0.18 * jax.random.normal(seeds[2], (D,), jnp.float32), 0.1, 1.9),
        "w_query": scatter_about(seeds[3], (D, QW), D ** -0.5, 0.125, ((0, 128),)),
        "w_key": scatter_about(seeds[4], (D, KW), D ** -0.5, 0.125, ((0, 128),)),
        "w_value": scatter_about(seeds[5], (D, KW), D ** -0.5, 0.125, ((0, 128),)),
        "w_out": scatter_about(seeds[6], (QW, D), (QW // 8) ** -0.5, 0.375, ((0, 128),)),
        "w_gate": scatter_about(seeds[7], (D, FF), D ** -0.5, 0.125, ((0, 128),)),
        "w_up": scatter_about(seeds[8], (D, FF), D ** -0.5, 0.125, ((0, 128),)),
        "w_down": scatter_about(seeds[9], (FF, D), FF ** -0.5, 0.0625, ((0, 128),)),
        "qkv_shrink": scatter_about(seeds[10], (D, 3 * ADAPTERS * RANK), D ** -0.5, 0.125),
        "query_expand": scatter_about(seeds[11], (ADAPTERS * RANK, QW), RANK ** -0.5, 1.5),
        "key_expand": scatter_about(seeds[12], (ADAPTERS * RANK, KW), RANK ** -0.5, 1.5),
        "value_expand": scatter_about(seeds[13], (ADAPTERS * RANK, KW), RANK ** -0.5, 1.5),
        "out_shrink": scatter_about(seeds[14], (QW, ADAPTERS * RANK), QW ** -0.5, 0.125),
        "out_expand": scatter_about(seeds[15], (ADAPTERS * RANK, D), RANK ** -0.5, 1.5),
        "gateup_shrink": scatter_about(seeds[16], (D, 2 * ADAPTERS * RANK), D ** -0.5, 0.125),
        "gate_expand": scatter_about(seeds[17], (ADAPTERS * RANK, FF), RANK ** -0.5, 1.5),
        "up_expand": scatter_about(seeds[18], (ADAPTERS * RANK, FF), RANK ** -0.5, 1.5),
        "down_shrink": scatter_about(seeds[19], (FF, ADAPTERS * RANK), FF ** -0.5, 0.0625),
        "down_expand": scatter_about(seeds[20], (ADAPTERS * RANK, D), RANK ** -0.5, 1.5),
        "lengths": uneven_parts(seeds[21], NSEQ, TOKEN_TOTAL, SEQ_MOST, 2).astype(jnp.int32),
        "adapter": plant(jax.random.randint(seeds[22], (NSEQ,), 0, ADAPTERS), jax.random.fold_in(seeds[22], 1), 0, ADAPTERS - 1).astype(jnp.int32),
        "packed_pos": draw_packed_pos(jax.random.fold_in(seeds[25], 71), 0),
        "cotangent": scatter_about(seeds[24], (TOKEN_TOTAL, D), 1.0, 6.0, ((0, 128),)),
    }


@jax.custom_vjp
def rank_factors(v):
    return lax.optimization_barrier(v.astype(jnp.bfloat16)).astype(jnp.float32)

@jax.custom_vjp
def rank_factors_grad(v):
    return v

def low_keep(v):
    return (rank_factors(v), None)

def low_pass(kept, grad):
    return (grad,)

def back_keep(v):
    return (v, None)

def back_low(kept, grad):
    return (rank_factors(grad),)
rank_factors.defvjp(low_keep, low_pass)
rank_factors_grad.defvjp(back_keep, back_low)
norm_eps = 1e-06
rope_theta = 1000042.0
neg_big = -1e+30
highest = lax.Precision.HIGHEST

def matmul(left, right):
    return jnp.dot(left, right, precision=highest)

def normalize(value_matrix, gain):
    return value_matrix * lax.rsqrt(lax.optimization_barrier(jnp.mean(value_matrix * value_matrix, axis=-1, keepdims=True)) + norm_eps) * gain

def rotate(value_matrix):
    middle = value_matrix.shape[-1] // 2
    return jnp.concatenate([-value_matrix[..., middle:], value_matrix[..., :middle]], axis=-1)

def rope_tables(positions, width):
    middle = width // 2
    inverse = rope_theta ** (-(jnp.arange(middle, dtype=jnp.float32) * 2.0) / width)
    angles = positions.astype(jnp.float32)[:, None] * inverse[None, :]
    cos_table = jnp.concatenate([jnp.cos(angles), jnp.cos(angles)], axis=-1)[:, None, :]
    sin_table = jnp.concatenate([jnp.sin(angles), jnp.sin(angles)], axis=-1)[:, None, :]
    return (cos_table, sin_table)

def token_meta(lengths, adapter, packed):
    seq_ends = jnp.cumsum(lengths).astype(jnp.int32)
    starts = seq_ends - lengths
    seq_count = lengths.shape[0]
    member = (packed[:, None] >= starts[None, :]) & (packed[:, None] < seq_ends[None, :])
    member_int = member.astype(jnp.int32)
    seq_ids = lax.optimization_barrier(jnp.sum(member_int * jnp.arange(seq_count, dtype=jnp.int32)[None, :], axis=1))
    positions = packed - lax.optimization_barrier(jnp.sum(member_int * starts[None, :], axis=1))
    owners = lax.optimization_barrier(jnp.sum(member_int * adapter[None, :], axis=1))
    return (seq_ids, positions, owners)

def attention(query_rows, key_matrix, value_matrix, seq_ids, positions):
    rows_per_block = min(512, TOKEN_TOTAL)
    causal_span = SEQ_MOST
    query_group_ratio = QUERY_HEADS // KEY_VALUE_HEADS
    factor = HEAD_SIZE ** (-0.5)
    padded_keys = jnp.concatenate([jnp.zeros((causal_span, KEY_VALUE_HEADS, HEAD_SIZE), jnp.float32), key_matrix], axis=0)
    padded_values = jnp.concatenate([jnp.zeros((causal_span, KEY_VALUE_HEADS, HEAD_SIZE), jnp.float32), value_matrix], axis=0)
    seq_pad = jnp.concatenate([jnp.full((causal_span,), -1, jnp.int32), seq_ids])
    pos_pad = jnp.concatenate([jnp.zeros((causal_span,), jnp.int32), positions])

    def one_block(leading_row):
        query_block_slice = lax.dynamic_slice_in_dim(query_rows, leading_row, rows_per_block, 0).reshape(rows_per_block, KEY_VALUE_HEADS, query_group_ratio, HEAD_SIZE)
        key_blk = lax.dynamic_slice_in_dim(padded_keys, leading_row, causal_span + rows_per_block, 0)
        value_blk = lax.dynamic_slice_in_dim(padded_values, leading_row, causal_span + rows_per_block, 0)
        q_seq = lax.dynamic_slice_in_dim(seq_ids, leading_row, rows_per_block)
        q_pos = lax.dynamic_slice_in_dim(positions, leading_row, rows_per_block)
        k_seq = lax.dynamic_slice_in_dim(seq_pad, leading_row, causal_span + rows_per_block)
        k_pos = lax.dynamic_slice_in_dim(pos_pad, leading_row, causal_span + rows_per_block)
        allowed = (k_seq[None, :] == q_seq[:, None]) & (k_pos[None, :] <= q_pos[:, None])
        scores = rank_factors_grad(jnp.einsum('qkgd,pkd->kgqp', query_block_slice, key_blk, precision=highest) * factor)
        scores = jnp.where(allowed, scores, neg_big)
        scores = scores - lax.optimization_barrier(jnp.max(scores, axis=-1, keepdims=True))
        weights_exp = jnp.exp(scores)
        softmax_p = rank_factors(weights_exp / lax.optimization_barrier(jnp.sum(weights_exp, axis=-1, keepdims=True)))
        mixed_out = jnp.einsum('kgqp,pkd->qkgd', softmax_p, value_blk, precision=highest)
        return mixed_out.reshape(rows_per_block, QUERY_HEADS * HEAD_SIZE)
    firsts = jnp.arange(TOKEN_TOTAL // rows_per_block, dtype=jnp.int32) * rows_per_block
    return lax.map(jax.checkpoint(one_block), firsts).reshape(TOKEN_TOTAL, QUERY_HEADS * HEAD_SIZE)

def reference(hidden_in, gain_attn, gain_ffn, w_query, w_key, w_value, w_out, w_gate, w_up, w_down, qkv_shrink, query_expand, key_expand, value_expand, out_shrink, out_expand, gateup_shrink, gate_expand, up_expand, down_shrink, down_expand, lengths, adapter, packed_pos, cotangent):
    low_rank = ADAPTERS * RANK
    packed = jnp.arange(TOKEN_TOTAL, dtype=jnp.int32)
    seq_ids, positions, owners = token_meta(lengths, adapter, packed)
    select = (owners[:, None] == (jnp.arange(low_rank, dtype=jnp.int32) // RANK)[None, :]).astype(jnp.float32)
    cos_table, sin_table = rope_tables(positions, HEAD_SIZE)
    query_weight = w_query.astype(jnp.float32)
    key_weight = w_key.astype(jnp.float32)
    value_weight = w_value.astype(jnp.float32)
    out_weight = w_out.astype(jnp.float32)
    gate_weight = w_gate.astype(jnp.float32)
    up_weight = w_up.astype(jnp.float32)
    down_weight = w_down.astype(jnp.float32)
    x_packed = jnp.zeros((TOKEN_TOTAL, D), jnp.float32).at[packed_pos].set(hidden_in.astype(jnp.float32))
    dy_packed = jnp.zeros((TOKEN_TOTAL, D), jnp.float32).at[packed_pos].set(cotangent.astype(jnp.float32))
    adapters = tuple((value.astype(jnp.float32) for value in (qkv_shrink, query_expand, key_expand, value_expand, out_shrink, out_expand, gateup_shrink, gate_expand, up_expand, down_shrink, down_expand)))

    def forward(inputs, params):
        qkv_a, query_b, key_b, value_b, out_a, out_b, gateup_a, gate_b, up_b, down_a, down_b = params
        normed = rank_factors(normalize(inputs, gain_attn))
        lowered = rank_factors(rank_factors_grad(matmul(normed, qkv_a)) * jnp.tile(select, (1, 3)))
        q_lin = rank_factors_grad(matmul(normed, query_weight) + matmul(lowered[:, :low_rank], query_b))
        key_linear = rank_factors_grad(matmul(normed, key_weight) + matmul(lowered[:, low_rank:2 * low_rank], key_b))
        value_linear = matmul(normed, value_weight) + matmul(lowered[:, 2 * low_rank:], value_b)
        q_heads = q_lin.reshape(TOKEN_TOTAL, QUERY_HEADS, HEAD_SIZE)
        key_head_rows = key_linear.reshape(TOKEN_TOTAL, KEY_VALUE_HEADS, HEAD_SIZE)
        query_rows = rank_factors(rank_factors_grad(q_heads * cos_table + rotate(q_heads) * sin_table))
        key_matrix = rank_factors(rank_factors_grad(key_head_rows * cos_table + rotate(key_head_rows) * sin_table))
        value_matrix = rank_factors(rank_factors_grad(value_linear.reshape(TOKEN_TOTAL, KEY_VALUE_HEADS, HEAD_SIZE)))
        mixed_all = rank_factors(rank_factors_grad(attention(query_rows, key_matrix, value_matrix, seq_ids, positions)))
        lowered_out = rank_factors(rank_factors_grad(matmul(mixed_all, out_a)) * select)
        attn_out = rank_factors_grad(matmul(mixed_all, out_weight) + matmul(lowered_out, out_b))
        middle = inputs + attn_out
        ffn_rows = min(2048, TOKEN_TOTAL)
        ffn_blocks = TOKEN_TOTAL // ffn_rows

        def ffn_step(blk_pair):
            mid_blk, select_blk = blk_pair
            normed_mid = rank_factors(normalize(mid_blk, gain_ffn))
            lowered_gu = rank_factors(rank_factors_grad(matmul(normed_mid, gateup_a)) * jnp.tile(select_blk, (1, 2)))
            gate_pre = rank_factors_grad(matmul(normed_mid, gate_weight) + matmul(lowered_gu[:, :low_rank], gate_b))
            up_pre = rank_factors_grad(matmul(normed_mid, up_weight) + matmul(lowered_gu[:, low_rank:], up_b))
            active = rank_factors(jax.nn.silu(gate_pre) * up_pre)
            reduced = rank_factors(rank_factors_grad(matmul(active, down_a)) * select_blk)
            return mid_blk + matmul(active, down_weight) + matmul(reduced, down_b)
        result = lax.map(jax.checkpoint(ffn_step), (middle.reshape(ffn_blocks, ffn_rows, D), select.reshape(ffn_blocks, ffn_rows, low_rank)))
        return result.reshape(TOKEN_TOTAL, D)
    out_packed, pullback = jax.vjp(forward, x_packed, adapters)
    dx_packed, grads = pullback(dy_packed)
    return (out_packed[packed_pos].astype(jnp.bfloat16), dx_packed[packed_pos].astype(jnp.bfloat16), grads[0], grads[1], grads[2], grads[3], grads[4], grads[5], grads[6], grads[7], grads[8], grads[9], grads[10])
```

```python
from functools import partial

import jax
import jax.numpy as jnp
from jax import lax
from jax.experimental import pallas as pl
from jax.experimental.pallas import tpu as pltpu
from jax.sharding import Mesh, PartitionSpec as P

HEAD_SIZE = 256
RANK = 16
HALF = 64
GROUP = 512

ALL = ("zh", "zl", "x", "y", "c")
PLANE = ("zh", "zl", "x")

norm_eps = 1e-06
rope_theta = 1000042.0
neg_big = -1e30
far = 1 << 30

f32 = jnp.float32
bf16 = jnp.bfloat16


def product(left, right):
    return jnp.dot(left, right, preferred_element_type=f32)


def times_transposed(left, right):
    return lax.dot_general(left, right, (((1,), (1,)), ((), ())), preferred_element_type=f32)


def inner_rows(left, right):
    return lax.dot_general(left, right, (((0,), (0,)), ((), ())), preferred_element_type=f32)


def row_scale(value_matrix):
    return lax.rsqrt(jnp.mean(value_matrix * value_matrix, axis=-1, keepdims=True) + norm_eps)


def norm_back(value_matrix, scale, gain, grad):
    scaled = gain * grad
    return scale * scaled - value_matrix * (scale * scale * scale) * jnp.mean(
        value_matrix * scaled, axis=-1, keepdims=True
    )


def rotate(value_matrix):
    middle = value_matrix.shape[-1] // 2
    return jnp.concatenate([-value_matrix[..., middle:], value_matrix[..., :middle]], axis=-1)


def rope_tables(positions, width):
    middle = width // 2
    inverse = rope_theta ** (-(jnp.arange(middle, dtype=f32) * 2.0) / width)
    angles = positions.astype(f32)[:, None] * inverse[None, :]
    cos_half, sin_half = jnp.cos(angles), jnp.sin(angles)
    cos_table = jnp.concatenate([cos_half, cos_half], axis=-1)[:, None, :]
    sin_table = jnp.concatenate([sin_half, sin_half], axis=-1)[:, None, :]
    return (cos_table, sin_table)


def swap_cores(value):
    return lax.ppermute(value, "c", [(0, 1), (1, 0)])


def shift_y(value, step):
    return lax.ppermute(value, "y", [(i, (i + step) % 4) for i in range(4)])


def gather_y(value):
    return lax.all_gather(value, "y", axis=0, tiled=True)


def sum_y(blocks_of, y):
    total = blocks_of(y).astype(f32)
    for step in (2, 1, 3):
        total = total + shift_y(blocks_of((y + step) % 4), step).astype(f32)
    return total


def allowed_mask(own_pos, own_start, key_pos):
    return (key_pos <= own_pos) & (key_pos >= own_start)


def attend_kernel(
    active, place, q_ref, pos_ref, start_ref, kpos_ref, prev_ref, own_ref, mixed_ref, lse_ref, top, total, accum
):
    step = pl.program_id(0)

    @pl.when(step == 0)
    def _():
        top[...] = jnp.full(top.shape, neg_big, f32)
        total[...] = jnp.zeros(total.shape, f32)
        accum[...] = jnp.zeros(accum.shape, f32)

    for side, kv_ref in ((0, prev_ref), (1, own_ref)):

        @pl.when(active[side * 8 + step] != 0)
        def _():
            key = kv_ref[0, 0, :, :HEAD_SIZE]
            value = kv_ref[0, 0, :, HEAD_SIZE:]
            allowed = allowed_mask(pos_ref[...], start_ref[...], kpos_ref[0, side])
            for head in range(2):
                scores = times_transposed(q_ref[:, head * HEAD_SIZE : (head + 1) * HEAD_SIZE], key)
                scores = jnp.where(allowed, scores, neg_big)
                top_old = top[head]
                top_new = jnp.maximum(top_old, jnp.max(scores, axis=-1, keepdims=True))
                weights_p = jnp.where(allowed, jnp.exp(scores - top_new), 0.0)
                damping = jnp.exp(top_old - top_new)
                total[head] = total[head] * damping + jnp.sum(weights_p, axis=-1, keepdims=True)
                accum[head] = accum[head] * damping + product(weights_p.astype(bf16), value)
                top[head] = top_new

    @pl.when(step == 7)
    def _():
        for head in range(2):
            mixed_ref[:, head * HEAD_SIZE : (head + 1) * HEAD_SIZE] = accum[head] / total[head]
            lse_ref[head] = top[head] + jnp.log(total[head])


def attend_back_kernel(
    active,
    place,
    q_ref,
    pos_ref,
    start_ref,
    kpos_ref,
    prev_ref,
    own_ref,
    mixed_ref,
    lse_ref,
    dout_ref,
    dq_ref,
    dprev_ref,
    down_ref,
    delta,
):
    step = pl.program_id(0)

    @pl.when(step == 0)
    def _():
        dq_ref[...] = jnp.zeros(dq_ref.shape, f32)
        for head in range(2):
            cols = slice(head * HEAD_SIZE, (head + 1) * HEAD_SIZE)
            delta[head] = jnp.sum(dout_ref[:, cols].astype(f32) * mixed_ref[:, cols], axis=-1, keepdims=True)

    for side, kv_ref, dkv_ref in ((0, prev_ref, dprev_ref), (1, own_ref, down_ref)):

        @pl.when(active[side * 8 + step] == 0)
        def _():
            dkv_ref[...] = jnp.zeros(dkv_ref.shape, bf16)

        @pl.when(active[side * 8 + step] != 0)
        def _():
            key = kv_ref[0, 0, :, :HEAD_SIZE]
            value = kv_ref[0, 0, :, HEAD_SIZE:]
            allowed = allowed_mask(pos_ref[...], start_ref[...], kpos_ref[0, side])
            dk = jnp.zeros((GROUP, HEAD_SIZE), f32)
            dv = jnp.zeros((GROUP, HEAD_SIZE), f32)
            for head in range(2):
                cols = slice(head * HEAD_SIZE, (head + 1) * HEAD_SIZE)
                query, dout = q_ref[:, cols], dout_ref[:, cols]
                scores = times_transposed(query, key)
                weights_p = jnp.where(allowed, jnp.exp(scores - lse_ref[head]), 0.0)
                dprobs = times_transposed(dout, value)
                dscores = (weights_p * (dprobs - delta[head])).astype(bf16)
                dq_ref[:, cols] += product(dscores, key)
                dk = dk + inner_rows(dscores, query)
                dv = dv + inner_rows(weights_p.astype(bf16), dout)
            dkv_ref[0, :, :HEAD_SIZE] = dk.astype(bf16)
            dkv_ref[0, :, HEAD_SIZE:] = dv.astype(bf16)


def whole(shape):
    return pl.BlockSpec(shape, lambda i, *refs: (0,) * len(shape))


def key_specs():
    return [
        pl.BlockSpec((1, 2, 1, GROUP), lambda i, active, place: (i, 0, 0, 0)),
        pl.BlockSpec((1, 1, GROUP, GROUP), lambda i, active, place: (0, i, 0, 0)),
        pl.BlockSpec((1, 1, GROUP, GROUP), lambda i, active, place: (place[0], i, 0, 0)),
    ]


def attend(active, place, query, pos_col, start_col, key_pos, prev, family):
    return pl.pallas_call(
        attend_kernel,
        grid_spec=pltpu.PrefetchScalarGridSpec(
            num_scalar_prefetch=2,
            grid=(8,),
            in_specs=[whole((GROUP, GROUP)), whole((GROUP, 1)), whole((GROUP, 1))] + key_specs(),
            out_specs=[whole((GROUP, GROUP)), whole((2, GROUP, 1))],
            scratch_shapes=[
                pltpu.VMEM((2, GROUP, 1), f32),
                pltpu.VMEM((2, GROUP, 1), f32),
                pltpu.VMEM((2, GROUP, HEAD_SIZE), f32),
            ],
        ),
        out_shape=[
            jax.ShapeDtypeStruct((GROUP, GROUP), f32),
            jax.ShapeDtypeStruct((2, GROUP, 1), f32),
        ],
        compiler_params=pltpu.CompilerParams(vmem_limit_bytes=40 << 20),
        name="attend",
    )(active, place, query, pos_col, start_col, key_pos, prev, family)


def attend_back(active, place, query, pos_col, start_col, key_pos, prev, family, mixed, lse, dout):
    return pl.pallas_call(
        attend_back_kernel,
        grid_spec=pltpu.PrefetchScalarGridSpec(
            num_scalar_prefetch=2,
            grid=(8,),
            in_specs=[whole((GROUP, GROUP)), whole((GROUP, 1)), whole((GROUP, 1))]
            + key_specs()
            + [whole((GROUP, GROUP)), whole((2, GROUP, 1)), whole((GROUP, GROUP))],
            out_specs=[
                whole((GROUP, GROUP)),
                pl.BlockSpec((1, GROUP, GROUP), lambda i, active, place: (i, 0, 0)),
                pl.BlockSpec((1, GROUP, GROUP), lambda i, active, place: (i, 0, 0)),
            ],
            scratch_shapes=[pltpu.VMEM((2, GROUP, 1), f32)],
        ),
        out_shape=[
            jax.ShapeDtypeStruct((GROUP, GROUP), f32),
            jax.ShapeDtypeStruct((8, GROUP, GROUP), bf16),
            jax.ShapeDtypeStruct((8, GROUP, GROUP), bf16),
        ],
        compiler_params=pltpu.CompilerParams(vmem_limit_bytes=40 << 20),
        name="attend_back",
    )(active, place, query, pos_col, start_col, key_pos, prev, family, mixed, lse, dout)


def local(
    hidden_in,
    gain_attn,
    gain_ffn,
    w_query,
    w_key,
    w_value,
    w_out,
    w_gate,
    w_up,
    w_down,
    qkv_shrink,
    query_expand,
    key_expand,
    value_expand,
    out_shrink,
    out_expand,
    gateup_shrink,
    gate_expand,
    up_expand,
    down_shrink,
    down_expand,
    lengths,
    adapter,
    packed_pos,
    cotangent,
):
    zh, zl, x, y, c = (lax.axis_index(name) for name in ALL)
    row = 2 * zh + c
    block = 4 * zl + x
    mine, other = 2 * y + c, 2 * y + 1 - c
    factor = HEAD_SIZE ** (-0.5)
    rank = out_shrink.shape[1]

    def to_rows(value):
        own = lax.dynamic_slice_in_dim(value, c * HALF, HALF, 0)
        sent = lax.dynamic_slice_in_dim(value, (1 - c) * HALF, HALF, 0)
        return jnp.concatenate([own, swap_cores(sent)], axis=0)

    def from_rows(value):
        own, got = value[:HALF], swap_cores(value[HALF:])
        return jnp.where(c == 0, jnp.concatenate([own, got], 0), jnp.concatenate([got, own], 0))

    hidden = to_rows(hidden_in)
    cot = to_rows(cotangent)

    spread = packed_pos.reshape(2, 8, 4, 2, 2, HALF)
    spread = jnp.transpose(spread, (0, 4, 1, 2, 3, 5))
    rows_pos = jnp.stack([spread[:, 0], spread[:, 1, :, :, ::-1]], axis=1).reshape(4, 8, GROUP)
    own_row = lax.dynamic_index_in_dim(rows_pos, row, 0, keepdims=False)
    prev_row = lax.dynamic_index_in_dim(rows_pos, jnp.maximum(row - 1, 0), 0, keepdims=False)
    prev_row = jnp.where(row == 0, far, prev_row)
    key_pos = jnp.stack([prev_row, own_row], axis=1)
    group_pos = lax.dynamic_index_in_dim(own_row, block, 0, keepdims=False)
    seq_ends = jnp.cumsum(lengths)
    starts = seq_ends - lengths
    member = (group_pos[:, None] >= starts[None, :]) & (group_pos[:, None] < seq_ends[None, :])
    member_int = member.astype(jnp.int32)
    group_start = jnp.sum(member_int * starts[None, :], axis=1)
    group_owner = jnp.sum(member_int * adapter[None, :], axis=1)
    low, high = jnp.min(group_start), jnp.max(group_pos)
    active = (jnp.min(key_pos, axis=2) <= high) & (jnp.max(key_pos, axis=2) >= low)
    active = jnp.transpose(active).reshape(16).astype(jnp.int32)
    place = zh.reshape(1).astype(jnp.int32)
    columns = jnp.arange(rank, dtype=jnp.int32) // RANK
    select_g = (group_owner[:, None] == columns[None, :]).astype(f32)
    select = lax.dynamic_slice_in_dim(select_g, y * 128, 128, 0)
    cos_table, sin_table = rope_tables(group_pos - group_start, HEAD_SIZE)

    def column_slices(weight):
        rows_here, width = weight.shape
        parts = jnp.transpose(weight.reshape(rows_here, 16, 8, width // 128), (2, 0, 1, 3))
        return parts.reshape(8, rows_here, width // 8)

    heads_q = w_query.reshape(16, 4, 512)
    heads_kv = jnp.concatenate([w_key.reshape(16, 4, 256), w_value.reshape(16, 4, 256)], axis=2)
    qkv_parts = jnp.transpose(jnp.stack([heads_q, heads_kv], axis=2), (1, 2, 0, 3)).reshape(8, 16, 512)
    qkv_mine = lax.all_to_all(qkv_parts, ("y", "c"), split_axis=0, concat_axis=0, tiled=True).reshape(128, 512)
    qkv_mine = lax.all_gather(qkv_mine, PLANE, axis=0, tiled=True)
    qkv_other = swap_cores(qkv_mine)
    wq = jnp.where(c == 0, qkv_mine, qkv_other)
    wkv = jnp.where(c == 0, qkv_other, qkv_mine)
    wo = lax.all_gather(w_out, ALL, axis=0, tiled=True)
    gate_up_parts = jnp.concatenate([column_slices(w_gate), column_slices(w_up)], axis=2)
    gate_up = lax.all_to_all(gate_up_parts, ("y", "c"), split_axis=0, concat_axis=0, tiled=True).reshape(128, 2048)
    wgu_mine = lax.all_gather(gate_up, PLANE, axis=0, tiled=True)
    wd_mine = lax.all_gather(w_down, PLANE, axis=0, tiled=True)
    wgu_other, wd_other = swap_cores(wgu_mine), swap_cores(wd_mine)

    def columns_of(array, width):
        return lax.dynamic_slice_in_dim(array, y * width, width, 1)

    inputs = hidden.astype(f32)
    scale_in = row_scale(inputs)
    normed = (inputs * scale_in * gain_attn).astype(bf16)
    normed_g = gather_y(normed)
    cot_g = gather_y(cot)
    q_expand = columns_of(query_expand, 512)
    k_expand = columns_of(key_expand, 256)
    v_expand = columns_of(value_expand, 256)
    low_qkv = (product(normed_g, qkv_shrink) * jnp.tile(select_g, (1, 3))).astype(bf16)
    query_lin = product(normed_g, wq) + product(low_qkv[:, :rank], q_expand)
    kv_lin = product(normed_g, wkv)
    key_lin = kv_lin[:, :256] + product(low_qkv[:, rank : 2 * rank], k_expand)
    value_lin = kv_lin[:, 256:] + product(low_qkv[:, 2 * rank :], v_expand)
    query_heads = query_lin.reshape(GROUP, 2, HEAD_SIZE)
    key_heads = key_lin.reshape(GROUP, 1, HEAD_SIZE)
    query = (query_heads * cos_table + rotate(query_heads) * sin_table).astype(bf16)
    query = (query * bf16(factor)).reshape(GROUP, 512)
    key = (key_heads * cos_table + rotate(key_heads) * sin_table).astype(bf16).reshape(GROUP, 256)
    key_value = jnp.concatenate([key, value_lin.astype(bf16)], axis=1)

    family = lax.all_gather(key_value, PLANE, axis=0, tiled=True).reshape(2, 8, GROUP, GROUP)
    wanted = jnp.where(c == 0, zh, 0)
    prev = swap_cores(lax.dynamic_slice_in_dim(family, wanted, 1, 0))

    pos_col, start_col = group_pos[:, None], group_start[:, None]
    key_pos4 = key_pos.reshape(8, 2, 1, GROUP)
    mixed_f, lse = attend(active, place, query, pos_col, start_col, key_pos4, prev, family)
    mixed = mixed_f.astype(bf16)

    mixed_tok = lax.all_to_all(mixed, "y", split_axis=0, concat_axis=1, tiled=True)
    low_out = (product(mixed_tok, out_shrink) * select).astype(bf16)
    middle = inputs + product(mixed_tok, wo) + product(low_out, out_expand)
    scale_mid = row_scale(middle)
    normed_mid = (middle * scale_mid * gain_ffn).astype(bf16)
    normed_mid_g = gather_y(normed_mid)

    select_two = jnp.tile(select_g, (1, 2))
    low_gu = (product(normed_mid_g, gateup_shrink) * select_two).astype(bf16)
    grad_low_down = (times_transposed(cot_g, down_expand) * select_g).astype(bf16)
    result = jnp.zeros((GROUP, 2048), f32)
    low_down_part = jnp.zeros((GROUP, rank), f32)
    grad_mid_part = jnp.zeros((GROUP, 2048), f32)
    grad_low_part = jnp.zeros((GROUP, 2 * rank), f32)
    unit_grads = []
    units = 1024
    for wgu, wd, at in ((wgu_mine, wd_mine, mine), (wgu_other, wd_other, other)):
        wg, wu = wgu[:, :units], wgu[:, units:]
        g_expand = lax.dynamic_slice_in_dim(gate_expand.reshape(rank, 16, 8, 64), at, 1, 2).reshape(rank, units)
        u_expand = lax.dynamic_slice_in_dim(up_expand.reshape(rank, 16, 8, 64), at, 1, 2).reshape(rank, units)
        d_shrink = lax.dynamic_slice_in_dim(down_shrink.reshape(16, 8, 64, rank), at, 1, 1).reshape(units, rank)
        gate_pre = product(normed_mid_g, wg) + product(low_gu[:, :rank], g_expand)
        up_pre = product(normed_mid_g, wu) + product(low_gu[:, rank:], u_expand)
        sigmoid_g = jax.nn.sigmoid(gate_pre)
        silu_gate = gate_pre * sigmoid_g
        active_units = (silu_gate * up_pre).astype(bf16)
        result = result + product(active_units, wd)
        low_down_part = low_down_part + product(active_units, d_shrink)
        grad_active = times_transposed(cot_g, wd) + times_transposed(grad_low_down, d_shrink)
        grad_gate = (grad_active * up_pre * sigmoid_g * (1.0 + gate_pre * (1.0 - sigmoid_g))).astype(bf16)
        grad_up = (grad_active * silu_gate).astype(bf16)
        grad_mid_part = grad_mid_part + times_transposed(grad_gate, wg) + times_transposed(grad_up, wu)
        grad_low_part = grad_low_part + jnp.concatenate(
            [times_transposed(grad_gate, g_expand), times_transposed(grad_up, u_expand)], axis=1
        )
        unit_grads.append(
            (
                inner_rows(grad_gate, low_gu[:, :rank]),
                inner_rows(grad_up, low_gu[:, rank:]),
                inner_rows(active_units, grad_low_down),
            )
        )

    def sum_tokens(*parts):
        packed = jnp.concatenate([part.astype(bf16) for part in parts], axis=1)
        return sum_y(lambda i: lax.dynamic_slice_in_dim(packed, i * 128, 128, 0), y)

    back = sum_tokens(grad_mid_part, grad_low_part)
    ahead = sum_tokens(result, low_down_part)

    low_down = (ahead[:, 2048:] * select).astype(bf16)
    output = (middle + ahead[:, :2048] + product(low_down, down_expand)).astype(bf16)
    grad_low_gu = (back[:, 2048:] * jnp.tile(select, (1, 2))).astype(bf16)
    grad_normed_mid = back[:, :2048] + times_transposed(grad_low_gu, gateup_shrink)
    cot_f = cot.astype(f32)
    grad_middle = cot_f + norm_back(middle, scale_mid, gain_ffn, grad_normed_mid)
    grad_attn_out = grad_middle.astype(bf16)
    grad_low_out = (times_transposed(grad_attn_out, out_expand) * select).astype(bf16)
    grad_mixed = (times_transposed(grad_attn_out, wo) + times_transposed(grad_low_out, out_shrink)).astype(bf16)

    dout = lax.all_to_all(grad_mixed, "y", split_axis=1, concat_axis=0, tiled=True)
    dq, dprev, downed = attend_back(
        active, place, query, pos_col, start_col, key_pos4, prev, family, mixed_f, lse, dout
    )
    other_row = swap_cores(dprev)
    place_own = jnp.arange(2, dtype=jnp.int32) == zh
    place_got = jnp.where(c == 0, place_own, (jnp.arange(2, dtype=jnp.int32) == 0) & (zh == 1))
    terms = jnp.where(place_own[:, None, None, None], downed[None], bf16(0)) + jnp.where(
        place_got[:, None, None, None], other_row[None], bf16(0)
    )
    dkv = lax.psum_scatter(terms.reshape(16 * GROUP, GROUP), PLANE, scatter_dimension=0, tiled=True)
    dkv = dkv.astype(f32)
    query_back = (dq * factor).astype(bf16).astype(f32).reshape(GROUP, 2, HEAD_SIZE)
    key_back = dkv[:, :256].astype(bf16).astype(f32).reshape(GROUP, 1, HEAD_SIZE)
    grad_value = dkv[:, 256:].astype(bf16)
    grad_query = (query_back * cos_table - rotate(query_back * sin_table)).astype(bf16).reshape(GROUP, 512)
    grad_key = (key_back * cos_table - rotate(key_back * sin_table)).astype(bf16).reshape(GROUP, 256)
    grad_kv = jnp.concatenate([grad_key, grad_value], axis=1)

    grad_low_part = jnp.concatenate(
        [
            times_transposed(grad_query, q_expand),
            times_transposed(grad_key, k_expand),
            times_transposed(grad_value, v_expand),
        ],
        axis=1,
    )
    grad_normed_part = times_transposed(grad_query, wq) + times_transposed(grad_kv, wkv)
    last = sum_tokens(grad_normed_part, grad_low_part)
    grad_low_qkv = (last[:, 2048:] * jnp.tile(select, (1, 3))).astype(bf16)
    grad_normed = last[:, :2048] + times_transposed(grad_low_qkv, qkv_shrink)
    grad_input = (grad_middle + norm_back(inputs, scale_in, gain_attn, grad_normed)).astype(bf16)

    def features(array):
        return lax.dynamic_slice_in_dim(array, y * 512, 512, 1)

    def by_halves(pair_at):
        own, others = unit_grads[0][pair_at], unit_grads[1][pair_at]
        own, others = own.reshape(16, 1, 64, rank), others.reshape(16, 1, 64, rank)
        ordered = jnp.where(c == 0, jnp.concatenate([own, others], 1), jnp.concatenate([others, own], 1))
        return ordered.reshape(32, 64, rank)

    def by_rows(array):
        return array.reshape(32, array.shape[0] // 32, rank)

    low_down_g = gather_y(low_down)
    grad_low_gu_g = gather_y(grad_low_gu)
    grad_low_out_g = gather_y(grad_low_out)
    grad_low_qkv_g = gather_y(grad_low_qkv)
    low_out_g = gather_y(low_out)
    grad_attn_out_g = lax.all_to_all(grad_attn_out, "y", split_axis=1, concat_axis=0, tiled=True)
    grad_gateup = inner_rows(features(normed_mid_g), grad_low_gu_g)
    grad_qkv = inner_rows(features(normed_g), grad_low_qkv_g)
    pieces = [
        by_halves(0),
        by_halves(1),
        by_halves(2),
        by_rows(inner_rows(grad_query, low_qkv[:, :rank])),
        by_rows(inner_rows(grad_key, low_qkv[:, rank : 2 * rank])),
        by_rows(inner_rows(grad_value, low_qkv[:, 2 * rank :])),
        by_rows(inner_rows(mixed, grad_low_out_g)),
        by_rows(inner_rows(grad_attn_out_g, low_out_g)),
        by_rows(inner_rows(features(cot_g), low_down_g)),
        by_rows(grad_gateup[:, :rank]),
        by_rows(grad_gateup[:, rank:]),
        by_rows(grad_qkv[:, :rank]),
        by_rows(grad_qkv[:, rank : 2 * rank]),
        by_rows(grad_qkv[:, 2 * rank :]),
    ]
    sizes = [piece.shape[1] for piece in pieces]
    packed = jnp.concatenate(pieces, axis=1)
    summed = lax.psum_scatter(packed, PLANE + ("c",), scatter_dimension=0, tiled=False)
    everyone = lax.all_gather(summed.astype(bf16), ALL, axis=0, tiled=False)
    found, at = [], 0
    for size in sizes:
        found.append(everyone[:, at : at + size].astype(f32))
        at += size

    def units_order(array):
        return array.reshape(-1, rank)

    def rows_order(array):
        rows_each = array.shape[1]
        ordered = jnp.transpose(array.reshape(16, 4, 2, rows_each, rank), (1, 0, 2, 3, 4))
        return ordered.reshape(-1, rank)

    g_gate, g_up, g_down_shrink = (units_order(array) for array in found[:3])
    rest = [rows_order(array) for array in found[3:]]
    g_q, g_k, g_v, g_out_shrink, g_out_expand, g_down_expand = rest[:6]
    return (
        from_rows(output),
        from_rows(grad_input),
        jnp.concatenate(rest[8:11], axis=1),
        g_q.T,
        g_k.T,
        g_v.T,
        g_out_shrink,
        g_out_expand.T,
        jnp.concatenate(rest[6:8], axis=1),
        g_gate.T,
        g_up.T,
        g_down_shrink,
        g_down_expand.T,
    )


def solution(mesh):
    fine = Mesh(mesh.devices.reshape(2, 2, 4, 4, 2), ALL)
    split = P(ALL, None)
    placed = (split, P(), P()) + (split,) * 7 + (P(),) * 14 + (split,)
    return jax.shard_map(
        local,
        mesh=fine,
        in_specs=placed,
        out_specs=(split, split) + (P(),) * 11,
        check_vma=False,
    )
```

```python
from functools import partial

import jax
import jax.numpy as jnp
from jax import lax
from jax.experimental import pallas as pl
from jax.experimental.pallas import tpu as pltpu
from jax.sharding import Mesh, PartitionSpec as P

HEAD_SIZE = 256
RANK = 16
HALF = 64
GROUP = 512

ALL = ("zh", "zl", "x", "y", "c")
PLANE = ("zh", "zl", "x")

norm_eps = 1e-06
rope_theta = 1000042.0
neg_big = -1e30
far = 1 << 30

f32 = jnp.float32
bf16 = jnp.bfloat16


def product(left, right):
    return jnp.dot(left, right, preferred_element_type=f32)


def times_transposed(left, right):
    return lax.dot_general(left, right, (((1,), (1,)), ((), ())), preferred_element_type=f32)


def inner_rows(left, right):
    return lax.dot_general(left, right, (((0,), (0,)), ((), ())), preferred_element_type=f32)


def row_scale(value_matrix):
    return lax.rsqrt(jnp.mean(value_matrix * value_matrix, axis=-1, keepdims=True) + norm_eps)


def norm_back(value_matrix, scale, gain, grad):
    scaled = gain * grad
    return scale * scaled - value_matrix * (scale * scale * scale) * jnp.mean(
        value_matrix * scaled, axis=-1, keepdims=True
    )


def rotate(value_matrix):
    middle = value_matrix.shape[-1] // 2
    return jnp.concatenate([-value_matrix[..., middle:], value_matrix[..., :middle]], axis=-1)


def rope_tables(positions, width):
    middle = width // 2
    inverse = rope_theta ** (-(jnp.arange(middle, dtype=f32) * 2.0) / width)
    angles = positions.astype(f32)[:, None] * inverse[None, :]
    cos_half, sin_half = jnp.cos(angles), jnp.sin(angles)
    cos_table = jnp.concatenate([cos_half, cos_half], axis=-1)[:, None, :]
    sin_table = jnp.concatenate([sin_half, sin_half], axis=-1)[:, None, :]
    return (cos_table, sin_table)


RING = {"x": ("x",), "y": ("y",), "z": ("zh", "zl")}


def swap_cores(value):
    return lax.ppermute(value, "c", [(0, 1), (1, 0)])


def shift(value, ring, step):
    return lax.ppermute(value, RING[ring], [(i, (i + step) % 4) for i in range(4)])


def place_in(ring):
    return lax.axis_index(RING[ring])


def gather_near(value, ring, axis=0):
    return jnp.concatenate([value] + [shift(value, ring, -step) for step in (1, 2, 3)], axis=axis)


def gather_ring(value, ring):
    at = place_in(ring)
    whole_ring = jnp.zeros((4,) + value.shape, value.dtype)
    whole_ring = lax.dynamic_update_index_in_dim(whole_ring, value, at, 0)
    for step in (1, 2, 3):
        got = shift(value, ring, -step)
        whole_ring = lax.dynamic_update_index_in_dim(whole_ring, got, (at + step) % 4, 0)
    return whole_ring


def sum_near(blocks):
    got = [shift(blocks[step], "y", step) for step in (2, 1, 3)]
    total = blocks[0].astype(f32)
    for term in got:
        total = total + term.astype(f32)
    return total


def sum_ring(terms, ring):
    at = place_in(ring)
    got = [
        shift(lax.dynamic_index_in_dim(terms, (at + step) % 4, 0, keepdims=False).astype(bf16), ring, step)
        for step in (1, 2, 3)
    ]
    total = lax.dynamic_index_in_dim(terms, at, 0, keepdims=False)
    for term in got:
        total = total + term.astype(f32)
    return total


CORNER = ("zh", "zl", "c")
PARTNER = [(4 * zh + 2 * zl + c, 4 * zh + 2 * (1 - zl) + c) for zh in (0, 1) for zl in (0, 1) for c in (0, 1)]
LATER = [[(2 * zl + 1, 4 + 2 * (zl ^ flip)) for zl in (0, 1)] for flip in (0, 1)]
EARLIER = [[(to, came) for came, to in pairs] for pairs in LATER]
ROW_AHEAD = ("zh", "x", "c")


def shift_ahead(value, step):
    return lax.ppermute(value, ROW_AHEAD, [(8 + 2 * i, 8 + 2 * ((i + step) % 4)) for i in range(4)])


def gather_keys(key):
    line = gather_near(key[None], "x")
    own = jnp.stack([line, lax.ppermute(line, CORNER, PARTNER)])
    ahead = jnp.stack([lax.ppermute(line, CORNER, LATER[0]), lax.ppermute(line, CORNER, LATER[1])])
    return own, ahead


def gather_values(value):
    pair = jnp.stack([value, lax.ppermute(value, CORNER, PARTNER)])
    pair_ahead = jnp.stack([lax.ppermute(value, CORNER, LATER[0]), lax.ppermute(value, CORNER, LATER[1])])
    own = gather_near(pair[None], "x")
    ahead = jnp.concatenate([pair_ahead[None]] + [shift_ahead(pair_ahead, -step)[None] for step in (1, 2, 3)])
    return own, ahead


def row_before(own, ahead, c):
    return jnp.where(c == 0, ahead, lax.ppermute(own, "c", [(0, 1)]))


def sum_keys(own, before, c):
    got = lax.ppermute(before, "c", [(1, 0)])
    own = own.astype(f32) + got.astype(f32)
    line = own[0] + lax.ppermute(own[1].astype(bf16), CORNER, PARTNER).astype(f32)
    for flip in (0, 1):
        line = line + lax.ppermute(before[flip], CORNER, EARLIER[flip]).astype(f32)
    sent = line.astype(bf16)
    total = line[0]
    for step in (1, 2, 3):
        total = total + shift(sent[step], "x", step).astype(f32)
    return total


def sum_values(own, before, c):
    got = lax.ppermute(before, "c", [(1, 0)])
    own = own.astype(f32) + got.astype(f32)
    sent = own.astype(bf16)
    pair, pair_before = own[0], before[0].astype(f32)
    for step in (1, 2, 3):
        pair = pair + shift(sent[step], "x", step).astype(f32)
        pair_before = pair_before + shift_ahead(before[step], step).astype(f32)
    sent_before = pair_before.astype(bf16)
    total = pair[0] + lax.ppermute(pair[1].astype(bf16), CORNER, PARTNER).astype(f32)
    for flip in (0, 1):
        total = total + lax.ppermute(sent_before[flip], CORNER, EARLIER[flip]).astype(f32)
    return total


def allowed_mask(own_pos, own_start, key_pos):
    return (key_pos <= own_pos) & (key_pos >= own_start)


def attend_kernel(
    active,
    q_ref,
    pos_ref,
    start_ref,
    kpos_ref,
    kprev_ref,
    kown_ref,
    vprev_ref,
    vown_ref,
    mixed_ref,
    lse_ref,
    top,
    total,
    accum,
):
    step = pl.program_id(0)

    @pl.when(step == 0)
    def _():
        top[...] = jnp.full(top.shape, neg_big, f32)
        total[...] = jnp.zeros(total.shape, f32)
        accum[...] = jnp.zeros(accum.shape, f32)

    for side, k_ref, v_ref in ((0, kprev_ref, vprev_ref), (1, kown_ref, vown_ref)):

        @pl.when(active[side * 8 + step] != 0)
        def _():
            key, value = k_ref[0, 0], v_ref[0, 0]
            allowed = allowed_mask(pos_ref[...], start_ref[...], kpos_ref[0, side])
            for head in range(2):
                scores = times_transposed(q_ref[:, head * HEAD_SIZE : (head + 1) * HEAD_SIZE], key)
                scores = jnp.where(allowed, scores, neg_big)
                top_old = top[head]
                top_new = jnp.maximum(top_old, jnp.max(scores, axis=-1, keepdims=True))
                weights_p = jnp.where(allowed, jnp.exp(scores - top_new), 0.0)
                damping = jnp.exp(top_old - top_new)
                total[head] = total[head] * damping + jnp.sum(weights_p, axis=-1, keepdims=True)
                accum[head] = accum[head] * damping + product(weights_p.astype(bf16), value)
                top[head] = top_new

    @pl.when(step == 7)
    def _():
        for head in range(2):
            mixed_ref[:, head * HEAD_SIZE : (head + 1) * HEAD_SIZE] = accum[head] / total[head]
            lse_ref[head] = top[head] + jnp.log(total[head])


def attend_back_kernel(
    active,
    q_ref,
    pos_ref,
    start_ref,
    kpos_ref,
    kprev_ref,
    kown_ref,
    vprev_ref,
    vown_ref,
    mixed_ref,
    lse_ref,
    dout_ref,
    dq_ref,
    dkprev_ref,
    dkown_ref,
    dvprev_ref,
    dvown_ref,
    delta,
):
    step = pl.program_id(0)

    @pl.when(step == 0)
    def _():
        dq_ref[...] = jnp.zeros(dq_ref.shape, f32)
        for head in range(2):
            cols = slice(head * HEAD_SIZE, (head + 1) * HEAD_SIZE)
            delta[head] = jnp.sum(dout_ref[:, cols].astype(f32) * mixed_ref[:, cols], axis=-1, keepdims=True)

    for side, k_ref, v_ref, dk_ref, dv_ref in (
        (0, kprev_ref, vprev_ref, dkprev_ref, dvprev_ref),
        (1, kown_ref, vown_ref, dkown_ref, dvown_ref),
    ):

        @pl.when(active[side * 8 + step] == 0)
        def _():
            dk_ref[...] = jnp.zeros(dk_ref.shape, bf16)
            dv_ref[...] = jnp.zeros(dv_ref.shape, bf16)

        @pl.when(active[side * 8 + step] != 0)
        def _():
            key, value = k_ref[0, 0], v_ref[0, 0]
            allowed = allowed_mask(pos_ref[...], start_ref[...], kpos_ref[0, side])
            dk = jnp.zeros((GROUP, HEAD_SIZE), f32)
            dv = jnp.zeros((GROUP, HEAD_SIZE), f32)
            for head in range(2):
                cols = slice(head * HEAD_SIZE, (head + 1) * HEAD_SIZE)
                query, dout = q_ref[:, cols], dout_ref[:, cols]
                scores = times_transposed(query, key)
                weights_p = jnp.where(allowed, jnp.exp(scores - lse_ref[head]), 0.0)
                dprobs = times_transposed(dout, value)
                dscores = (weights_p * (dprobs - delta[head])).astype(bf16)
                dq_ref[:, cols] += product(dscores, key)
                dk = dk + inner_rows(dscores, query)
                dv = dv + inner_rows(weights_p.astype(bf16), dout)
            dk_ref[0, 0] = dk.astype(bf16)
            dv_ref[0, 0] = dv.astype(bf16)


def whole(shape):
    return pl.BlockSpec(shape, lambda i, *refs: (0,) * len(shape))


def key_spec():
    return pl.BlockSpec((1, 1, GROUP, HEAD_SIZE), lambda i, active: (i // 4, i % 4, 0, 0))


def value_spec():
    return pl.BlockSpec((1, 1, GROUP, HEAD_SIZE), lambda i, active: (i % 4, i // 4, 0, 0))


def common_specs():
    return [
        whole((GROUP, GROUP)),
        whole((GROUP, 1)),
        whole((GROUP, 1)),
        pl.BlockSpec((1, 2, 1, GROUP), lambda i, active: (i, 0, 0, 0)),
        key_spec(),
        key_spec(),
        value_spec(),
        value_spec(),
    ]


def attend(active, *operands):
    return pl.pallas_call(
        attend_kernel,
        grid_spec=pltpu.PrefetchScalarGridSpec(
            num_scalar_prefetch=1,
            grid=(8,),
            in_specs=common_specs(),
            out_specs=[whole((GROUP, GROUP)), whole((2, GROUP, 1))],
            scratch_shapes=[
                pltpu.VMEM((2, GROUP, 1), f32),
                pltpu.VMEM((2, GROUP, 1), f32),
                pltpu.VMEM((2, GROUP, HEAD_SIZE), f32),
            ],
        ),
        out_shape=[
            jax.ShapeDtypeStruct((GROUP, GROUP), f32),
            jax.ShapeDtypeStruct((2, GROUP, 1), f32),
        ],
        compiler_params=pltpu.CompilerParams(vmem_limit_bytes=40 << 20),
        cost_estimate=pl.CostEstimate(flops=6 << 30, bytes_accessed=10 << 20, transcendentals=8 << 20),
        name="attend",
    )(active, *operands)


def attend_back(active, *operands):
    return pl.pallas_call(
        attend_back_kernel,
        grid_spec=pltpu.PrefetchScalarGridSpec(
            num_scalar_prefetch=1,
            grid=(8,),
            in_specs=common_specs() + [whole((GROUP, GROUP)), whole((2, GROUP, 1)), whole((GROUP, GROUP))],
            out_specs=[whole((GROUP, GROUP)), key_spec(), key_spec(), value_spec(), value_spec()],
            scratch_shapes=[pltpu.VMEM((2, GROUP, 1), f32)],
        ),
        out_shape=[jax.ShapeDtypeStruct((GROUP, GROUP), f32)]
        + [jax.ShapeDtypeStruct((2, 4, GROUP, HEAD_SIZE), bf16)] * 2
        + [jax.ShapeDtypeStruct((4, 2, GROUP, HEAD_SIZE), bf16)] * 2,
        compiler_params=pltpu.CompilerParams(vmem_limit_bytes=40 << 20),
        cost_estimate=pl.CostEstimate(flops=12 << 30, bytes_accessed=20 << 20, transcendentals=8 << 20),
        name="attend_back",
    )(active, *operands)


def local(
    hidden_in,
    gain_attn,
    gain_ffn,
    w_query,
    w_key,
    w_value,
    w_out,
    w_gate,
    w_up,
    w_down,
    qkv_shrink,
    query_expand,
    key_expand,
    value_expand,
    out_shrink,
    out_expand,
    gateup_shrink,
    gate_expand,
    up_expand,
    down_shrink,
    down_expand,
    lengths,
    adapter,
    packed_pos,
    cotangent,
):
    zh, zl, x, y, c = (lax.axis_index(name) for name in ALL)
    row = 2 * zh + c
    mine, other = 2 * y + c, 2 * y + 1 - c
    factor = HEAD_SIZE ** (-0.5)
    rank = out_shrink.shape[1]

    def to_rows(value):
        own = lax.dynamic_slice_in_dim(value, c * HALF, HALF, 0)
        sent = lax.dynamic_slice_in_dim(value, (1 - c) * HALF, HALF, 0)
        return jnp.concatenate([own, swap_cores(sent)], axis=0)

    def from_rows(value):
        own, got = value[:HALF], swap_cores(value[HALF:])
        return jnp.where(c == 0, jnp.concatenate([own, got], 0), jnp.concatenate([got, own], 0))

    hidden = to_rows(hidden_in)
    cot = to_rows(cotangent)

    def roll(array, by, axis):
        return lax.dynamic_slice_in_dim(jnp.concatenate([array, array], axis), by, array.shape[axis], axis)

    spread = packed_pos.reshape(2, 2, 4, 4, 2, 2, HALF)
    spread = jnp.transpose(spread, (0, 5, 1, 2, 3, 4, 6))
    rows_pos = jnp.stack([spread[:, 0], spread[:, 1, :, :, :, ::-1]], axis=1).reshape(4, 2, 4, 4, 128)
    rows_pos = roll(roll(roll(rows_pos, zl, 1), x, 2), y, 3).reshape(4, 8, GROUP)
    own_row = lax.dynamic_index_in_dim(rows_pos, row, 0, keepdims=False)
    prev_row = lax.dynamic_index_in_dim(rows_pos, jnp.maximum(row - 1, 0), 0, keepdims=False)
    prev_row = jnp.where(row == 0, far, prev_row)
    key_pos = jnp.stack([prev_row, own_row], axis=1)
    group_pos = own_row[0]
    seq_ends = jnp.cumsum(lengths)
    starts = seq_ends - lengths
    member = (group_pos[:, None] >= starts[None, :]) & (group_pos[:, None] < seq_ends[None, :])
    member_int = member.astype(jnp.int32)
    group_start = jnp.sum(member_int * starts[None, :], axis=1)
    group_owner = jnp.sum(member_int * adapter[None, :], axis=1)
    low, high = jnp.min(group_start), jnp.max(group_pos)
    active = (jnp.min(key_pos, axis=2) <= high) & (jnp.max(key_pos, axis=2) >= low)
    active = jnp.transpose(active).reshape(16).astype(jnp.int32)
    columns = jnp.arange(rank, dtype=jnp.int32) // RANK
    select_g = (group_owner[:, None] == columns[None, :]).astype(f32)
    select = select_g[:128]
    cos_table, sin_table = rope_tables(group_pos - group_start, HEAD_SIZE)

    def column_slices(weight):
        rows_here, width = weight.shape
        parts = jnp.transpose(weight.reshape(rows_here, 16, 8, width // 128), (2, 0, 1, 3))
        return parts.reshape(8, rows_here, width // 8)

    heads_q = w_query.reshape(16, 4, 512)
    heads_kv = jnp.concatenate([w_key.reshape(16, 4, 256), w_value.reshape(16, 4, 256)], axis=2)
    qkv_parts = jnp.transpose(jnp.stack([heads_q, heads_kv], axis=2), (1, 2, 0, 3)).reshape(8, 16, 512)
    parts = jnp.concatenate([qkv_parts, column_slices(w_gate), column_slices(w_up)], axis=2)
    parts = lax.all_to_all(parts, ("y", "c"), split_axis=0, concat_axis=0, tiled=True).reshape(128, 2560)
    first = gather_ring(gather_ring(parts[:, :256], "x"), "z").reshape(2048, 256)
    second = jnp.swapaxes(gather_ring(gather_ring(parts[:, 256:512], "z"), "x"), 0, 1).reshape(2048, 256)
    qkv_mine = jnp.concatenate([first, second], axis=1)
    qkv_other = swap_cores(qkv_mine)
    wo = lax.all_gather(w_out, ALL, axis=0, tiled=True)
    wd_mine = lax.all_gather(w_down, PLANE, axis=0, tiled=True)
    wgu_mine = lax.all_gather(parts[:, 512:], PLANE, axis=0, tiled=True)
    wgu_other, wd_other = swap_cores(wgu_mine), swap_cores(wd_mine)

    def columns_of(array, width):
        return lax.dynamic_slice_in_dim(array, y * width, width, 1)

    inputs = hidden.astype(f32)
    scale_in = row_scale(inputs)
    normed = (inputs * scale_in * gain_attn).astype(bf16)
    normed_g = gather_near(normed, "y")
    cot_g = gather_near(cot, "y")
    q_expand = columns_of(query_expand, 512)
    k_expand = columns_of(key_expand, 256)
    v_expand = columns_of(value_expand, 256)
    low_qkv = (product(normed_g, qkv_shrink) * jnp.tile(select_g, (1, 3))).astype(bf16)
    lin_mine, lin_other = product(normed_g, qkv_mine), product(normed_g, qkv_other)
    query_lin = jnp.where(c == 0, lin_mine, lin_other) + product(low_qkv[:, :rank], q_expand)
    kv_lin = jnp.where(c == 0, lin_other, lin_mine)
    key_lin = kv_lin[:, :256] + product(low_qkv[:, rank : 2 * rank], k_expand)
    value_lin = kv_lin[:, 256:] + product(low_qkv[:, 2 * rank :], v_expand)
    query_heads = query_lin.reshape(GROUP, 2, HEAD_SIZE)
    key_heads = key_lin.reshape(GROUP, 1, HEAD_SIZE)
    query = (query_heads * cos_table + rotate(query_heads) * sin_table).astype(bf16)
    query = (query * bf16(factor)).reshape(GROUP, 512)
    key = (key_heads * cos_table + rotate(key_heads) * sin_table).astype(bf16).reshape(GROUP, 256)

    k_own, k_ahead = gather_keys(key)
    v_own, v_ahead = gather_values(value_lin.astype(bf16))
    k_prev, v_prev = row_before(k_own, k_ahead, c), row_before(v_own, v_ahead, c)
    attended = (
        query,
        group_pos[:, None],
        group_start[:, None],
        key_pos.reshape(8, 2, 1, GROUP),
        k_prev,
        k_own,
        v_prev,
        v_own,
    )
    mixed_f, lse = attend(active, *attended)
    mixed = mixed_f.astype(bf16)

    heads = jnp.zeros((4, 128, 512), bf16)
    heads = lax.dynamic_update_index_in_dim(heads, mixed[:128], y, 0)
    for step in (1, 2, 3):
        got = shift(mixed[step * 128 : (step + 1) * 128], "y", step)
        heads = lax.dynamic_update_index_in_dim(heads, got, (y - step) % 4, 0)
    mixed_tok = jnp.transpose(heads, (1, 0, 2)).reshape(128, 2048)
    low_out = (product(mixed_tok, out_shrink) * select).astype(bf16)
    middle = inputs + product(mixed_tok, wo) + product(low_out, out_expand)
    scale_mid = row_scale(middle)
    normed_mid = (middle * scale_mid * gain_ffn).astype(bf16)
    normed_mid_g = gather_near(normed_mid, "y")

    select_two = jnp.tile(select_g, (1, 2))
    low_gu = (product(normed_mid_g, gateup_shrink) * select_two).astype(bf16)
    grad_low_down = (times_transposed(cot_g, down_expand) * select_g).astype(bf16)
    result = jnp.zeros((GROUP, 2048), f32)
    low_down_part = jnp.zeros((GROUP, rank), f32)
    grad_mid_part = jnp.zeros((GROUP, 2048), f32)
    grad_low_part = jnp.zeros((GROUP, 2 * rank), f32)
    unit_grads = []
    units = 1024
    for wgu, wd, at in ((wgu_mine, wd_mine, mine), (wgu_other, wd_other, other)):
        wg, wu = wgu[:, :units], wgu[:, units:]
        g_expand = lax.dynamic_slice_in_dim(gate_expand.reshape(rank, 16, 8, 64), at, 1, 2).reshape(rank, units)
        u_expand = lax.dynamic_slice_in_dim(up_expand.reshape(rank, 16, 8, 64), at, 1, 2).reshape(rank, units)
        d_shrink = lax.dynamic_slice_in_dim(down_shrink.reshape(16, 8, 64, rank), at, 1, 1).reshape(units, rank)
        gate_pre = product(normed_mid_g, wg) + product(low_gu[:, :rank], g_expand)
        up_pre = product(normed_mid_g, wu) + product(low_gu[:, rank:], u_expand)
        sigmoid_g = jax.nn.sigmoid(gate_pre)
        silu_gate = gate_pre * sigmoid_g
        active_units = (silu_gate * up_pre).astype(bf16)
        result = result + product(active_units, wd)
        low_down_part = low_down_part + product(active_units, d_shrink)
        grad_active = times_transposed(cot_g, wd) + times_transposed(grad_low_down, d_shrink)
        grad_gate = (grad_active * up_pre * sigmoid_g * (1.0 + gate_pre * (1.0 - sigmoid_g))).astype(bf16)
        grad_up = (grad_active * silu_gate).astype(bf16)
        grad_mid_part = grad_mid_part + times_transposed(grad_gate, wg) + times_transposed(grad_up, wu)
        grad_low_part = grad_low_part + jnp.concatenate(
            [times_transposed(grad_gate, g_expand), times_transposed(grad_up, u_expand)], axis=1
        )
        unit_grads.append(
            (
                inner_rows(grad_gate, low_gu[:, :rank]),
                inner_rows(grad_up, low_gu[:, rank:]),
                inner_rows(active_units, grad_low_down),
            )
        )

    def sum_tokens(part):
        sent = part.astype(bf16)
        return sum_near([sent[i * 128 : (i + 1) * 128] for i in range(4)])

    back_low = sum_tokens(grad_low_part)
    back = sum_tokens(grad_mid_part)
    ahead_low = sum_tokens(low_down_part)
    ahead = sum_tokens(result)
    low_down = (ahead_low * select).astype(bf16)
    output = (middle + ahead + product(low_down, down_expand)).astype(bf16)
    grad_low_gu = (back_low * jnp.tile(select, (1, 2))).astype(bf16)
    grad_normed_mid = back + times_transposed(grad_low_gu, gateup_shrink)
    cot_f = cot.astype(f32)
    grad_middle = cot_f + norm_back(middle, scale_mid, gain_ffn, grad_normed_mid)
    grad_attn_out = grad_middle.astype(bf16)
    grad_low_out = (times_transposed(grad_attn_out, out_expand) * select).astype(bf16)
    grad_mixed = (times_transposed(grad_attn_out, wo) + times_transposed(grad_low_out, out_shrink)).astype(bf16)

    def slices_near(array):
        def columns_at(step):
            return lax.dynamic_slice_in_dim(array, ((y + step) % 4) * 512, 512, 1)

        return jnp.concatenate([columns_at(0)] + [shift(columns_at(4 - step), "y", -step) for step in (1, 2, 3)])

    dout = slices_near(grad_mixed)
    dq, dk_prev, dk_own, dv_prev, dv_own = attend_back(active, *attended, mixed_f, lse, dout)
    dk, dv = sum_keys(dk_own, dk_prev, c), sum_values(dv_own, dv_prev, c)
    query_back = (dq * factor).astype(bf16).astype(f32).reshape(GROUP, 2, HEAD_SIZE)
    key_back = dk.astype(bf16).astype(f32).reshape(GROUP, 1, HEAD_SIZE)
    grad_value = dv.astype(bf16)
    grad_query = (query_back * cos_table - rotate(query_back * sin_table)).astype(bf16).reshape(GROUP, 512)
    grad_key = (key_back * cos_table - rotate(key_back * sin_table)).astype(bf16).reshape(GROUP, 256)
    grad_kv = jnp.concatenate([grad_key, grad_value], axis=1)

    grad_low_part = jnp.concatenate(
        [
            times_transposed(grad_query, q_expand),
            times_transposed(grad_key, k_expand),
            times_transposed(grad_value, v_expand),
        ],
        axis=1,
    )
    grad_low_qkv = (sum_tokens(grad_low_part) * jnp.tile(select, (1, 3))).astype(bf16)
    for_mine = jnp.where(c == 0, grad_query, grad_kv)
    for_other = jnp.where(c == 0, grad_kv, grad_query)
    grad_normed_part = times_transposed(for_mine, qkv_mine) + times_transposed(for_other, qkv_other)
    grad_normed = sum_tokens(grad_normed_part) + times_transposed(grad_low_qkv, qkv_shrink)
    grad_input = (grad_middle + norm_back(inputs, scale_in, gain_attn, grad_normed)).astype(bf16)

    def features(array):
        return lax.dynamic_slice_in_dim(array, y * 512, 512, 1)

    def by_halves(pair_at):
        own, others = unit_grads[0][pair_at], unit_grads[1][pair_at]
        own, others = own.reshape(16, 1, 64, rank), others.reshape(16, 1, 64, rank)
        ordered = jnp.where(c == 0, jnp.concatenate([own, others], 1), jnp.concatenate([others, own], 1))
        return ordered.reshape(32, 64, rank)

    def by_rows(array):
        return array.reshape(32, array.shape[0] // 32, rank)

    low_near = gather_near(jnp.concatenate([low_down, grad_low_gu, grad_low_out, low_out], axis=1), "y")
    low_down_g, grad_low_gu_g = low_near[:, :rank], low_near[:, rank : 3 * rank]
    grad_low_out_g, low_out_g = low_near[:, 3 * rank : 4 * rank], low_near[:, 4 * rank :]
    grad_gateup = inner_rows(features(normed_mid_g), grad_low_gu_g)
    early = [
        by_halves(0),
        by_halves(1),
        by_halves(2),
        by_rows(inner_rows(mixed, grad_low_out_g)),
        by_rows(inner_rows(slices_near(grad_attn_out), low_out_g)),
        by_rows(inner_rows(features(cot_g), low_down_g)),
        by_rows(grad_gateup[:, :rank]),
        by_rows(grad_gateup[:, rank:]),
    ]
    early_sum = lax.psum_scatter(
        jnp.concatenate(early, axis=1), PLANE + ("c",), scatter_dimension=0, tiled=False
    )
    early_all = lax.all_gather(early_sum.astype(bf16), ALL, axis=0, tiled=False)

    grad_qkv = inner_rows(features(normed_g), gather_near(grad_low_qkv, "y"))
    late = [
        by_rows(inner_rows(grad_query, low_qkv[:, :rank])),
        by_rows(inner_rows(grad_key, low_qkv[:, rank : 2 * rank])),
        by_rows(inner_rows(grad_value, low_qkv[:, 2 * rank :])),
        by_rows(grad_qkv[:, :rank]),
        by_rows(grad_qkv[:, rank : 2 * rank]),
        by_rows(grad_qkv[:, 2 * rank :]),
    ]
    terms = jnp.concatenate(late, axis=1)
    terms = terms.reshape(16, 2, terms.shape[1], rank)
    kept = lax.dynamic_index_in_dim(terms, c, 1, keepdims=False)
    given = lax.dynamic_index_in_dim(terms, 1 - c, 1, keepdims=False).astype(bf16)
    terms = (kept + swap_cores(given).astype(f32)).reshape(4, 4, -1, rank)
    late_sum = sum_ring(sum_ring(terms, "z"), "x").astype(bf16)
    late_all = gather_ring(gather_ring(gather_ring(late_sum, "x"), "z"), "y")
    late_other = swap_cores(late_all)
    late_all = jnp.where(c == 0, jnp.stack([late_all, late_other], 3), jnp.stack([late_other, late_all], 3))

    def cut(array, axis, pieces):
        found, at = [], 0
        for piece in pieces:
            found.append(lax.slice_in_dim(array, at, at + piece.shape[1], axis=axis).astype(f32))
            at += piece.shape[1]
        return found

    def rows_order(array):
        ordered = jnp.transpose(array.reshape(16, 4, 2, array.shape[1], rank), (1, 0, 2, 3, 4))
        return ordered.reshape(-1, rank)

    early_found = cut(early_all, 1, early)
    g_gate, g_up, g_down_shrink = (array.reshape(-1, rank) for array in early_found[:3])
    g_out_shrink, g_out_expand, g_down_expand, g_gate_low, g_up_low = (rows_order(a) for a in early_found[3:])
    g_q, g_k, g_v, g_q_low, g_k_low, g_v_low = (a.reshape(-1, rank) for a in cut(late_all, 4, late))
    return (
        from_rows(output),
        from_rows(grad_input),
        jnp.concatenate([g_q_low, g_k_low, g_v_low], axis=1),
        g_q.T,
        g_k.T,
        g_v.T,
        g_out_shrink,
        g_out_expand.T,
        jnp.concatenate([g_gate_low, g_up_low], axis=1),
        g_gate.T,
        g_up.T,
        g_down_shrink,
        g_down_expand.T,
    )


def solution(mesh):
    fine = Mesh(mesh.devices.reshape(2, 2, 4, 4, 2), ALL)
    split = P(ALL, None)
    placed = (split, P(), P()) + (split,) * 7 + (P(),) * 14 + (split,)
    return jax.shard_map(
        local,
        mesh=fine,
        in_specs=placed,
        out_specs=(split, split) + (P(),) * 11,
        check_vma=False,
    )
```

```python
from functools import partial

import jax
import jax.numpy as jnp
from jax import lax
from jax.experimental import pallas as pl
from jax.experimental.pallas import tpu as pltpu
from jax.sharding import Mesh, PartitionSpec as P

HEAD_SIZE = 256
RANK = 16
HALF = 64
GROUP = 512

ALL = ("zh", "zl", "x", "y", "c")

norm_eps = 1e-06
rope_theta = 1000042.0
neg_big = -1e30
far = 1 << 30

f32 = jnp.float32
bf16 = jnp.bfloat16


def product(left, right):
    return jnp.dot(left, right, preferred_element_type=f32)


def times_transposed(left, right):
    return lax.dot_general(left, right, (((1,), (1,)), ((), ())), preferred_element_type=f32)


def inner_rows(left, right):
    return lax.dot_general(left, right, (((0,), (0,)), ((), ())), preferred_element_type=f32)


def row_scale(value_matrix):
    return lax.rsqrt(jnp.mean(value_matrix * value_matrix, axis=-1, keepdims=True) + norm_eps)


def norm_back(value_matrix, scale, gain, grad):
    scaled = gain * grad
    return scale * scaled - value_matrix * (scale * scale * scale) * jnp.mean(
        value_matrix * scaled, axis=-1, keepdims=True
    )


def rotate(value_matrix):
    middle = value_matrix.shape[-1] // 2
    return jnp.concatenate([-value_matrix[..., middle:], value_matrix[..., :middle]], axis=-1)


def rope_tables(positions, width):
    middle = width // 2
    inverse = rope_theta ** (-(jnp.arange(middle, dtype=f32) * 2.0) / width)
    angles = positions.astype(f32)[:, None] * inverse[None, :]
    cos_half, sin_half = jnp.cos(angles), jnp.sin(angles)
    cos_table = jnp.concatenate([cos_half, cos_half], axis=-1)[:, None, :]
    sin_table = jnp.concatenate([sin_half, sin_half], axis=-1)[:, None, :]
    return (cos_table, sin_table)


RING = {"x": ("x",), "y": ("y",), "z": ("zh", "zl")}


def swap_cores(value):
    return lax.ppermute(value, "c", [(0, 1), (1, 0)])


def shift(value, ring, step):
    return lax.ppermute(value, RING[ring], [(i, (i + step) % 4) for i in range(4)])


def place_in(ring):
    return lax.axis_index(RING[ring])


def gather_near(value, ring, axis=0):
    return jnp.concatenate([value] + [shift(value, ring, -step) for step in (1, 2, 3)], axis=axis)


def gather_ring(value, ring):
    at = place_in(ring)
    whole_ring = jnp.zeros((4,) + value.shape, value.dtype)
    whole_ring = lax.dynamic_update_index_in_dim(whole_ring, value, at, 0)
    for step in (1, 2, 3):
        got = shift(value, ring, -step)
        whole_ring = lax.dynamic_update_index_in_dim(whole_ring, got, (at + step) % 4, 0)
    return whole_ring


def sum_near(blocks, ring):
    got = [shift(blocks[step], ring, step) for step in (2, 1, 3)]
    total = blocks[0].astype(f32)
    for term in got:
        total = total + term.astype(f32)
    return total


def sum_ring(terms, ring):
    at = place_in(ring)
    got = [
        shift(lax.dynamic_index_in_dim(terms, (at + step) % 4, 0, keepdims=False).astype(bf16), ring, step)
        for step in (1, 2, 3)
    ]
    total = lax.dynamic_index_in_dim(terms, at, 0, keepdims=False)
    for term in got:
        total = total + term.astype(f32)
    return total


CORNER = ("zh", "zl", "c")
PARTNER = [(4 * zh + 2 * zl + c, 4 * zh + 2 * (1 - zl) + c) for zh in (0, 1) for zl in (0, 1) for c in (0, 1)]
LATER = [[(2 * zl + 1, 4 + 2 * (zl ^ flip)) for zl in (0, 1)] for flip in (0, 1)]
EARLIER = [[(to, came) for came, to in pairs] for pairs in LATER]
ROW_AHEAD = ("zh", "x", "c")


def shift_ahead(value, step):
    return lax.ppermute(value, ROW_AHEAD, [(8 + 2 * i, 8 + 2 * ((i + step) % 4)) for i in range(4)])


def after(value, *others):
    return lax.optimization_barrier((value,) + others)[0]


def gather_row(key, value, c):
    lines = [key] + [shift(key, "x", -step) for step in (1, 2, 3)]
    pair = [value, lax.ppermute(value, CORNER, PARTNER)]
    pair_ahead = [lax.ppermute(value, CORNER, pairs) for pairs in LATER]
    lines, pair, pair_ahead = lax.optimization_barrier((lines, pair, pair_ahead))
    line, pair, pair_ahead = jnp.stack(lines), jnp.stack(pair), jnp.stack(pair_ahead)
    k_own = jnp.stack([line, lax.ppermute(line, CORNER, PARTNER)])
    k_ahead = jnp.stack([lax.ppermute(line, CORNER, pairs) for pairs in LATER])
    v_own = jnp.stack([pair] + [shift(pair, "x", -step) for step in (1, 2, 3)])
    v_ahead = jnp.stack([pair_ahead] + [shift_ahead(pair_ahead, -step) for step in (1, 2, 3)])
    k_prev = jnp.where(c == 0, k_ahead, lax.ppermute(k_own, "c", [(0, 1)]))
    v_prev = jnp.where(c == 0, v_ahead, lax.ppermute(v_own, "c", [(0, 1)]))
    return k_own, k_prev, v_own, v_prev


def sum_row(k_own, k_prev, v_own, v_prev):
    k_got, v_got = (lax.ppermute(prev, "c", [(1, 0)]) for prev in (k_prev, v_prev))
    k_own, v_own = k_own.astype(f32) + k_got.astype(f32), v_own.astype(f32) + v_got.astype(f32)
    k_sent, v_sent = k_own[1].astype(bf16), v_own.astype(bf16)
    line, pair, pair_prev = k_own[0], v_own[0], v_prev[0].astype(f32)
    lines = [lax.ppermute(k_sent, CORNER, PARTNER)]
    lines += [lax.ppermute(k_prev[flip], CORNER, EARLIER[flip]) for flip in (0, 1)]
    pairs = [shift(v_sent[step], "x", step) for step in (1, 2, 3)]
    pairs_prev = [shift_ahead(v_prev[step], step) for step in (1, 2, 3)]
    lines, pairs, pairs_prev = lax.optimization_barrier((lines, pairs, pairs_prev))
    for term in lines:
        line = line + term.astype(f32)
    for term in pairs:
        pair = pair + term.astype(f32)
    for term in pairs_prev:
        pair_prev = pair_prev + term.astype(f32)
    k_total, v_total = line[0], pair[0]
    k_sent, v_sent, prev_sent = line.astype(bf16), pair[1].astype(bf16), pair_prev.astype(bf16)
    for step in (1, 2, 3):
        k_total = k_total + shift(k_sent[step], "x", step).astype(f32)
    v_total = v_total + lax.ppermute(v_sent, CORNER, PARTNER).astype(f32)
    for flip in (0, 1):
        v_total = v_total + lax.ppermute(prev_sent[flip], CORNER, EARLIER[flip]).astype(f32)
    return k_total, v_total


def allowed_mask(own_pos, own_start, key_pos):
    return (key_pos <= own_pos) & (key_pos >= own_start)


def attend_kernel(
    active,
    q_ref,
    pos_ref,
    start_ref,
    kpos_ref,
    kprev_ref,
    kown_ref,
    vprev_ref,
    vown_ref,
    mixed_ref,
    lse_ref,
    top,
    total,
    accum,
):
    step = pl.program_id(0)

    @pl.when(step == 0)
    def _():
        top[...] = jnp.full(top.shape, neg_big, f32)
        total[...] = jnp.zeros(total.shape, f32)
        accum[...] = jnp.zeros(accum.shape, f32)

    for side, k_ref, v_ref in ((0, kprev_ref, vprev_ref), (1, kown_ref, vown_ref)):

        @pl.when(active[side * 8 + step] != 0)
        def _():
            key, value = k_ref[0, 0], v_ref[0, 0]
            allowed = allowed_mask(pos_ref[...], start_ref[...], kpos_ref[0, side])
            for head in range(2):
                scores = times_transposed(q_ref[:, head * HEAD_SIZE : (head + 1) * HEAD_SIZE], key)
                scores = jnp.where(allowed, scores, neg_big)
                top_old = top[head]
                top_new = jnp.maximum(top_old, jnp.max(scores, axis=-1, keepdims=True))
                weights_p = jnp.where(allowed, jnp.exp(scores - top_new), 0.0)
                damping = jnp.exp(top_old - top_new)
                total[head] = total[head] * damping + jnp.sum(weights_p, axis=-1, keepdims=True)
                accum[head] = accum[head] * damping + product(weights_p.astype(bf16), value)
                top[head] = top_new

    @pl.when(step == 7)
    def _():
        for head in range(2):
            mixed_ref[:, head * HEAD_SIZE : (head + 1) * HEAD_SIZE] = accum[head] / total[head]
            lse_ref[head] = top[head] + jnp.log(total[head])


def attend_back_kernel(
    active,
    q_ref,
    pos_ref,
    start_ref,
    kpos_ref,
    kprev_ref,
    kown_ref,
    vprev_ref,
    vown_ref,
    mixed_ref,
    lse_ref,
    dout_ref,
    dq_ref,
    dkprev_ref,
    dkown_ref,
    dvprev_ref,
    dvown_ref,
    delta,
):
    step = pl.program_id(0)

    @pl.when(step == 0)
    def _():
        dq_ref[...] = jnp.zeros(dq_ref.shape, f32)
        for head in range(2):
            cols = slice(head * HEAD_SIZE, (head + 1) * HEAD_SIZE)
            delta[head] = jnp.sum(dout_ref[:, cols].astype(f32) * mixed_ref[:, cols], axis=-1, keepdims=True)

    for side, k_ref, v_ref, dk_ref, dv_ref in (
        (0, kprev_ref, vprev_ref, dkprev_ref, dvprev_ref),
        (1, kown_ref, vown_ref, dkown_ref, dvown_ref),
    ):

        @pl.when(active[side * 8 + step] == 0)
        def _():
            dk_ref[...] = jnp.zeros(dk_ref.shape, bf16)
            dv_ref[...] = jnp.zeros(dv_ref.shape, bf16)

        @pl.when(active[side * 8 + step] != 0)
        def _():
            key, value = k_ref[0, 0], v_ref[0, 0]
            allowed = allowed_mask(pos_ref[...], start_ref[...], kpos_ref[0, side])
            dk = jnp.zeros((GROUP, HEAD_SIZE), f32)
            dv = jnp.zeros((GROUP, HEAD_SIZE), f32)
            for head in range(2):
                cols = slice(head * HEAD_SIZE, (head + 1) * HEAD_SIZE)
                query, dout = q_ref[:, cols], dout_ref[:, cols]
                scores = times_transposed(query, key)
                weights_p = jnp.where(allowed, jnp.exp(scores - lse_ref[head]), 0.0)
                dprobs = times_transposed(dout, value)
                dscores = (weights_p * (dprobs - delta[head])).astype(bf16)
                dq_ref[:, cols] += product(dscores, key)
                dk = dk + inner_rows(dscores, query)
                dv = dv + inner_rows(weights_p.astype(bf16), dout)
            dk_ref[0, 0] = dk.astype(bf16)
            dv_ref[0, 0] = dv.astype(bf16)


def whole(shape):
    return pl.BlockSpec(shape, lambda i, *refs: (0,) * len(shape))


def key_spec():
    return pl.BlockSpec((1, 1, GROUP, HEAD_SIZE), lambda i, active: (i // 4, i % 4, 0, 0))


def value_spec():
    return pl.BlockSpec((1, 1, GROUP, HEAD_SIZE), lambda i, active: (i % 4, i // 4, 0, 0))


def common_specs():
    return [
        whole((GROUP, GROUP)),
        whole((GROUP, 1)),
        whole((GROUP, 1)),
        pl.BlockSpec((1, 2, 1, GROUP), lambda i, active: (i, 0, 0, 0)),
        key_spec(),
        key_spec(),
        value_spec(),
        value_spec(),
    ]


def attend(active, *operands):
    return pl.pallas_call(
        attend_kernel,
        grid_spec=pltpu.PrefetchScalarGridSpec(
            num_scalar_prefetch=1,
            grid=(8,),
            in_specs=common_specs(),
            out_specs=[whole((GROUP, GROUP)), whole((2, GROUP, 1))],
            scratch_shapes=[
                pltpu.VMEM((2, GROUP, 1), f32),
                pltpu.VMEM((2, GROUP, 1), f32),
                pltpu.VMEM((2, GROUP, HEAD_SIZE), f32),
            ],
        ),
        out_shape=[
            jax.ShapeDtypeStruct((GROUP, GROUP), f32),
            jax.ShapeDtypeStruct((2, GROUP, 1), f32),
        ],
        compiler_params=pltpu.CompilerParams(vmem_limit_bytes=40 << 20),
        cost_estimate=pl.CostEstimate(flops=6 << 30, bytes_accessed=10 << 20, transcendentals=8 << 20),
        name="attend",
    )(active, *operands)


def attend_back(active, *operands):
    return pl.pallas_call(
        attend_back_kernel,
        grid_spec=pltpu.PrefetchScalarGridSpec(
            num_scalar_prefetch=1,
            grid=(8,),
            in_specs=common_specs() + [whole((GROUP, GROUP)), whole((2, GROUP, 1)), whole((GROUP, GROUP))],
            out_specs=[whole((GROUP, GROUP)), key_spec(), key_spec(), value_spec(), value_spec()],
            scratch_shapes=[pltpu.VMEM((2, GROUP, 1), f32)],
        ),
        out_shape=[jax.ShapeDtypeStruct((GROUP, GROUP), f32)]
        + [jax.ShapeDtypeStruct((2, 4, GROUP, HEAD_SIZE), bf16)] * 2
        + [jax.ShapeDtypeStruct((4, 2, GROUP, HEAD_SIZE), bf16)] * 2,
        compiler_params=pltpu.CompilerParams(vmem_limit_bytes=40 << 20),
        cost_estimate=pl.CostEstimate(flops=12 << 30, bytes_accessed=20 << 20, transcendentals=8 << 20),
        name="attend_back",
    )(active, *operands)


def local(
    hidden_in,
    gain_attn,
    gain_ffn,
    w_query,
    w_key,
    w_value,
    w_out,
    w_gate,
    w_up,
    w_down,
    qkv_shrink,
    query_expand,
    key_expand,
    value_expand,
    out_shrink,
    out_expand,
    gateup_shrink,
    gate_expand,
    up_expand,
    down_shrink,
    down_expand,
    lengths,
    adapter,
    packed_pos,
    cotangent,
):
    zh, zl, x, y, c = (lax.axis_index(name) for name in ALL)
    row = 2 * zh + c
    factor = HEAD_SIZE ** (-0.5)
    rank = out_shrink.shape[1]

    def to_rows(value):
        own = lax.dynamic_slice_in_dim(value, c * HALF, HALF, 0)
        sent = lax.dynamic_slice_in_dim(value, (1 - c) * HALF, HALF, 0)
        return jnp.concatenate([own, swap_cores(sent)], axis=0)

    def from_rows(value):
        own, got = value[:HALF], swap_cores(value[HALF:])
        return jnp.where(c == 0, jnp.concatenate([own, got], 0), jnp.concatenate([got, own], 0))

    hidden = to_rows(hidden_in)
    cot = to_rows(cotangent)

    def roll(array, by, axis):
        return lax.dynamic_slice_in_dim(jnp.concatenate([array, array], axis), by, array.shape[axis], axis)

    spread = packed_pos.reshape(2, 2, 4, 4, 2, 2, HALF)
    spread = jnp.transpose(spread, (0, 5, 1, 2, 3, 4, 6))
    rows_pos = jnp.stack([spread[:, 0], spread[:, 1, :, :, :, ::-1]], axis=1).reshape(4, 2, 4, 4, 128)
    rows_pos = roll(roll(roll(rows_pos, zl, 1), x, 2), y, 3).reshape(4, 8, GROUP)
    own_row = lax.dynamic_index_in_dim(rows_pos, row, 0, keepdims=False)
    prev_row = lax.dynamic_index_in_dim(rows_pos, jnp.maximum(row - 1, 0), 0, keepdims=False)
    prev_row = jnp.where(row == 0, far, prev_row)
    key_pos = jnp.stack([prev_row, own_row], axis=1)
    group_pos = own_row[0]
    seq_ends = jnp.cumsum(lengths)
    starts = seq_ends - lengths
    member = (group_pos[:, None] >= starts[None, :]) & (group_pos[:, None] < seq_ends[None, :])
    member_int = member.astype(jnp.int32)
    group_start = jnp.sum(member_int * starts[None, :], axis=1)

    def selected(pos):
        inside = (pos[:, None] >= starts[None, :]) & (pos[:, None] < seq_ends[None, :])
        owner = jnp.sum(inside.astype(jnp.int32) * adapter[None, :], axis=1)
        return (owner[:, None] == (jnp.arange(rank, dtype=jnp.int32) // RANK)[None, :]).astype(f32)

    low, high = jnp.min(group_start), jnp.max(group_pos)
    active = (jnp.min(key_pos, axis=2) <= high) & (jnp.max(key_pos, axis=2) >= low)
    active = jnp.transpose(active).reshape(16).astype(jnp.int32)
    select_y = selected(group_pos)
    select_x = selected(own_row.reshape(2, 4, 4, 128)[0, :, 0].reshape(GROUP))
    select = select_y[:128]
    cos_table, sin_table = rope_tables(group_pos - group_start, HEAD_SIZE)

    def column_slices(weight):
        parts = weight.reshape(16, 4, 4, 4, 2, 64)
        return jnp.transpose(parts, (2, 4, 0, 1, 3, 5)).reshape(8, 16, 1024)

    def units_at(array, axis, core):
        shape = array.shape
        array = array.reshape(shape[:axis] + (4, 4, 4, 2, 64) + shape[axis + 1 :])
        array = lax.dynamic_slice_in_dim(array, x, 1, axis + 1)
        array = lax.dynamic_slice_in_dim(array, core, 1, axis + 3)
        return array.reshape(shape[:axis] + (1024,) + shape[axis + 1 :])

    heads_q = w_query.reshape(16, 4, 512)
    heads_kv = jnp.concatenate([w_key.reshape(16, 4, 256), w_value.reshape(16, 4, 256)], axis=2)
    qkv_parts = jnp.transpose(jnp.stack([heads_q, heads_kv], axis=2), (1, 2, 0, 3)).reshape(8, 16, 512)
    qkv_parts = lax.all_to_all(qkv_parts, ("y", "c"), split_axis=0, concat_axis=0, tiled=True).reshape(128, 512)
    gate_up = jnp.concatenate([column_slices(w_gate), column_slices(w_up)], axis=2)
    gate_up = lax.all_to_all(gate_up, ("x", "c"), split_axis=0, concat_axis=0, tiled=True).reshape(128, 2048)
    wo = lax.all_gather(w_out, ALL, axis=0, tiled=True)
    ffn = jnp.concatenate([gate_up, w_down], axis=0)
    ffn = lax.all_gather(ffn, ("zh", "zl", "y"), axis=0, tiled=False)
    wd_mine = ffn[:, 128:].reshape(1024, 2048)
    wgu_mine = jnp.transpose(ffn[:, :128].reshape(4, 4, 4, 32, 2048), (0, 2, 1, 3, 4)).reshape(2048, 2048)
    wgu_other, wd_other = swap_cores(wgu_mine), swap_cores(wd_mine)

    def columns_of(array, width):
        return lax.dynamic_slice_in_dim(array, y * width, width, 1)

    inputs = hidden.astype(f32)
    scale_in = row_scale(inputs)
    normed = (inputs * scale_in * gain_attn).astype(bf16)
    normed_g = gather_near(normed, "y")
    qkv_parts = after(qkv_parts, normed)
    first = gather_ring(gather_ring(qkv_parts[:, :256], "x"), "z").reshape(2048, 256)
    second = jnp.swapaxes(gather_ring(gather_ring(qkv_parts[:, 256:], "z"), "x"), 0, 1).reshape(2048, 256)
    qkv_mine = jnp.concatenate([first, second], axis=1)
    qkv_other = swap_cores(qkv_mine)
    q_expand = columns_of(query_expand, 512)
    k_expand = columns_of(key_expand, 256)
    v_expand = columns_of(value_expand, 256)
    low_qkv = (product(normed_g, qkv_shrink) * jnp.tile(select_y, (1, 3))).astype(bf16)
    lin_mine, lin_other = product(normed_g, qkv_mine), product(normed_g, qkv_other)
    query_lin = jnp.where(c == 0, lin_mine, lin_other) + product(low_qkv[:, :rank], q_expand)
    kv_lin = jnp.where(c == 0, lin_other, lin_mine)
    key_lin = kv_lin[:, :256] + product(low_qkv[:, rank : 2 * rank], k_expand)
    value_lin = kv_lin[:, 256:] + product(low_qkv[:, 2 * rank :], v_expand)
    query_heads = query_lin.reshape(GROUP, 2, HEAD_SIZE)
    key_heads = key_lin.reshape(GROUP, 1, HEAD_SIZE)
    query = (query_heads * cos_table + rotate(query_heads) * sin_table).astype(bf16)
    query = (query * bf16(factor)).reshape(GROUP, 512)
    key = (key_heads * cos_table + rotate(key_heads) * sin_table).astype(bf16).reshape(GROUP, 256)

    k_own, k_prev, v_own, v_prev = gather_row(key, value_lin.astype(bf16), c)
    attended = (
        query,
        group_pos[:, None],
        group_start[:, None],
        key_pos.reshape(8, 2, 1, GROUP),
        k_prev,
        k_own,
        v_prev,
        v_own,
    )
    mixed_f, lse = attend(active, *attended)
    mixed = mixed_f.astype(bf16)
    cot_g = gather_near(after(cot, k_prev, v_prev), "x")

    heads = jnp.zeros((4, 128, 512), bf16)
    heads = lax.dynamic_update_index_in_dim(heads, mixed[:128], y, 0)
    for step in (1, 2, 3):
        got = shift(mixed[step * 128 : (step + 1) * 128], "y", step)
        heads = lax.dynamic_update_index_in_dim(heads, got, (y - step) % 4, 0)
    mixed_tok = jnp.transpose(heads, (1, 0, 2)).reshape(128, 2048)
    low_out = (product(mixed_tok, out_shrink) * select).astype(bf16)
    middle = inputs + product(mixed_tok, wo) + product(low_out, out_expand)
    scale_mid = row_scale(middle)
    normed_mid = (middle * scale_mid * gain_ffn).astype(bf16)
    normed_mid_g = gather_near(normed_mid, "x")

    select_two = jnp.tile(select_x, (1, 2))
    low_gu = (product(normed_mid_g, gateup_shrink) * select_two).astype(bf16)
    grad_low_down = (times_transposed(cot_g, down_expand) * select_x).astype(bf16)
    result = jnp.zeros((GROUP, 2048), f32)
    low_down_part = jnp.zeros((GROUP, rank), f32)
    grad_mid_part = jnp.zeros((GROUP, 2048), f32)
    grad_low_part = jnp.zeros((GROUP, 2 * rank), f32)
    unit_grads = []
    units = 1024
    for wgu, wd, core in ((wgu_mine, wd_mine, c), (wgu_other, wd_other, 1 - c)):
        wg, wu = wgu[:, :units], wgu[:, units:]
        g_expand, u_expand = units_at(gate_expand, 1, core), units_at(up_expand, 1, core)
        d_shrink = units_at(down_shrink, 0, core)
        gate_pre = product(normed_mid_g, wg) + product(low_gu[:, :rank], g_expand)
        up_pre = product(normed_mid_g, wu) + product(low_gu[:, rank:], u_expand)
        sigmoid_g = jax.nn.sigmoid(gate_pre)
        silu_gate = gate_pre * sigmoid_g
        active_units = (silu_gate * up_pre).astype(bf16)
        result = result + product(active_units, wd)
        low_down_part = low_down_part + product(active_units, d_shrink)
        grad_active = times_transposed(cot_g, wd) + times_transposed(grad_low_down, d_shrink)
        grad_gate = (grad_active * up_pre * sigmoid_g * (1.0 + gate_pre * (1.0 - sigmoid_g))).astype(bf16)
        grad_up = (grad_active * silu_gate).astype(bf16)
        grad_mid_part = grad_mid_part + times_transposed(grad_gate, wg) + times_transposed(grad_up, wu)
        grad_low_part = grad_low_part + jnp.concatenate(
            [times_transposed(grad_gate, g_expand), times_transposed(grad_up, u_expand)], axis=1
        )
        unit_grads.append(
            (
                inner_rows(grad_gate, low_gu[:, :rank]),
                inner_rows(grad_up, low_gu[:, rank:]),
                inner_rows(active_units, grad_low_down),
            )
        )

    def sum_tokens(part, ring):
        sent = part.astype(bf16)
        return sum_near([sent[i * 128 : (i + 1) * 128] for i in range(4)], ring)

    back_low = sum_tokens(grad_low_part, "x")
    back = sum_tokens(grad_mid_part, "x")
    low_down_sum = sum_tokens(low_down_part, "x")

    low_down = (low_down_sum * select).astype(bf16)
    grad_low_gu = (back_low * jnp.tile(select, (1, 2))).astype(bf16)
    grad_normed_mid = back + times_transposed(grad_low_gu, gateup_shrink)
    cot_f = cot.astype(f32)
    grad_middle = cot_f + norm_back(middle, scale_mid, gain_ffn, grad_normed_mid)
    grad_attn_out = grad_middle.astype(bf16)
    grad_low_out = (times_transposed(grad_attn_out, out_expand) * select).astype(bf16)
    grad_mixed = (times_transposed(grad_attn_out, wo) + times_transposed(grad_low_out, out_shrink)).astype(bf16)

    def slices_near(array):
        def columns_at(step):
            return lax.dynamic_slice_in_dim(array, ((y + step) % 4) * 512, 512, 1)

        return jnp.concatenate([columns_at(0)] + [shift(columns_at(4 - step), "y", -step) for step in (1, 2, 3)])

    dout = slices_near(grad_mixed)
    ahead = sum_tokens(after(result.astype(bf16), dout), "x")
    output = (middle + ahead + product(low_down, down_expand)).astype(bf16)
    dq, dk_prev, dk_own, dv_prev, dv_own = attend_back(active, *attended, mixed_f, lse, dout)
    dk, dv = sum_row(dk_own, dk_prev, dv_own, dv_prev)
    query_back = (dq * factor).astype(bf16).astype(f32).reshape(GROUP, 2, HEAD_SIZE)
    key_back = dk.astype(bf16).astype(f32).reshape(GROUP, 1, HEAD_SIZE)
    grad_value = dv.astype(bf16)
    grad_query = (query_back * cos_table - rotate(query_back * sin_table)).astype(bf16).reshape(GROUP, 512)
    grad_key = (key_back * cos_table - rotate(key_back * sin_table)).astype(bf16).reshape(GROUP, 256)
    grad_kv = jnp.concatenate([grad_key, grad_value], axis=1)

    grad_low_part = jnp.concatenate(
        [
            times_transposed(grad_query, q_expand),
            times_transposed(grad_key, k_expand),
            times_transposed(grad_value, v_expand),
        ],
        axis=1,
    )
    grad_low_qkv = (sum_tokens(grad_low_part, "y") * jnp.tile(select, (1, 3))).astype(bf16)
    for_mine = jnp.where(c == 0, grad_query, grad_kv)
    for_other = jnp.where(c == 0, grad_kv, grad_query)
    grad_normed_part = times_transposed(for_mine, qkv_mine) + times_transposed(for_other, qkv_other)
    grad_normed = sum_tokens(grad_normed_part, "y") + times_transposed(grad_low_qkv, qkv_shrink)
    grad_input = (grad_middle + norm_back(inputs, scale_in, gain_attn, grad_normed)).astype(bf16)

    def features(array, at):
        return lax.dynamic_slice_in_dim(array, at * 512, 512, 1)

    def by_halves(pair_at):
        own, others = unit_grads[0][pair_at], unit_grads[1][pair_at]
        own, others = own.reshape(16, 1, 64, rank), others.reshape(16, 1, 64, rank)
        ordered = jnp.where(c == 0, jnp.concatenate([own, others], 1), jnp.concatenate([others, own], 1))
        return ordered.reshape(32, 64, rank)

    def by_rows(array):
        return array.reshape(32, array.shape[0] // 32, rank)

    low_near = gather_near(jnp.concatenate([low_down, grad_low_gu], axis=1), "x")
    grad_gateup = inner_rows(features(normed_mid_g, x), low_near[:, rank:])
    out_terms = jnp.concatenate([inner_rows(mixed_tok, grad_low_out), inner_rows(grad_attn_out, low_out)], axis=1)
    out_terms = out_terms.astype(bf16).reshape(4, 512, 2 * rank)
    out_terms = sum_near(
        [lax.dynamic_index_in_dim(out_terms, (x + step) % 4, 0, keepdims=False) for step in range(4)], "x"
    )
    early = [
        by_halves(0),
        by_halves(1),
        by_halves(2),
        by_rows(out_terms[:, :rank]),
        by_rows(out_terms[:, rank:]),
        by_rows(inner_rows(features(cot_g, x), low_near[:, :rank])),
        by_rows(grad_gateup[:, :rank]),
        by_rows(grad_gateup[:, rank:]),
    ]
    early_sum = lax.psum_scatter(
        jnp.concatenate(early, axis=1), ("zh", "zl", "y", "c"), scatter_dimension=0, tiled=False
    )
    early_sum = after(early_sum.astype(bf16), dq)
    early_all = lax.all_gather(early_sum, ALL, axis=0, tiled=False)

    grad_qkv = inner_rows(features(normed_g, y), gather_near(grad_low_qkv, "y"))
    late = [
        by_rows(inner_rows(grad_query, low_qkv[:, :rank])),
        by_rows(inner_rows(grad_key, low_qkv[:, rank : 2 * rank])),
        by_rows(inner_rows(grad_value, low_qkv[:, 2 * rank :])),
        by_rows(grad_qkv[:, :rank]),
        by_rows(grad_qkv[:, rank : 2 * rank]),
        by_rows(grad_qkv[:, 2 * rank :]),
    ]
    terms = jnp.concatenate(late, axis=1)
    terms = terms.reshape(16, 2, terms.shape[1], rank)
    kept = lax.dynamic_index_in_dim(terms, c, 1, keepdims=False)
    given = lax.dynamic_index_in_dim(terms, 1 - c, 1, keepdims=False).astype(bf16)
    terms = (kept + swap_cores(given).astype(f32)).reshape(4, 4, -1, rank)
    late_sum = sum_ring(sum_ring(terms, "z"), "x").astype(bf16)
    late_all = gather_ring(gather_ring(gather_ring(late_sum, "x"), "z"), "y")
    late_other = swap_cores(late_all)
    late_all = jnp.where(c == 0, jnp.stack([late_all, late_other], 3), jnp.stack([late_other, late_all], 3))

    def cut(array, axis, pieces):
        found, at = [], 0
        for piece in pieces:
            found.append(lax.slice_in_dim(array, at, at + piece.shape[1], axis=axis).astype(f32))
            at += piece.shape[1]
        return found

    def rows_order(array):
        ordered = jnp.transpose(array.reshape(4, 4, 8, array.shape[1], rank), (1, 0, 2, 3, 4))
        return ordered.reshape(-1, rank)

    early_found = cut(early_all, 1, early)
    g_gate, g_up, g_down_shrink = (array.reshape(-1, rank) for array in early_found[:3])
    g_out_shrink, g_out_expand, g_down_expand, g_gate_low, g_up_low = (rows_order(a) for a in early_found[3:])
    g_q, g_k, g_v, g_q_low, g_k_low, g_v_low = (a.reshape(-1, rank) for a in cut(late_all, 4, late))
    return (
        from_rows(output),
        from_rows(grad_input),
        jnp.concatenate([g_q_low, g_k_low, g_v_low], axis=1),
        g_q.T,
        g_k.T,
        g_v.T,
        g_out_shrink,
        g_out_expand.T,
        jnp.concatenate([g_gate_low, g_up_low], axis=1),
        g_gate.T,
        g_up.T,
        g_down_shrink,
        g_down_expand.T,
    )


def solution(mesh):
    fine = Mesh(mesh.devices.reshape(2, 2, 4, 4, 2), ALL)
    split = P(ALL, None)
    placed = (split, P(), P()) + (split,) * 7 + (P(),) * 14 + (split,)
    return jax.shard_map(
        local,
        mesh=fine,
        in_specs=placed,
        out_specs=(split, split) + (P(),) * 11,
        check_vma=False,
    )
```

```python
from functools import partial

import jax
import jax.numpy as jnp
from jax import lax
from jax.experimental import pallas as pl
from jax.experimental.pallas import tpu as pltpu
from jax.sharding import Mesh, PartitionSpec as P

HEAD_SIZE = 256
RANK = 16
HALF = 64
GROUP = 512

ALL = ("zh", "zl", "x", "y", "c")

norm_eps = 1e-06
rope_theta = 1000042.0
neg_big = -1e30
far = 1 << 30

f32 = jnp.float32
bf16 = jnp.bfloat16


def product(left, right):
    return jnp.dot(left, right, preferred_element_type=f32)


def times_transposed(left, right):
    return lax.dot_general(left, right, (((1,), (1,)), ((), ())), preferred_element_type=f32)


def inner_rows(left, right):
    return lax.dot_general(left, right, (((0,), (0,)), ((), ())), preferred_element_type=f32)


def row_scale(value_matrix):
    return lax.rsqrt(jnp.mean(value_matrix * value_matrix, axis=-1, keepdims=True) + norm_eps)


def norm_back(value_matrix, scale, gain, grad):
    scaled = gain * grad
    return scale * scaled - value_matrix * (scale * scale * scale) * jnp.mean(
        value_matrix * scaled, axis=-1, keepdims=True
    )


def rotate(value_matrix):
    middle = value_matrix.shape[-1] // 2
    return jnp.concatenate([-value_matrix[..., middle:], value_matrix[..., :middle]], axis=-1)


def rope_tables(positions, width):
    middle = width // 2
    inverse = rope_theta ** (-(jnp.arange(middle, dtype=f32) * 2.0) / width)
    angles = positions.astype(f32)[:, None] * inverse[None, :]
    cos_half, sin_half = jnp.cos(angles), jnp.sin(angles)
    cos_table = jnp.concatenate([cos_half, cos_half], axis=-1)[:, None, :]
    sin_table = jnp.concatenate([sin_half, sin_half], axis=-1)[:, None, :]
    return (cos_table, sin_table)


RING = {"x": ("x",), "y": ("y",), "z": ("zh", "zl")}


def swap_cores(value):
    return lax.ppermute(value, "c", [(0, 1), (1, 0)])


def shift(value, ring, step):
    return lax.ppermute(value, RING[ring], [(i, (i + step) % 4) for i in range(4)])


def place_in(ring):
    return lax.axis_index(RING[ring])


def gather_near(value, ring, axis=0):
    return jnp.concatenate([value] + [shift(value, ring, -step) for step in (1, 2, 3)], axis=axis)


def gather_ring(value, ring):
    at = place_in(ring)
    whole_ring = jnp.zeros((4,) + value.shape, value.dtype)
    whole_ring = lax.dynamic_update_index_in_dim(whole_ring, value, at, 0)
    for step in (1, 2, 3):
        got = shift(value, ring, -step)
        whole_ring = lax.dynamic_update_index_in_dim(whole_ring, got, (at + step) % 4, 0)
    return whole_ring


def sum_near(blocks, ring):
    got = [shift(blocks[step], ring, step) for step in (2, 1, 3)]
    total = blocks[0].astype(f32)
    for term in got:
        total = total + term.astype(f32)
    return total


def sum_ring(terms, ring):
    at = place_in(ring)
    got = [
        shift(lax.dynamic_index_in_dim(terms, (at + step) % 4, 0, keepdims=False).astype(bf16), ring, step)
        for step in (1, 2, 3)
    ]
    total = lax.dynamic_index_in_dim(terms, at, 0, keepdims=False)
    for term in got:
        total = total + term.astype(f32)
    return total


CORNER = ("zh", "zl", "c")
PARTNER = [(4 * zh + 2 * zl + c, 4 * zh + 2 * (1 - zl) + c) for zh in (0, 1) for zl in (0, 1) for c in (0, 1)]
LATER = [[(2 * zl + 1, 4 + 2 * (zl ^ flip)) for zl in (0, 1)] for flip in (0, 1)]
EARLIER = [[(to, came) for came, to in pairs] for pairs in LATER]
def after(value, *others):
    return lax.optimization_barrier((value,) + others)[0]


def gather_row(key_value):
    line = jnp.stack([key_value] + [shift(key_value, "x", -step) for step in (1, 2, 3)])
    ahead = [lax.ppermute(line, CORNER, pairs) for pairs in LATER]
    partner = lax.ppermute(line, CORNER, PARTNER)
    beside = [lax.ppermute(value, "c", [(0, 1)]) for value in (line, partner)]
    return line, partner, ahead[0], ahead[1], beside[0], beside[1]


def sum_row(own, own_partner, prev, prev_partner):
    got = [lax.ppermute(value, "c", [(1, 0)]) for value in (prev_partner, prev)]
    terms = [lax.ppermute(value, CORNER, pairs) for value, pairs in zip((prev, prev_partner), EARLIER)]
    sent = (own_partner.astype(f32) + got[0].astype(f32)).astype(bf16)
    terms = [got[1], lax.ppermute(sent, CORNER, PARTNER)] + terms
    line = own.astype(f32)
    for term in terms:
        line = line + term.astype(f32)
    sent = line.astype(bf16)
    total = line[0]
    for step in (2, 1, 3):
        total = total + shift(sent[step], "x", step).astype(f32)
    return total


def allowed_mask(own_pos, own_start, key_pos):
    return (key_pos <= own_pos) & (key_pos >= own_start)


def tiles_of(own_ref, partner_ref, ahead_ref, ahead_partner_ref, beside_ref, beside_partner_ref):
    return (
        lambda: ahead_ref[0] + beside_ref[0],
        lambda: ahead_partner_ref[0] + beside_partner_ref[0],
        lambda: own_ref[0],
        lambda: partner_ref[0],
    )


def attend_kernel(active, q_ref, pos_ref, start_ref, kpos_ref, *refs):
    mixed_ref, lse_ref, top, total, accum = refs[6:]
    step = pl.program_id(0)

    @pl.when(step == 0)
    def _():
        top[...] = jnp.full(top.shape, neg_big, f32)
        total[...] = jnp.zeros(total.shape, f32)
        accum[...] = jnp.zeros(accum.shape, f32)

    def visit(tile, read, masked):
        key_value = read()
        key, value = key_value[:, :HEAD_SIZE], key_value[:, HEAD_SIZE:]
        if masked:
            allowed = allowed_mask(pos_ref[...], start_ref[...], kpos_ref[0, tile])
        for head in range(2):
            scores = times_transposed(q_ref[:, head * HEAD_SIZE : (head + 1) * HEAD_SIZE], key)
            if masked:
                scores = jnp.where(allowed, scores, neg_big)
            top_old = top[head]
            top_new = jnp.maximum(top_old, jnp.max(scores, axis=-1, keepdims=True))
            weights_p = jnp.exp(scores - top_new)
            if masked:
                weights_p = jnp.where(allowed, weights_p, 0.0)
            damping = jnp.exp(top_old - top_new)
            total[head] = total[head] * damping + jnp.sum(weights_p, axis=-1, keepdims=True)
            accum[head] = accum[head] * damping + product(weights_p.astype(bf16), value)
            top[head] = top_new

    for tile, read in enumerate(tiles_of(*refs[:6])):
        state = active[step * 4 + tile]
        pl.when(state == 1)(partial(visit, tile, read, True))
        pl.when(state == 2)(partial(visit, tile, read, False))

    @pl.when(step == 3)
    def _():
        for head in range(2):
            mixed_ref[:, head * HEAD_SIZE : (head + 1) * HEAD_SIZE] = accum[head] / total[head]
            lse_ref[head] = top[head] + jnp.log(total[head])


def attend_back_kernel(active, q_ref, pos_ref, start_ref, kpos_ref, *refs):
    mixed_ref, lse_ref, dout_ref, dq_ref, down_ref, dpartner_ref, dprev_ref, dprev_partner_ref, delta = refs[6:]
    step = pl.program_id(0)

    @pl.when(step == 0)
    def _():
        dq_ref[...] = jnp.zeros(dq_ref.shape, f32)
        for head in range(2):
            cols = slice(head * HEAD_SIZE, (head + 1) * HEAD_SIZE)
            delta[head] = jnp.sum(dout_ref[:, cols].astype(f32) * mixed_ref[:, cols], axis=-1, keepdims=True)

    def visit(tile, read, out_ref, masked):
        key_value = read()
        key, value = key_value[:, :HEAD_SIZE], key_value[:, HEAD_SIZE:]
        if masked:
            allowed = allowed_mask(pos_ref[...], start_ref[...], kpos_ref[0, tile])
        dk = jnp.zeros((GROUP, HEAD_SIZE), f32)
        dv = jnp.zeros((GROUP, HEAD_SIZE), f32)
        for head in range(2):
            cols = slice(head * HEAD_SIZE, (head + 1) * HEAD_SIZE)
            query, dout = q_ref[:, cols], dout_ref[:, cols]
            weights_p = jnp.exp(times_transposed(query, key) - lse_ref[head])
            if masked:
                weights_p = jnp.where(allowed, weights_p, 0.0)
            dprobs = times_transposed(dout, value)
            dscores = (weights_p * (dprobs - delta[head])).astype(bf16)
            dq_ref[:, cols] += product(dscores, key)
            dk = dk + inner_rows(dscores, query)
            dv = dv + inner_rows(weights_p.astype(bf16), dout)
        out_ref[0, :, :HEAD_SIZE] = dk.astype(bf16)
        out_ref[0, :, HEAD_SIZE:] = dv.astype(bf16)

    outs = (dprev_ref, dprev_partner_ref, down_ref, dpartner_ref)
    for tile, (read, out_ref) in enumerate(zip(tiles_of(*refs[:6]), outs)):
        state = active[step * 4 + tile]

        @pl.when(state == 0)
        def _():
            out_ref[...] = jnp.zeros(out_ref.shape, bf16)

        pl.when(state == 1)(partial(visit, tile, read, out_ref, True))
        pl.when(state == 2)(partial(visit, tile, read, out_ref, False))


def whole(shape):
    return pl.BlockSpec(shape, lambda *grid_and_refs: (0,) * len(shape))


def line_spec():
    return pl.BlockSpec((1, GROUP, GROUP), lambda i, active: (i, 0, 0))


def common_specs():
    return [
        whole((GROUP, GROUP)),
        whole((GROUP, 1)),
        whole((GROUP, 1)),
        pl.BlockSpec((1, 4, 1, GROUP), lambda i, active: (i, 0, 0, 0)),
    ] + [line_spec() for _ in range(6)]


def attend(active, *operands):
    return pl.pallas_call(
        attend_kernel,
        grid_spec=pltpu.PrefetchScalarGridSpec(
            num_scalar_prefetch=1,
            grid=(4,),
            in_specs=common_specs(),
            out_specs=[whole((GROUP, GROUP)), whole((2, GROUP, 1))],
            scratch_shapes=[
                pltpu.VMEM((2, GROUP, 1), f32),
                pltpu.VMEM((2, GROUP, 1), f32),
                pltpu.VMEM((2, GROUP, HEAD_SIZE), f32),
            ],
        ),
        out_shape=[
            jax.ShapeDtypeStruct((GROUP, GROUP), f32),
            jax.ShapeDtypeStruct((2, GROUP, 1), f32),
        ],
        compiler_params=pltpu.CompilerParams(vmem_limit_bytes=48 << 20),
        cost_estimate=pl.CostEstimate(flops=6 << 30, bytes_accessed=10 << 20, transcendentals=8 << 20),
        name="attend",
    )(active, *operands)


def attend_back(active, *operands):
    return pl.pallas_call(
        attend_back_kernel,
        grid_spec=pltpu.PrefetchScalarGridSpec(
            num_scalar_prefetch=1,
            grid=(4,),
            in_specs=common_specs() + [whole((GROUP, GROUP)), whole((2, GROUP, 1)), whole((GROUP, GROUP))],
            out_specs=[whole((GROUP, GROUP))] + [line_spec() for _ in range(4)],
            scratch_shapes=[pltpu.VMEM((2, GROUP, 1), f32)],
        ),
        out_shape=[jax.ShapeDtypeStruct((GROUP, GROUP), f32)]
        + [jax.ShapeDtypeStruct((4, GROUP, GROUP), bf16)] * 4,
        compiler_params=pltpu.CompilerParams(vmem_limit_bytes=48 << 20),
        cost_estimate=pl.CostEstimate(flops=12 << 30, bytes_accessed=20 << 20, transcendentals=8 << 20),
        name="attend_back",
    )(active, *operands)


UNITS = 1024
CHUNK = 256


def ffn_kernel(last, nm_ref, cot_ref, lgu_ref, gld_ref, wg_ref, wu_ref, wd_ref, ge_ref, ue_ref, ds_ref, perm_ref, *refs):
    if last:
        result_in, grad_in, low_in, glow_in = refs[:4]
        refs = refs[4:]
    result_ref, grad_ref, low_ref, glow_ref, gge_ref, gue_ref, gds_ref, nmp, result, grad = refs
    step = pl.program_id(0)
    rank = ds_ref.shape[1]

    @pl.when(step == 0)
    def _():
        for zone in range(4):
            cols = slice(zone * GROUP, (zone + 1) * GROUP)
            nmp[:, cols] = product(nm_ref[:, cols], perm_ref[...]).astype(bf16)
        if last:
            result[...] = result_in[...]
            grad[...] = grad_in[...]
            low_ref[...] = low_in[...]
            glow_ref[...] = glow_in[...]
        else:
            result[...] = jnp.zeros(result.shape, f32)
            grad[...] = jnp.zeros(grad.shape, f32)
            low_ref[...] = jnp.zeros(low_ref.shape, f32)
            glow_ref[...] = jnp.zeros(glow_ref.shape, f32)

    wg, wu = wg_ref[...].reshape(2048, CHUNK), wu_ref[...].reshape(2048, CHUNK)
    wd = wd_ref[...].reshape(CHUNK, 2048)
    low_gate, low_up = lgu_ref[:, :rank], lgu_ref[:, rank:]
    gate_pre = product(nmp[...], wg) + product(low_gate, ge_ref[...])
    up_pre = product(nmp[...], wu) + product(low_up, ue_ref[...])
    sigmoid_g = jax.nn.sigmoid(gate_pre)
    silu_gate = gate_pre * sigmoid_g
    active_units = (silu_gate * up_pre).astype(bf16)
    grad_active = times_transposed(cot_ref[...], wd) + times_transposed(gld_ref[...], ds_ref[...])
    grad_gate = (grad_active * up_pre * sigmoid_g * (1.0 + gate_pre * (1.0 - sigmoid_g))).astype(bf16)
    grad_up = (grad_active * silu_gate).astype(bf16)
    result[...] += product(active_units, wd)
    low_ref[...] += product(active_units, ds_ref[...])
    grad[...] += times_transposed(grad_gate, wg) + times_transposed(grad_up, wu)
    glow_ref[:, :rank] += times_transposed(grad_gate, ge_ref[...])
    glow_ref[:, rank:] += times_transposed(grad_up, ue_ref[...])
    gge_ref[...] = inner_rows(grad_gate, low_gate)
    gue_ref[...] = inner_rows(grad_up, low_up)
    gds_ref[...] = inner_rows(active_units, gld_ref[...])

    @pl.when(step == UNITS // CHUNK - 1)
    def _():
        if last:
            result_ref[...] = result[...].astype(bf16)
            for zone in range(4):
                cols = slice(zone * GROUP, (zone + 1) * GROUP)
                grad_ref[:, cols] = product(grad[:, cols].astype(bf16), perm_ref[...]).astype(bf16)
        else:
            result_ref[...] = result[...]
            grad_ref[...] = grad[...]


def ffn_part(normed_mid, cot, low_gu, grad_low_down, weights, expands, perm, sums=None):
    last = sums is not None
    rank = low_gu.shape[1] // 2
    wide = bf16 if last else f32
    weight_specs = [
        pl.BlockSpec((16, 128, CHUNK), lambda u: (0, 0, u)),
        pl.BlockSpec((16, 128, CHUNK), lambda u: (0, 0, UNITS // CHUNK + u)),
        pl.BlockSpec((4, 64, 2048), lambda u: (u, 2, 0)),
        pl.BlockSpec((rank, CHUNK), lambda u: (0, u)),
        pl.BlockSpec((rank, CHUNK), lambda u: (0, u)),
        pl.BlockSpec((CHUNK, rank), lambda u: (u, 0)),
    ]
    sum_specs = [whole((GROUP, 2048)), whole((GROUP, 2048)), whole((GROUP, rank)), whole((GROUP, 2 * rank))]
    return pl.pallas_call(
        partial(ffn_kernel, last),
        grid=(UNITS // CHUNK,),
        in_specs=[whole((GROUP, 2048)), whole((GROUP, 2048)), whole((GROUP, 2 * rank)), whole((GROUP, rank))]
        + weight_specs
        + [whole((GROUP, GROUP))]
        + (sum_specs if last else []),
        out_specs=sum_specs + [pl.BlockSpec((CHUNK, rank), lambda u: (u, 0))] * 3,
        out_shape=[
            jax.ShapeDtypeStruct((GROUP, 2048), wide),
            jax.ShapeDtypeStruct((GROUP, 2048), wide),
            jax.ShapeDtypeStruct((GROUP, rank), f32),
            jax.ShapeDtypeStruct((GROUP, 2 * rank), f32),
        ]
        + [jax.ShapeDtypeStruct((UNITS, rank), f32)] * 3,
        scratch_shapes=[
            pltpu.VMEM((GROUP, 2048), bf16),
            pltpu.VMEM((GROUP, 2048), f32),
            pltpu.VMEM((GROUP, 2048), f32),
        ],
        compiler_params=pltpu.CompilerParams(vmem_limit_bytes=60 << 20),
        cost_estimate=pl.CostEstimate(flops=14 << 30, bytes_accessed=30 << 20, transcendentals=1 << 20),
        name="feed_forward",
    )(normed_mid, cot, low_gu, grad_low_down, weights, weights, weights, *expands, perm, *(sums or ()))


EARLY = (64, 64, 64, 16, 16, 16, 16, 16)
LATE = (16, 8, 8, 16, 16, 16)


def cut(array, sizes):
    found, at = [], 0
    for size in sizes:
        found.append(array[..., at : at + size, :])
        at += size
    return found


def early_kernel(all_ref, gate_ref, up_ref, down_ref, oshrink_ref, oexpand_ref, dexpand_ref, gateup_ref):
    pieces = [piece.astype(f32).reshape(-1, 128) for piece in cut(all_ref[...], EARLY)]
    gate_ref[...] = pieces[0].T
    up_ref[...] = pieces[1].T
    down_ref[...] = pieces[2]
    oshrink_ref[...] = pieces[3]
    oexpand_ref[...] = pieces[4].T
    dexpand_ref[...] = pieces[5].T
    gateup_ref[:, :128] = pieces[6]
    gateup_ref[:, 128:] = pieces[7]


def unpack_early(everyone):
    def rows_at(i):
        return (i % 4) * 4 + i // 4

    return pl.pallas_call(
        early_kernel,
        grid=(16,),
        in_specs=[pl.BlockSpec((8, sum(EARLY), 128), lambda i: (i, 0, 0))],
        out_specs=[
            pl.BlockSpec((128, 512), lambda i: (0, i)),
            pl.BlockSpec((128, 512), lambda i: (0, i)),
            pl.BlockSpec((512, 128), lambda i: (i, 0)),
            pl.BlockSpec((128, 128), lambda i: (rows_at(i), 0)),
            pl.BlockSpec((128, 128), lambda i: (0, rows_at(i))),
            pl.BlockSpec((128, 128), lambda i: (0, rows_at(i))),
            pl.BlockSpec((128, 256), lambda i: (rows_at(i), 0)),
        ],
        out_shape=[
            jax.ShapeDtypeStruct(shape, f32)
            for shape in ((128, 8192), (128, 8192), (8192, 128), (2048, 128), (128, 2048), (128, 2048), (2048, 256))
        ],
        cost_estimate=pl.CostEstimate(flops=1 << 20, bytes_accessed=27 << 20, transcendentals=0),
        name="unpack_early",
    )(everyone)


def late_kernel(core, mine_ref, other_ref, q_ref, k_ref, v_ref, low_ref):
    mine, other = mine_ref[0].astype(f32), other_ref[0].astype(f32)
    first, second = jnp.where(core[0] == 0, mine, other), jnp.where(core[0] == 0, other, mine)
    pieces = [
        jnp.stack(pair, axis=1).reshape(-1, 128) for pair in zip(cut(first, LATE), cut(second, LATE))
    ]
    q_ref[...] = pieces[0].T
    k_ref[...] = pieces[1].T
    v_ref[...] = pieces[2].T
    for at in range(3):
        low_ref[:, at * 128 : (at + 1) * 128] = pieces[3 + at]


def unpack_late(core, mine, other):
    half = pl.BlockSpec((1, 8, sum(LATE), 128), lambda i, core: (i // 2, i % 2, 0, 0))
    return pl.pallas_call(
        late_kernel,
        grid_spec=pltpu.PrefetchScalarGridSpec(
            num_scalar_prefetch=1,
            grid=(8,),
            in_specs=[half, half],
            out_specs=[
                pl.BlockSpec((128, 256), lambda i, core: (0, i)),
                pl.BlockSpec((128, 128), lambda i, core: (0, i)),
                pl.BlockSpec((128, 128), lambda i, core: (0, i)),
                pl.BlockSpec((256, 384), lambda i, core: (i, 0)),
            ],
        ),
        out_shape=[
            jax.ShapeDtypeStruct(shape, f32) for shape in ((128, 2048), (128, 1024), (128, 1024), (2048, 384))
        ],
        cost_estimate=pl.CostEstimate(flops=1 << 20, bytes_accessed=8 << 20, transcendentals=0),
        name="unpack_late",
    )(core, mine, other)


def local(
    hidden_in,
    gain_attn,
    gain_ffn,
    w_query,
    w_key,
    w_value,
    w_out,
    w_gate,
    w_up,
    w_down,
    qkv_shrink,
    query_expand,
    key_expand,
    value_expand,
    out_shrink,
    out_expand,
    gateup_shrink,
    gate_expand,
    up_expand,
    down_shrink,
    down_expand,
    lengths,
    adapter,
    packed_pos,
    cotangent,
):
    zh, zl, x, y, c = (lax.axis_index(name) for name in ALL)
    row = 2 * zh + c
    factor = HEAD_SIZE ** (-0.5)
    rank = out_shrink.shape[1]

    def to_rows(value):
        own = lax.dynamic_slice_in_dim(value, c * HALF, HALF, 0)
        sent = lax.dynamic_slice_in_dim(value, (1 - c) * HALF, HALF, 0)
        return jnp.concatenate([own, swap_cores(sent)], axis=0)

    def from_rows(value):
        own, got = value[:HALF], swap_cores(value[HALF:])
        return jnp.where(c == 0, jnp.concatenate([own, got], 0), jnp.concatenate([got, own], 0))

    hidden = to_rows(hidden_in)
    cot = to_rows(cotangent)

    def roll(array, by, axis):
        return lax.dynamic_slice_in_dim(jnp.concatenate([array, array], axis), by, array.shape[axis], axis)

    spread = packed_pos.reshape(2, 2, 4, 4, 2, 2, HALF)
    spread = jnp.transpose(spread, (0, 5, 1, 2, 3, 4, 6))
    rows_pos = jnp.stack([spread[:, 0], spread[:, 1, :, :, :, ::-1]], axis=1).reshape(4, 2, 4, 4, 128)
    rows_pos = roll(roll(roll(rows_pos, zl, 1), x, 2), y, 3).reshape(4, 8, GROUP)
    own_row = lax.dynamic_index_in_dim(rows_pos, row, 0, keepdims=False)
    prev_row = lax.dynamic_index_in_dim(rows_pos, jnp.maximum(row - 1, 0), 0, keepdims=False)
    prev_row = jnp.where(row == 0, far, prev_row)
    tiles_pos = jnp.concatenate([prev_row, own_row]).reshape(4, 4, GROUP)
    tiles_pos = jnp.swapaxes(tiles_pos, 0, 1)
    group_pos = own_row[0]
    seq_ends = jnp.cumsum(lengths)
    starts = seq_ends - lengths
    member = (group_pos[:, None] >= starts[None, :]) & (group_pos[:, None] < seq_ends[None, :])
    member_int = member.astype(jnp.int32)
    group_start = jnp.sum(member_int * starts[None, :], axis=1)

    def selected(pos):
        inside = (pos[:, None] >= starts[None, :]) & (pos[:, None] < seq_ends[None, :])
        owner = jnp.sum(inside.astype(jnp.int32) * adapter[None, :], axis=1)
        return (owner[:, None] == (jnp.arange(rank, dtype=jnp.int32) // RANK)[None, :]).astype(f32)

    tile_low, tile_high = jnp.min(tiles_pos, axis=2), jnp.max(tiles_pos, axis=2)
    some = (tile_low <= jnp.max(group_pos)) & (tile_high >= jnp.min(group_start))
    every = (tile_high <= jnp.min(group_pos)) & (tile_low >= jnp.max(group_start))
    active = (some.astype(jnp.int32) + (some & every).astype(jnp.int32)).reshape(16)
    select_y = selected(group_pos)
    select_x = selected(own_row.reshape(2, 4, 4, 128)[0, :, 0].reshape(GROUP))
    select = select_y[:128]
    cos_table, sin_table = rope_tables(group_pos - group_start, HEAD_SIZE)

    def column_slices(weight):
        parts = weight.reshape(16, 4, 4, 4, 2, 64)
        return jnp.transpose(parts, (2, 4, 0, 1, 3, 5)).reshape(8, 16, 1024)

    def units_at(array, axis, core):
        shape = array.shape
        array = array.reshape(shape[:axis] + (4, 4, 4, 2, 64) + shape[axis + 1 :])
        array = lax.dynamic_slice_in_dim(array, x, 1, axis + 1)
        array = lax.dynamic_slice_in_dim(array, core, 1, axis + 3)
        return array.reshape(shape[:axis] + (1024,) + shape[axis + 1 :])

    heads_q = w_query.reshape(16, 4, 512)
    heads_kv = jnp.concatenate([w_key.reshape(16, 4, 256), w_value.reshape(16, 4, 256)], axis=2)
    qkv_parts = jnp.transpose(jnp.stack([heads_q, heads_kv], axis=2), (1, 2, 0, 3)).reshape(8, 16, 512)
    qkv_parts = lax.all_to_all(qkv_parts, ("y", "c"), split_axis=0, concat_axis=0, tiled=True).reshape(128, 512)
    gate_up = jnp.concatenate([column_slices(w_gate), column_slices(w_up)], axis=2)
    gate_up = lax.all_to_all(after(gate_up, qkv_parts), ("x", "c"), split_axis=0, concat_axis=0, tiled=True).reshape(128, 2048)
    wo = lax.all_gather(w_out, ALL, axis=0, tiled=True)
    expands = [
        (units_at(gate_expand, 1, core), units_at(up_expand, 1, core), units_at(down_shrink, 0, core))
        for core in (c, 1 - c)
    ]

    def columns_of(array, width):
        return lax.dynamic_slice_in_dim(array, y * width, width, 1)

    inputs = hidden.astype(f32)
    scale_in = row_scale(inputs)
    normed = (inputs * scale_in * gain_attn).astype(bf16)
    normed, cot = lax.optimization_barrier((normed, cot))
    normed_g = gather_near(normed, "y")
    cot_g = gather_near(cot, "x")
    qkv_parts = after(qkv_parts, normed_g, cot_g)
    qkv_mine = gather_ring(gather_ring(qkv_parts, "x"), "z").reshape(2048, 512)
    qkv_other = swap_cores(qkv_mine)
    ffn = after(jnp.concatenate([gate_up, w_down], axis=0), normed_g)
    ffn_mine = lax.all_gather(ffn, ("zh", "zl", "y"), axis=0, tiled=False)
    q_expand = columns_of(query_expand, 512)
    k_expand = columns_of(key_expand, 256)
    v_expand = columns_of(value_expand, 256)
    low_qkv = (product(normed_g, qkv_shrink) * jnp.tile(select_y, (1, 3))).astype(bf16)
    lin_mine, lin_other = product(normed_g, qkv_mine), product(normed_g, qkv_other)
    query_lin = jnp.where(c == 0, lin_mine, lin_other) + product(low_qkv[:, :rank], q_expand)
    kv_lin = jnp.where(c == 0, lin_other, lin_mine)
    key_lin = kv_lin[:, :256] + product(low_qkv[:, rank : 2 * rank], k_expand)
    value_lin = kv_lin[:, 256:] + product(low_qkv[:, 2 * rank :], v_expand)
    query_heads = query_lin.reshape(GROUP, 2, HEAD_SIZE)
    key_heads = key_lin.reshape(GROUP, 1, HEAD_SIZE)
    query = (query_heads * cos_table + rotate(query_heads) * sin_table).astype(bf16)
    query = (query * bf16(factor)).reshape(GROUP, 512)
    key = (key_heads * cos_table + rotate(key_heads) * sin_table).astype(bf16).reshape(GROUP, 256)

    lines = gather_row(jnp.concatenate([key, value_lin.astype(bf16)], axis=1))
    attended = (query, group_pos[:, None], group_start[:, None], tiles_pos.reshape(4, 4, 1, GROUP)) + lines
    mixed_f, lse = attend(active, *attended)
    mixed = mixed_f.astype(bf16)

    heads = jnp.zeros((4, 128, 512), bf16)
    heads = lax.dynamic_update_index_in_dim(heads, mixed[:128], y, 0)
    for step in (1, 2, 3):
        got = shift(mixed[step * 128 : (step + 1) * 128], "y", step)
        heads = lax.dynamic_update_index_in_dim(heads, got, (y - step) % 4, 0)
    mixed_tok = jnp.transpose(heads, (1, 0, 2)).reshape(128, 2048)
    low_out = (product(mixed_tok, out_shrink) * select).astype(bf16)
    middle = inputs + product(mixed_tok, wo) + product(low_out, out_expand)
    scale_mid = row_scale(middle)
    normed_mid = (middle * scale_mid * gain_ffn).astype(bf16)
    normed_mid_g = gather_near(normed_mid, "x")
    ffn_other = swap_cores(after(ffn_mine, normed_mid))

    select_two = jnp.tile(select_x, (1, 2))
    low_gu = (product(normed_mid_g, gateup_shrink) * select_two).astype(bf16)
    grad_low_down = (times_transposed(cot_g, down_expand) * select_x).astype(bf16)
    place = jnp.arange(GROUP, dtype=jnp.int32)
    turned = (place // 32 % 4) * 128 + (place // 128) * 32 + place % 32
    perm = (turned[:, None] == place[None, :]).astype(bf16)
    given = (normed_mid_g, cot_g, low_gu, grad_low_down)
    sums = ffn_part(*given, ffn_mine, expands[0], perm)
    units_mine, sums = sums[4:], sums[:4]
    sums = ffn_part(*given, ffn_other, expands[1], perm, sums)
    units_other = sums[4:]
    result, grad_mid_part, low_down_part, grad_low_part = sums[:4]
    unit_grads = (units_mine, units_other)

    def sum_tokens(part, ring):
        sent = part.astype(bf16)
        return sum_near([sent[i * 128 : (i + 1) * 128] for i in range(4)], ring)

    back_low = sum_tokens(grad_low_part, "x")
    back = sum_tokens(grad_mid_part, "x")
    low_down_sum = sum_tokens(low_down_part, "x")

    low_down = (low_down_sum * select).astype(bf16)
    grad_low_gu = (back_low * jnp.tile(select, (1, 2))).astype(bf16)
    grad_normed_mid = back + times_transposed(grad_low_gu, gateup_shrink)
    cot_f = cot.astype(f32)
    grad_middle = cot_f + norm_back(middle, scale_mid, gain_ffn, grad_normed_mid)
    grad_attn_out = grad_middle.astype(bf16)
    grad_low_out = (times_transposed(grad_attn_out, out_expand) * select).astype(bf16)
    grad_mixed = (times_transposed(grad_attn_out, wo) + times_transposed(grad_low_out, out_shrink)).astype(bf16)

    def slices_near(array):
        def columns_at(step):
            return lax.dynamic_slice_in_dim(array, ((y + step) % 4) * 512, 512, 1)

        return jnp.concatenate([columns_at(0)] + [shift(columns_at(4 - step), "y", -step) for step in (1, 2, 3)])

    dout = slices_near(grad_mixed)
    dq, *terms = attend_back(active, *attended, mixed_f, lse, dout)
    dkv = sum_row(*terms)
    dk, dv = dkv[:, :HEAD_SIZE], dkv[:, HEAD_SIZE:]
    query_back = (dq * factor).astype(bf16).astype(f32).reshape(GROUP, 2, HEAD_SIZE)
    key_back = dk.astype(bf16).astype(f32).reshape(GROUP, 1, HEAD_SIZE)
    grad_value = dv.astype(bf16)
    grad_query = (query_back * cos_table - rotate(query_back * sin_table)).astype(bf16).reshape(GROUP, 512)
    grad_key = (key_back * cos_table - rotate(key_back * sin_table)).astype(bf16).reshape(GROUP, 256)
    grad_kv = jnp.concatenate([grad_key, grad_value], axis=1)

    grad_low_part = jnp.concatenate(
        [
            times_transposed(grad_query, q_expand),
            times_transposed(grad_key, k_expand),
            times_transposed(grad_value, v_expand),
        ],
        axis=1,
    )
    grad_low_qkv = (sum_tokens(grad_low_part, "y") * jnp.tile(select, (1, 3))).astype(bf16)
    for_mine = jnp.where(c == 0, grad_query, grad_kv)
    for_other = jnp.where(c == 0, grad_kv, grad_query)
    grad_normed_part = times_transposed(for_mine, qkv_mine) + times_transposed(for_other, qkv_other)
    grad_normed = sum_tokens(grad_normed_part, "y") + times_transposed(grad_low_qkv, qkv_shrink)
    ahead = sum_tokens(after(result, grad_normed), "x")
    output = (middle + ahead + product(low_down, down_expand)).astype(bf16)
    grad_input = (grad_middle + norm_back(inputs, scale_in, gain_attn, grad_normed)).astype(bf16)

    def features(array, at):
        return lax.dynamic_slice_in_dim(array, at * 512, 512, 1)

    def by_halves(pair_at):
        own, others = unit_grads[0][pair_at], unit_grads[1][pair_at]
        own, others = own.reshape(16, 1, 64, rank), others.reshape(16, 1, 64, rank)
        ordered = jnp.where(c == 0, jnp.concatenate([own, others], 1), jnp.concatenate([others, own], 1))
        return ordered.reshape(32, 64, rank)

    def by_rows(array):
        return array.reshape(32, array.shape[0] // 32, rank)

    low_near = gather_near(jnp.concatenate([low_down, grad_low_gu], axis=1), "x")
    grad_gateup = inner_rows(features(normed_mid_g, x), low_near[:, rank:])
    out_terms = jnp.concatenate([inner_rows(mixed_tok, grad_low_out), inner_rows(grad_attn_out, low_out)], axis=1)
    out_terms = after(out_terms.astype(bf16).reshape(4, 512, 2 * rank), dout)
    out_terms = sum_near(
        [lax.dynamic_index_in_dim(out_terms, (x + step) % 4, 0, keepdims=False) for step in range(4)], "x"
    )
    early = [
        by_halves(0),
        by_halves(1),
        by_halves(2),
        by_rows(out_terms[:, :rank]),
        by_rows(out_terms[:, rank:]),
        by_rows(inner_rows(features(cot_g, x), low_near[:, :rank])),
        by_rows(grad_gateup[:, :rank]),
        by_rows(grad_gateup[:, rank:]),
    ]
    early_sum = lax.psum_scatter(
        jnp.concatenate(early, axis=1), ("zh", "zl", "y", "c"), scatter_dimension=0, tiled=False
    )
    early_sum = after(early_sum.astype(bf16), dkv)
    early_all = lax.all_gather(early_sum, ALL, axis=0, tiled=False)

    grad_qkv = inner_rows(features(normed_g, y), gather_near(grad_low_qkv, "y"))
    late = [
        by_rows(inner_rows(grad_query, low_qkv[:, :rank])),
        by_rows(inner_rows(grad_key, low_qkv[:, rank : 2 * rank])),
        by_rows(inner_rows(grad_value, low_qkv[:, 2 * rank :])),
        by_rows(grad_qkv[:, :rank]),
        by_rows(grad_qkv[:, rank : 2 * rank]),
        by_rows(grad_qkv[:, 2 * rank :]),
    ]
    terms = jnp.concatenate(late, axis=1)
    terms = terms.reshape(16, 2, terms.shape[1], rank)
    kept = lax.dynamic_index_in_dim(terms, c, 1, keepdims=False)
    given = lax.dynamic_index_in_dim(terms, 1 - c, 1, keepdims=False).astype(bf16)
    terms = (kept + swap_cores(given).astype(f32)).reshape(4, 4, -1, rank)
    late_sum = sum_ring(sum_ring(terms, "z"), "x").astype(bf16)
    late_all = gather_ring(gather_ring(gather_ring(late_sum, "x"), "z"), "y")
    late_all = late_all.reshape(4, 16, -1, rank)
    g_gate, g_up, g_down_shrink, g_out_shrink, g_out_expand, g_down_expand, g_gateup = unpack_early(early_all)
    g_q, g_k, g_v, g_qkv = unpack_late(c.reshape(1).astype(jnp.int32), late_all, swap_cores(late_all))
    return (
        from_rows(output),
        from_rows(grad_input),
        g_qkv,
        g_q,
        g_k,
        g_v,
        g_out_shrink,
        g_out_expand,
        g_gateup,
        g_gate,
        g_up,
        g_down_shrink,
        g_down_expand,
    )


def solution(mesh):
    fine = Mesh(mesh.devices.reshape(2, 2, 4, 4, 2), ALL)
    split = P(ALL, None)
    placed = (split, P(), P()) + (split,) * 7 + (P(),) * 14 + (split,)
    return jax.shard_map(
        local,
        mesh=fine,
        in_specs=placed,
        out_specs=(split, split) + (P(),) * 11,
        check_vma=False,
    )
```

```python
from functools import partial

import jax
import jax.numpy as jnp
from jax import lax
from jax.experimental import pallas as pl
from jax.experimental.pallas import tpu as pltpu
from jax.sharding import Mesh, PartitionSpec as P

HEAD_SIZE = 256
RANK = 16
HALF = 64
GROUP = 512

ALL = ("zh", "zl", "x", "y", "c")

norm_eps = 1e-06
rope_theta = 1000042.0
neg_big = -1e30
far = 1 << 30

f32 = jnp.float32
bf16 = jnp.bfloat16


def product(left, right):
    return jnp.dot(left, right, preferred_element_type=f32)


def times_transposed(left, right):
    return lax.dot_general(left, right, (((1,), (1,)), ((), ())), preferred_element_type=f32)


def inner_rows(left, right):
    return lax.dot_general(left, right, (((0,), (0,)), ((), ())), preferred_element_type=f32)


def row_scale(value_matrix):
    return lax.rsqrt(jnp.mean(value_matrix * value_matrix, axis=-1, keepdims=True) + norm_eps)


def norm_back(value_matrix, scale, gain, grad):
    scaled = gain * grad
    return scale * scaled - value_matrix * (scale * scale * scale) * jnp.mean(
        value_matrix * scaled, axis=-1, keepdims=True
    )


def rotate(value_matrix):
    middle = value_matrix.shape[-1] // 2
    return jnp.concatenate([-value_matrix[..., middle:], value_matrix[..., :middle]], axis=-1)


def rope_tables(positions, width):
    middle = width // 2
    inverse = rope_theta ** (-(jnp.arange(middle, dtype=f32) * 2.0) / width)
    angles = positions.astype(f32)[:, None] * inverse[None, :]
    cos_half, sin_half = jnp.cos(angles), jnp.sin(angles)
    cos_table = jnp.concatenate([cos_half, cos_half], axis=-1)[:, None, :]
    sin_table = jnp.concatenate([sin_half, sin_half], axis=-1)[:, None, :]
    return (cos_table, sin_table)


OVER_X = ("zh", "zl", "y", "c")
RING = {"x": ("x",), "y": ("y",), "z": ("zh", "zl")}


def swap_cores(value):
    return lax.ppermute(value, "c", [(0, 1), (1, 0)])


def shift(value, ring, step):
    return lax.ppermute(value, RING[ring], [(i, (i + step) % 4) for i in range(4)])


def place_in(ring):
    return lax.axis_index(RING[ring])


def gather_near(value, ring, axis=0):
    return jnp.concatenate([value] + [shift(value, ring, -step) for step in (1, 2, 3)], axis=axis)


def gather_ring(value, ring):
    at = place_in(ring)
    whole_ring = jnp.zeros((4,) + value.shape, value.dtype)
    whole_ring = lax.dynamic_update_index_in_dim(whole_ring, value, at, 0)
    for step in (1, 2, 3):
        got = shift(value, ring, -step)
        whole_ring = lax.dynamic_update_index_in_dim(whole_ring, got, (at + step) % 4, 0)
    return whole_ring


def sum_near(blocks, ring):
    got = [shift(blocks[step], ring, step) for step in (2, 1, 3)]
    total = blocks[0].astype(f32)
    for term in got:
        total = total + term.astype(f32)
    return total


def sum_ring(terms, ring):
    at = place_in(ring)
    got = [
        shift(lax.dynamic_index_in_dim(terms, (at + step) % 4, 0, keepdims=False).astype(bf16), ring, step)
        for step in (1, 2, 3)
    ]
    total = lax.dynamic_index_in_dim(terms, at, 0, keepdims=False)
    for term in got:
        total = total + term.astype(f32)
    return total


CORNER = ("zh", "zl", "c")
PARTNER = [(4 * zh + 2 * zl + c, 4 * zh + 2 * (1 - zl) + c) for zh in (0, 1) for zl in (0, 1) for c in (0, 1)]
LATER = [[(2 * zl + 1, 4 + 2 * (zl ^ flip)) for zl in (0, 1)] for flip in (0, 1)]
EARLIER = [[(to, came) for came, to in pairs] for pairs in LATER]
def after(value, *others):
    return lax.optimization_barrier((value,) + others)[0]


def zero_of(value):
    return value[(slice(0, 1),) * value.ndim].reshape(()).astype(f32) * 0.0


def gather_row(key_value):
    line = jnp.stack([key_value] + [shift(key_value, "x", -step) for step in (1, 2, 3)])
    ahead = [lax.ppermute(line, CORNER, pairs) for pairs in LATER]
    partner = lax.ppermute(line, CORNER, PARTNER)
    beside = [lax.ppermute(value, "c", [(0, 1)]) for value in (line, partner)]
    return line, partner, ahead[0], ahead[1], beside[0], beside[1]


def sum_row(own, own_partner, prev, prev_partner):
    got = [lax.ppermute(value, "c", [(1, 0)]) for value in (prev_partner, prev)]
    terms = [lax.ppermute(value, CORNER, pairs) for value, pairs in zip((prev, prev_partner), EARLIER)]
    sent = (own_partner.astype(f32) + got[0].astype(f32)).astype(bf16)
    terms = [got[1], lax.ppermute(sent, CORNER, PARTNER)] + terms
    line = own.astype(f32)
    for term in terms:
        line = line + term.astype(f32)
    sent = line.astype(bf16)
    total = line[0]
    for step in (2, 1, 3):
        total = total + shift(sent[step], "x", step).astype(f32)
    return total


def allowed_mask(own_pos, own_start, key_pos):
    return (key_pos <= own_pos) & (key_pos >= own_start)


def load_tile(tile, tile_buf, own_ref, partner_ref, ahead_ref, ahead_partner_ref, beside_ref, beside_partner_ref):
    @pl.when(tile == 0)
    def _():
        tile_buf[...] = ahead_ref[0] + beside_ref[0]

    @pl.when(tile == 1)
    def _():
        tile_buf[...] = ahead_partner_ref[0] + beside_partner_ref[0]

    @pl.when(tile == 2)
    def _():
        tile_buf[...] = own_ref[0]

    @pl.when(tile == 3)
    def _():
        tile_buf[...] = partner_ref[0]


def attend_kernel(active, q_ref, pos_ref, start_ref, kpos_ref, *refs):
    mixed_ref, lse_ref, tile_buf, top, total, accum = refs[6:]
    step = pl.program_id(0)

    @pl.when(step == 0)
    def _():
        top[...] = jnp.full(top.shape, neg_big, f32)
        total[...] = jnp.zeros(total.shape, f32)
        accum[...] = jnp.zeros(accum.shape, f32)

    @pl.when(active[step] != 0)
    def _():
        load_tile(step // 4, tile_buf, *refs[:6])
        allowed = allowed_mask(pos_ref[...], start_ref[...], kpos_ref[0])
        for head in range(2):
            scores = times_transposed(q_ref[:, head * HEAD_SIZE : (head + 1) * HEAD_SIZE], tile_buf[:, :HEAD_SIZE])
            scores = jnp.where(allowed, scores, neg_big)
            top_old = top[head]
            top_new = jnp.maximum(top_old, jnp.max(scores, axis=-1, keepdims=True))
            weights_p = jnp.where(allowed, jnp.exp(scores - top_new), 0.0)
            damping = jnp.exp(top_old - top_new)
            total[head] = total[head] * damping + jnp.sum(weights_p, axis=-1, keepdims=True)
            accum[head] = accum[head] * damping + product(weights_p.astype(bf16), tile_buf[:, HEAD_SIZE:])
            top[head] = top_new

    @pl.when(step == 15)
    def _():
        for head in range(2):
            mixed_ref[:, head * HEAD_SIZE : (head + 1) * HEAD_SIZE] = accum[head] / total[head]
            lse_ref[head] = top[head] + jnp.log(total[head])


def attend_back_kernel(active, q_ref, pos_ref, start_ref, kpos_ref, *refs):
    mixed_ref, lse_ref, dout_ref, dq_ref, down_ref, dpartner_ref, dprev_ref, dprev_partner_ref = refs[6:14]
    tile_buf, delta, sums = refs[14:]
    step = pl.program_id(0)
    tile = step // 4

    @pl.when(step == 0)
    def _():
        dq_ref[...] = jnp.zeros(dq_ref.shape, f32)
        for head in range(2):
            cols = slice(head * HEAD_SIZE, (head + 1) * HEAD_SIZE)
            delta[head] = jnp.sum(dout_ref[:, cols].astype(f32) * mixed_ref[:, cols], axis=-1, keepdims=True)

    @pl.when(active[step] == 0)
    def _():
        sums[...] = jnp.zeros(sums.shape, bf16)

    @pl.when(active[step] != 0)
    def _():
        load_tile(tile, tile_buf, *refs[:6])
        allowed = allowed_mask(pos_ref[...], start_ref[...], kpos_ref[0])
        dk = jnp.zeros((GROUP, HEAD_SIZE), f32)
        dv = jnp.zeros((GROUP, HEAD_SIZE), f32)
        for head in range(2):
            cols = slice(head * HEAD_SIZE, (head + 1) * HEAD_SIZE)
            query, dout = q_ref[:, cols], dout_ref[:, cols]
            scores = times_transposed(query, tile_buf[:, :HEAD_SIZE])
            weights_p = jnp.where(allowed, jnp.exp(scores - lse_ref[head]), 0.0)
            dprobs = times_transposed(dout, tile_buf[:, HEAD_SIZE:])
            dscores = (weights_p * (dprobs - delta[head])).astype(bf16)
            dq_ref[:, cols] += product(dscores, tile_buf[:, :HEAD_SIZE])
            dk = dk + inner_rows(dscores, query)
            dv = dv + inner_rows(weights_p.astype(bf16), dout)
        sums[:, :HEAD_SIZE] = dk.astype(bf16)
        sums[:, HEAD_SIZE:] = dv.astype(bf16)

    for at, out_ref in enumerate((dprev_ref, dprev_partner_ref, down_ref, dpartner_ref)):

        @pl.when(tile == at)
        def _():
            out_ref[0] = sums[...]


def whole(shape):
    return pl.BlockSpec(shape, lambda *grid_and_refs: (0,) * len(shape))


def line_spec(tile):
    return pl.BlockSpec((1, GROUP, GROUP), lambda i, active: (jnp.clip(i - 4 * tile, 0, 3), 0, 0))


def common_specs():
    return [
        whole((GROUP, GROUP)),
        whole((GROUP, 1)),
        whole((GROUP, 1)),
        pl.BlockSpec((1, 1, GROUP), lambda i, active: (i, 0, 0)),
    ] + [line_spec(tile) for tile in (2, 3, 0, 1, 0, 1)]


def attend(active, *operands):
    return pl.pallas_call(
        attend_kernel,
        grid_spec=pltpu.PrefetchScalarGridSpec(
            num_scalar_prefetch=1,
            grid=(16,),
            in_specs=common_specs(),
            out_specs=[whole((GROUP, GROUP)), whole((2, GROUP, 1))],
            scratch_shapes=[
                pltpu.VMEM((GROUP, GROUP), bf16),
                pltpu.VMEM((2, GROUP, 1), f32),
                pltpu.VMEM((2, GROUP, 1), f32),
                pltpu.VMEM((2, GROUP, HEAD_SIZE), f32),
            ],
        ),
        out_shape=[
            jax.ShapeDtypeStruct((GROUP, GROUP), f32),
            jax.ShapeDtypeStruct((2, GROUP, 1), f32),
        ],
        compiler_params=pltpu.CompilerParams(vmem_limit_bytes=48 << 20),
        cost_estimate=pl.CostEstimate(flops=6 << 30, bytes_accessed=10 << 20, transcendentals=8 << 20),
        name="attend",
    )(active, *operands)


def attend_back(active, *operands):
    return pl.pallas_call(
        attend_back_kernel,
        grid_spec=pltpu.PrefetchScalarGridSpec(
            num_scalar_prefetch=1,
            grid=(16,),
            in_specs=common_specs() + [whole((GROUP, GROUP)), whole((2, GROUP, 1)), whole((GROUP, GROUP))],
            out_specs=[whole((GROUP, GROUP))] + [line_spec(tile) for tile in (2, 3, 0, 1)],
            scratch_shapes=[
                pltpu.VMEM((GROUP, GROUP), bf16),
                pltpu.VMEM((2, GROUP, 1), f32),
                pltpu.VMEM((GROUP, GROUP), bf16),
            ],
        ),
        out_shape=[jax.ShapeDtypeStruct((GROUP, GROUP), f32)]
        + [jax.ShapeDtypeStruct((4, GROUP, GROUP), bf16)] * 4,
        compiler_params=pltpu.CompilerParams(vmem_limit_bytes=48 << 20),
        cost_estimate=pl.CostEstimate(flops=12 << 30, bytes_accessed=20 << 20, transcendentals=8 << 20),
        name="attend_back",
    )(active, *operands)


UNITS = 1024
CHUNK = 256


def ffn_kernel(last, nm_ref, cot_ref, lgu_ref, gld_ref, wg_ref, wu_ref, wd_ref, ge_ref, ue_ref, ds_ref, perm_ref, *refs):
    if last:
        result_in, grad_in, low_in, glow_in = refs[:4]
        refs = refs[4:]
    result_ref, grad_ref, low_ref, glow_ref, gge_ref, gue_ref, gds_ref, nmp, result, grad = refs
    step = pl.program_id(0)
    rank = ds_ref.shape[1]

    @pl.when(step == 0)
    def _():
        for zone in range(4):
            cols = slice(zone * GROUP, (zone + 1) * GROUP)
            nmp[:, cols] = product(nm_ref[:, cols], perm_ref[...]).astype(bf16)
        if last:
            result[...] = result_in[...]
            grad[...] = grad_in[...]
            low_ref[...] = low_in[...]
            glow_ref[...] = glow_in[...]
        else:
            result[...] = jnp.zeros(result.shape, f32)
            grad[...] = jnp.zeros(grad.shape, f32)
            low_ref[...] = jnp.zeros(low_ref.shape, f32)
            glow_ref[...] = jnp.zeros(glow_ref.shape, f32)

    wg, wu = wg_ref[...].reshape(2048, CHUNK), wu_ref[...].reshape(2048, CHUNK)
    wd = wd_ref[...].reshape(CHUNK, 2048)
    low_gate, low_up = lgu_ref[:, :rank], lgu_ref[:, rank:]
    gate_pre = product(nmp[...], wg) + product(low_gate, ge_ref[...])
    up_pre = product(nmp[...], wu) + product(low_up, ue_ref[...])
    sigmoid_g = jax.nn.sigmoid(gate_pre)
    silu_gate = gate_pre * sigmoid_g
    active_units = (silu_gate * up_pre).astype(bf16)
    grad_active = times_transposed(cot_ref[...], wd) + times_transposed(gld_ref[...], ds_ref[...])
    grad_gate = (grad_active * up_pre * sigmoid_g * (1.0 + gate_pre * (1.0 - sigmoid_g))).astype(bf16)
    grad_up = (grad_active * silu_gate).astype(bf16)
    result[...] += product(active_units, wd)
    low_ref[...] += product(active_units, ds_ref[...])
    grad[...] += times_transposed(grad_gate, wg) + times_transposed(grad_up, wu)
    glow_ref[:, :rank] += times_transposed(grad_gate, ge_ref[...])
    glow_ref[:, rank:] += times_transposed(grad_up, ue_ref[...])
    gge_ref[...] = inner_rows(grad_gate, low_gate)
    gue_ref[...] = inner_rows(grad_up, low_up)
    gds_ref[...] = inner_rows(active_units, gld_ref[...])

    @pl.when(step == UNITS // CHUNK - 1)
    def _():
        if last:
            result_ref[...] = result[...].astype(bf16)
            for zone in range(4):
                cols = slice(zone * GROUP, (zone + 1) * GROUP)
                grad_ref[:, cols] = product(grad[:, cols].astype(bf16), perm_ref[...]).astype(bf16)
            grad_ref[:, 2048 : 2048 + 2 * rank] = glow_ref[...].astype(bf16)
            grad_ref[:, 2048 + 2 * rank :] = low_ref[...].astype(bf16)
        else:
            result_ref[...] = result[...]
            grad_ref[...] = grad[...]


def ffn_part(normed_mid, cot, low_gu, grad_low_down, weights, expands, perm, sums=None):
    last = sums is not None
    rank = low_gu.shape[1] // 2
    wide = bf16 if last else f32
    grad_width = 2048 + 3 * rank if last else 2048
    weight_specs = [
        pl.BlockSpec((16, 128, CHUNK), lambda u: (0, 0, u)),
        pl.BlockSpec((16, 128, CHUNK), lambda u: (0, 0, UNITS // CHUNK + u)),
        pl.BlockSpec((4, 64, 2048), lambda u: (u, 2, 0)),
        pl.BlockSpec((rank, CHUNK), lambda u: (0, u)),
        pl.BlockSpec((rank, CHUNK), lambda u: (0, u)),
        pl.BlockSpec((CHUNK, rank), lambda u: (u, 0)),
    ]
    sum_specs = [whole((GROUP, 2048)), whole((GROUP, 2048)), whole((GROUP, rank)), whole((GROUP, 2 * rank))]
    return pl.pallas_call(
        partial(ffn_kernel, last),
        grid=(UNITS // CHUNK,),
        in_specs=[whole((GROUP, 2048)), whole((GROUP, 2048)), whole((GROUP, 2 * rank)), whole((GROUP, rank))]
        + weight_specs
        + [whole((GROUP, GROUP))]
        + (sum_specs if last else []),
        out_specs=[whole((GROUP, 2048)), whole((GROUP, grad_width))]
        + sum_specs[2:]
        + [pl.BlockSpec((CHUNK, rank), lambda u: (u, 0))] * 3,
        out_shape=[
            jax.ShapeDtypeStruct((GROUP, 2048), wide),
            jax.ShapeDtypeStruct((GROUP, grad_width), wide),
            jax.ShapeDtypeStruct((GROUP, rank), f32),
            jax.ShapeDtypeStruct((GROUP, 2 * rank), f32),
        ]
        + [jax.ShapeDtypeStruct((UNITS, rank), f32)] * 3,
        scratch_shapes=[
            pltpu.VMEM((GROUP, 2048), bf16),
            pltpu.VMEM((GROUP, 2048), f32),
            pltpu.VMEM((GROUP, 2048), f32),
        ],
        compiler_params=pltpu.CompilerParams(vmem_limit_bytes=60 << 20),
        cost_estimate=pl.CostEstimate(flops=14 << 30, bytes_accessed=30 << 20, transcendentals=1 << 20),
        name="feed_forward",
    )(normed_mid, cot, low_gu, grad_low_down, weights, weights, weights, *expands, perm, *(sums or ()))


EARLY = (64, 64, 64, 16, 16, 16, 16, 16)
LATE = (16, 8, 8, 16, 16, 16)


def cut(array, sizes):
    found, at = [], 0
    for size in sizes:
        found.append(array[..., at : at + size, :])
        at += size
    return found


def early_kernel(all_ref, gate_ref, up_ref, down_ref, oshrink_ref, oexpand_ref, dexpand_ref, gateup_ref):
    pieces = [piece.astype(f32).reshape(-1, 128) for piece in cut(all_ref[...], EARLY)]
    gate_ref[...] = pieces[0].T
    up_ref[...] = pieces[1].T
    down_ref[...] = pieces[2]
    oshrink_ref[...] = pieces[3]
    oexpand_ref[...] = pieces[4].T
    dexpand_ref[...] = pieces[5].T
    gateup_ref[:, :128] = pieces[6]
    gateup_ref[:, 128:] = pieces[7]


def unpack_early(everyone):
    def rows_at(i):
        return (i % 4) * 4 + i // 4

    return pl.pallas_call(
        early_kernel,
        grid=(16,),
        in_specs=[pl.BlockSpec((8, sum(EARLY), 128), lambda i: (i, 0, 0))],
        out_specs=[
            pl.BlockSpec((128, 512), lambda i: (0, i)),
            pl.BlockSpec((128, 512), lambda i: (0, i)),
            pl.BlockSpec((512, 128), lambda i: (i, 0)),
            pl.BlockSpec((128, 128), lambda i: (rows_at(i), 0)),
            pl.BlockSpec((128, 128), lambda i: (0, rows_at(i))),
            pl.BlockSpec((128, 128), lambda i: (0, rows_at(i))),
            pl.BlockSpec((128, 256), lambda i: (rows_at(i), 0)),
        ],
        out_shape=[
            jax.ShapeDtypeStruct(shape, f32)
            for shape in ((128, 8192), (128, 8192), (8192, 128), (2048, 128), (128, 2048), (128, 2048), (2048, 256))
        ],
        cost_estimate=pl.CostEstimate(flops=1 << 20, bytes_accessed=27 << 20, transcendentals=0),
        name="unpack_early",
    )(everyone)


def late_kernel(core, mine_ref, other_ref, q_ref, k_ref, v_ref, low_ref):
    mine, other = mine_ref[0].astype(f32), other_ref[0].astype(f32)
    first, second = jnp.where(core[0] == 0, mine, other), jnp.where(core[0] == 0, other, mine)
    pieces = [
        jnp.stack(pair, axis=1).reshape(-1, 128) for pair in zip(cut(first, LATE), cut(second, LATE))
    ]
    q_ref[...] = pieces[0].T
    k_ref[...] = pieces[1].T
    v_ref[...] = pieces[2].T
    for at in range(3):
        low_ref[:, at * 128 : (at + 1) * 128] = pieces[3 + at]


def unpack_late(core, mine, other):
    half = pl.BlockSpec((1, 8, sum(LATE), 128), lambda i, core: (i // 2, i % 2, 0, 0))
    return pl.pallas_call(
        late_kernel,
        grid_spec=pltpu.PrefetchScalarGridSpec(
            num_scalar_prefetch=1,
            grid=(8,),
            in_specs=[half, half],
            out_specs=[
                pl.BlockSpec((128, 256), lambda i, core: (0, i)),
                pl.BlockSpec((128, 128), lambda i, core: (0, i)),
                pl.BlockSpec((128, 128), lambda i, core: (0, i)),
                pl.BlockSpec((256, 384), lambda i, core: (i, 0)),
            ],
        ),
        out_shape=[
            jax.ShapeDtypeStruct(shape, f32) for shape in ((128, 2048), (128, 1024), (128, 1024), (2048, 384))
        ],
        cost_estimate=pl.CostEstimate(flops=1 << 20, bytes_accessed=8 << 20, transcendentals=0),
        name="unpack_late",
    )(core, mine, other)


def local(
    hidden_in,
    gain_attn,
    gain_ffn,
    w_query,
    w_key,
    w_value,
    w_out,
    w_gate,
    w_up,
    w_down,
    qkv_shrink,
    query_expand,
    key_expand,
    value_expand,
    out_shrink,
    out_expand,
    gateup_shrink,
    gate_expand,
    up_expand,
    down_shrink,
    down_expand,
    lengths,
    adapter,
    packed_pos,
    cotangent,
):
    zh, zl, x, y, c = (lax.axis_index(name) for name in ALL)
    row = 2 * zh + c
    factor = HEAD_SIZE ** (-0.5)
    rank = out_shrink.shape[1]

    def to_rows(value):
        own = lax.dynamic_slice_in_dim(value, c * HALF, HALF, 0)
        sent = lax.dynamic_slice_in_dim(value, (1 - c) * HALF, HALF, 0)
        return jnp.concatenate([own, swap_cores(sent)], axis=0)

    def from_rows(value):
        own, got = value[:HALF], swap_cores(value[HALF:])
        return jnp.where(c == 0, jnp.concatenate([own, got], 0), jnp.concatenate([got, own], 0))

    hidden = to_rows(hidden_in)
    cot = to_rows(cotangent)

    def roll(array, by, axis):
        return lax.dynamic_slice_in_dim(jnp.concatenate([array, array], axis), by, array.shape[axis], axis)

    spread = packed_pos.reshape(2, 2, 4, 4, 2, 2, HALF)
    spread = jnp.transpose(spread, (0, 5, 1, 2, 3, 4, 6))
    rows_pos = jnp.stack([spread[:, 0], spread[:, 1, :, :, :, ::-1]], axis=1).reshape(4, 2, 4, 4, 128)
    rows_pos = roll(roll(roll(rows_pos, zl, 1), x, 2), y, 3).reshape(4, 8, GROUP)
    own_row = lax.dynamic_index_in_dim(rows_pos, row, 0, keepdims=False)
    prev_row = lax.dynamic_index_in_dim(rows_pos, jnp.maximum(row - 1, 0), 0, keepdims=False)
    prev_row = jnp.where(row == 0, far, prev_row)
    tiles_pos = jnp.concatenate([prev_row, own_row])
    group_pos = own_row[0]
    seq_ends = jnp.cumsum(lengths)
    starts = seq_ends - lengths
    member = (group_pos[:, None] >= starts[None, :]) & (group_pos[:, None] < seq_ends[None, :])
    member_int = member.astype(jnp.int32)
    group_start = jnp.sum(member_int * starts[None, :], axis=1)

    def selected(pos):
        inside = (pos[:, None] >= starts[None, :]) & (pos[:, None] < seq_ends[None, :])
        owner = jnp.sum(inside.astype(jnp.int32) * adapter[None, :], axis=1)
        return (owner[:, None] == (jnp.arange(rank, dtype=jnp.int32) // RANK)[None, :]).astype(f32)

    tile_low, tile_high = jnp.min(tiles_pos, axis=1), jnp.max(tiles_pos, axis=1)
    active = (tile_low <= jnp.max(group_pos)) & (tile_high >= jnp.min(group_start))
    active = active.astype(jnp.int32)
    select_y = selected(group_pos)
    select_x = selected(own_row.reshape(2, 4, 4, 128)[0, :, 0].reshape(GROUP))
    select = select_y[:128]
    cos_table, sin_table = rope_tables(group_pos - group_start, HEAD_SIZE)

    def column_slices(weight):
        parts = weight.reshape(16, 4, 4, 4, 2, 64)
        return jnp.transpose(parts, (2, 4, 0, 1, 3, 5)).reshape(8, 16, 1024)

    def units_at(array, axis, core):
        shape = array.shape
        array = array.reshape(shape[:axis] + (4, 4, 4, 2, 64) + shape[axis + 1 :])
        array = lax.dynamic_slice_in_dim(array, x, 1, axis + 1)
        array = lax.dynamic_slice_in_dim(array, core, 1, axis + 3)
        return array.reshape(shape[:axis] + (1024,) + shape[axis + 1 :])

    heads_q = w_query.reshape(16, 4, 512)
    heads_kv = jnp.concatenate([w_key.reshape(16, 4, 256), w_value.reshape(16, 4, 256)], axis=2)
    qkv_parts = jnp.transpose(jnp.stack([heads_q, heads_kv], axis=2), (1, 2, 0, 3)).reshape(8, 16, 512)
    qkv_parts = lax.all_to_all(qkv_parts, ("y", "c"), split_axis=0, concat_axis=0, tiled=True).reshape(128, 512)
    gate_up = jnp.concatenate([column_slices(w_gate), column_slices(w_up)], axis=2)
    gate_up = lax.all_to_all(after(gate_up, qkv_parts), ("x", "c"), split_axis=0, concat_axis=0, tiled=True).reshape(128, 2048)
    expands = [
        (units_at(gate_expand, 1, core), units_at(up_expand, 1, core), units_at(down_shrink, 0, core))
        for core in (c, 1 - c)
    ]

    def columns_of(array, width):
        return lax.dynamic_slice_in_dim(array, y * width, width, 1)

    inputs = hidden.astype(f32)
    scale_in = row_scale(inputs)
    normed = (inputs * scale_in * gain_attn).astype(bf16)
    normed, cot, qkv_parts, gate_up = lax.optimization_barrier((normed, cot, qkv_parts, gate_up))
    normed_g = gather_near(normed, "y")
    cot_g = gather_near(cot, "x")
    qkv_parts = after(qkv_parts, normed_g, cot_g, expands)
    wo = lax.all_gather(after(w_out, normed_g, cot_g), ALL, axis=0, tiled=True)
    qkv_mine = gather_ring(gather_ring(qkv_parts, "x"), "z").reshape(2048, 512)
    qkv_other = swap_cores(qkv_mine)
    ffn = after(jnp.concatenate([gate_up, w_down], axis=0), normed_g, cot_g)
    ffn_mine = lax.all_gather(ffn, ("zh", "zl", "y"), axis=0, tiled=False)
    q_expand = columns_of(query_expand, 512)
    k_expand = columns_of(key_expand, 256)
    v_expand = columns_of(value_expand, 256)
    low_qkv = (product(normed_g, qkv_shrink) * jnp.tile(select_y, (1, 3))).astype(bf16)
    lin_mine, lin_other = product(normed_g, qkv_mine), product(normed_g, qkv_other)
    query_lin = jnp.where(c == 0, lin_mine, lin_other) + product(low_qkv[:, :rank], q_expand)
    kv_lin = jnp.where(c == 0, lin_other, lin_mine)
    key_lin = kv_lin[:, :256] + product(low_qkv[:, rank : 2 * rank], k_expand)
    value_lin = kv_lin[:, 256:] + product(low_qkv[:, 2 * rank :], v_expand)
    query_heads = query_lin.reshape(GROUP, 2, HEAD_SIZE)
    key_heads = key_lin.reshape(GROUP, 1, HEAD_SIZE)
    query = (query_heads * cos_table + rotate(query_heads) * sin_table).astype(bf16)
    query = (query * bf16(factor)).reshape(GROUP, 512)
    key = (key_heads * cos_table + rotate(key_heads) * sin_table).astype(bf16).reshape(GROUP, 256)

    lines = gather_row(jnp.concatenate([key, value_lin.astype(bf16)], axis=1))
    attended = (query, group_pos[:, None], group_start[:, None], tiles_pos.reshape(16, 1, GROUP)) + lines
    mixed_f, lse = attend(active, *attended)
    mixed = mixed_f.astype(bf16)

    heads = jnp.zeros((4, 128, 512), bf16)
    heads = lax.dynamic_update_index_in_dim(heads, mixed[:128], y, 0)
    for step in (1, 2, 3):
        got = shift(mixed[step * 128 : (step + 1) * 128], "y", step)
        heads = lax.dynamic_update_index_in_dim(heads, got, (y - step) % 4, 0)
    mixed_tok = jnp.transpose(heads, (1, 0, 2)).reshape(128, 2048)
    low_out = (product(mixed_tok, out_shrink) * select).astype(bf16)
    middle = inputs + product(mixed_tok, wo) + product(low_out, out_expand)
    scale_mid = row_scale(middle)
    normed_mid = (middle * scale_mid * gain_ffn).astype(bf16)
    normed_mid_g = gather_near(normed_mid, "x")
    ffn_other = swap_cores(after(ffn_mine, normed_mid))

    select_two = jnp.tile(select_x, (1, 2))
    low_gu = (product(normed_mid_g, gateup_shrink) * select_two).astype(bf16)
    grad_low_down = (times_transposed(cot_g, down_expand) * select_x).astype(bf16)
    place = jnp.arange(GROUP, dtype=jnp.int32)
    turned = (place // 32 % 4) * 128 + (place // 128) * 32 + place % 32
    perm = (turned[:, None] == place[None, :]).astype(bf16)
    given = (normed_mid_g, cot_g, low_gu, grad_low_down)
    sums = ffn_part(*given, ffn_mine, expands[0], perm)
    units_mine, sums = sums[4:], sums[:4]
    sums = ffn_part(*given, ffn_other, expands[1], perm, sums)
    units_other = sums[4:]
    result, back_part = sums[:2]
    unit_grads = (units_mine, units_other)

    def reduce_units(unit_grads):
        def by_halves(pair_at):
            own, others = unit_grads[0][pair_at], unit_grads[1][pair_at]
            own, others = own.reshape(16, 1, 64, rank), others.reshape(16, 1, 64, rank)
            ordered = jnp.where(c == 0, jnp.concatenate([own, others], 1), jnp.concatenate([others, own], 1))
            return ordered.reshape(32, 64, rank)

        unit_terms = jnp.concatenate([by_halves(0), by_halves(1), by_halves(2)], axis=1)
        return lax.psum_scatter(unit_terms, OVER_X, scatter_dimension=0, tiled=False)

    def sum_tokens(part, ring):
        sent = part.astype(bf16)
        return sum_near([sent[i * 128 : (i + 1) * 128] for i in range(4)], ring)

    back = sum_tokens(back_part, "x")
    back, back_low, low_down_sum = back[:, :2048], back[:, 2048 : 2048 + 2 * rank], back[:, 2048 + 2 * rank :]

    low_down = (low_down_sum * select).astype(bf16)
    grad_low_gu = (back_low * jnp.tile(select, (1, 2))).astype(bf16)
    grad_normed_mid = back + times_transposed(grad_low_gu, gateup_shrink)
    cot_f = cot.astype(f32)
    grad_middle = cot_f + norm_back(middle, scale_mid, gain_ffn, grad_normed_mid)
    grad_attn_out = grad_middle.astype(bf16)
    grad_low_out = (times_transposed(grad_attn_out, out_expand) * select).astype(bf16)
    grad_mixed = (times_transposed(grad_attn_out, wo) + times_transposed(grad_low_out, out_shrink)).astype(bf16)

    def slices_near(array):
        def columns_at(step):
            return lax.dynamic_slice_in_dim(array, ((y + step) % 4) * 512, 512, 1)

        return jnp.concatenate([columns_at(0)] + [shift(columns_at(4 - step), "y", -step) for step in (1, 2, 3)])

    unit_sum = reduce_units(unit_grads)
    dout = slices_near(grad_mixed)
    dout = dout + zero_of(unit_sum).astype(bf16)
    dq, *terms = attend_back(active, *attended, mixed_f, lse, dout)
    dkv = sum_row(*terms)
    dk, dv = dkv[:, :HEAD_SIZE], dkv[:, HEAD_SIZE:]
    query_back = (dq * factor).astype(bf16).astype(f32).reshape(GROUP, 2, HEAD_SIZE)
    key_back = dk.astype(bf16).astype(f32).reshape(GROUP, 1, HEAD_SIZE)
    grad_value = dv.astype(bf16)
    grad_query = (query_back * cos_table - rotate(query_back * sin_table)).astype(bf16).reshape(GROUP, 512)
    grad_key = (key_back * cos_table - rotate(key_back * sin_table)).astype(bf16).reshape(GROUP, 256)
    grad_kv = jnp.concatenate([grad_key, grad_value], axis=1)

    grad_low_part = jnp.concatenate(
        [
            times_transposed(grad_query, q_expand),
            times_transposed(grad_key, k_expand),
            times_transposed(grad_value, v_expand),
        ],
        axis=1,
    )
    grad_low_qkv = (sum_tokens(grad_low_part, "y") * jnp.tile(select, (1, 3))).astype(bf16)
    for_mine = jnp.where(c == 0, grad_query, grad_kv)
    for_other = jnp.where(c == 0, grad_kv, grad_query)
    grad_normed_part = times_transposed(for_mine, qkv_mine) + times_transposed(for_other, qkv_other)
    grad_normed = sum_tokens(grad_normed_part, "y") + times_transposed(grad_low_qkv, qkv_shrink)
    ahead = sum_tokens(after(result, grad_normed), "x")
    output = (middle + ahead + product(low_down, down_expand)).astype(bf16)
    grad_input = (grad_middle + norm_back(inputs, scale_in, gain_attn, grad_normed)).astype(bf16)

    def features(array, at):
        return lax.dynamic_slice_in_dim(array, at * 512, 512, 1)

    def by_rows(array):
        return array.reshape(32, array.shape[0] // 32, rank)

    low_near = gather_near(after(jnp.concatenate([low_down, grad_low_gu], axis=1), dout), "x")
    grad_gateup = inner_rows(features(normed_mid_g, x), low_near[:, rank:])
    out_terms = jnp.concatenate([inner_rows(mixed_tok, grad_low_out), inner_rows(grad_attn_out, low_out)], axis=1)
    out_terms = after(out_terms.astype(bf16).reshape(4, 512, 2 * rank), dout)
    out_terms = sum_near(
        [lax.dynamic_index_in_dim(out_terms, (x + step) % 4, 0, keepdims=False) for step in range(4)], "x"
    )
    row_terms = [
        by_rows(out_terms[:, :rank]),
        by_rows(out_terms[:, rank:]),
        by_rows(inner_rows(features(cot_g, x), low_near[:, :rank])),
        by_rows(grad_gateup[:, :rank]),
        by_rows(grad_gateup[:, rank:]),
    ]
    row_sum = lax.psum_scatter(jnp.concatenate(row_terms, axis=1) + zero_of(unit_sum), OVER_X, scatter_dimension=0, tiled=False)
    early_sum = jnp.concatenate([unit_sum, row_sum], axis=0)
    early_sum = after(early_sum.astype(bf16), dkv)
    early_all = lax.all_gather(early_sum, ALL, axis=0, tiled=False)

    grad_qkv = inner_rows(features(normed_g, y), gather_near(grad_low_qkv, "y"))
    late = [
        by_rows(inner_rows(grad_query, low_qkv[:, :rank])),
        by_rows(inner_rows(grad_key, low_qkv[:, rank : 2 * rank])),
        by_rows(inner_rows(grad_value, low_qkv[:, 2 * rank :])),
        by_rows(grad_qkv[:, :rank]),
        by_rows(grad_qkv[:, rank : 2 * rank]),
        by_rows(grad_qkv[:, 2 * rank :]),
    ]
    terms = jnp.concatenate(late, axis=1)
    terms = terms.reshape(16, 2, terms.shape[1], rank)
    kept = lax.dynamic_index_in_dim(terms, c, 1, keepdims=False)
    given = lax.dynamic_index_in_dim(terms, 1 - c, 1, keepdims=False).astype(bf16)
    terms = (kept + swap_cores(given).astype(f32)).reshape(4, 4, -1, rank)
    late_sum = sum_ring(sum_ring(terms, "z"), "x").astype(bf16)
    late_all = gather_ring(gather_ring(gather_ring(late_sum, "x"), "z"), "y")
    late_all = late_all.reshape(4, 16, -1, rank)
    g_gate, g_up, g_down_shrink, g_out_shrink, g_out_expand, g_down_expand, g_gateup = unpack_early(early_all)
    late_other = swap_cores(late_all)
    late_all = after(late_all, g_gate, g_gateup)
    g_q, g_k, g_v, g_qkv = unpack_late(c.reshape(1).astype(jnp.int32), late_all, late_other)
    return (
        from_rows(output),
        from_rows(grad_input),
        g_qkv,
        g_q,
        g_k,
        g_v,
        g_out_shrink,
        g_out_expand,
        g_gateup,
        g_gate,
        g_up,
        g_down_shrink,
        g_down_expand,
    )


def solution(mesh):
    fine = Mesh(mesh.devices.reshape(2, 2, 4, 4, 2), ALL)
    split = P(ALL, None)
    placed = (split, P(), P()) + (split,) * 7 + (P(),) * 14 + (split,)
    return jax.shard_map(
        local,
        mesh=fine,
        in_specs=placed,
        out_specs=(split, split) + (P(),) * 11,
        check_vma=False,
    )
```

```python
from functools import partial

import jax
import jax.numpy as jnp
from jax import lax
from jax.experimental import pallas as pl
from jax.experimental.pallas import tpu as pltpu
from jax.sharding import Mesh, PartitionSpec as P

HEAD_SIZE = 256
RANK = 16
HALF = 64
GROUP = 512

ALL = ("zh", "zl", "x", "y", "c")

norm_eps = 1e-06
rope_theta = 1000042.0
neg_big = -1e30
far = 1 << 30

f32 = jnp.float32
bf16 = jnp.bfloat16


def product(left, right):
    return jnp.dot(left, right, preferred_element_type=f32)


def times_transposed(left, right):
    return lax.dot_general(left, right, (((1,), (1,)), ((), ())), preferred_element_type=f32)


def inner_rows(left, right):
    return lax.dot_general(left, right, (((0,), (0,)), ((), ())), preferred_element_type=f32)


def row_scale(value_matrix):
    return lax.rsqrt(jnp.mean(value_matrix * value_matrix, axis=-1, keepdims=True) + norm_eps)


def norm_back(value_matrix, scale, gain, grad):
    scaled = gain * grad
    return scale * scaled - value_matrix * (scale * scale * scale) * jnp.mean(
        value_matrix * scaled, axis=-1, keepdims=True
    )


def rotate(value_matrix):
    middle = value_matrix.shape[-1] // 2
    return jnp.concatenate([-value_matrix[..., middle:], value_matrix[..., :middle]], axis=-1)


def rope_tables(positions, width):
    middle = width // 2
    inverse = rope_theta ** (-(jnp.arange(middle, dtype=f32) * 2.0) / width)
    angles = positions.astype(f32)[:, None] * inverse[None, :]
    cos_half, sin_half = jnp.cos(angles), jnp.sin(angles)
    cos_table = jnp.concatenate([cos_half, cos_half], axis=-1)[:, None, :]
    sin_table = jnp.concatenate([sin_half, sin_half], axis=-1)[:, None, :]
    return (cos_table, sin_table)


OVER_X = ("zh", "zl", "y", "c")
RING = {"x": ("x",), "y": ("y",), "z": ("zh", "zl")}


def swap_cores(value):
    return lax.ppermute(value, "c", [(0, 1), (1, 0)])


def shift(value, ring, step):
    return lax.ppermute(value, RING[ring], [(i, (i + step) % 4) for i in range(4)])


def place_in(ring):
    return lax.axis_index(RING[ring])


def gather_near(value, ring, axis=0):
    return jnp.concatenate([value] + [shift(value, ring, -step) for step in (1, 2, 3)], axis=axis)


def gather_ring(value, ring):
    at = place_in(ring)
    whole_ring = jnp.zeros((4,) + value.shape, value.dtype)
    whole_ring = lax.dynamic_update_index_in_dim(whole_ring, value, at, 0)
    for step in (1, 2, 3):
        got = shift(value, ring, -step)
        whole_ring = lax.dynamic_update_index_in_dim(whole_ring, got, (at + step) % 4, 0)
    return whole_ring


def sum_near(blocks, ring):
    got = [shift(blocks[step], ring, step) for step in (2, 1, 3)]
    total = blocks[0].astype(f32)
    for term in got:
        total = total + term.astype(f32)
    return total


def sum_ring(terms, ring):
    at = place_in(ring)
    got = [
        shift(lax.dynamic_index_in_dim(terms, (at + step) % 4, 0, keepdims=False).astype(bf16), ring, step)
        for step in (1, 2, 3)
    ]
    total = lax.dynamic_index_in_dim(terms, at, 0, keepdims=False)
    for term in got:
        total = total + term.astype(f32)
    return total


CORNER = ("zh", "zl", "c")
PARTNER = [(4 * zh + 2 * zl + c, 4 * zh + 2 * (1 - zl) + c) for zh in (0, 1) for zl in (0, 1) for c in (0, 1)]
LATER = [[(2 * zl + 1, 4 + 2 * (zl ^ flip)) for zl in (0, 1)] for flip in (0, 1)]
EARLIER = [[(to, came) for came, to in pairs] for pairs in LATER]
def after(value, *others):
    return lax.optimization_barrier((value,) + others)[0]


def zero_of(value):
    return value[(slice(0, 1),) * value.ndim].reshape(()).astype(f32) * 0.0


def gather_row(key_value):
    line = jnp.stack([key_value] + [shift(key_value, "x", -step) for step in (1, 2, 3)])
    ahead = [lax.ppermute(line, CORNER, pairs) for pairs in LATER]
    partner = lax.ppermute(line, CORNER, PARTNER)
    beside = [lax.ppermute(value, "c", [(0, 1)]) for value in (line, partner)]
    return line, partner, ahead[0], ahead[1], beside[0], beside[1]


def sum_row(own, own_partner, prev, prev_partner):
    got = [lax.ppermute(value, "c", [(1, 0)]) for value in (prev_partner, prev)]
    terms = [lax.ppermute(value, CORNER, pairs) for value, pairs in zip((prev, prev_partner), EARLIER)]
    sent = (own_partner.astype(f32) + got[0].astype(f32)).astype(bf16)
    terms = [got[1], lax.ppermute(sent, CORNER, PARTNER)] + terms
    line = own.astype(f32)
    for term in terms:
        line = line + term.astype(f32)
    sent = line.astype(bf16)
    total = line[0]
    for step in (2, 1, 3):
        total = total + shift(sent[step], "x", step).astype(f32)
    return total


def allowed_mask(own_pos, own_start, key_pos):
    return (key_pos <= own_pos) & (key_pos >= own_start)


def load_tile(tile, tile_buf, own_ref, partner_ref, ahead_ref, ahead_partner_ref, beside_ref, beside_partner_ref):
    @pl.when(tile == 0)
    def _():
        tile_buf[...] = ahead_ref[0] + beside_ref[0]

    @pl.when(tile == 1)
    def _():
        tile_buf[...] = ahead_partner_ref[0] + beside_partner_ref[0]

    @pl.when(tile == 2)
    def _():
        tile_buf[...] = own_ref[0]

    @pl.when(tile == 3)
    def _():
        tile_buf[...] = partner_ref[0]


def attend_kernel(active, q_ref, pos_ref, start_ref, kpos_ref, *refs):
    mixed_ref, lse_ref, tile_buf, top, total, accum = refs[6:]
    step = pl.program_id(0)

    @pl.when(step == 0)
    def _():
        top[...] = jnp.full(top.shape, neg_big, f32)
        total[...] = jnp.zeros(total.shape, f32)
        accum[...] = jnp.zeros(accum.shape, f32)

    @pl.when(active[step] != 0)
    def _():
        load_tile(step // 4, tile_buf, *refs[:6])
        allowed = allowed_mask(pos_ref[...], start_ref[...], kpos_ref[0])
        for head in range(2):
            scores = times_transposed(q_ref[:, head * HEAD_SIZE : (head + 1) * HEAD_SIZE], tile_buf[:, :HEAD_SIZE])
            scores = jnp.where(allowed, scores, neg_big)
            top_old = top[head]
            top_new = jnp.maximum(top_old, jnp.max(scores, axis=-1, keepdims=True))
            weights_p = jnp.where(allowed, jnp.exp(scores - top_new), 0.0)
            damping = jnp.exp(top_old - top_new)
            total[head] = total[head] * damping + jnp.sum(weights_p, axis=-1, keepdims=True)
            accum[head] = accum[head] * damping + product(weights_p.astype(bf16), tile_buf[:, HEAD_SIZE:])
            top[head] = top_new

    @pl.when(step == 15)
    def _():
        for head in range(2):
            mixed_ref[:, head * HEAD_SIZE : (head + 1) * HEAD_SIZE] = accum[head] / total[head]
            lse_ref[head] = top[head] + jnp.log(total[head])


def attend_back_kernel(active, q_ref, pos_ref, start_ref, kpos_ref, *refs):
    mixed_ref, lse_ref, dout_ref, dq_ref, down_ref, dpartner_ref, dprev_ref, dprev_partner_ref = refs[6:14]
    tile_buf, delta, sums = refs[14:]
    step = pl.program_id(0)
    tile = step // 4

    @pl.when(step == 0)
    def _():
        dq_ref[...] = jnp.zeros(dq_ref.shape, f32)
        for head in range(2):
            cols = slice(head * HEAD_SIZE, (head + 1) * HEAD_SIZE)
            delta[head] = jnp.sum(dout_ref[:, cols].astype(f32) * mixed_ref[:, cols], axis=-1, keepdims=True)

    @pl.when(active[step] == 0)
    def _():
        sums[...] = jnp.zeros(sums.shape, bf16)

    @pl.when(active[step] != 0)
    def _():
        load_tile(tile, tile_buf, *refs[:6])
        allowed = allowed_mask(pos_ref[...], start_ref[...], kpos_ref[0])
        dk = jnp.zeros((GROUP, HEAD_SIZE), f32)
        dv = jnp.zeros((GROUP, HEAD_SIZE), f32)
        for head in range(2):
            cols = slice(head * HEAD_SIZE, (head + 1) * HEAD_SIZE)
            query, dout = q_ref[:, cols], dout_ref[:, cols]
            scores = times_transposed(query, tile_buf[:, :HEAD_SIZE])
            weights_p = jnp.where(allowed, jnp.exp(scores - lse_ref[head]), 0.0)
            dprobs = times_transposed(dout, tile_buf[:, HEAD_SIZE:])
            dscores = (weights_p * (dprobs - delta[head])).astype(bf16)
            dq_ref[:, cols] += product(dscores, tile_buf[:, :HEAD_SIZE])
            dk = dk + inner_rows(dscores, query)
            dv = dv + inner_rows(weights_p.astype(bf16), dout)
        sums[:, :HEAD_SIZE] = dk.astype(bf16)
        sums[:, HEAD_SIZE:] = dv.astype(bf16)

    for at, out_ref in enumerate((dprev_ref, dprev_partner_ref, down_ref, dpartner_ref)):

        @pl.when(tile == at)
        def _():
            out_ref[0] = sums[...]


def whole(shape):
    return pl.BlockSpec(shape, lambda *grid_and_refs: (0,) * len(shape))


def line_spec(tile):
    return pl.BlockSpec((1, GROUP, GROUP), lambda i, active: (jnp.clip(i - 4 * tile, 0, 3), 0, 0))


def active_spec(tile, table):
    return pl.BlockSpec(
        (1, GROUP, GROUP), lambda i, active: (active[16 * table + 4 * tile + jnp.clip(i - 4 * tile, 0, 3)], 0, 0)
    )


def step_tables(active, c):
    marks = active.reshape(4, 4)
    at = jnp.arange(4, dtype=jnp.int32)
    seen = jnp.where((marks[:, None, :] != 0) & (at[None, None, :] <= at[None, :, None]), at[None, None, :], -1)
    last = jnp.max(seen, axis=2)
    first = jnp.min(jnp.where(marks != 0, at[None, :], 3), axis=1, keepdims=True)
    blocks = jnp.where(last >= 0, last, first).reshape(16).astype(jnp.int32)
    return jnp.concatenate([active, blocks, jnp.where(c == 0, blocks, 0), jnp.where(c == 0, 0, blocks)])


def common_specs():
    return [
        whole((GROUP, GROUP)),
        whole((GROUP, 1)),
        whole((GROUP, 1)),
        pl.BlockSpec((1, 1, GROUP), lambda i, active: (i, 0, 0)),
    ] + [active_spec(tile, table) for tile, table in ((2, 1), (3, 1), (0, 2), (1, 2), (0, 3), (1, 3))]


def attend(active, *operands):
    return pl.pallas_call(
        attend_kernel,
        grid_spec=pltpu.PrefetchScalarGridSpec(
            num_scalar_prefetch=1,
            grid=(16,),
            in_specs=common_specs(),
            out_specs=[whole((GROUP, GROUP)), whole((2, GROUP, 1))],
            scratch_shapes=[
                pltpu.VMEM((GROUP, GROUP), bf16),
                pltpu.VMEM((2, GROUP, 1), f32),
                pltpu.VMEM((2, GROUP, 1), f32),
                pltpu.VMEM((2, GROUP, HEAD_SIZE), f32),
            ],
        ),
        out_shape=[
            jax.ShapeDtypeStruct((GROUP, GROUP), f32),
            jax.ShapeDtypeStruct((2, GROUP, 1), f32),
        ],
        compiler_params=pltpu.CompilerParams(vmem_limit_bytes=48 << 20),
        cost_estimate=pl.CostEstimate(flops=6 << 30, bytes_accessed=10 << 20, transcendentals=8 << 20),
        name="attend",
    )(active, *operands)


def attend_back(active, *operands):
    return pl.pallas_call(
        attend_back_kernel,
        grid_spec=pltpu.PrefetchScalarGridSpec(
            num_scalar_prefetch=1,
            grid=(16,),
            in_specs=common_specs() + [whole((GROUP, GROUP)), whole((2, GROUP, 1)), whole((GROUP, GROUP))],
            out_specs=[whole((GROUP, GROUP))] + [line_spec(tile) for tile in (2, 3, 0, 1)],
            scratch_shapes=[
                pltpu.VMEM((GROUP, GROUP), bf16),
                pltpu.VMEM((2, GROUP, 1), f32),
                pltpu.VMEM((GROUP, GROUP), bf16),
            ],
        ),
        out_shape=[jax.ShapeDtypeStruct((GROUP, GROUP), f32)]
        + [jax.ShapeDtypeStruct((4, GROUP, GROUP), bf16)] * 4,
        compiler_params=pltpu.CompilerParams(vmem_limit_bytes=48 << 20),
        cost_estimate=pl.CostEstimate(flops=12 << 30, bytes_accessed=20 << 20, transcendentals=8 << 20),
        name="attend_back",
    )(active, *operands)


UNITS = 1024
CHUNK = 256


def ffn_kernel(
    at,
    nm_ref,
    cot_ref,
    lgu_ref,
    gld_ref,
    wg_ref,
    wu_ref,
    wd_ref,
    ge_ref,
    ue_ref,
    ds_ref,
    perm_ref,
    pick_ref,
    result_ref,
    back_ref,
    gge_ref,
    gue_ref,
    gds_ref,
    nmp,
    result,
    grad,
    low,
):
    step = pl.program_id(0)
    rank = ds_ref.shape[1]

    @pl.when(step == 0)
    def _():
        for zone in range(4):
            cols = slice(zone * GROUP, (zone + 1) * GROUP)
            nmp[:, cols] = product(nm_ref[:, cols], perm_ref[...]).astype(bf16)
        result[...] = jnp.zeros(result.shape, f32)
        grad[...] = jnp.zeros(grad.shape, f32)
        low[...] = jnp.zeros(low.shape, f32)

    wg, wu = wg_ref[...].reshape(2048, CHUNK), wu_ref[...].reshape(2048, CHUNK)
    wd = wd_ref[...].reshape(CHUNK, 2048)
    ge, ue = product(ge_ref[...], pick_ref[0]).astype(bf16), product(ue_ref[...], pick_ref[0]).astype(bf16)
    ds = inner_rows(pick_ref[0], ds_ref[...]).astype(bf16)
    low_gate, low_up = lgu_ref[:, :rank], lgu_ref[:, rank:]
    gate_pre = product(nmp[...], wg) + product(low_gate, ge)
    up_pre = product(nmp[...], wu) + product(low_up, ue)
    sigmoid_g = jax.nn.sigmoid(gate_pre)
    silu_gate = gate_pre * sigmoid_g
    active_units = (silu_gate * up_pre).astype(bf16)
    grad_active = times_transposed(cot_ref[...], wd) + times_transposed(gld_ref[...], ds)
    grad_gate = (grad_active * up_pre * sigmoid_g * (1.0 + gate_pre * (1.0 - sigmoid_g))).astype(bf16)
    grad_up = (grad_active * silu_gate).astype(bf16)
    result[...] += product(active_units, wd)
    grad[...] += times_transposed(grad_gate, wg) + times_transposed(grad_up, wu)
    low[:, :rank] += times_transposed(grad_gate, ge)
    low[:, rank : 2 * rank] += times_transposed(grad_up, ue)
    low[:, 2 * rank :] += product(active_units, ds)
    gge_ref[0] = inner_rows(grad_gate, low_gate)
    gue_ref[0] = inner_rows(grad_up, low_up)
    gds_ref[0] = inner_rows(active_units, gld_ref[...])

    @pl.when(step == 2 * UNITS // CHUNK - 1)
    def _():
        result_ref[...] = result[...].astype(bf16)
        for zone in range(4):
            cols = slice(zone * GROUP, (zone + 1) * GROUP)
            back_ref[:, cols] = product(grad[:, cols].astype(bf16), perm_ref[...]).astype(bf16)
        back_ref[:, 2048:] = low[...].astype(bf16)


def feed_forward(at, normed_mid, cot, low_gu, grad_low_down, weights, expands, perm, picks):
    rank = low_gu.shape[1] // 2
    steps = UNITS // CHUNK
    unit_spec = pl.BlockSpec((1, CHUNK, rank), lambda i, at: (i // steps, i % steps, 0))
    return pl.pallas_call(
        ffn_kernel,
        grid_spec=pltpu.PrefetchScalarGridSpec(
            num_scalar_prefetch=1,
            grid=(2 * steps,),
            in_specs=[
                whole((GROUP, 2048)),
                whole((GROUP, 2048)),
                whole((GROUP, 2 * rank)),
                whole((GROUP, rank)),
                pl.BlockSpec((16, 1, 128, CHUNK), lambda i, at: (0, i // steps, 0, i % steps)),
                pl.BlockSpec((16, 1, 128, CHUNK), lambda i, at: (0, i // steps, 0, steps + i % steps)),
                pl.BlockSpec((4, 1, 64, 2048), lambda i, at: (i % steps, i // steps, 2, 0)),
                pl.BlockSpec((rank, 2 * CHUNK), lambda i, at: (0, 4 * (i % steps) + at[0])),
                pl.BlockSpec((rank, 2 * CHUNK), lambda i, at: (0, 4 * (i % steps) + at[0])),
                pl.BlockSpec((2 * CHUNK, rank), lambda i, at: (4 * (i % steps) + at[0], 0)),
                whole((GROUP, GROUP)),
                pl.BlockSpec((1, 2 * CHUNK, CHUNK), lambda i, at: (i // steps, 0, 0)),
            ],
            out_specs=[whole((GROUP, 2048)), whole((GROUP, 2048 + 3 * rank)), unit_spec, unit_spec, unit_spec],
            scratch_shapes=[
                pltpu.VMEM((GROUP, 2048), bf16),
                pltpu.VMEM((GROUP, 2048), f32),
                pltpu.VMEM((GROUP, 2048), f32),
                pltpu.VMEM((GROUP, 3 * rank), f32),
            ],
        ),
        out_shape=[
            jax.ShapeDtypeStruct((GROUP, 2048), bf16),
            jax.ShapeDtypeStruct((GROUP, 2048 + 3 * rank), bf16),
        ]
        + [jax.ShapeDtypeStruct((2, UNITS, rank), f32)] * 3,
        compiler_params=pltpu.CompilerParams(vmem_limit_bytes=60 << 20),
        cost_estimate=pl.CostEstimate(flops=28 << 30, bytes_accessed=40 << 20, transcendentals=2 << 20),
        name="feed_forward",
    )(at, normed_mid, cot, low_gu, grad_low_down, weights, weights, weights, *expands, perm, picks)


EARLY = (64, 64, 64, 16, 16, 16, 16, 16)
LATE = (16, 8, 8, 16, 16, 16)


def cut(array, sizes):
    found, at = [], 0
    for size in sizes:
        found.append(array[..., at : at + size, :])
        at += size
    return found


def early_kernel(all_ref, gate_ref, up_ref, down_ref, oshrink_ref, oexpand_ref, dexpand_ref, gateup_ref):
    pieces = [piece.astype(f32).reshape(-1, 128) for piece in cut(all_ref[...], EARLY)]
    gate_ref[...] = pieces[0].T
    up_ref[...] = pieces[1].T
    down_ref[...] = pieces[2]
    oshrink_ref[...] = pieces[3]
    oexpand_ref[...] = pieces[4].T
    dexpand_ref[...] = pieces[5].T
    gateup_ref[:, :128] = pieces[6]
    gateup_ref[:, 128:] = pieces[7]


def unpack_early(everyone):
    def rows_at(i):
        return (i % 4) * 4 + i // 4

    return pl.pallas_call(
        early_kernel,
        grid=(16,),
        in_specs=[pl.BlockSpec((8, sum(EARLY), 128), lambda i: (i, 0, 0))],
        out_specs=[
            pl.BlockSpec((128, 512), lambda i: (0, i)),
            pl.BlockSpec((128, 512), lambda i: (0, i)),
            pl.BlockSpec((512, 128), lambda i: (i, 0)),
            pl.BlockSpec((128, 128), lambda i: (rows_at(i), 0)),
            pl.BlockSpec((128, 128), lambda i: (0, rows_at(i))),
            pl.BlockSpec((128, 128), lambda i: (0, rows_at(i))),
            pl.BlockSpec((128, 256), lambda i: (rows_at(i), 0)),
        ],
        out_shape=[
            jax.ShapeDtypeStruct(shape, f32)
            for shape in ((128, 8192), (128, 8192), (8192, 128), (2048, 128), (128, 2048), (128, 2048), (2048, 256))
        ],
        cost_estimate=pl.CostEstimate(flops=1 << 20, bytes_accessed=27 << 20, transcendentals=0),
        name="unpack_early",
    )(everyone)


def late_kernel(core, mine_ref, other_ref, q_ref, k_ref, v_ref, low_ref):
    mine, other = mine_ref[0].astype(f32), other_ref[0].astype(f32)
    first, second = jnp.where(core[0] == 0, mine, other), jnp.where(core[0] == 0, other, mine)
    pieces = [
        jnp.stack(pair, axis=1).reshape(-1, 128) for pair in zip(cut(first, LATE), cut(second, LATE))
    ]
    q_ref[...] = pieces[0].T
    k_ref[...] = pieces[1].T
    v_ref[...] = pieces[2].T
    for at in range(3):
        low_ref[:, at * 128 : (at + 1) * 128] = pieces[3 + at]


def unpack_late(core, mine, other):
    half = pl.BlockSpec((1, 8, sum(LATE), 128), lambda i, core: (i // 2, i % 2, 0, 0))
    return pl.pallas_call(
        late_kernel,
        grid_spec=pltpu.PrefetchScalarGridSpec(
            num_scalar_prefetch=1,
            grid=(8,),
            in_specs=[half, half],
            out_specs=[
                pl.BlockSpec((128, 256), lambda i, core: (0, i)),
                pl.BlockSpec((128, 128), lambda i, core: (0, i)),
                pl.BlockSpec((128, 128), lambda i, core: (0, i)),
                pl.BlockSpec((256, 384), lambda i, core: (i, 0)),
            ],
        ),
        out_shape=[
            jax.ShapeDtypeStruct(shape, f32) for shape in ((128, 2048), (128, 1024), (128, 1024), (2048, 384))
        ],
        cost_estimate=pl.CostEstimate(flops=1 << 20, bytes_accessed=8 << 20, transcendentals=0),
        name="unpack_late",
    )(core, mine, other)


def local(
    hidden_in,
    gain_attn,
    gain_ffn,
    w_query,
    w_key,
    w_value,
    w_out,
    w_gate,
    w_up,
    w_down,
    qkv_shrink,
    query_expand,
    key_expand,
    value_expand,
    out_shrink,
    out_expand,
    gateup_shrink,
    gate_expand,
    up_expand,
    down_shrink,
    down_expand,
    lengths,
    adapter,
    packed_pos,
    cotangent,
):
    zh, zl, x, y, c = (lax.axis_index(name) for name in ALL)
    row = 2 * zh + c
    factor = HEAD_SIZE ** (-0.5)
    rank = out_shrink.shape[1]

    def to_rows(value):
        own = lax.dynamic_slice_in_dim(value, c * HALF, HALF, 0)
        sent = lax.dynamic_slice_in_dim(value, (1 - c) * HALF, HALF, 0)
        return jnp.concatenate([own, swap_cores(sent)], axis=0)

    def from_rows(value):
        own, got = value[:HALF], swap_cores(value[HALF:])
        return jnp.where(c == 0, jnp.concatenate([own, got], 0), jnp.concatenate([got, own], 0))

    hidden = to_rows(hidden_in)
    cot = to_rows(cotangent)

    def roll(array, by, axis):
        return lax.dynamic_slice_in_dim(jnp.concatenate([array, array], axis), by, array.shape[axis], axis)

    spread = packed_pos.reshape(2, 2, 4, 4, 2, 2, HALF)
    spread = jnp.transpose(spread, (0, 5, 1, 2, 3, 4, 6))
    rows_pos = jnp.stack([spread[:, 0], spread[:, 1, :, :, :, ::-1]], axis=1).reshape(4, 2, 4, 4, 128)
    rows_pos = roll(roll(roll(rows_pos, zl, 1), x, 2), y, 3).reshape(4, 8, GROUP)
    own_row = lax.dynamic_index_in_dim(rows_pos, row, 0, keepdims=False)
    prev_row = lax.dynamic_index_in_dim(rows_pos, jnp.maximum(row - 1, 0), 0, keepdims=False)
    prev_row = jnp.where(row == 0, far, prev_row)
    tiles_pos = jnp.concatenate([prev_row, own_row])
    group_pos = own_row[0]
    seq_ends = jnp.cumsum(lengths)
    starts = seq_ends - lengths
    member = (group_pos[:, None] >= starts[None, :]) & (group_pos[:, None] < seq_ends[None, :])
    member_int = member.astype(jnp.int32)
    group_start = jnp.sum(member_int * starts[None, :], axis=1)

    def selected(pos):
        inside = (pos[:, None] >= starts[None, :]) & (pos[:, None] < seq_ends[None, :])
        owner = jnp.sum(inside.astype(jnp.int32) * adapter[None, :], axis=1)
        return (owner[:, None] == (jnp.arange(rank, dtype=jnp.int32) // RANK)[None, :]).astype(f32)

    tile_low, tile_high = jnp.min(tiles_pos, axis=1), jnp.max(tiles_pos, axis=1)
    active = (tile_low <= jnp.max(group_pos)) & (tile_high >= jnp.min(group_start))
    active = step_tables(active.astype(jnp.int32), c)
    select_y = selected(group_pos)
    select_x = selected(own_row.reshape(2, 4, 4, 128)[0, :, 0].reshape(GROUP))
    select = select_y[:128]
    cos_table, sin_table = rope_tables(group_pos - group_start, HEAD_SIZE)

    def column_slices(weight):
        parts = weight.reshape(16, 4, 4, 4, 2, 64)
        return jnp.transpose(parts, (2, 4, 0, 1, 3, 5)).reshape(8, 16, 1024)

    heads_q = w_query.reshape(16, 4, 512)
    heads_kv = jnp.concatenate([w_key.reshape(16, 4, 256), w_value.reshape(16, 4, 256)], axis=2)
    qkv_parts = jnp.transpose(jnp.stack([heads_q, heads_kv], axis=2), (1, 2, 0, 3)).reshape(8, 16, 512)
    qkv_parts = lax.all_to_all(qkv_parts, ("y", "c"), split_axis=0, concat_axis=0, tiled=True).reshape(128, 512)
    gate_up = jnp.concatenate([column_slices(w_gate), column_slices(w_up)], axis=2)
    gate_up = lax.all_to_all(after(gate_up, qkv_parts), ("x", "c"), split_axis=0, concat_axis=0, tiled=True).reshape(128, 2048)
    def columns_of(array, width):
        return lax.dynamic_slice_in_dim(array, y * width, width, 1)

    inputs = hidden.astype(f32)
    scale_in = row_scale(inputs)
    normed = (inputs * scale_in * gain_attn).astype(bf16)
    normed, cot, qkv_parts, gate_up = lax.optimization_barrier((normed, cot, qkv_parts, gate_up))
    normed_g = gather_near(normed, "y")
    cot_g = gather_near(cot, "x")
    qkv_parts = after(qkv_parts, normed_g, cot_g)
    wo = lax.all_gather(w_out, ALL, axis=0, tiled=True)
    qkv_mine = gather_ring(gather_ring(qkv_parts, "x"), "z").reshape(2048, 512)
    qkv_other = swap_cores(qkv_mine)
    q_expand = columns_of(query_expand, 512)
    k_expand = columns_of(key_expand, 256)
    v_expand = columns_of(value_expand, 256)
    low_qkv = (product(normed_g, qkv_shrink) * jnp.tile(select_y, (1, 3))).astype(bf16)
    lin_mine, lin_other = product(normed_g, qkv_mine), product(normed_g, qkv_other)
    query_lin = jnp.where(c == 0, lin_mine, lin_other) + product(low_qkv[:, :rank], q_expand)
    kv_lin = jnp.where(c == 0, lin_other, lin_mine)
    key_lin = kv_lin[:, :256] + product(low_qkv[:, rank : 2 * rank], k_expand)
    value_lin = kv_lin[:, 256:] + product(low_qkv[:, 2 * rank :], v_expand)
    query_heads = query_lin.reshape(GROUP, 2, HEAD_SIZE)
    key_heads = key_lin.reshape(GROUP, 1, HEAD_SIZE)
    query = (query_heads * cos_table + rotate(query_heads) * sin_table).astype(bf16)
    query = (query * bf16(factor)).reshape(GROUP, 512)
    key = (key_heads * cos_table + rotate(key_heads) * sin_table).astype(bf16).reshape(GROUP, 256)

    lines = gather_row(jnp.concatenate([key, value_lin.astype(bf16)], axis=1))
    waited = zero_of(lines[1]) + zero_of(lines[2]) + zero_of(lines[3]) + zero_of(wo)
    ffn = jnp.concatenate([gate_up, w_down], axis=0) + waited.astype(bf16)
    ffn = lax.all_gather(ffn, OVER_X, axis=0, tiled=False).reshape(16, 2, 192, 2048)
    attended = (query, group_pos[:, None], group_start[:, None], tiles_pos.reshape(16, 1, GROUP)) + lines
    mixed_f, lse = attend(active, *attended)
    mixed = mixed_f.astype(bf16)

    heads = jnp.zeros((4, 128, 512), bf16)
    heads = lax.dynamic_update_index_in_dim(heads, mixed[:128], y, 0)
    for step in (1, 2, 3):
        got = shift(mixed[step * 128 : (step + 1) * 128], "y", step)
        heads = lax.dynamic_update_index_in_dim(heads, got, (y - step) % 4, 0)
    mixed_tok = jnp.transpose(heads, (1, 0, 2)).reshape(128, 2048)
    low_out = (product(mixed_tok, out_shrink) * select).astype(bf16)
    middle = inputs + product(mixed_tok, wo) + product(low_out, out_expand)
    scale_mid = row_scale(middle)
    normed_mid = (middle * scale_mid * gain_ffn).astype(bf16)
    normed_mid_g = gather_near(normed_mid, "x")

    select_two = jnp.tile(select_x, (1, 2))
    low_gu = (product(normed_mid_g, gateup_shrink) * select_two).astype(bf16)
    grad_low_down = (times_transposed(cot_g, down_expand) * select_x).astype(bf16)
    place = jnp.arange(GROUP, dtype=jnp.int32)
    turned = (place // 32 % 4) * 128 + (place // 128) * 32 + place % 32
    perm = (turned[:, None] == place[None, :]).astype(bf16)
    wide, narrow = jnp.arange(2 * CHUNK, dtype=jnp.int32), jnp.arange(CHUNK, dtype=jnp.int32)
    picks = jnp.stack(
        [(wide[:, None] == (narrow // 64 * 128 + core * 64 + narrow % 64)[None, :]).astype(bf16) for core in (0, 1)]
    )
    result, back_part, *unit_grads = feed_forward(
        x.reshape(1).astype(jnp.int32),
        normed_mid_g,
        cot_g,
        low_gu,
        grad_low_down,
        ffn,
        (gate_expand, up_expand, down_shrink),
        perm,
        picks,
    )

    def sum_tokens(part, ring):
        sent = part.astype(bf16)
        return sum_near([sent[i * 128 : (i + 1) * 128] for i in range(4)], ring)

    back = sum_tokens(back_part, "x")
    back, back_low, low_down_sum = back[:, :2048], back[:, 2048 : 2048 + 2 * rank], back[:, 2048 + 2 * rank :]

    low_down = (low_down_sum * select).astype(bf16)
    grad_low_gu = (back_low * jnp.tile(select, (1, 2))).astype(bf16)
    grad_normed_mid = back + times_transposed(grad_low_gu, gateup_shrink)
    cot_f = cot.astype(f32)
    grad_middle = cot_f + norm_back(middle, scale_mid, gain_ffn, grad_normed_mid)
    grad_attn_out = grad_middle.astype(bf16)
    grad_low_out = (times_transposed(grad_attn_out, out_expand) * select).astype(bf16)
    grad_mixed = (times_transposed(grad_attn_out, wo) + times_transposed(grad_low_out, out_shrink)).astype(bf16)

    def slices_near(array):
        def columns_at(step):
            return lax.dynamic_slice_in_dim(array, ((y + step) % 4) * 512, 512, 1)

        return jnp.concatenate([columns_at(0)] + [shift(columns_at(4 - step), "y", -step) for step in (1, 2, 3)])

    dout = slices_near(grad_mixed)
    dq, *terms = attend_back(active, *attended, mixed_f, lse, dout)
    dkv = sum_row(*terms)
    dk, dv = dkv[:, :HEAD_SIZE], dkv[:, HEAD_SIZE:]
    query_back = (dq * factor).astype(bf16).astype(f32).reshape(GROUP, 2, HEAD_SIZE)
    key_back = dk.astype(bf16).astype(f32).reshape(GROUP, 1, HEAD_SIZE)
    grad_value = dv.astype(bf16)
    grad_query = (query_back * cos_table - rotate(query_back * sin_table)).astype(bf16).reshape(GROUP, 512)
    grad_key = (key_back * cos_table - rotate(key_back * sin_table)).astype(bf16).reshape(GROUP, 256)
    grad_kv = jnp.concatenate([grad_key, grad_value], axis=1)

    grad_low_part = jnp.concatenate(
        [
            times_transposed(grad_query, q_expand),
            times_transposed(grad_key, k_expand),
            times_transposed(grad_value, v_expand),
        ],
        axis=1,
    )
    grad_low_qkv = (sum_tokens(grad_low_part, "y") * jnp.tile(select, (1, 3))).astype(bf16)
    for_mine = jnp.where(c == 0, grad_query, grad_kv)
    for_other = jnp.where(c == 0, grad_kv, grad_query)
    grad_normed_part = times_transposed(for_mine, qkv_mine) + times_transposed(for_other, qkv_other)
    grad_normed = sum_tokens(grad_normed_part, "y") + times_transposed(grad_low_qkv, qkv_shrink)
    ahead = sum_tokens(after(result, grad_normed), "x")
    output = (middle + ahead + product(low_down, down_expand)).astype(bf16)
    grad_input = (grad_middle + norm_back(inputs, scale_in, gain_attn, grad_normed)).astype(bf16)

    def features(array, at):
        return lax.dynamic_slice_in_dim(array, at * 512, 512, 1)

    def by_cores(arrays):
        parts = jnp.concatenate([array.reshape(16, 2, array.shape[0] // 32, rank) for array in arrays], axis=2)
        kept = lax.dynamic_index_in_dim(parts, c, 1, keepdims=False)
        return kept, lax.dynamic_index_in_dim(parts, 1 - c, 1, keepdims=False)

    def sum_plane(kept, given, ring):
        terms = kept + swap_cores(given.astype(bf16)).astype(f32)
        return sum_ring(sum_ring(terms.reshape(4, 4, -1, rank), "z"), ring)

    attended_back = zero_of(dq)
    low_near = jnp.concatenate([low_down, grad_low_gu], axis=1) + attended_back.astype(bf16)
    low_near = gather_near(low_near, "x")
    grad_gateup = inner_rows(features(normed_mid_g, x), low_near[:, rank:])
    out_terms = jnp.concatenate([inner_rows(mixed_tok, grad_low_out), inner_rows(grad_attn_out, low_out)], axis=1)
    out_terms = (out_terms + attended_back).astype(bf16).reshape(4, 512, 2 * rank)
    out_terms = sum_near(
        [lax.dynamic_index_in_dim(out_terms, (x + step) % 4, 0, keepdims=False) for step in range(4)], "x"
    )
    kept, other = by_cores(
        [
            out_terms[:, :rank],
            out_terms[:, rank:],
            inner_rows(features(cot_g, x), low_near[:, :rank]),
            grad_gateup[:, :rank],
            grad_gateup[:, rank:],
        ]
    )
    unit_grads = jnp.concatenate([array.reshape(2, 16, 64, rank) for array in unit_grads], axis=2)
    kept = jnp.concatenate([lax.dynamic_index_in_dim(unit_grads, c, 0, keepdims=False), kept], axis=1)
    other = jnp.concatenate([lax.dynamic_index_in_dim(unit_grads, 1 - c, 0, keepdims=False), other], axis=1)
    early_sum = sum_plane(kept, other, "y").astype(bf16)
    early_all = lax.all_gather(early_sum, ALL, axis=0, tiled=False)

    grad_qkv = inner_rows(features(normed_g, y), gather_near(grad_low_qkv, "y"))
    kept, other = by_cores(
        [
            inner_rows(grad_query, low_qkv[:, :rank]),
            inner_rows(grad_key, low_qkv[:, rank : 2 * rank]),
            inner_rows(grad_value, low_qkv[:, 2 * rank :]),
            grad_qkv[:, :rank],
            grad_qkv[:, rank : 2 * rank],
            grad_qkv[:, 2 * rank :],
        ]
    )
    g_gate, g_up, g_down_shrink, g_out_shrink, g_out_expand, g_down_expand, g_gateup = unpack_early(early_all)
    late_sum = (sum_plane(kept, other, "x") + zero_of(g_gateup)).astype(bf16)
    late_all = gather_ring(gather_ring(gather_ring(late_sum, "x"), "z"), "y")
    late_all = late_all.reshape(4, 16, -1, rank)
    late_other = swap_cores(late_all)
    g_q, g_k, g_v, g_qkv = unpack_late(c.reshape(1).astype(jnp.int32), late_all, late_other)
    return (
        from_rows(output),
        from_rows(grad_input),
        g_qkv,
        g_q,
        g_k,
        g_v,
        g_out_shrink,
        g_out_expand,
        g_gateup,
        g_gate,
        g_up,
        g_down_shrink,
        g_down_expand,
    )


def solution(mesh):
    fine = Mesh(mesh.devices.reshape(2, 2, 4, 4, 2), ALL)
    split = P(ALL, None)
    placed = (split, P(), P()) + (split,) * 7 + (P(),) * 14 + (split,)
    return jax.shard_map(
        local,
        mesh=fine,
        in_specs=placed,
        out_specs=(split, split) + (P(),) * 11,
        check_vma=False,
    )
```

```python
from functools import partial

import jax
import jax.numpy as jnp
from jax import lax
from jax.experimental import pallas as pl
from jax.experimental.pallas import tpu as pltpu
from jax.sharding import Mesh, PartitionSpec as P

HEAD_SIZE = 256
RANK = 16
HALF = 64
GROUP = 512

ALL = ("zh", "zl", "x", "y", "c")

norm_eps = 1e-06
rope_theta = 1000042.0
neg_big = -1e30
far = 1 << 30

f32 = jnp.float32
bf16 = jnp.bfloat16


def product(left, right):
    return jnp.dot(left, right, preferred_element_type=f32)


def times_transposed(left, right):
    return lax.dot_general(left, right, (((1,), (1,)), ((), ())), preferred_element_type=f32)


def inner_rows(left, right):
    return lax.dot_general(left, right, (((0,), (0,)), ((), ())), preferred_element_type=f32)


def row_scale(value_matrix):
    return lax.rsqrt(jnp.mean(value_matrix * value_matrix, axis=-1, keepdims=True) + norm_eps)


def norm_back(value_matrix, scale, gain, grad):
    scaled = gain * grad
    return scale * scaled - value_matrix * (scale * scale * scale) * jnp.mean(
        value_matrix * scaled, axis=-1, keepdims=True
    )


def rotate(value_matrix):
    middle = value_matrix.shape[-1] // 2
    return jnp.concatenate([-value_matrix[..., middle:], value_matrix[..., :middle]], axis=-1)


def rope_tables(positions, width):
    middle = width // 2
    inverse = rope_theta ** (-(jnp.arange(middle, dtype=f32) * 2.0) / width)
    angles = positions.astype(f32)[:, None] * inverse[None, :]
    cos_half, sin_half = jnp.cos(angles), jnp.sin(angles)
    cos_table = jnp.concatenate([cos_half, cos_half], axis=-1)[:, None, :]
    sin_table = jnp.concatenate([sin_half, sin_half], axis=-1)[:, None, :]
    return (cos_table, sin_table)


OVER_X = ("zh", "zl", "y", "c")
RING = {"x": ("x",), "y": ("y",), "z": ("zh", "zl")}


def swap_cores(value):
    return lax.ppermute(value, "c", [(0, 1), (1, 0)])


def shift(value, ring, step):
    return lax.ppermute(value, RING[ring], [(i, (i + step) % 4) for i in range(4)])


def place_in(ring):
    return lax.axis_index(RING[ring])


def gather_near(value, ring, axis=0):
    return jnp.concatenate([value] + [shift(value, ring, -step) for step in (1, 2, 3)], axis=axis)


def gather_ring(value, ring):
    at = place_in(ring)
    whole_ring = jnp.zeros((4,) + value.shape, value.dtype)
    whole_ring = lax.dynamic_update_index_in_dim(whole_ring, value, at, 0)
    for step in (1, 2, 3):
        got = shift(value, ring, -step)
        whole_ring = lax.dynamic_update_index_in_dim(whole_ring, got, (at + step) % 4, 0)
    return whole_ring


def sum_near(blocks, ring):
    got = [shift(blocks[step], ring, step) for step in (2, 1, 3)]
    total = blocks[0].astype(f32)
    for term in got:
        total = total + term.astype(f32)
    return total


def sum_ring(terms, ring):
    at = place_in(ring)
    got = [
        shift(lax.dynamic_index_in_dim(terms, (at + step) % 4, 0, keepdims=False).astype(bf16), ring, step)
        for step in (1, 2, 3)
    ]
    total = lax.dynamic_index_in_dim(terms, at, 0, keepdims=False)
    for term in got:
        total = total + term.astype(f32)
    return total


CORNER = ("zh", "zl", "c")
PARTNER = [(4 * zh + 2 * zl + c, 4 * zh + 2 * (1 - zl) + c) for zh in (0, 1) for zl in (0, 1) for c in (0, 1)]
LATER = [[(2 * zl + 1, 4 + 2 * (zl ^ flip)) for zl in (0, 1)] for flip in (0, 1)]
EARLIER = [[(to, came) for came, to in pairs] for pairs in LATER]
def after(value, *others):
    return lax.optimization_barrier((value,) + others)[0]


def zero_of(value):
    return value[(slice(0, 1),) * value.ndim].reshape(()).astype(f32) * 0.0


def gather_row(key_value):
    line = jnp.stack([key_value] + [shift(key_value, "x", -step) for step in (1, 2, 3)])
    ahead = [lax.ppermute(line, CORNER, pairs) for pairs in LATER]
    partner = lax.ppermute(line, CORNER, PARTNER)
    beside = [lax.ppermute(value, "c", [(0, 1)]) for value in (line, partner)]
    return line, partner, ahead[0], ahead[1], beside[0], beside[1]


def sum_row(own, own_partner, prev, prev_partner, beside):
    got = [lax.ppermute(value, "c", [(1, 0)]) for value in (prev_partner, prev)]
    terms = [lax.ppermute(value, CORNER, pairs) for value, pairs in zip((prev, prev_partner), EARLIER)]
    sent = (own_partner.astype(f32) + got[0].astype(f32)).astype(bf16)
    terms = [got[1], lax.ppermute(sent, CORNER, PARTNER)] + terms
    start = zero_of(sent)
    line = own.astype(f32)
    for term in terms:
        line = line + term.astype(f32)
    sent = (line + beside(start)).astype(bf16)
    total = line[0]
    for step in (2, 1, 3):
        total = total + shift(sent[step], "x", step).astype(f32)
    return total


def allowed_mask(own_pos, own_start, key_pos):
    return (key_pos <= own_pos) & (key_pos >= own_start)


def load_tile(tile, tile_buf, own_ref, partner_ref, ahead_ref, ahead_partner_ref, beside_ref, beside_partner_ref):
    @pl.when(tile == 0)
    def _():
        tile_buf[...] = ahead_ref[0] + beside_ref[0]

    @pl.when(tile == 1)
    def _():
        tile_buf[...] = ahead_partner_ref[0] + beside_partner_ref[0]

    @pl.when(tile == 2)
    def _():
        tile_buf[...] = own_ref[0]

    @pl.when(tile == 3)
    def _():
        tile_buf[...] = partner_ref[0]


def attend_kernel(active, q_ref, pos_ref, start_ref, kpos_ref, *refs):
    mixed_ref, lse_ref, tile_buf, top, total, accum = refs[6:]
    step = pl.program_id(0)

    @pl.when(step == 0)
    def _():
        top[...] = jnp.full(top.shape, neg_big, f32)
        total[...] = jnp.zeros(total.shape, f32)
        accum[...] = jnp.zeros(accum.shape, f32)

    @pl.when(active[step] != 0)
    def _():
        load_tile(step // 4, tile_buf, *refs[:6])
        allowed = allowed_mask(pos_ref[...], start_ref[...], kpos_ref[0])
        for head in range(2):
            scores = times_transposed(q_ref[:, head * HEAD_SIZE : (head + 1) * HEAD_SIZE], tile_buf[:, :HEAD_SIZE])
            scores = jnp.where(allowed, scores, neg_big)
            top_old = top[head]
            top_new = jnp.maximum(top_old, jnp.max(scores, axis=-1, keepdims=True))
            weights_p = jnp.where(allowed, jnp.exp(scores - top_new), 0.0)
            damping = jnp.exp(top_old - top_new)
            total[head] = total[head] * damping + jnp.sum(weights_p, axis=-1, keepdims=True)
            accum[head] = accum[head] * damping + product(weights_p.astype(bf16), tile_buf[:, HEAD_SIZE:])
            top[head] = top_new

    @pl.when(step == 15)
    def _():
        for head in range(2):
            mixed_ref[:, head * HEAD_SIZE : (head + 1) * HEAD_SIZE] = accum[head] / total[head]
            lse_ref[head] = top[head] + jnp.log(total[head])


def attend_back_kernel(active, q_ref, pos_ref, start_ref, kpos_ref, *refs):
    mixed_ref, lse_ref, dout_ref, dq_ref, down_ref, dpartner_ref, dprev_ref, dprev_partner_ref = refs[6:14]
    tile_buf, delta, sums = refs[14:]
    step = pl.program_id(0)
    tile = step // 4

    @pl.when(step == 0)
    def _():
        dq_ref[...] = jnp.zeros(dq_ref.shape, f32)
        for head in range(2):
            cols = slice(head * HEAD_SIZE, (head + 1) * HEAD_SIZE)
            delta[head] = jnp.sum(dout_ref[:, cols].astype(f32) * mixed_ref[:, cols], axis=-1, keepdims=True)

    @pl.when(active[step] == 0)
    def _():
        sums[...] = jnp.zeros(sums.shape, bf16)

    @pl.when(active[step] != 0)
    def _():
        load_tile(tile, tile_buf, *refs[:6])
        allowed = allowed_mask(pos_ref[...], start_ref[...], kpos_ref[0])
        dk = jnp.zeros((GROUP, HEAD_SIZE), f32)
        dv = jnp.zeros((GROUP, HEAD_SIZE), f32)
        for head in range(2):
            cols = slice(head * HEAD_SIZE, (head + 1) * HEAD_SIZE)
            query, dout = q_ref[:, cols], dout_ref[:, cols]
            scores = times_transposed(query, tile_buf[:, :HEAD_SIZE])
            weights_p = jnp.where(allowed, jnp.exp(scores - lse_ref[head]), 0.0)
            dprobs = times_transposed(dout, tile_buf[:, HEAD_SIZE:])
            dscores = (weights_p * (dprobs - delta[head])).astype(bf16)
            dq_ref[:, cols] += product(dscores, tile_buf[:, :HEAD_SIZE])
            dk = dk + inner_rows(dscores, query)
            dv = dv + inner_rows(weights_p.astype(bf16), dout)
        sums[:, :HEAD_SIZE] = dk.astype(bf16)
        sums[:, HEAD_SIZE:] = dv.astype(bf16)

    for at, out_ref in enumerate((dprev_ref, dprev_partner_ref, down_ref, dpartner_ref)):

        @pl.when(tile == at)
        def _():
            out_ref[0] = sums[...]


def whole(shape):
    return pl.BlockSpec(shape, lambda *grid_and_refs: (0,) * len(shape))


def line_spec(tile):
    return pl.BlockSpec((1, GROUP, GROUP), lambda i, active: (jnp.clip(i - 4 * tile, 0, 3), 0, 0))


def active_spec(tile, table):
    return pl.BlockSpec(
        (1, GROUP, GROUP), lambda i, active: (active[16 * table + 4 * tile + jnp.clip(i - 4 * tile, 0, 3)], 0, 0)
    )


def step_tables(active, c):
    marks = active.reshape(4, 4)
    at = jnp.arange(4, dtype=jnp.int32)
    seen = jnp.where((marks[:, None, :] != 0) & (at[None, None, :] <= at[None, :, None]), at[None, None, :], -1)
    last = jnp.max(seen, axis=2)
    first = jnp.min(jnp.where(marks != 0, at[None, :], 3), axis=1, keepdims=True)
    blocks = jnp.where(last >= 0, last, first).reshape(16).astype(jnp.int32)
    return jnp.concatenate([active, blocks, jnp.where(c == 0, blocks, 0), jnp.where(c == 0, 0, blocks)])


def common_specs():
    return [
        whole((GROUP, GROUP)),
        whole((GROUP, 1)),
        whole((GROUP, 1)),
        pl.BlockSpec((1, 1, GROUP), lambda i, active: (i, 0, 0)),
    ] + [active_spec(tile, table) for tile, table in ((2, 1), (3, 1), (0, 2), (1, 2), (0, 3), (1, 3))]


def attend(active, *operands):
    return pl.pallas_call(
        attend_kernel,
        grid_spec=pltpu.PrefetchScalarGridSpec(
            num_scalar_prefetch=1,
            grid=(16,),
            in_specs=common_specs(),
            out_specs=[whole((GROUP, GROUP)), whole((2, GROUP, 1))],
            scratch_shapes=[
                pltpu.VMEM((GROUP, GROUP), bf16),
                pltpu.VMEM((2, GROUP, 1), f32),
                pltpu.VMEM((2, GROUP, 1), f32),
                pltpu.VMEM((2, GROUP, HEAD_SIZE), f32),
            ],
        ),
        out_shape=[
            jax.ShapeDtypeStruct((GROUP, GROUP), f32),
            jax.ShapeDtypeStruct((2, GROUP, 1), f32),
        ],
        compiler_params=pltpu.CompilerParams(vmem_limit_bytes=48 << 20),
        cost_estimate=pl.CostEstimate(flops=6 << 30, bytes_accessed=10 << 20, transcendentals=8 << 20),
        name="attend",
    )(active, *operands)


def attend_back(active, *operands):
    return pl.pallas_call(
        attend_back_kernel,
        grid_spec=pltpu.PrefetchScalarGridSpec(
            num_scalar_prefetch=1,
            grid=(16,),
            in_specs=common_specs() + [whole((GROUP, GROUP)), whole((2, GROUP, 1)), whole((GROUP, GROUP))],
            out_specs=[whole((GROUP, GROUP))] + [line_spec(tile) for tile in (2, 3, 0, 1)],
            scratch_shapes=[
                pltpu.VMEM((GROUP, GROUP), bf16),
                pltpu.VMEM((2, GROUP, 1), f32),
                pltpu.VMEM((GROUP, GROUP), bf16),
            ],
        ),
        out_shape=[jax.ShapeDtypeStruct((GROUP, GROUP), f32)]
        + [jax.ShapeDtypeStruct((4, GROUP, GROUP), bf16)] * 4,
        compiler_params=pltpu.CompilerParams(vmem_limit_bytes=48 << 20),
        cost_estimate=pl.CostEstimate(flops=12 << 30, bytes_accessed=20 << 20, transcendentals=8 << 20),
        name="attend_back",
    )(active, *operands)


UNITS = 1024
CHUNK = 256


def ffn_kernel(
    at,
    nm_ref,
    cot_ref,
    lgu_ref,
    gld_ref,
    wg_ref,
    wu_ref,
    wd_ref,
    ge_ref,
    ue_ref,
    ds_ref,
    perm_ref,
    pick_ref,
    result_ref,
    back_ref,
    units_ref,
    nmp,
    result,
    grad,
    low,
):
    step = pl.program_id(0)
    rank = ds_ref.shape[1]

    @pl.when(step == 0)
    def _():
        for zone in range(4):
            cols = slice(zone * GROUP, (zone + 1) * GROUP)
            nmp[:, cols] = product(nm_ref[:, cols], perm_ref[...]).astype(bf16)
        result[...] = jnp.zeros(result.shape, f32)
        grad[...] = jnp.zeros(grad.shape, f32)
        low[...] = jnp.zeros(low.shape, f32)

    wg, wu = wg_ref[...].reshape(2048, CHUNK), wu_ref[...].reshape(2048, CHUNK)
    wd = wd_ref[...].reshape(CHUNK, 2048)
    ge, ue = product(ge_ref[...], pick_ref[0]).astype(bf16), product(ue_ref[...], pick_ref[0]).astype(bf16)
    ds = inner_rows(pick_ref[0], ds_ref[...]).astype(bf16)
    low_gate, low_up = lgu_ref[:, :rank], lgu_ref[:, rank:]
    gate_pre = product(nmp[...], wg) + product(low_gate, ge)
    up_pre = product(nmp[...], wu) + product(low_up, ue)
    sigmoid_g = jax.nn.sigmoid(gate_pre)
    silu_gate = gate_pre * sigmoid_g
    active_units = (silu_gate * up_pre).astype(bf16)
    grad_active = times_transposed(cot_ref[...], wd) + times_transposed(gld_ref[...], ds)
    grad_gate = (grad_active * up_pre * sigmoid_g * (1.0 + gate_pre * (1.0 - sigmoid_g))).astype(bf16)
    grad_up = (grad_active * silu_gate).astype(bf16)
    result[...] += product(active_units, wd)
    grad[...] += times_transposed(grad_gate, wg) + times_transposed(grad_up, wu)
    low[:, :rank] += times_transposed(grad_gate, ge)
    low[:, rank : 2 * rank] += times_transposed(grad_up, ue)
    low[:, 2 * rank :] += product(active_units, ds)
    units_ref[0, :, 0, :64] = inner_rows(grad_gate, low_gate).reshape(4, 64, rank)
    units_ref[0, :, 0, 64:128] = inner_rows(grad_up, low_up).reshape(4, 64, rank)
    units_ref[0, :, 0, 128:] = inner_rows(active_units, gld_ref[...]).reshape(4, 64, rank)

    @pl.when(step == 2 * UNITS // CHUNK - 1)
    def _():
        result_ref[...] = result[...].astype(bf16)
        for zone in range(4):
            cols = slice(zone * GROUP, (zone + 1) * GROUP)
            back_ref[:, cols] = product(grad[:, cols].astype(bf16), perm_ref[...]).astype(bf16)
        back_ref[:, 2048:] = low[...].astype(bf16)


def feed_forward(at, normed_mid, cot, low_gu, grad_low_down, weights, expands, perm, picks):
    rank = low_gu.shape[1] // 2
    steps = UNITS // CHUNK
    unit_spec = pl.BlockSpec((1, 4, 1, 192, rank), lambda i, at: (i % steps, 0, i // steps, 0, 0))
    return pl.pallas_call(
        ffn_kernel,
        grid_spec=pltpu.PrefetchScalarGridSpec(
            num_scalar_prefetch=1,
            grid=(2 * steps,),
            in_specs=[
                whole((GROUP, 2048)),
                whole((GROUP, 2048)),
                whole((GROUP, 2 * rank)),
                whole((GROUP, rank)),
                pl.BlockSpec((16, 1, 128, CHUNK), lambda i, at: (0, i // steps, 0, i % steps)),
                pl.BlockSpec((16, 1, 128, CHUNK), lambda i, at: (0, i // steps, 0, steps + i % steps)),
                pl.BlockSpec((4, 1, 64, 2048), lambda i, at: (i % steps, i // steps, 2, 0)),
                pl.BlockSpec((rank, 2 * CHUNK), lambda i, at: (0, 4 * (i % steps) + at[0])),
                pl.BlockSpec((rank, 2 * CHUNK), lambda i, at: (0, 4 * (i % steps) + at[0])),
                pl.BlockSpec((2 * CHUNK, rank), lambda i, at: (4 * (i % steps) + at[0], 0)),
                whole((GROUP, GROUP)),
                pl.BlockSpec((1, 2 * CHUNK, CHUNK), lambda i, at: (i // steps, 0, 0)),
            ],
            out_specs=[whole((GROUP, 2048)), whole((GROUP, 2048 + 3 * rank)), unit_spec],
            scratch_shapes=[
                pltpu.VMEM((GROUP, 2048), bf16),
                pltpu.VMEM((GROUP, 2048), f32),
                pltpu.VMEM((GROUP, 2048), f32),
                pltpu.VMEM((GROUP, 3 * rank), f32),
            ],
        ),
        out_shape=[
            jax.ShapeDtypeStruct((GROUP, 2048), bf16),
            jax.ShapeDtypeStruct((GROUP, 2048 + 3 * rank), bf16),
            jax.ShapeDtypeStruct((4, 4, 2, 192, rank), f32),
        ],
        compiler_params=pltpu.CompilerParams(vmem_limit_bytes=60 << 20),
        cost_estimate=pl.CostEstimate(flops=28 << 30, bytes_accessed=40 << 20, transcendentals=2 << 20),
        name="feed_forward",
    )(at, normed_mid, cot, low_gu, grad_low_down, weights, weights, weights, *expands, perm, picks)


EARLY = (64, 64, 64, 16, 16, 16, 16, 16)
LATE = (16, 8, 8, 16, 16, 16)


def cut(array, sizes):
    found, at = [], 0
    for size in sizes:
        found.append(array[..., at : at + size, :])
        at += size
    return found


def early_kernel(all_ref, gate_ref, up_ref, down_ref, oshrink_ref, oexpand_ref, dexpand_ref, gateup_ref):
    pieces = [piece.astype(f32).reshape(-1, 128) for piece in cut(all_ref[...], EARLY)]
    gate_ref[...] = pieces[0].T
    up_ref[...] = pieces[1].T
    down_ref[...] = pieces[2]
    oshrink_ref[...] = pieces[3]
    oexpand_ref[...] = pieces[4].T
    dexpand_ref[...] = pieces[5].T
    gateup_ref[:, :128] = pieces[6]
    gateup_ref[:, 128:] = pieces[7]


def unpack_early(everyone):
    return pl.pallas_call(
        early_kernel,
        grid=(16,),
        in_specs=[pl.BlockSpec((8, sum(EARLY), 128), lambda i: (i, 0, 0))],
        out_specs=[
            pl.BlockSpec((128, 512), lambda i: (0, i)),
            pl.BlockSpec((128, 512), lambda i: (0, i)),
            pl.BlockSpec((512, 128), lambda i: (i, 0)),
            pl.BlockSpec((128, 128), lambda i: (i, 0)),
            pl.BlockSpec((128, 128), lambda i: (0, i)),
            pl.BlockSpec((128, 128), lambda i: (0, i)),
            pl.BlockSpec((128, 256), lambda i: (i, 0)),
        ],
        out_shape=[
            jax.ShapeDtypeStruct(shape, f32)
            for shape in ((128, 8192), (128, 8192), (8192, 128), (2048, 128), (128, 2048), (128, 2048), (2048, 256))
        ],
        cost_estimate=pl.CostEstimate(flops=1 << 20, bytes_accessed=27 << 20, transcendentals=0),
        name="unpack_early",
    )(everyone)


def late_kernel(core, mine_ref, other_ref, q_ref, k_ref, v_ref, low_ref):
    mine, other = mine_ref[0].astype(f32), other_ref[0].astype(f32)
    first, second = jnp.where(core[0] == 0, mine, other), jnp.where(core[0] == 0, other, mine)
    pieces = [
        jnp.stack(pair, axis=1).reshape(-1, 128) for pair in zip(cut(first, LATE), cut(second, LATE))
    ]
    q_ref[...] = pieces[0].T
    k_ref[...] = pieces[1].T
    v_ref[...] = pieces[2].T
    for at in range(3):
        low_ref[:, at * 128 : (at + 1) * 128] = pieces[3 + at]


def unpack_late(core, mine, other):
    half = pl.BlockSpec((1, 8, sum(LATE), 128), lambda i, core: (i // 2, i % 2, 0, 0))
    return pl.pallas_call(
        late_kernel,
        grid_spec=pltpu.PrefetchScalarGridSpec(
            num_scalar_prefetch=1,
            grid=(8,),
            in_specs=[half, half],
            out_specs=[
                pl.BlockSpec((128, 256), lambda i, core: (0, i)),
                pl.BlockSpec((128, 128), lambda i, core: (0, i)),
                pl.BlockSpec((128, 128), lambda i, core: (0, i)),
                pl.BlockSpec((256, 384), lambda i, core: (i, 0)),
            ],
        ),
        out_shape=[
            jax.ShapeDtypeStruct(shape, f32) for shape in ((128, 2048), (128, 1024), (128, 1024), (2048, 384))
        ],
        cost_estimate=pl.CostEstimate(flops=1 << 20, bytes_accessed=8 << 20, transcendentals=0),
        name="unpack_late",
    )(core, mine, other)


def local(
    hidden_in,
    gain_attn,
    gain_ffn,
    w_query,
    w_key,
    w_value,
    w_out,
    w_gate,
    w_up,
    w_down,
    qkv_shrink,
    query_expand,
    key_expand,
    value_expand,
    out_shrink,
    out_expand,
    gateup_shrink,
    gate_expand,
    up_expand,
    down_shrink,
    down_expand,
    lengths,
    adapter,
    packed_pos,
    cotangent,
):
    zh, zl, x, y, c = (lax.axis_index(name) for name in ALL)
    row = 2 * zh + c
    factor = HEAD_SIZE ** (-0.5)
    rank = out_shrink.shape[1]

    def to_rows(value):
        own = lax.dynamic_slice_in_dim(value, c * HALF, HALF, 0)
        sent = lax.dynamic_slice_in_dim(value, (1 - c) * HALF, HALF, 0)
        return jnp.concatenate([own, swap_cores(sent)], axis=0)

    def from_rows(value):
        own, got = value[:HALF], swap_cores(value[HALF:])
        return jnp.where(c == 0, jnp.concatenate([own, got], 0), jnp.concatenate([got, own], 0))

    hidden = to_rows(hidden_in)
    cot = to_rows(cotangent)

    def roll(array, by, axis):
        return lax.dynamic_slice_in_dim(jnp.concatenate([array, array], axis), by, array.shape[axis], axis)

    spread = packed_pos.reshape(2, 2, 4, 4, 2, 2, HALF)
    spread = jnp.transpose(spread, (0, 5, 1, 2, 3, 4, 6))
    rows_pos = jnp.stack([spread[:, 0], spread[:, 1, :, :, :, ::-1]], axis=1).reshape(4, 2, 4, 4, 128)
    rows_pos = roll(roll(roll(rows_pos, zl, 1), x, 2), y, 3).reshape(4, 8, GROUP)
    own_row = lax.dynamic_index_in_dim(rows_pos, row, 0, keepdims=False)
    prev_row = lax.dynamic_index_in_dim(rows_pos, jnp.maximum(row - 1, 0), 0, keepdims=False)
    prev_row = jnp.where(row == 0, far, prev_row)
    tiles_pos = jnp.concatenate([prev_row, own_row])
    group_pos = own_row[0]
    seq_ends = jnp.cumsum(lengths)
    starts = seq_ends - lengths
    member = (group_pos[:, None] >= starts[None, :]) & (group_pos[:, None] < seq_ends[None, :])
    member_int = member.astype(jnp.int32)
    group_start = jnp.sum(member_int * starts[None, :], axis=1)

    def selected(pos):
        inside = (pos[:, None] >= starts[None, :]) & (pos[:, None] < seq_ends[None, :])
        owner = jnp.sum(inside.astype(jnp.int32) * adapter[None, :], axis=1)
        return (owner[:, None] == (jnp.arange(rank, dtype=jnp.int32) // RANK)[None, :]).astype(f32)

    key_runs, pos_runs, start_runs = tiles_pos.reshape(64, 128), group_pos.reshape(4, 128), group_start.reshape(4, 128)
    key_low, key_high = jnp.min(key_runs, axis=1)[:, None], jnp.max(key_runs, axis=1)[:, None]
    seen = (key_low <= jnp.max(pos_runs, axis=1)[None, :]) & (key_high >= jnp.min(start_runs, axis=1)[None, :])
    active = jnp.max(seen.astype(jnp.int32).reshape(16, 16), axis=1)
    active = step_tables(active, c)
    select_y = selected(group_pos)
    select_x = selected(own_row.reshape(2, 4, 4, 128)[0, :, 0].reshape(GROUP))
    select = select_y[:128]
    cos_table, sin_table = rope_tables(group_pos - group_start, HEAD_SIZE)

    def column_slices(weight):
        parts = weight.reshape(16, 4, 4, 4, 2, 64)
        return jnp.transpose(parts, (2, 4, 0, 1, 3, 5)).reshape(8, 16, 1024)

    heads_q = w_query.reshape(16, 4, 512)
    heads_kv = jnp.concatenate([w_key.reshape(16, 4, 256), w_value.reshape(16, 4, 256)], axis=2)
    qkv_parts = jnp.transpose(jnp.stack([heads_q, heads_kv], axis=2), (1, 2, 0, 3)).reshape(8, 16, 512)
    qkv_parts = lax.all_to_all(qkv_parts, ("y", "c"), split_axis=0, concat_axis=0, tiled=True).reshape(128, 512)
    gate_up = jnp.concatenate([column_slices(w_gate), column_slices(w_up)], axis=2)
    gate_up = lax.all_to_all(after(gate_up, qkv_parts), ("x", "c"), split_axis=0, concat_axis=0, tiled=True).reshape(128, 2048)
    def columns_of(array, width):
        return lax.dynamic_slice_in_dim(array, y * width, width, 1)

    inputs = hidden.astype(f32)
    scale_in = row_scale(inputs)
    normed = (inputs * scale_in * gain_attn).astype(bf16)
    normed, cot, qkv_parts, gate_up = lax.optimization_barrier((normed, cot, qkv_parts, gate_up))
    normed_g = gather_near(normed, "y")
    cot_g = gather_near(cot, "x")
    qkv_parts = after(qkv_parts, normed_g, cot_g)
    wo = lax.all_gather(w_out, ALL, axis=0, tiled=True)
    qkv_mine = gather_ring(gather_ring(qkv_parts, "x"), "z").reshape(2048, 512)
    qkv_other = swap_cores(qkv_mine)
    q_expand = columns_of(query_expand, 512)
    k_expand = columns_of(key_expand, 256)
    v_expand = columns_of(value_expand, 256)
    low_qkv = (product(normed_g, qkv_shrink) * jnp.tile(select_y, (1, 3))).astype(bf16)
    lin_mine, lin_other = product(normed_g, qkv_mine), product(normed_g, qkv_other)
    query_lin = jnp.where(c == 0, lin_mine, lin_other) + product(low_qkv[:, :rank], q_expand)
    kv_lin = jnp.where(c == 0, lin_other, lin_mine)
    key_lin = kv_lin[:, :256] + product(low_qkv[:, rank : 2 * rank], k_expand)
    value_lin = kv_lin[:, 256:] + product(low_qkv[:, 2 * rank :], v_expand)
    query_heads = query_lin.reshape(GROUP, 2, HEAD_SIZE)
    key_heads = key_lin.reshape(GROUP, 1, HEAD_SIZE)
    query = (query_heads * cos_table + rotate(query_heads) * sin_table).astype(bf16)
    query = (query * bf16(factor)).reshape(GROUP, 512)
    key = (key_heads * cos_table + rotate(key_heads) * sin_table).astype(bf16).reshape(GROUP, 256)

    lines = gather_row(jnp.concatenate([key, value_lin.astype(bf16)], axis=1))
    waited = zero_of(lines[1]) + zero_of(lines[2]) + zero_of(lines[3]) + zero_of(lines[4]) + zero_of(wo)
    ffn = jnp.concatenate([gate_up, w_down], axis=0) + waited.astype(bf16)
    ffn = lax.all_gather(ffn, OVER_X, axis=0, tiled=False).reshape(16, 2, 192, 2048)
    attended = (query, group_pos[:, None], group_start[:, None], tiles_pos.reshape(16, 1, GROUP)) + lines
    mixed_f, lse = attend(active, *attended)
    mixed = mixed_f.astype(bf16)

    heads = jnp.zeros((4, 128, 512), bf16)
    heads = lax.dynamic_update_index_in_dim(heads, mixed[:128], y, 0)
    for step in (1, 2, 3):
        got = shift(mixed[step * 128 : (step + 1) * 128], "y", step)
        heads = lax.dynamic_update_index_in_dim(heads, got, (y - step) % 4, 0)
    mixed_tok = jnp.transpose(heads, (1, 0, 2)).reshape(128, 2048)
    low_out = (product(mixed_tok, out_shrink) * select).astype(bf16)
    middle = inputs + product(mixed_tok, wo) + product(low_out, out_expand)
    scale_mid = row_scale(middle)
    normed_mid = (middle * scale_mid * gain_ffn).astype(bf16)
    normed_mid_g = gather_near(normed_mid, "x")

    select_two = jnp.tile(select_x, (1, 2))
    low_gu = (product(normed_mid_g, gateup_shrink) * select_two).astype(bf16)
    grad_low_down = (times_transposed(cot_g, down_expand) * select_x).astype(bf16)
    place = jnp.arange(GROUP, dtype=jnp.int32)
    turned = (place // 32 % 4) * 128 + (place // 128) * 32 + place % 32
    perm = (turned[:, None] == place[None, :]).astype(bf16)
    wide, narrow = jnp.arange(2 * CHUNK, dtype=jnp.int32), jnp.arange(CHUNK, dtype=jnp.int32)
    picks = jnp.stack(
        [(wide[:, None] == (narrow // 64 * 128 + core * 64 + narrow % 64)[None, :]).astype(bf16) for core in (0, 1)]
    )
    result, back_part, unit_grads = feed_forward(
        x.reshape(1).astype(jnp.int32),
        normed_mid_g,
        cot_g,
        low_gu,
        grad_low_down,
        ffn,
        (gate_expand, up_expand, down_shrink),
        perm,
        picks,
    )

    def sum_tokens(part, ring):
        sent = part.astype(bf16)
        return sum_near([sent[i * 128 : (i + 1) * 128] for i in range(4)], ring)

    back = sum_tokens(back_part, "x")
    back, back_low, low_down_sum = back[:, :2048], back[:, 2048 : 2048 + 2 * rank], back[:, 2048 + 2 * rank :]

    low_down = (low_down_sum * select).astype(bf16)
    grad_low_gu = (back_low * jnp.tile(select, (1, 2))).astype(bf16)
    grad_normed_mid = back + times_transposed(grad_low_gu, gateup_shrink)
    cot_f = cot.astype(f32)
    grad_middle = cot_f + norm_back(middle, scale_mid, gain_ffn, grad_normed_mid)
    grad_attn_out = grad_middle.astype(bf16)
    grad_low_out = (times_transposed(grad_attn_out, out_expand) * select).astype(bf16)
    grad_mixed = (times_transposed(grad_attn_out, wo) + times_transposed(grad_low_out, out_shrink)).astype(bf16)

    def slices_near(array):
        def columns_at(step):
            return lax.dynamic_slice_in_dim(array, ((y + step) % 4) * 512, 512, 1)

        return jnp.concatenate([columns_at(0)] + [shift(columns_at(4 - step), "y", -step) for step in (1, 2, 3)])

    dout = slices_near(grad_mixed)
    dq, *terms = attend_back(active, *attended, mixed_f, lse, dout)
    unit_sum = lax.psum_scatter(
        unit_grads.reshape(32, 192, rank), OVER_X, scatter_dimension=0, tiled=False
    )
    aheads = []

    def beside(start):
        aheads.append(sum_tokens(result + start.astype(bf16), "x"))
        return zero_of(aheads[0]) + zero_of(unit_sum)

    dkv = sum_row(*terms, beside)
    dk, dv = dkv[:, :HEAD_SIZE], dkv[:, HEAD_SIZE:]
    query_back = (dq * factor).astype(bf16).astype(f32).reshape(GROUP, 2, HEAD_SIZE)
    key_back = dk.astype(bf16).astype(f32).reshape(GROUP, 1, HEAD_SIZE)
    grad_value = dv.astype(bf16)
    grad_query = (query_back * cos_table - rotate(query_back * sin_table)).astype(bf16).reshape(GROUP, 512)
    grad_key = (key_back * cos_table - rotate(key_back * sin_table)).astype(bf16).reshape(GROUP, 256)
    grad_kv = jnp.concatenate([grad_key, grad_value], axis=1)

    grad_low_part = jnp.concatenate(
        [
            times_transposed(grad_query, q_expand),
            times_transposed(grad_key, k_expand),
            times_transposed(grad_value, v_expand),
        ],
        axis=1,
    )
    grad_low_qkv = (sum_tokens(grad_low_part, "y") * jnp.tile(select, (1, 3))).astype(bf16)
    for_mine = jnp.where(c == 0, grad_query, grad_kv)
    for_other = jnp.where(c == 0, grad_kv, grad_query)
    grad_normed_part = times_transposed(for_mine, qkv_mine) + times_transposed(for_other, qkv_other)
    grad_normed = sum_tokens(grad_normed_part, "y") + times_transposed(grad_low_qkv, qkv_shrink)
    output = (middle + aheads[0] + product(low_down, down_expand)).astype(bf16)
    grad_input = (grad_middle + norm_back(inputs, scale_in, gain_attn, grad_normed)).astype(bf16)

    def features(array, at):
        return lax.dynamic_slice_in_dim(array, at * 512, 512, 1)

    def by_cores(arrays):
        parts = jnp.concatenate([array.reshape(16, 2, array.shape[0] // 32, rank) for array in arrays], axis=2)
        kept = lax.dynamic_index_in_dim(parts, c, 1, keepdims=False)
        return kept, lax.dynamic_index_in_dim(parts, 1 - c, 1, keepdims=False)

    def sum_plane(kept, given, ring):
        terms = kept + swap_cores(given.astype(bf16)).astype(f32)
        return sum_ring(sum_ring(terms.reshape(4, 4, -1, rank), "z"), ring)

    row_terms = [
        inner_rows(mixed_tok, grad_low_out),
        inner_rows(grad_attn_out, low_out),
        inner_rows(cot, low_down),
        inner_rows(normed_mid, grad_low_gu[:, :rank]),
        inner_rows(normed_mid, grad_low_gu[:, rank:]),
    ]
    row_terms = jnp.concatenate([array.reshape(128, 16, rank) for array in row_terms], axis=1)
    row_sum = lax.psum_scatter(row_terms, ALL, scatter_dimension=0, tiled=False)
    early_sum = (jnp.concatenate([unit_sum, row_sum], axis=0) + zero_of(dkv)).astype(bf16)
    early_all = lax.all_gather(early_sum, ALL, axis=0, tiled=False)

    grad_qkv = inner_rows(features(normed_g, y), gather_near(grad_low_qkv, "y"))
    kept, other = by_cores(
        [
            inner_rows(grad_query, low_qkv[:, :rank]),
            inner_rows(grad_key, low_qkv[:, rank : 2 * rank]),
            inner_rows(grad_value, low_qkv[:, 2 * rank :]),
            grad_qkv[:, :rank],
            grad_qkv[:, rank : 2 * rank],
            grad_qkv[:, 2 * rank :],
        ]
    )
    g_gate, g_up, g_down_shrink, g_out_shrink, g_out_expand, g_down_expand, g_gateup = unpack_early(early_all)
    late_sum = sum_plane(kept, other, "x").astype(bf16)
    late_all = gather_ring(gather_ring(late_sum, "x"), "z") + zero_of(g_gateup).astype(bf16)
    late_all = gather_ring(late_all, "y")
    late_all = late_all.reshape(4, 16, -1, rank)
    late_other = swap_cores(late_all)
    g_q, g_k, g_v, g_qkv = unpack_late(c.reshape(1).astype(jnp.int32), late_all, late_other)
    return (
        from_rows(output),
        from_rows(grad_input),
        g_qkv,
        g_q,
        g_k,
        g_v,
        g_out_shrink,
        g_out_expand,
        g_gateup,
        g_gate,
        g_up,
        g_down_shrink,
        g_down_expand,
    )


def solution(mesh):
    fine = Mesh(mesh.devices.reshape(2, 2, 4, 4, 2), ALL)
    split = P(ALL, None)
    placed = (split, P(), P()) + (split,) * 7 + (P(),) * 14 + (split,)
    return jax.shard_map(
        local,
        mesh=fine,
        in_specs=placed,
        out_specs=(split, split) + (P(),) * 11,
        check_vma=False,
    )
```

```python
from functools import partial

import jax
import jax.numpy as jnp
from jax import lax
from jax.experimental import pallas as pl
from jax.experimental.pallas import tpu as pltpu
from jax.sharding import Mesh, PartitionSpec as P

HEAD_SIZE = 256
RANK = 16
HALF = 64
GROUP = 512

ALL = ("zh", "zl", "x", "y", "c")

norm_eps = 1e-06
rope_theta = 1000042.0
neg_big = -1e30
far = 1 << 30

f32 = jnp.float32
bf16 = jnp.bfloat16


def product(left, right):
    return jnp.dot(left, right, preferred_element_type=f32)


def times_transposed(left, right):
    return lax.dot_general(left, right, (((1,), (1,)), ((), ())), preferred_element_type=f32)


def inner_rows(left, right):
    return lax.dot_general(left, right, (((0,), (0,)), ((), ())), preferred_element_type=f32)


def row_scale(value_matrix):
    return lax.rsqrt(jnp.mean(value_matrix * value_matrix, axis=-1, keepdims=True) + norm_eps)


def norm_back(value_matrix, scale, gain, grad):
    scaled = gain * grad
    return scale * scaled - value_matrix * (scale * scale * scale) * jnp.mean(
        value_matrix * scaled, axis=-1, keepdims=True
    )


def rotate(value_matrix):
    middle = value_matrix.shape[-1] // 2
    return jnp.concatenate([-value_matrix[..., middle:], value_matrix[..., :middle]], axis=-1)


def rope_tables(positions, width):
    middle = width // 2
    inverse = rope_theta ** (-(jnp.arange(middle, dtype=f32) * 2.0) / width)
    angles = positions.astype(f32)[:, None] * inverse[None, :]
    cos_half, sin_half = jnp.cos(angles), jnp.sin(angles)
    cos_table = jnp.concatenate([cos_half, cos_half], axis=-1)[:, None, :]
    sin_table = jnp.concatenate([sin_half, sin_half], axis=-1)[:, None, :]
    return (cos_table, sin_table)


OVER_X = ("zh", "zl", "y", "c")
RING = {"x": ("x",), "y": ("y",), "z": ("zh", "zl")}


def swap_cores(value):
    return lax.ppermute(value, "c", [(0, 1), (1, 0)])


def shift(value, ring, step):
    return lax.ppermute(value, RING[ring], [(i, (i + step) % 4) for i in range(4)])


def place_in(ring):
    return lax.axis_index(RING[ring])


def gather_near(value, ring, axis=0):
    return jnp.concatenate([value] + [shift(value, ring, -step) for step in (1, 2, 3)], axis=axis)


def gather_ring(value, ring):
    at = place_in(ring)
    whole_ring = jnp.zeros((4,) + value.shape, value.dtype)
    whole_ring = lax.dynamic_update_index_in_dim(whole_ring, value, at, 0)
    for step in (1, 2, 3):
        got = shift(value, ring, -step)
        whole_ring = lax.dynamic_update_index_in_dim(whole_ring, got, (at + step) % 4, 0)
    return whole_ring


def sum_near(blocks, ring):
    got = [shift(blocks[step], ring, step) for step in (2, 1, 3)]
    total = blocks[0].astype(f32)
    for term in got:
        total = total + term.astype(f32)
    return total


def sum_ring(terms, ring):
    at = place_in(ring)
    got = [
        shift(lax.dynamic_index_in_dim(terms, (at + step) % 4, 0, keepdims=False).astype(bf16), ring, step)
        for step in (1, 2, 3)
    ]
    total = lax.dynamic_index_in_dim(terms, at, 0, keepdims=False)
    for term in got:
        total = total + term.astype(f32)
    return total


CORNER = ("zh", "zl", "c")
PARTNER = [(4 * zh + 2 * zl + c, 4 * zh + 2 * (1 - zl) + c) for zh in (0, 1) for zl in (0, 1) for c in (0, 1)]
LATER = [[(2 * zl + 1, 4 + 2 * (zl ^ flip)) for zl in (0, 1)] for flip in (0, 1)]
EARLIER = [[(to, came) for came, to in pairs] for pairs in LATER]
def after(value, *others):
    return lax.optimization_barrier((value,) + others)[0]


def zero_of(value):
    return value[(slice(0, 1),) * value.ndim].reshape(()).astype(f32) * 0.0


def gather_row(key_value):
    line = jnp.stack([key_value] + [shift(key_value, "x", -step) for step in (1, 2, 3)])
    ahead = [lax.ppermute(line, CORNER, pairs) for pairs in LATER]
    partner = lax.ppermute(line, CORNER, PARTNER)
    beside = [lax.ppermute(value, "c", [(0, 1)]) for value in (line, partner)]
    return line, partner, ahead[0], ahead[1], beside[0], beside[1]


def sum_row(own, own_partner, prev, prev_partner, beside):
    got = [lax.ppermute(value, "c", [(1, 0)]) for value in (prev_partner, prev)]
    terms = [lax.ppermute(value, CORNER, pairs) for value, pairs in zip((prev, prev_partner), EARLIER)]
    sent = (own_partner.astype(f32) + got[0].astype(f32)).astype(bf16)
    terms = [got[1], lax.ppermute(sent, CORNER, PARTNER)] + terms
    start = zero_of(sent)
    line = own.astype(f32)
    for term in terms:
        line = line + term.astype(f32)
    sent = (line + beside(start)).astype(bf16)
    total = line[0]
    for step in (2, 1, 3):
        total = total + shift(sent[step], "x", step).astype(f32)
    return total


def allowed_mask(own_pos, own_start, key_pos):
    return (key_pos <= own_pos) & (key_pos >= own_start)


def load_tile(tile, tile_buf, own_ref, partner_ref, ahead_ref, ahead_partner_ref, beside_ref, beside_partner_ref):
    @pl.when(tile == 0)
    def _():
        tile_buf[...] = ahead_ref[0] + beside_ref[0]

    @pl.when(tile == 1)
    def _():
        tile_buf[...] = ahead_partner_ref[0] + beside_partner_ref[0]

    @pl.when(tile == 2)
    def _():
        tile_buf[...] = own_ref[0]

    @pl.when(tile == 3)
    def _():
        tile_buf[...] = partner_ref[0]


def attend_kernel(active, q_ref, pos_ref, start_ref, kpos_ref, *refs):
    mixed_ref, lse_ref, tile_buf, top, total, accum = refs[6:]
    step = pl.program_id(0)

    @pl.when(step == 0)
    def _():
        top[...] = jnp.full(top.shape, neg_big, f32)
        total[...] = jnp.zeros(total.shape, f32)
        accum[...] = jnp.zeros(accum.shape, f32)

    @pl.when(active[step] != 0)
    def _():
        load_tile(step // 4, tile_buf, *refs[:6])
        allowed = allowed_mask(pos_ref[...], start_ref[...], kpos_ref[0])
        for head in range(2):
            scores = times_transposed(q_ref[:, head * HEAD_SIZE : (head + 1) * HEAD_SIZE], tile_buf[:, :HEAD_SIZE])
            scores = jnp.where(allowed, scores, neg_big)
            top_old = top[head]
            top_new = jnp.maximum(top_old, jnp.max(scores, axis=-1, keepdims=True))
            weights_p = jnp.where(allowed, jnp.exp(scores - top_new), 0.0)
            damping = jnp.exp(top_old - top_new)
            total[head] = total[head] * damping + jnp.sum(weights_p, axis=-1, keepdims=True)
            accum[head] = accum[head] * damping + product(weights_p.astype(bf16), tile_buf[:, HEAD_SIZE:])
            top[head] = top_new

    @pl.when(step == 15)
    def _():
        for head in range(2):
            mixed_ref[:, head * HEAD_SIZE : (head + 1) * HEAD_SIZE] = accum[head] / total[head]
            lse_ref[head] = top[head] + jnp.log(total[head])


def attend_back_kernel(active, q_ref, pos_ref, start_ref, kpos_ref, *refs):
    mixed_ref, lse_ref, dout_ref, dq_ref, down_ref, dpartner_ref, dprev_ref, dprev_partner_ref = refs[6:14]
    tile_buf, delta, sums = refs[14:]
    step = pl.program_id(0)
    tile = step // 4

    @pl.when(step == 0)
    def _():
        dq_ref[...] = jnp.zeros(dq_ref.shape, f32)
        for head in range(2):
            cols = slice(head * HEAD_SIZE, (head + 1) * HEAD_SIZE)
            delta[head] = jnp.sum(dout_ref[:, cols].astype(f32) * mixed_ref[:, cols], axis=-1, keepdims=True)

    @pl.when(active[step] == 0)
    def _():
        sums[...] = jnp.zeros(sums.shape, bf16)

    @pl.when(active[step] != 0)
    def _():
        load_tile(tile, tile_buf, *refs[:6])
        allowed = allowed_mask(pos_ref[...], start_ref[...], kpos_ref[0])
        dk = jnp.zeros((GROUP, HEAD_SIZE), f32)
        dv = jnp.zeros((GROUP, HEAD_SIZE), f32)
        for head in range(2):
            cols = slice(head * HEAD_SIZE, (head + 1) * HEAD_SIZE)
            query, dout = q_ref[:, cols], dout_ref[:, cols]
            scores = times_transposed(query, tile_buf[:, :HEAD_SIZE])
            weights_p = jnp.where(allowed, jnp.exp(scores - lse_ref[head]), 0.0)
            dprobs = times_transposed(dout, tile_buf[:, HEAD_SIZE:])
            dscores = (weights_p * (dprobs - delta[head])).astype(bf16)
            dq_ref[:, cols] += product(dscores, tile_buf[:, :HEAD_SIZE])
            dk = dk + inner_rows(dscores, query)
            dv = dv + inner_rows(weights_p.astype(bf16), dout)
        sums[:, :HEAD_SIZE] = dk.astype(bf16)
        sums[:, HEAD_SIZE:] = dv.astype(bf16)

    for at, out_ref in enumerate((dprev_ref, dprev_partner_ref, down_ref, dpartner_ref)):

        @pl.when(tile == at)
        def _():
            out_ref[0] = sums[...]


def whole(shape):
    return pl.BlockSpec(shape, lambda *grid_and_refs: (0,) * len(shape))


def line_spec(tile):
    return pl.BlockSpec((1, GROUP, GROUP), lambda i, active: (jnp.clip(i - 4 * tile, 0, 3), 0, 0))


def active_spec(tile, table):
    return pl.BlockSpec(
        (1, GROUP, GROUP), lambda i, active: (active[16 * table + 4 * tile + jnp.clip(i - 4 * tile, 0, 3)], 0, 0)
    )


def step_tables(active, c):
    marks = active.reshape(4, 4)
    at = jnp.arange(4, dtype=jnp.int32)
    seen = jnp.where((marks[:, None, :] != 0) & (at[None, None, :] <= at[None, :, None]), at[None, None, :], -1)
    last = jnp.max(seen, axis=2)
    first = jnp.min(jnp.where(marks != 0, at[None, :], 3), axis=1, keepdims=True)
    blocks = jnp.where(last >= 0, last, first).reshape(16).astype(jnp.int32)
    return jnp.concatenate([active, blocks, jnp.where(c == 0, blocks, 0), jnp.where(c == 0, 0, blocks)])


def common_specs():
    return [
        whole((GROUP, GROUP)),
        whole((GROUP, 1)),
        whole((GROUP, 1)),
        pl.BlockSpec((1, 1, GROUP), lambda i, active: (i, 0, 0)),
    ] + [active_spec(tile, table) for tile, table in ((2, 1), (3, 1), (0, 2), (1, 2), (0, 3), (1, 3))]


def attend(active, *operands):
    return pl.pallas_call(
        attend_kernel,
        grid_spec=pltpu.PrefetchScalarGridSpec(
            num_scalar_prefetch=1,
            grid=(16,),
            in_specs=common_specs(),
            out_specs=[whole((GROUP, GROUP)), whole((2, GROUP, 1))],
            scratch_shapes=[
                pltpu.VMEM((GROUP, GROUP), bf16),
                pltpu.VMEM((2, GROUP, 1), f32),
                pltpu.VMEM((2, GROUP, 1), f32),
                pltpu.VMEM((2, GROUP, HEAD_SIZE), f32),
            ],
        ),
        out_shape=[
            jax.ShapeDtypeStruct((GROUP, GROUP), f32),
            jax.ShapeDtypeStruct((2, GROUP, 1), f32),
        ],
        compiler_params=pltpu.CompilerParams(vmem_limit_bytes=48 << 20),
        cost_estimate=pl.CostEstimate(flops=6 << 30, bytes_accessed=10 << 20, transcendentals=8 << 20),
        name="attend",
    )(active, *operands)


def attend_back(active, *operands):
    return pl.pallas_call(
        attend_back_kernel,
        grid_spec=pltpu.PrefetchScalarGridSpec(
            num_scalar_prefetch=1,
            grid=(16,),
            in_specs=common_specs() + [whole((GROUP, GROUP)), whole((2, GROUP, 1)), whole((GROUP, GROUP))],
            out_specs=[whole((GROUP, GROUP))] + [line_spec(tile) for tile in (2, 3, 0, 1)],
            scratch_shapes=[
                pltpu.VMEM((GROUP, GROUP), bf16),
                pltpu.VMEM((2, GROUP, 1), f32),
                pltpu.VMEM((GROUP, GROUP), bf16),
            ],
        ),
        out_shape=[jax.ShapeDtypeStruct((GROUP, GROUP), f32)]
        + [jax.ShapeDtypeStruct((4, GROUP, GROUP), bf16)] * 4,
        compiler_params=pltpu.CompilerParams(vmem_limit_bytes=48 << 20),
        cost_estimate=pl.CostEstimate(flops=12 << 30, bytes_accessed=20 << 20, transcendentals=8 << 20),
        name="attend_back",
    )(active, *operands)


UNITS = 1024
CHUNK = 256


def ffn_kernel(
    at,
    nm_ref,
    cot_ref,
    lgu_ref,
    gld_ref,
    wg_ref,
    wu_ref,
    wd_ref,
    ge_ref,
    ue_ref,
    ds_ref,
    perm_ref,
    pick_ref,
    result_ref,
    back_ref,
    units_ref,
    nmp,
    result,
    grad,
    low,
):
    step = pl.program_id(0)
    rank = ds_ref.shape[1]

    @pl.when(step == 0)
    def _():
        for zone in range(4):
            cols = slice(zone * GROUP, (zone + 1) * GROUP)
            nmp[:, cols] = product(nm_ref[:, cols], perm_ref[...]).astype(bf16)
        result[...] = jnp.zeros(result.shape, f32)
        grad[...] = jnp.zeros(grad.shape, f32)
        low[...] = jnp.zeros(low.shape, f32)

    wg, wu = wg_ref[...].reshape(2048, CHUNK), wu_ref[...].reshape(2048, CHUNK)
    wd = wd_ref[...].reshape(CHUNK, 2048)
    ge, ue = product(ge_ref[...], pick_ref[0]).astype(bf16), product(ue_ref[...], pick_ref[0]).astype(bf16)
    ds = inner_rows(pick_ref[0], ds_ref[...]).astype(bf16)
    low_gate, low_up = lgu_ref[:, :rank], lgu_ref[:, rank:]
    gate_pre = product(nmp[...], wg) + product(low_gate, ge)
    up_pre = product(nmp[...], wu) + product(low_up, ue)
    sigmoid_g = jax.nn.sigmoid(gate_pre)
    silu_gate = gate_pre * sigmoid_g
    active_units = (silu_gate * up_pre).astype(bf16)
    grad_active = times_transposed(cot_ref[...], wd) + times_transposed(gld_ref[...], ds)
    grad_gate = (grad_active * up_pre * sigmoid_g * (1.0 + gate_pre * (1.0 - sigmoid_g))).astype(bf16)
    grad_up = (grad_active * silu_gate).astype(bf16)
    result[...] += product(active_units, wd)
    grad[...] += times_transposed(grad_gate, wg) + times_transposed(grad_up, wu)
    low[:, :rank] += times_transposed(grad_gate, ge)
    low[:, rank : 2 * rank] += times_transposed(grad_up, ue)
    low[:, 2 * rank :] += product(active_units, ds)
    units_ref[0, :, 0, :64] = inner_rows(grad_gate, low_gate).reshape(4, 64, rank)
    units_ref[0, :, 0, 64:128] = inner_rows(grad_up, low_up).reshape(4, 64, rank)
    units_ref[0, :, 0, 128:] = inner_rows(active_units, gld_ref[...]).reshape(4, 64, rank)

    @pl.when(step == 2 * UNITS // CHUNK - 1)
    def _():
        result_ref[...] = result[...].astype(bf16)
        for zone in range(4):
            cols = slice(zone * GROUP, (zone + 1) * GROUP)
            back_ref[:, cols] = product(grad[:, cols].astype(bf16), perm_ref[...]).astype(bf16)
        back_ref[:, 2048:] = low[...].astype(bf16)


def feed_forward(at, normed_mid, cot, low_gu, grad_low_down, weights, expands, perm, picks):
    rank = low_gu.shape[1] // 2
    steps = UNITS // CHUNK
    unit_spec = pl.BlockSpec((1, 4, 1, 192, rank), lambda i, at: (i % steps, 0, i // steps, 0, 0))
    return pl.pallas_call(
        ffn_kernel,
        grid_spec=pltpu.PrefetchScalarGridSpec(
            num_scalar_prefetch=1,
            grid=(2 * steps,),
            in_specs=[
                whole((GROUP, 2048)),
                whole((GROUP, 2048)),
                whole((GROUP, 2 * rank)),
                whole((GROUP, rank)),
                pl.BlockSpec((16, 1, 128, CHUNK), lambda i, at: (0, i // steps, 0, i % steps)),
                pl.BlockSpec((16, 1, 128, CHUNK), lambda i, at: (0, i // steps, 0, steps + i % steps)),
                pl.BlockSpec((4, 1, 64, 2048), lambda i, at: (i % steps, i // steps, 2, 0)),
                pl.BlockSpec((rank, 2 * CHUNK), lambda i, at: (0, 4 * (i % steps) + at[0])),
                pl.BlockSpec((rank, 2 * CHUNK), lambda i, at: (0, 4 * (i % steps) + at[0])),
                pl.BlockSpec((2 * CHUNK, rank), lambda i, at: (4 * (i % steps) + at[0], 0)),
                whole((GROUP, GROUP)),
                pl.BlockSpec((1, 2 * CHUNK, CHUNK), lambda i, at: (i // steps, 0, 0)),
            ],
            out_specs=[whole((GROUP, 2048)), whole((GROUP, 2048 + 3 * rank)), unit_spec],
            scratch_shapes=[
                pltpu.VMEM((GROUP, 2048), bf16),
                pltpu.VMEM((GROUP, 2048), f32),
                pltpu.VMEM((GROUP, 2048), f32),
                pltpu.VMEM((GROUP, 3 * rank), f32),
            ],
        ),
        out_shape=[
            jax.ShapeDtypeStruct((GROUP, 2048), bf16),
            jax.ShapeDtypeStruct((GROUP, 2048 + 3 * rank), bf16),
            jax.ShapeDtypeStruct((4, 4, 2, 192, rank), f32),
        ],
        compiler_params=pltpu.CompilerParams(vmem_limit_bytes=60 << 20),
        cost_estimate=pl.CostEstimate(flops=28 << 30, bytes_accessed=40 << 20, transcendentals=2 << 20),
        name="feed_forward",
    )(at, normed_mid, cot, low_gu, grad_low_down, weights, weights, weights, *expands, perm, picks)


EARLY = (64, 64, 64, 16, 16, 16, 16, 16)
LATE = (16, 8, 8, 16, 16, 16)


def cut(array, sizes):
    found, at = [], 0
    for size in sizes:
        found.append(array[..., at : at + size, :])
        at += size
    return found


def early_kernel(all_ref, gate_ref, up_ref, down_ref, oshrink_ref, oexpand_ref, dexpand_ref, gateup_ref):
    pieces = [piece.astype(f32).reshape(-1, 128) for piece in cut(all_ref[...], EARLY)]
    gate_ref[...] = pieces[0].T
    up_ref[...] = pieces[1].T
    down_ref[...] = pieces[2]
    oshrink_ref[...] = pieces[3]
    oexpand_ref[...] = pieces[4].T
    dexpand_ref[...] = pieces[5].T
    gateup_ref[:, :128] = pieces[6]
    gateup_ref[:, 128:] = pieces[7]


def unpack_early(everyone):
    return pl.pallas_call(
        early_kernel,
        grid=(16,),
        in_specs=[pl.BlockSpec((8, sum(EARLY), 128), lambda i: (i, 0, 0))],
        out_specs=[
            pl.BlockSpec((128, 512), lambda i: (0, i)),
            pl.BlockSpec((128, 512), lambda i: (0, i)),
            pl.BlockSpec((512, 128), lambda i: (i, 0)),
            pl.BlockSpec((128, 128), lambda i: (i, 0)),
            pl.BlockSpec((128, 128), lambda i: (0, i)),
            pl.BlockSpec((128, 128), lambda i: (0, i)),
            pl.BlockSpec((128, 256), lambda i: (i, 0)),
        ],
        out_shape=[
            jax.ShapeDtypeStruct(shape, f32)
            for shape in ((128, 8192), (128, 8192), (8192, 128), (2048, 128), (128, 2048), (128, 2048), (2048, 256))
        ],
        cost_estimate=pl.CostEstimate(flops=1 << 20, bytes_accessed=27 << 20, transcendentals=0),
        name="unpack_early",
    )(everyone)


def late_kernel(core, mine_ref, other_ref, q_ref, k_ref, v_ref, low_ref):
    mine, other = mine_ref[0].astype(f32), other_ref[0].astype(f32)
    first, second = jnp.where(core[0] == 0, mine, other), jnp.where(core[0] == 0, other, mine)
    pieces = [
        jnp.stack(pair, axis=1).reshape(-1, 128) for pair in zip(cut(first, LATE), cut(second, LATE))
    ]
    q_ref[...] = pieces[0].T
    k_ref[...] = pieces[1].T
    v_ref[...] = pieces[2].T
    for at in range(3):
        low_ref[:, at * 128 : (at + 1) * 128] = pieces[3 + at]


def unpack_late(core, mine, other):
    half = pl.BlockSpec((1, 8, sum(LATE), 128), lambda i, core: (i // 2, i % 2, 0, 0))
    return pl.pallas_call(
        late_kernel,
        grid_spec=pltpu.PrefetchScalarGridSpec(
            num_scalar_prefetch=1,
            grid=(8,),
            in_specs=[half, half],
            out_specs=[
                pl.BlockSpec((128, 256), lambda i, core: (0, i)),
                pl.BlockSpec((128, 128), lambda i, core: (0, i)),
                pl.BlockSpec((128, 128), lambda i, core: (0, i)),
                pl.BlockSpec((256, 384), lambda i, core: (i, 0)),
            ],
        ),
        out_shape=[
            jax.ShapeDtypeStruct(shape, f32) for shape in ((128, 2048), (128, 1024), (128, 1024), (2048, 384))
        ],
        cost_estimate=pl.CostEstimate(flops=1 << 20, bytes_accessed=8 << 20, transcendentals=0),
        name="unpack_late",
    )(core, mine, other)


def local(
    hidden_in,
    gain_attn,
    gain_ffn,
    w_query,
    w_key,
    w_value,
    w_out,
    w_gate,
    w_up,
    w_down,
    qkv_shrink,
    query_expand,
    key_expand,
    value_expand,
    out_shrink,
    out_expand,
    gateup_shrink,
    gate_expand,
    up_expand,
    down_shrink,
    down_expand,
    lengths,
    adapter,
    packed_pos,
    cotangent,
):
    zh, zl, x, y, c = (lax.axis_index(name) for name in ALL)
    row = 2 * zh + c
    factor = HEAD_SIZE ** (-0.5)
    rank = out_shrink.shape[1]

    def to_rows(value):
        own = lax.dynamic_slice_in_dim(value, c * HALF, HALF, 0)
        sent = lax.dynamic_slice_in_dim(value, (1 - c) * HALF, HALF, 0)
        return jnp.concatenate([own, swap_cores(sent)], axis=0)

    def from_rows(value):
        own, got = value[:HALF], swap_cores(value[HALF:])
        return jnp.where(c == 0, jnp.concatenate([own, got], 0), jnp.concatenate([got, own], 0))

    hidden = to_rows(hidden_in)
    cot = to_rows(cotangent)

    def roll(array, by, axis):
        return lax.dynamic_slice_in_dim(jnp.concatenate([array, array], axis), by, array.shape[axis], axis)

    spread = packed_pos.reshape(2, 2, 4, 4, 2, 2, HALF)
    spread = jnp.transpose(spread, (0, 5, 1, 2, 3, 4, 6))
    rows_pos = jnp.stack([spread[:, 0], spread[:, 1, :, :, :, ::-1]], axis=1).reshape(4, 2, 4, 4, 128)
    rows_pos = roll(roll(roll(rows_pos, zl, 1), x, 2), y, 3).reshape(4, 8, GROUP)
    own_row = lax.dynamic_index_in_dim(rows_pos, row, 0, keepdims=False)
    prev_row = lax.dynamic_index_in_dim(rows_pos, jnp.maximum(row - 1, 0), 0, keepdims=False)
    prev_row = jnp.where(row == 0, far, prev_row)
    tiles_pos = jnp.concatenate([prev_row, own_row])
    group_pos = own_row[0]
    seq_ends = jnp.cumsum(lengths)
    starts = seq_ends - lengths
    member = (group_pos[:, None] >= starts[None, :]) & (group_pos[:, None] < seq_ends[None, :])
    member_int = member.astype(jnp.int32)
    group_start = jnp.sum(member_int * starts[None, :], axis=1)

    def selected(pos):
        inside = (pos[:, None] >= starts[None, :]) & (pos[:, None] < seq_ends[None, :])
        owner = jnp.sum(inside.astype(jnp.int32) * adapter[None, :], axis=1)
        return (owner[:, None] == (jnp.arange(rank, dtype=jnp.int32) // RANK)[None, :]).astype(f32)

    key_runs, pos_runs, start_runs = tiles_pos.reshape(64, 128), group_pos.reshape(4, 128), group_start.reshape(4, 128)
    key_low, key_high = jnp.min(key_runs, axis=1)[:, None], jnp.max(key_runs, axis=1)[:, None]
    seen = (key_low <= jnp.max(pos_runs, axis=1)[None, :]) & (key_high >= jnp.min(start_runs, axis=1)[None, :])
    active = jnp.max(seen.astype(jnp.int32).reshape(16, 16), axis=1)
    active = step_tables(active, c)
    select_y = selected(group_pos)
    select_x = selected(own_row.reshape(2, 4, 4, 128)[0, :, 0].reshape(GROUP))
    select = select_y[:128]
    cos_table, sin_table = rope_tables(group_pos - group_start, HEAD_SIZE)

    def column_slices(weight):
        parts = weight.reshape(16, 4, 4, 4, 2, 64)
        return jnp.transpose(parts, (2, 4, 0, 1, 3, 5)).reshape(8, 16, 1024)

    heads_q = w_query.reshape(16, 4, 512)
    heads_kv = jnp.concatenate([w_key.reshape(16, 4, 256), w_value.reshape(16, 4, 256)], axis=2)
    qkv_parts = jnp.transpose(jnp.stack([heads_q, heads_kv], axis=2), (1, 2, 0, 3)).reshape(8, 16, 512)
    qkv_parts = lax.all_to_all(qkv_parts, ("y", "c"), split_axis=0, concat_axis=0, tiled=True).reshape(128, 512)
    gate_up = jnp.concatenate([column_slices(w_gate), column_slices(w_up)], axis=2)
    gate_up = lax.all_to_all(after(gate_up, qkv_parts), ("x", "c"), split_axis=0, concat_axis=0, tiled=True).reshape(128, 2048)
    def columns_of(array, width):
        return lax.dynamic_slice_in_dim(array, y * width, width, 1)

    inputs = hidden.astype(f32)
    scale_in = row_scale(inputs)
    normed = (inputs * scale_in * gain_attn).astype(bf16)
    normed, cot, qkv_parts, gate_up = lax.optimization_barrier((normed, cot, qkv_parts, gate_up))
    normed_g = gather_near(normed, "y")
    cot_g = gather_near(cot, "x")
    qkv_parts = after(qkv_parts, normed_g, cot_g)
    wo = lax.all_gather(w_out, ALL, axis=0, tiled=True)
    qkv_mine = gather_ring(gather_ring(qkv_parts, "x"), "z").reshape(2048, 512)
    qkv_other = swap_cores(qkv_mine)
    q_expand = columns_of(query_expand, 512)
    k_expand = columns_of(key_expand, 256)
    v_expand = columns_of(value_expand, 256)
    low_qkv = (product(normed_g, qkv_shrink) * jnp.tile(select_y, (1, 3))).astype(bf16)
    lin_mine, lin_other = product(normed_g, qkv_mine), product(normed_g, qkv_other)
    query_lin = jnp.where(c == 0, lin_mine, lin_other) + product(low_qkv[:, :rank], q_expand)
    kv_lin = jnp.where(c == 0, lin_other, lin_mine)
    key_lin = kv_lin[:, :256] + product(low_qkv[:, rank : 2 * rank], k_expand)
    value_lin = kv_lin[:, 256:] + product(low_qkv[:, 2 * rank :], v_expand)
    query_heads = query_lin.reshape(GROUP, 2, HEAD_SIZE)
    key_heads = key_lin.reshape(GROUP, 1, HEAD_SIZE)
    query = (query_heads * cos_table + rotate(query_heads) * sin_table).astype(bf16)
    query = (query * bf16(factor)).reshape(GROUP, 512)
    key = (key_heads * cos_table + rotate(key_heads) * sin_table).astype(bf16).reshape(GROUP, 256)

    lines = gather_row(jnp.concatenate([key, value_lin.astype(bf16)], axis=1))
    waited = zero_of(lines[1]) + zero_of(lines[2]) + zero_of(lines[3]) + zero_of(lines[4]) + zero_of(wo)
    ffn = jnp.concatenate([gate_up, w_down], axis=0) + waited.astype(bf16)
    ffn = lax.all_gather(ffn, OVER_X, axis=0, tiled=False).reshape(16, 2, 192, 2048)
    attended = (query, group_pos[:, None], group_start[:, None], tiles_pos.reshape(16, 1, GROUP)) + lines
    mixed_f, lse = attend(active, *attended)
    mixed = mixed_f.astype(bf16)

    heads = jnp.zeros((4, 128, 512), bf16)
    heads = lax.dynamic_update_index_in_dim(heads, mixed[:128], y, 0)
    for step in (1, 2, 3):
        got = shift(mixed[step * 128 : (step + 1) * 128], "y", step)
        heads = lax.dynamic_update_index_in_dim(heads, got, (y - step) % 4, 0)
    mixed_tok = jnp.transpose(heads, (1, 0, 2)).reshape(128, 2048)
    low_out = (product(mixed_tok, out_shrink) * select).astype(bf16)
    middle = inputs + product(mixed_tok, wo) + product(low_out, out_expand)
    scale_mid = row_scale(middle)
    normed_mid = (middle * scale_mid * gain_ffn).astype(bf16)
    normed_mid_g = gather_near(normed_mid, "x")

    select_two = jnp.tile(select_x, (1, 2))
    low_gu = (product(normed_mid_g, gateup_shrink) * select_two).astype(bf16)
    grad_low_down = (times_transposed(cot_g, down_expand) * select_x).astype(bf16)
    place = jnp.arange(GROUP, dtype=jnp.int32)
    turned = (place // 32 % 4) * 128 + (place // 128) * 32 + place % 32
    perm = (turned[:, None] == place[None, :]).astype(bf16)
    wide, narrow = jnp.arange(2 * CHUNK, dtype=jnp.int32), jnp.arange(CHUNK, dtype=jnp.int32)
    picks = jnp.stack(
        [(wide[:, None] == (narrow // 64 * 128 + core * 64 + narrow % 64)[None, :]).astype(bf16) for core in (0, 1)]
    )
    result, back_part, unit_grads = feed_forward(
        x.reshape(1).astype(jnp.int32),
        normed_mid_g,
        cot_g,
        low_gu,
        grad_low_down,
        ffn,
        (gate_expand, up_expand, down_shrink),
        perm,
        picks,
    )

    def sum_tokens(part, ring):
        sent = part.astype(bf16)
        return sum_near([sent[i * 128 : (i + 1) * 128] for i in range(4)], ring)

    back = sum_tokens(back_part, "x")
    back, back_low, low_down_sum = back[:, :2048], back[:, 2048 : 2048 + 2 * rank], back[:, 2048 + 2 * rank :]

    low_down = (low_down_sum * select).astype(bf16)
    grad_low_gu = (back_low * jnp.tile(select, (1, 2))).astype(bf16)
    grad_normed_mid = back + times_transposed(grad_low_gu, gateup_shrink)
    cot_f = cot.astype(f32)
    grad_middle = cot_f + norm_back(middle, scale_mid, gain_ffn, grad_normed_mid)
    grad_attn_out = grad_middle.astype(bf16)
    grad_low_out = (times_transposed(grad_attn_out, out_expand) * select).astype(bf16)
    grad_mixed = (times_transposed(grad_attn_out, wo) + times_transposed(grad_low_out, out_shrink)).astype(bf16)

    def slices_near(array):
        def columns_at(step):
            return lax.dynamic_slice_in_dim(array, ((y + step) % 4) * 512, 512, 1)

        return jnp.concatenate([columns_at(0)] + [shift(columns_at(4 - step), "y", -step) for step in (1, 2, 3)])

    dout = slices_near(grad_mixed)
    dq, *terms = attend_back(active, *attended, mixed_f, lse, dout)
    unit_sum = lax.psum_scatter(
        unit_grads.reshape(32, 192, rank), OVER_X, scatter_dimension=0, tiled=False
    )
    aheads = []

    def beside(start):
        aheads.append(sum_tokens(result + start.astype(bf16), "x"))
        return zero_of(aheads[0]) + zero_of(unit_sum)

    dkv = sum_row(*terms, beside)
    dk, dv = dkv[:, :HEAD_SIZE], dkv[:, HEAD_SIZE:]
    query_back = (dq * factor).astype(bf16).astype(f32).reshape(GROUP, 2, HEAD_SIZE)
    key_back = dk.astype(bf16).astype(f32).reshape(GROUP, 1, HEAD_SIZE)
    grad_value = dv.astype(bf16)
    grad_query = (query_back * cos_table - rotate(query_back * sin_table)).astype(bf16).reshape(GROUP, 512)
    grad_key = (key_back * cos_table - rotate(key_back * sin_table)).astype(bf16).reshape(GROUP, 256)
    grad_kv = jnp.concatenate([grad_key, grad_value], axis=1)

    grad_low_part = jnp.concatenate(
        [
            times_transposed(grad_query, q_expand),
            times_transposed(grad_key, k_expand),
            times_transposed(grad_value, v_expand),
        ],
        axis=1,
    )
    grad_low_qkv = (sum_tokens(grad_low_part, "y") * jnp.tile(select, (1, 3))).astype(bf16)
    for_mine = jnp.where(c == 0, grad_query, grad_kv)
    for_other = jnp.where(c == 0, grad_kv, grad_query)
    grad_normed_part = times_transposed(for_mine, qkv_mine) + times_transposed(for_other, qkv_other)
    grad_normed = sum_tokens(grad_normed_part, "y") + times_transposed(grad_low_qkv, qkv_shrink)
    output = (middle + aheads[0] + product(low_down, down_expand)).astype(bf16)
    grad_input = (grad_middle + norm_back(inputs, scale_in, gain_attn, grad_normed)).astype(bf16)

    def features(array, at):
        return lax.dynamic_slice_in_dim(array, at * 512, 512, 1)

    def by_cores(arrays):
        parts = jnp.concatenate([array.reshape(16, 2, array.shape[0] // 32, rank) for array in arrays], axis=2)
        kept = lax.dynamic_index_in_dim(parts, c, 1, keepdims=False)
        return kept, lax.dynamic_index_in_dim(parts, 1 - c, 1, keepdims=False)

    def sum_plane(kept, given, ring):
        terms = kept + swap_cores(given.astype(bf16)).astype(f32)
        return sum_ring(sum_ring(terms.reshape(4, 4, -1, rank), "z"), ring)

    row_terms = [
        inner_rows(mixed_tok, grad_low_out),
        inner_rows(grad_attn_out, low_out),
        inner_rows(cot, low_down),
        inner_rows(normed_mid, grad_low_gu[:, :rank]),
        inner_rows(normed_mid, grad_low_gu[:, rank:]),
    ]
    row_terms = jnp.concatenate([array.reshape(128, 16, rank) for array in row_terms], axis=1)
    row_terms = jnp.swapaxes(row_terms.reshape(4, 4, 8, 80, rank), 1, 2).reshape(32, 320, rank)
    row_sum = lax.psum_scatter(row_terms, OVER_X, scatter_dimension=0, tiled=False)
    row_sum = sum_ring((row_sum + zero_of(dkv)).reshape(4, 80, rank), "x")
    early_sum = jnp.concatenate([unit_sum, row_sum], axis=0).astype(bf16)
    early_all = lax.all_gather(early_sum, ALL, axis=0, tiled=False)

    grad_qkv = inner_rows(features(normed_g, y), gather_near(grad_low_qkv, "y"))
    kept, other = by_cores(
        [
            inner_rows(grad_query, low_qkv[:, :rank]),
            inner_rows(grad_key, low_qkv[:, rank : 2 * rank]),
            inner_rows(grad_value, low_qkv[:, 2 * rank :]),
            grad_qkv[:, :rank],
            grad_qkv[:, rank : 2 * rank],
            grad_qkv[:, 2 * rank :],
        ]
    )
    g_gate, g_up, g_down_shrink, g_out_shrink, g_out_expand, g_down_expand, g_gateup = unpack_early(early_all)
    late_sum = sum_plane(kept, other, "x").astype(bf16)
    late_all = gather_ring(gather_ring(late_sum, "x"), "z") + zero_of(g_gateup).astype(bf16)
    late_all = gather_ring(late_all, "y")
    late_all = late_all.reshape(4, 16, -1, rank)
    late_other = swap_cores(late_all)
    g_q, g_k, g_v, g_qkv = unpack_late(c.reshape(1).astype(jnp.int32), late_all, late_other)
    return (
        from_rows(output),
        from_rows(grad_input),
        g_qkv,
        g_q,
        g_k,
        g_v,
        g_out_shrink,
        g_out_expand,
        g_gateup,
        g_gate,
        g_up,
        g_down_shrink,
        g_down_expand,
    )


def solution(mesh):
    fine = Mesh(mesh.devices.reshape(2, 2, 4, 4, 2), ALL)
    split = P(ALL, None)
    placed = (split, P(), P()) + (split,) * 7 + (P(),) * 14 + (split,)
    return jax.shard_map(
        local,
        mesh=fine,
        in_specs=placed,
        out_specs=(split, split) + (P(),) * 11,
        check_vma=False,
    )
```

```python
from functools import partial

import jax
import jax.numpy as jnp
from jax import lax
from jax.experimental import pallas as pl
from jax.experimental.pallas import tpu as pltpu
from jax.sharding import Mesh, PartitionSpec as P

HEAD_SIZE = 256
RANK = 16
HALF = 64
GROUP = 512

ALL = ("zh", "zl", "x", "y", "c")

norm_eps = 1e-06
rope_theta = 1000042.0
neg_big = -1e30
far = 1 << 30

f32 = jnp.float32
bf16 = jnp.bfloat16


def product(left, right):
    return jnp.dot(left, right, preferred_element_type=f32)


def times_transposed(left, right):
    return lax.dot_general(left, right, (((1,), (1,)), ((), ())), preferred_element_type=f32)


def inner_rows(left, right):
    return lax.dot_general(left, right, (((0,), (0,)), ((), ())), preferred_element_type=f32)


def row_scale(value_matrix):
    return lax.rsqrt(jnp.mean(value_matrix * value_matrix, axis=-1, keepdims=True) + norm_eps)


def norm_back(value_matrix, scale, gain, grad):
    scaled = gain * grad
    return scale * scaled - value_matrix * (scale * scale * scale) * jnp.mean(
        value_matrix * scaled, axis=-1, keepdims=True
    )


def rotate(value_matrix):
    middle = value_matrix.shape[-1] // 2
    return jnp.concatenate([-value_matrix[..., middle:], value_matrix[..., :middle]], axis=-1)


def rope_tables(positions, width):
    middle = width // 2
    inverse = rope_theta ** (-(jnp.arange(middle, dtype=f32) * 2.0) / width)
    angles = positions.astype(f32)[:, None] * inverse[None, :]
    cos_half, sin_half = jnp.cos(angles), jnp.sin(angles)
    cos_table = jnp.concatenate([cos_half, cos_half], axis=-1)[:, None, :]
    sin_table = jnp.concatenate([sin_half, sin_half], axis=-1)[:, None, :]
    return (cos_table, sin_table)


OVER_X = ("zh", "zl", "y", "c")
RING = {"x": ("x",), "y": ("y",), "z": ("zh", "zl")}


def swap_cores(value):
    return lax.ppermute(value, "c", [(0, 1), (1, 0)])


def shift(value, ring, step):
    return lax.ppermute(value, RING[ring], [(i, (i + step) % 4) for i in range(4)])


def place_in(ring):
    return lax.axis_index(RING[ring])


def gather_near(value, ring, axis=0):
    return jnp.concatenate([value] + [shift(value, ring, -step) for step in (1, 2, 3)], axis=axis)


def gather_ring(value, ring):
    at = place_in(ring)
    whole_ring = jnp.zeros((4,) + value.shape, value.dtype)
    whole_ring = lax.dynamic_update_index_in_dim(whole_ring, value, at, 0)
    for step in (1, 2, 3):
        got = shift(value, ring, -step)
        whole_ring = lax.dynamic_update_index_in_dim(whole_ring, got, (at + step) % 4, 0)
    return whole_ring


def sum_near(blocks, ring):
    got = [shift(blocks[step], ring, step) for step in (2, 1, 3)]
    total = blocks[0].astype(f32)
    for term in got:
        total = total + term.astype(f32)
    return total


def sum_ring(terms, ring):
    at = place_in(ring)
    got = [
        shift(lax.dynamic_index_in_dim(terms, (at + step) % 4, 0, keepdims=False).astype(bf16), ring, step)
        for step in (1, 2, 3)
    ]
    total = lax.dynamic_index_in_dim(terms, at, 0, keepdims=False)
    for term in got:
        total = total + term.astype(f32)
    return total


CORNER = ("zh", "zl", "c")
PARTNER = [(4 * zh + 2 * zl + c, 4 * zh + 2 * (1 - zl) + c) for zh in (0, 1) for zl in (0, 1) for c in (0, 1)]
LATER = [[(2 * zl + 1, 4 + 2 * (zl ^ flip)) for zl in (0, 1)] for flip in (0, 1)]
EARLIER = [[(to, came) for came, to in pairs] for pairs in LATER]
def after(value, *others):
    return lax.optimization_barrier((value,) + others)[0]


def zero_of(value):
    return value[(slice(0, 1),) * value.ndim].reshape(()).astype(f32) * 0.0


def gather_row(key_value):
    line = jnp.stack([key_value] + [shift(key_value, "x", -step) for step in (1, 2, 3)])
    ahead = [lax.ppermute(line, CORNER, pairs) for pairs in LATER]
    partner = lax.ppermute(line, CORNER, PARTNER)
    beside = [lax.ppermute(value, "c", [(0, 1)]) for value in (line, partner)]
    return line, partner, ahead[0], ahead[1], beside[0], beside[1]


def sum_row(own, own_partner, prev, prev_partner, beside):
    got = [lax.ppermute(value, "c", [(1, 0)]) for value in (prev_partner, prev)]
    terms = [lax.ppermute(value, CORNER, pairs) for value, pairs in zip((prev, prev_partner), EARLIER)]
    sent = (own_partner.astype(f32) + got[0].astype(f32)).astype(bf16)
    terms = [got[1], lax.ppermute(sent, CORNER, PARTNER)] + terms
    start = zero_of(sent)
    line = own.astype(f32)
    for term in terms:
        line = line + term.astype(f32)
    sent = (line + beside(start)).astype(bf16)
    total = line[0]
    for step in (2, 1, 3):
        total = total + shift(sent[step], "x", step).astype(f32)
    return total


def allowed_mask(own_pos, own_start, key_pos):
    return (key_pos <= own_pos) & (key_pos >= own_start)


def load_tile(tile, tile_buf, own_ref, partner_ref, ahead_ref, ahead_partner_ref, beside_ref, beside_partner_ref):
    @pl.when(tile == 0)
    def _():
        tile_buf[...] = ahead_ref[0] + beside_ref[0]

    @pl.when(tile == 1)
    def _():
        tile_buf[...] = ahead_partner_ref[0] + beside_partner_ref[0]

    @pl.when(tile == 2)
    def _():
        tile_buf[...] = own_ref[0]

    @pl.when(tile == 3)
    def _():
        tile_buf[...] = partner_ref[0]


def attend_kernel(active, q_ref, pos_ref, start_ref, kpos_ref, *refs):
    mixed_ref, lse_ref, tile_buf, top, total, accum = refs[6:]
    step = pl.program_id(0)

    @pl.when(step == 0)
    def _():
        top[...] = jnp.full(top.shape, neg_big, f32)
        total[...] = jnp.zeros(total.shape, f32)
        accum[...] = jnp.zeros(accum.shape, f32)

    @pl.when(active[step] != 0)
    def _():
        load_tile(step // 4, tile_buf, *refs[:6])
        allowed = allowed_mask(pos_ref[...], start_ref[...], kpos_ref[0])
        for head in range(2):
            scores = times_transposed(q_ref[:, head * HEAD_SIZE : (head + 1) * HEAD_SIZE], tile_buf[:, :HEAD_SIZE])
            scores = jnp.where(allowed, scores, neg_big)
            top_old = top[head]
            top_new = jnp.maximum(top_old, jnp.max(scores, axis=-1, keepdims=True))
            weights_p = jnp.exp(scores - top_new)
            damping = jnp.exp(top_old - top_new)
            total[head] = total[head] * damping + jnp.sum(weights_p, axis=-1, keepdims=True)
            accum[head] = accum[head] * damping + product(weights_p.astype(bf16), tile_buf[:, HEAD_SIZE:])
            top[head] = top_new

    @pl.when(step == 15)
    def _():
        for head in range(2):
            mixed_ref[:, head * HEAD_SIZE : (head + 1) * HEAD_SIZE] = accum[head] / total[head]
            lse_ref[head] = top[head] + jnp.log(total[head])


def attend_back_kernel(active, q_ref, pos_ref, start_ref, kpos_ref, *refs):
    mixed_ref, lse_ref, dout_ref, dq_ref, down_ref, dpartner_ref, dprev_ref, dprev_partner_ref = refs[6:14]
    tile_buf, delta, sums = refs[14:]
    step = pl.program_id(0)
    tile = step // 4

    @pl.when(step == 0)
    def _():
        dq_ref[...] = jnp.zeros(dq_ref.shape, f32)
        for head in range(2):
            cols = slice(head * HEAD_SIZE, (head + 1) * HEAD_SIZE)
            delta[head] = jnp.sum(dout_ref[:, cols].astype(f32) * mixed_ref[:, cols], axis=-1, keepdims=True)

    @pl.when(active[step] == 0)
    def _():
        sums[...] = jnp.zeros(sums.shape, bf16)

    @pl.when(active[step] != 0)
    def _():
        load_tile(tile, tile_buf, *refs[:6])
        allowed = allowed_mask(pos_ref[...], start_ref[...], kpos_ref[0])
        dk = jnp.zeros((GROUP, HEAD_SIZE), f32)
        dv = jnp.zeros((GROUP, HEAD_SIZE), f32)
        for head in range(2):
            cols = slice(head * HEAD_SIZE, (head + 1) * HEAD_SIZE)
            query, dout = q_ref[:, cols], dout_ref[:, cols]
            scores = times_transposed(query, tile_buf[:, :HEAD_SIZE])
            weights_p = jnp.where(allowed, jnp.exp(scores - lse_ref[head]), 0.0)
            dprobs = times_transposed(dout, tile_buf[:, HEAD_SIZE:])
            dscores = (weights_p * (dprobs - delta[head])).astype(bf16)
            dq_ref[:, cols] += product(dscores, tile_buf[:, :HEAD_SIZE])
            dk = dk + inner_rows(dscores, query)
            dv = dv + inner_rows(weights_p.astype(bf16), dout)
        sums[:, :HEAD_SIZE] = dk.astype(bf16)
        sums[:, HEAD_SIZE:] = dv.astype(bf16)

    for at, out_ref in enumerate((dprev_ref, dprev_partner_ref, down_ref, dpartner_ref)):

        @pl.when(tile == at)
        def _():
            out_ref[0] = sums[...]


def whole(shape):
    return pl.BlockSpec(shape, lambda *grid_and_refs: (0,) * len(shape))


def line_spec(tile):
    return pl.BlockSpec((1, GROUP, GROUP), lambda i, active: (jnp.clip(i - 4 * tile, 0, 3), 0, 0))


def active_spec(tile, table):
    return pl.BlockSpec(
        (1, GROUP, GROUP), lambda i, active: (active[16 * table + 4 * tile + jnp.clip(i - 4 * tile, 0, 3)], 0, 0)
    )


def step_tables(active, c):
    marks = active.reshape(4, 4)
    at = jnp.arange(4, dtype=jnp.int32)
    seen = jnp.where((marks[:, None, :] != 0) & (at[None, None, :] <= at[None, :, None]), at[None, None, :], -1)
    last = jnp.max(seen, axis=2)
    first = jnp.min(jnp.where(marks != 0, at[None, :], 3), axis=1, keepdims=True)
    blocks = jnp.where(last >= 0, last, first).reshape(16).astype(jnp.int32)
    return jnp.concatenate([active, blocks, jnp.where(c == 0, blocks, 0), jnp.where(c == 0, 0, blocks)])


def common_specs():
    return [
        whole((GROUP, GROUP)),
        whole((GROUP, 1)),
        whole((GROUP, 1)),
        pl.BlockSpec((1, 1, GROUP), lambda i, active: (i, 0, 0)),
    ] + [active_spec(tile, table) for tile, table in ((2, 1), (3, 1), (0, 2), (1, 2), (0, 3), (1, 3))]


def attend(active, *operands):
    return pl.pallas_call(
        attend_kernel,
        grid_spec=pltpu.PrefetchScalarGridSpec(
            num_scalar_prefetch=1,
            grid=(16,),
            in_specs=common_specs(),
            out_specs=[whole((GROUP, GROUP)), whole((2, GROUP, 1))],
            scratch_shapes=[
                pltpu.VMEM((GROUP, GROUP), bf16),
                pltpu.VMEM((2, GROUP, 1), f32),
                pltpu.VMEM((2, GROUP, 1), f32),
                pltpu.VMEM((2, GROUP, HEAD_SIZE), f32),
            ],
        ),
        out_shape=[
            jax.ShapeDtypeStruct((GROUP, GROUP), f32),
            jax.ShapeDtypeStruct((2, GROUP, 1), f32),
        ],
        compiler_params=pltpu.CompilerParams(vmem_limit_bytes=48 << 20),
        cost_estimate=pl.CostEstimate(flops=6 << 30, bytes_accessed=10 << 20, transcendentals=8 << 20),
        name="attend",
    )(active, *operands)


def attend_back(active, *operands):
    return pl.pallas_call(
        attend_back_kernel,
        grid_spec=pltpu.PrefetchScalarGridSpec(
            num_scalar_prefetch=1,
            grid=(16,),
            in_specs=common_specs() + [whole((GROUP, GROUP)), whole((2, GROUP, 1)), whole((GROUP, GROUP))],
            out_specs=[whole((GROUP, GROUP))] + [line_spec(tile) for tile in (2, 3, 0, 1)],
            scratch_shapes=[
                pltpu.VMEM((GROUP, GROUP), bf16),
                pltpu.VMEM((2, GROUP, 1), f32),
                pltpu.VMEM((GROUP, GROUP), bf16),
            ],
        ),
        out_shape=[jax.ShapeDtypeStruct((GROUP, GROUP), f32)]
        + [jax.ShapeDtypeStruct((4, GROUP, GROUP), bf16)] * 4,
        compiler_params=pltpu.CompilerParams(vmem_limit_bytes=48 << 20),
        cost_estimate=pl.CostEstimate(flops=12 << 30, bytes_accessed=20 << 20, transcendentals=8 << 20),
        name="attend_back",
    )(active, *operands)


UNITS = 1024
CHUNK = 256


def ffn_kernel(
    at,
    nm_ref,
    cot_ref,
    lgu_ref,
    gld_ref,
    wg_ref,
    wu_ref,
    wd_ref,
    ge_ref,
    ue_ref,
    ds_ref,
    perm_ref,
    pick_ref,
    result_ref,
    back_ref,
    units_ref,
    nmp,
    result,
    grad,
    low,
):
    step = pl.program_id(0)
    rank = ds_ref.shape[1]

    @pl.when(step == 0)
    def _():
        for zone in range(4):
            cols = slice(zone * GROUP, (zone + 1) * GROUP)
            nmp[:, cols] = product(nm_ref[:, cols], perm_ref[...]).astype(bf16)
        result[...] = jnp.zeros(result.shape, f32)
        grad[...] = jnp.zeros(grad.shape, f32)
        low[...] = jnp.zeros(low.shape, f32)

    wg, wu = wg_ref[...].reshape(2048, CHUNK), wu_ref[...].reshape(2048, CHUNK)
    wd = wd_ref[...].reshape(CHUNK, 2048)
    ge, ue = product(ge_ref[...], pick_ref[0]).astype(bf16), product(ue_ref[...], pick_ref[0]).astype(bf16)
    ds = inner_rows(pick_ref[0], ds_ref[...]).astype(bf16)
    low_gate, low_up = lgu_ref[:, :rank], lgu_ref[:, rank:]
    gate_pre = product(nmp[...], wg) + product(low_gate, ge)
    up_pre = product(nmp[...], wu) + product(low_up, ue)
    sigmoid_g = jax.nn.sigmoid(gate_pre)
    silu_gate = gate_pre * sigmoid_g
    active_units = (silu_gate * up_pre).astype(bf16)
    grad_active = times_transposed(cot_ref[...], wd) + times_transposed(gld_ref[...], ds)
    grad_gate = (grad_active * up_pre * sigmoid_g * (1.0 + gate_pre * (1.0 - sigmoid_g))).astype(bf16)
    grad_up = (grad_active * silu_gate).astype(bf16)
    result[...] += product(active_units, wd)
    grad[...] += times_transposed(grad_gate, wg) + times_transposed(grad_up, wu)
    low[:, :rank] += times_transposed(grad_gate, ge)
    low[:, rank : 2 * rank] += times_transposed(grad_up, ue)
    low[:, 2 * rank :] += product(active_units, ds)
    units_ref[0, :, 0, :64] = inner_rows(grad_gate, low_gate).reshape(4, 64, rank)
    units_ref[0, :, 0, 64:128] = inner_rows(grad_up, low_up).reshape(4, 64, rank)
    units_ref[0, :, 0, 128:] = inner_rows(active_units, gld_ref[...]).reshape(4, 64, rank)

    @pl.when(step == 2 * UNITS // CHUNK - 1)
    def _():
        result_ref[...] = result[...].astype(bf16)
        for zone in range(4):
            cols = slice(zone * GROUP, (zone + 1) * GROUP)
            back_ref[:, cols] = product(grad[:, cols].astype(bf16), perm_ref[...]).astype(bf16)
        back_ref[:, 2048:] = low[...].astype(bf16)


def feed_forward(at, normed_mid, cot, low_gu, grad_low_down, weights, expands, perm, picks):
    rank = low_gu.shape[1] // 2
    steps = UNITS // CHUNK
    unit_spec = pl.BlockSpec((1, 4, 1, 192, rank), lambda i, at: (i % steps, 0, i // steps, 0, 0))
    return pl.pallas_call(
        ffn_kernel,
        grid_spec=pltpu.PrefetchScalarGridSpec(
            num_scalar_prefetch=1,
            grid=(2 * steps,),
            in_specs=[
                whole((GROUP, 2048)),
                whole((GROUP, 2048)),
                whole((GROUP, 2 * rank)),
                whole((GROUP, rank)),
                pl.BlockSpec((16, 1, 128, CHUNK), lambda i, at: (0, i // steps, 0, i % steps)),
                pl.BlockSpec((16, 1, 128, CHUNK), lambda i, at: (0, i // steps, 0, steps + i % steps)),
                pl.BlockSpec((4, 1, 64, 2048), lambda i, at: (i % steps, i // steps, 2, 0)),
                pl.BlockSpec((rank, 2 * CHUNK), lambda i, at: (0, 4 * (i % steps) + at[0])),
                pl.BlockSpec((rank, 2 * CHUNK), lambda i, at: (0, 4 * (i % steps) + at[0])),
                pl.BlockSpec((2 * CHUNK, rank), lambda i, at: (4 * (i % steps) + at[0], 0)),
                whole((GROUP, GROUP)),
                pl.BlockSpec((1, 2 * CHUNK, CHUNK), lambda i, at: (i // steps, 0, 0)),
            ],
            out_specs=[whole((GROUP, 2048)), whole((GROUP, 2048 + 3 * rank)), unit_spec],
            scratch_shapes=[
                pltpu.VMEM((GROUP, 2048), bf16),
                pltpu.VMEM((GROUP, 2048), f32),
                pltpu.VMEM((GROUP, 2048), f32),
                pltpu.VMEM((GROUP, 3 * rank), f32),
            ],
        ),
        out_shape=[
            jax.ShapeDtypeStruct((GROUP, 2048), bf16),
            jax.ShapeDtypeStruct((GROUP, 2048 + 3 * rank), bf16),
            jax.ShapeDtypeStruct((4, 4, 2, 192, rank), f32),
        ],
        compiler_params=pltpu.CompilerParams(vmem_limit_bytes=60 << 20),
        cost_estimate=pl.CostEstimate(flops=28 << 30, bytes_accessed=40 << 20, transcendentals=2 << 20),
        name="feed_forward",
    )(at, normed_mid, cot, low_gu, grad_low_down, weights, weights, weights, *expands, perm, picks)


EARLY = (64, 64, 64, 16, 16, 16, 16, 16)
LATE = (16, 8, 8, 16, 16, 16)


def cut(array, sizes):
    found, at = [], 0
    for size in sizes:
        found.append(array[..., at : at + size, :])
        at += size
    return found


def turned(array):
    at = lax.broadcasted_iota(jnp.int32, (128, 128), 0), lax.broadcasted_iota(jnp.int32, (128, 128), 1)
    return times_transposed((at[0] == at[1]).astype(f32).astype(bf16), array)


def early_kernel(all_ref, gate_ref, up_ref, down_ref, oshrink_ref, oexpand_ref, dexpand_ref, gateup_ref):
    pieces = [piece.reshape(-1, 128) for piece in cut(all_ref[...], EARLY)]
    gate_ref[...] = turned(pieces[0])
    up_ref[...] = turned(pieces[1])
    down_ref[...] = pieces[2].astype(f32)
    oshrink_ref[...] = pieces[3].astype(f32)
    oexpand_ref[...] = turned(pieces[4])
    dexpand_ref[...] = turned(pieces[5])
    gateup_ref[:, :128] = pieces[6].astype(f32)
    gateup_ref[:, 128:] = pieces[7].astype(f32)


def unpack_early(everyone):
    return pl.pallas_call(
        early_kernel,
        grid=(16,),
        in_specs=[pl.BlockSpec((8, sum(EARLY), 128), lambda i: (i, 0, 0))],
        out_specs=[
            pl.BlockSpec((128, 512), lambda i: (0, i)),
            pl.BlockSpec((128, 512), lambda i: (0, i)),
            pl.BlockSpec((512, 128), lambda i: (i, 0)),
            pl.BlockSpec((128, 128), lambda i: (i, 0)),
            pl.BlockSpec((128, 128), lambda i: (0, i)),
            pl.BlockSpec((128, 128), lambda i: (0, i)),
            pl.BlockSpec((128, 256), lambda i: (i, 0)),
        ],
        out_shape=[
            jax.ShapeDtypeStruct(shape, f32)
            for shape in ((128, 8192), (128, 8192), (8192, 128), (2048, 128), (128, 2048), (128, 2048), (2048, 256))
        ],
        cost_estimate=pl.CostEstimate(flops=1 << 20, bytes_accessed=27 << 20, transcendentals=0),
        name="unpack_early",
    )(everyone)


def late_kernel(core, mine_ref, other_ref, q_ref, k_ref, v_ref, low_ref):
    mine, other = mine_ref[0].astype(f32), other_ref[0].astype(f32)
    first, second = jnp.where(core[0] == 0, mine, other), jnp.where(core[0] == 0, other, mine)
    pieces = [
        jnp.stack(pair, axis=1).reshape(-1, 128) for pair in zip(cut(first, LATE), cut(second, LATE))
    ]
    q_ref[...] = turned(pieces[0].astype(bf16))
    k_ref[...] = turned(pieces[1].astype(bf16))
    v_ref[...] = turned(pieces[2].astype(bf16))
    for at in range(3):
        low_ref[:, at * 128 : (at + 1) * 128] = pieces[3 + at]


def unpack_late(core, mine, other):
    half = pl.BlockSpec((1, 8, sum(LATE), 128), lambda i, core: (i // 2, i % 2, 0, 0))
    return pl.pallas_call(
        late_kernel,
        grid_spec=pltpu.PrefetchScalarGridSpec(
            num_scalar_prefetch=1,
            grid=(8,),
            in_specs=[half, half],
            out_specs=[
                pl.BlockSpec((128, 256), lambda i, core: (0, i)),
                pl.BlockSpec((128, 128), lambda i, core: (0, i)),
                pl.BlockSpec((128, 128), lambda i, core: (0, i)),
                pl.BlockSpec((256, 384), lambda i, core: (i, 0)),
            ],
        ),
        out_shape=[
            jax.ShapeDtypeStruct(shape, f32) for shape in ((128, 2048), (128, 1024), (128, 1024), (2048, 384))
        ],
        cost_estimate=pl.CostEstimate(flops=1 << 20, bytes_accessed=8 << 20, transcendentals=0),
        name="unpack_late",
    )(core, mine, other)


def local(
    hidden_in,
    gain_attn,
    gain_ffn,
    w_query,
    w_key,
    w_value,
    w_out,
    w_gate,
    w_up,
    w_down,
    qkv_shrink,
    query_expand,
    key_expand,
    value_expand,
    out_shrink,
    out_expand,
    gateup_shrink,
    gate_expand,
    up_expand,
    down_shrink,
    down_expand,
    lengths,
    adapter,
    packed_pos,
    cotangent,
):
    zh, zl, x, y, c = (lax.axis_index(name) for name in ALL)
    row = 2 * zh + c
    factor = HEAD_SIZE ** (-0.5)
    rank = out_shrink.shape[1]

    def to_rows(value):
        own = lax.dynamic_slice_in_dim(value, c * HALF, HALF, 0)
        sent = lax.dynamic_slice_in_dim(value, (1 - c) * HALF, HALF, 0)
        return jnp.concatenate([own, swap_cores(sent)], axis=0)

    def from_rows(value):
        own, got = value[:HALF], swap_cores(value[HALF:])
        return jnp.where(c == 0, jnp.concatenate([own, got], 0), jnp.concatenate([got, own], 0))

    hidden = to_rows(hidden_in)
    cot = to_rows(cotangent)

    def roll(array, by, axis):
        return lax.dynamic_slice_in_dim(jnp.concatenate([array, array], axis), by, array.shape[axis], axis)

    spread = packed_pos.reshape(2, 2, 4, 4, 2, 2, HALF)
    spread = jnp.transpose(spread, (0, 5, 1, 2, 3, 4, 6))
    rows_pos = jnp.stack([spread[:, 0], spread[:, 1, :, :, :, ::-1]], axis=1).reshape(4, 2, 4, 4, 128)
    rows_pos = roll(roll(roll(rows_pos, zl, 1), x, 2), y, 3).reshape(4, 8, GROUP)
    own_row = lax.dynamic_index_in_dim(rows_pos, row, 0, keepdims=False)
    prev_row = lax.dynamic_index_in_dim(rows_pos, jnp.maximum(row - 1, 0), 0, keepdims=False)
    prev_row = jnp.where(row == 0, far, prev_row)
    tiles_pos = jnp.concatenate([prev_row, own_row])
    group_pos = own_row[0]
    seq_ends = jnp.cumsum(lengths)
    starts = seq_ends - lengths
    member = (group_pos[:, None] >= starts[None, :]) & (group_pos[:, None] < seq_ends[None, :])
    member_int = member.astype(jnp.int32)
    group_start = jnp.sum(member_int * starts[None, :], axis=1)

    def selected(pos):
        inside = (pos[:, None] >= starts[None, :]) & (pos[:, None] < seq_ends[None, :])
        owner = jnp.sum(inside.astype(jnp.int32) * adapter[None, :], axis=1)
        return (owner[:, None] == (jnp.arange(rank, dtype=jnp.int32) // RANK)[None, :]).astype(f32)

    key_runs, pos_runs, start_runs = tiles_pos.reshape(64, 128), group_pos.reshape(4, 128), group_start.reshape(4, 128)
    key_low, key_high = jnp.min(key_runs, axis=1)[:, None], jnp.max(key_runs, axis=1)[:, None]
    seen = (key_low <= jnp.max(pos_runs, axis=1)[None, :]) & (key_high >= jnp.min(start_runs, axis=1)[None, :])
    active = jnp.max(seen.astype(jnp.int32).reshape(16, 16), axis=1)
    active = step_tables(active, c)
    select_y = selected(group_pos)
    select_x = selected(own_row.reshape(2, 4, 4, 128)[0, :, 0].reshape(GROUP))
    select = select_y[:128]
    cos_table, sin_table = rope_tables(group_pos - group_start, HEAD_SIZE)

    def column_slices(weight):
        parts = weight.reshape(16, 4, 4, 4, 2, 64)
        return jnp.transpose(parts, (2, 4, 0, 1, 3, 5)).reshape(8, 16, 1024)

    heads_q = w_query.reshape(16, 4, 512)
    heads_kv = jnp.concatenate([w_key.reshape(16, 4, 256), w_value.reshape(16, 4, 256)], axis=2)
    qkv_parts = jnp.transpose(jnp.stack([heads_q, heads_kv], axis=2), (1, 2, 0, 3)).reshape(8, 16, 512)
    qkv_parts = lax.all_to_all(qkv_parts, ("y", "c"), split_axis=0, concat_axis=0, tiled=True).reshape(128, 512)
    gate_up = jnp.concatenate([column_slices(w_gate), column_slices(w_up)], axis=2)
    def columns_of(array, width):
        return lax.dynamic_slice_in_dim(array, y * width, width, 1)

    inputs = hidden.astype(f32)
    scale_in = row_scale(inputs)
    normed = (inputs * scale_in * gain_attn).astype(bf16)
    normed, cot, qkv_parts = lax.optimization_barrier((normed, cot, qkv_parts))
    normed_g = gather_near(normed, "y")
    cot_g = gather_near(cot, "x")
    qkv_parts = after(qkv_parts, normed_g, cot_g)
    wo = lax.all_gather(w_out, ALL, axis=0, tiled=True)
    qkv_mine = gather_ring(gather_ring(qkv_parts, "x"), "z").reshape(2048, 512)
    qkv_other = swap_cores(qkv_mine)
    q_expand = columns_of(query_expand, 512)
    k_expand = columns_of(key_expand, 256)
    v_expand = columns_of(value_expand, 256)
    low_qkv = (product(normed_g, qkv_shrink) * jnp.tile(select_y, (1, 3))).astype(bf16)
    lin_mine, lin_other = product(normed_g, qkv_mine), product(normed_g, qkv_other)
    query_lin = jnp.where(c == 0, lin_mine, lin_other) + product(low_qkv[:, :rank], q_expand)
    kv_lin = jnp.where(c == 0, lin_other, lin_mine)
    key_lin = kv_lin[:, :256] + product(low_qkv[:, rank : 2 * rank], k_expand)
    value_lin = kv_lin[:, 256:] + product(low_qkv[:, 2 * rank :], v_expand)
    query_heads = query_lin.reshape(GROUP, 2, HEAD_SIZE)
    key_heads = key_lin.reshape(GROUP, 1, HEAD_SIZE)
    query = (query_heads * cos_table + rotate(query_heads) * sin_table).astype(bf16)
    query = (query * bf16(factor)).reshape(GROUP, 512)
    key = (key_heads * cos_table + rotate(key_heads) * sin_table).astype(bf16).reshape(GROUP, 256)

    lines = gather_row(jnp.concatenate([key, value_lin.astype(bf16)], axis=1))
    gate_up = gate_up + zero_of(lines[0]).astype(bf16)
    gate_up = lax.all_to_all(gate_up, ("x", "c"), split_axis=0, concat_axis=0, tiled=True).reshape(128, 2048)
    waited = zero_of(lines[1]) + zero_of(lines[2]) + zero_of(lines[3]) + zero_of(lines[4]) + zero_of(wo)
    ffn = jnp.concatenate([gate_up, w_down], axis=0) + waited.astype(bf16)
    ffn = lax.all_gather(ffn, OVER_X, axis=0, tiled=False).reshape(16, 2, 192, 2048)
    attended = (query, group_pos[:, None], group_start[:, None], tiles_pos.reshape(16, 1, GROUP)) + lines
    mixed_f, lse = attend(active, *attended)
    mixed = mixed_f.astype(bf16)

    heads = jnp.zeros((4, 128, 512), bf16)
    heads = lax.dynamic_update_index_in_dim(heads, mixed[:128], y, 0)
    for step in (1, 2, 3):
        got = shift(mixed[step * 128 : (step + 1) * 128], "y", step)
        heads = lax.dynamic_update_index_in_dim(heads, got, (y - step) % 4, 0)
    mixed_tok = jnp.transpose(heads, (1, 0, 2)).reshape(128, 2048)
    low_out = (product(mixed_tok, out_shrink) * select).astype(bf16)
    middle = inputs + product(mixed_tok, wo) + product(low_out, out_expand)
    scale_mid = row_scale(middle)
    normed_mid = (middle * scale_mid * gain_ffn).astype(bf16)
    normed_mid_g = gather_near(normed_mid, "x")

    select_two = jnp.tile(select_x, (1, 2))
    low_gu = (product(normed_mid_g, gateup_shrink) * select_two).astype(bf16)
    grad_low_down = (times_transposed(cot_g, down_expand) * select_x).astype(bf16)
    place = jnp.arange(GROUP, dtype=jnp.int32)
    turned = (place // 32 % 4) * 128 + (place // 128) * 32 + place % 32
    perm = (turned[:, None] == place[None, :]).astype(bf16)
    wide, narrow = jnp.arange(2 * CHUNK, dtype=jnp.int32), jnp.arange(CHUNK, dtype=jnp.int32)
    picks = jnp.stack(
        [(wide[:, None] == (narrow // 64 * 128 + core * 64 + narrow % 64)[None, :]).astype(bf16) for core in (0, 1)]
    )
    result, back_part, unit_grads = feed_forward(
        x.reshape(1).astype(jnp.int32),
        normed_mid_g,
        cot_g,
        low_gu,
        grad_low_down,
        ffn,
        (gate_expand, up_expand, down_shrink),
        perm,
        picks,
    )

    def sum_tokens(part, ring):
        sent = part.astype(bf16)
        return sum_near([sent[i * 128 : (i + 1) * 128] for i in range(4)], ring)

    back = sum_tokens(back_part, "x")
    back, back_low, low_down_sum = back[:, :2048], back[:, 2048 : 2048 + 2 * rank], back[:, 2048 + 2 * rank :]

    low_down = (low_down_sum * select).astype(bf16)
    grad_low_gu = (back_low * jnp.tile(select, (1, 2))).astype(bf16)
    grad_normed_mid = back + times_transposed(grad_low_gu, gateup_shrink)
    cot_f = cot.astype(f32)
    grad_middle = cot_f + norm_back(middle, scale_mid, gain_ffn, grad_normed_mid)
    grad_attn_out = grad_middle.astype(bf16)
    grad_low_out = (times_transposed(grad_attn_out, out_expand) * select).astype(bf16)
    grad_mixed = (times_transposed(grad_attn_out, wo) + times_transposed(grad_low_out, out_shrink)).astype(bf16)

    def slices_near(array):
        def columns_at(step):
            return lax.dynamic_slice_in_dim(array, ((y + step) % 4) * 512, 512, 1)

        return jnp.concatenate([columns_at(0)] + [shift(columns_at(4 - step), "y", -step) for step in (1, 2, 3)])

    dout = slices_near(grad_mixed)
    dq, *terms = attend_back(active, *attended, mixed_f, lse, dout)
    unit_sum = lax.psum_scatter(
        unit_grads.reshape(32, 192, rank), OVER_X, scatter_dimension=0, tiled=False
    )
    aheads = []

    def beside(start):
        aheads.append(sum_tokens(result + start.astype(bf16), "x"))
        return zero_of(aheads[0]) + zero_of(unit_sum)

    dkv = sum_row(*terms, beside)
    dk, dv = dkv[:, :HEAD_SIZE], dkv[:, HEAD_SIZE:]
    query_back = (dq * factor).astype(bf16).astype(f32).reshape(GROUP, 2, HEAD_SIZE)
    key_back = dk.astype(bf16).astype(f32).reshape(GROUP, 1, HEAD_SIZE)
    grad_value = dv.astype(bf16)
    grad_query = (query_back * cos_table - rotate(query_back * sin_table)).astype(bf16).reshape(GROUP, 512)
    grad_key = (key_back * cos_table - rotate(key_back * sin_table)).astype(bf16).reshape(GROUP, 256)
    grad_kv = jnp.concatenate([grad_key, grad_value], axis=1)

    grad_low_part = jnp.concatenate(
        [
            times_transposed(grad_query, q_expand),
            times_transposed(grad_key, k_expand),
            times_transposed(grad_value, v_expand),
        ],
        axis=1,
    )
    grad_low_qkv = (sum_tokens(grad_low_part, "y") * jnp.tile(select, (1, 3))).astype(bf16)
    for_mine = jnp.where(c == 0, grad_query, grad_kv)
    for_other = jnp.where(c == 0, grad_kv, grad_query)
    grad_normed_part = times_transposed(for_mine, qkv_mine) + times_transposed(for_other, qkv_other)
    grad_normed = sum_tokens(grad_normed_part, "y") + times_transposed(grad_low_qkv, qkv_shrink)
    output = (middle + aheads[0] + product(low_down, down_expand)).astype(bf16)
    grad_input = (grad_middle + norm_back(inputs, scale_in, gain_attn, grad_normed)).astype(bf16)

    def features(array, at):
        return lax.dynamic_slice_in_dim(array, at * 512, 512, 1)

    def by_cores(arrays):
        parts = jnp.concatenate([array.reshape(16, 2, array.shape[0] // 32, rank) for array in arrays], axis=2)
        kept = lax.dynamic_index_in_dim(parts, c, 1, keepdims=False)
        return kept, lax.dynamic_index_in_dim(parts, 1 - c, 1, keepdims=False)

    def sum_plane(kept, given, ring):
        terms = kept + swap_cores(given.astype(bf16)).astype(f32)
        return sum_ring(sum_ring(terms.reshape(4, 4, -1, rank), "z"), ring)

    row_terms = [
        inner_rows(mixed_tok, grad_low_out),
        inner_rows(grad_attn_out, low_out),
        inner_rows(cot, low_down),
        inner_rows(normed_mid, grad_low_gu[:, :rank]),
        inner_rows(normed_mid, grad_low_gu[:, rank:]),
    ]
    row_terms = jnp.concatenate([array.reshape(128, 16, rank) for array in row_terms], axis=1)
    row_terms = jnp.swapaxes(row_terms.reshape(4, 4, 8, 80, rank), 1, 2).reshape(32, 320, rank)
    row_sum = lax.psum_scatter(row_terms, OVER_X, scatter_dimension=0, tiled=False)
    row_sum = sum_ring((row_sum + zero_of(dkv)).reshape(4, 80, rank), "x")
    early_sum = jnp.concatenate([unit_sum, row_sum], axis=0).astype(bf16)
    early_all = lax.all_gather(early_sum, ALL, axis=0, tiled=False)

    grad_qkv = inner_rows(features(normed_g, y), gather_near(grad_low_qkv, "y"))
    kept, other = by_cores(
        [
            inner_rows(grad_query, low_qkv[:, :rank]),
            inner_rows(grad_key, low_qkv[:, rank : 2 * rank]),
            inner_rows(grad_value, low_qkv[:, 2 * rank :]),
            grad_qkv[:, :rank],
            grad_qkv[:, rank : 2 * rank],
            grad_qkv[:, 2 * rank :],
        ]
    )
    g_gate, g_up, g_down_shrink, g_out_shrink, g_out_expand, g_down_expand, g_gateup = unpack_early(early_all)
    late_sum = sum_plane(kept, other, "x").astype(bf16)
    late_all = gather_ring(gather_ring(late_sum, "x"), "z") + zero_of(g_gateup).astype(bf16)
    late_all = gather_ring(late_all, "y")
    late_all = late_all.reshape(4, 16, -1, rank)
    late_other = swap_cores(late_all)
    g_q, g_k, g_v, g_qkv = unpack_late(c.reshape(1).astype(jnp.int32), late_all, late_other)
    return (
        from_rows(output),
        from_rows(grad_input),
        g_qkv,
        g_q,
        g_k,
        g_v,
        g_out_shrink,
        g_out_expand,
        g_gateup,
        g_gate,
        g_up,
        g_down_shrink,
        g_down_expand,
    )


def solution(mesh):
    fine = Mesh(mesh.devices.reshape(2, 2, 4, 4, 2), ALL)
    split = P(ALL, None)
    placed = (split, P(), P()) + (split,) * 7 + (P(),) * 14 + (split,)
    return jax.shard_map(
        local,
        mesh=fine,
        in_specs=placed,
        out_specs=(split, split) + (P(),) * 11,
        check_vma=False,
    )
```

```python
from functools import partial

import jax
import jax.numpy as jnp
from jax import lax
from jax.experimental import pallas as pl
from jax.experimental.pallas import tpu as pltpu
from jax.sharding import Mesh, PartitionSpec as P

HEAD_SIZE = 256
RANK = 16
HALF = 64
GROUP = 512

ALL = ("zh", "zl", "x", "y", "c")

norm_eps = 1e-06
rope_theta = 1000042.0
neg_big = -1e30
far = 1 << 30

f32 = jnp.float32
bf16 = jnp.bfloat16


def product(left, right):
    return jnp.dot(left, right, preferred_element_type=f32)


def times_transposed(left, right):
    return lax.dot_general(left, right, (((1,), (1,)), ((), ())), preferred_element_type=f32)


def inner_rows(left, right):
    return lax.dot_general(left, right, (((0,), (0,)), ((), ())), preferred_element_type=f32)


def row_scale(value_matrix):
    return lax.rsqrt(jnp.mean(value_matrix * value_matrix, axis=-1, keepdims=True) + norm_eps)


def norm_back(value_matrix, scale, gain, grad):
    scaled = gain * grad
    return scale * scaled - value_matrix * (scale * scale * scale) * jnp.mean(
        value_matrix * scaled, axis=-1, keepdims=True
    )


def rotate(value_matrix):
    middle = value_matrix.shape[-1] // 2
    return jnp.concatenate([-value_matrix[..., middle:], value_matrix[..., :middle]], axis=-1)


def rope_tables(positions, width):
    middle = width // 2
    inverse = rope_theta ** (-(jnp.arange(middle, dtype=f32) * 2.0) / width)
    angles = positions.astype(f32)[:, None] * inverse[None, :]
    cos_half, sin_half = jnp.cos(angles), jnp.sin(angles)
    cos_table = jnp.concatenate([cos_half, cos_half], axis=-1)[:, None, :]
    sin_table = jnp.concatenate([sin_half, sin_half], axis=-1)[:, None, :]
    return (cos_table, sin_table)


OVER_X = ("zh", "zl", "y", "c")
RING = {"x": ("x",), "y": ("y",), "z": ("zh", "zl")}


def swap_cores(value):
    return lax.ppermute(value, "c", [(0, 1), (1, 0)])


def shift(value, ring, step):
    return lax.ppermute(value, RING[ring], [(i, (i + step) % 4) for i in range(4)])


def place_in(ring):
    return lax.axis_index(RING[ring])


def gather_near(value, ring, axis=0):
    return jnp.concatenate([value] + [shift(value, ring, -step) for step in (1, 2, 3)], axis=axis)


def gather_ring(value, ring, base=0.0):
    at = place_in(ring)
    whole_ring = jnp.full((4,) + value.shape, base, value.dtype)
    whole_ring = lax.dynamic_update_index_in_dim(whole_ring, value, at, 0)
    for step in (1, 2, 3):
        got = shift(value, ring, -step)
        whole_ring = lax.dynamic_update_index_in_dim(whole_ring, got, (at + step) % 4, 0)
    return whole_ring


def sum_near(blocks, ring):
    got = [shift(blocks[step], ring, step) for step in (2, 1, 3)]
    total = blocks[0].astype(f32)
    for term in got:
        total = total + term.astype(f32)
    return total


def sum_ring(terms, ring):
    at = place_in(ring)
    got = [
        shift(lax.dynamic_index_in_dim(terms, (at + step) % 4, 0, keepdims=False).astype(bf16), ring, step)
        for step in (1, 2, 3)
    ]
    total = lax.dynamic_index_in_dim(terms, at, 0, keepdims=False)
    for term in got:
        total = total + term.astype(f32)
    return total


CORNER = ("zh", "zl", "c")
PARTNER = [(4 * zh + 2 * zl + c, 4 * zh + 2 * (1 - zl) + c) for zh in (0, 1) for zl in (0, 1) for c in (0, 1)]
LATER = [[(2 * zl + 1, 4 + 2 * (zl ^ flip)) for zl in (0, 1)] for flip in (0, 1)]
EARLIER = [[(to, came) for came, to in pairs] for pairs in LATER]
def after(value, *others):
    return lax.optimization_barrier((value,) + others)[0]


def zero_of(value):
    return value[(slice(0, 1),) * value.ndim].reshape(()).astype(f32) * 0.0


def gather_row(key_value):
    line = jnp.stack([key_value] + [shift(key_value, "x", -step) for step in (1, 2, 3)])
    ahead = [lax.ppermute(line, CORNER, pairs) for pairs in LATER]
    partner = lax.ppermute(line, CORNER, PARTNER)
    beside = [lax.ppermute(value, "c", [(0, 1)]) for value in (line, partner)]
    return line, partner, ahead[0], ahead[1], beside[0], beside[1]


def sum_row(own, own_partner, prev, prev_partner, beside):
    got = [lax.ppermute(value, "c", [(1, 0)]) for value in (prev_partner, prev)]
    terms = [lax.ppermute(value, CORNER, pairs) for value, pairs in zip((prev, prev_partner), EARLIER)]
    sent = (own_partner.astype(f32) + got[0].astype(f32)).astype(bf16)
    terms = [got[1], lax.ppermute(sent, CORNER, PARTNER)] + terms
    start = zero_of(sent)
    line = own.astype(f32)
    for term in terms:
        line = line + term.astype(f32)
    sent = (line + beside(start)).astype(bf16)
    total = line[0]
    for step in (2, 1, 3):
        total = total + shift(sent[step], "x", step).astype(f32)
    return total


def allowed_mask(own_pos, own_start, key_pos):
    return (key_pos <= own_pos) & (key_pos >= own_start)


def load_tile(tile, tile_buf, own_ref, partner_ref, ahead_ref, ahead_partner_ref, beside_ref, beside_partner_ref):
    @pl.when(tile == 0)
    def _():
        tile_buf[...] = ahead_ref[0] + beside_ref[0]

    @pl.when(tile == 1)
    def _():
        tile_buf[...] = ahead_partner_ref[0] + beside_partner_ref[0]

    @pl.when(tile == 2)
    def _():
        tile_buf[...] = own_ref[0]

    @pl.when(tile == 3)
    def _():
        tile_buf[...] = partner_ref[0]


def attend_kernel(active, q_ref, pos_ref, start_ref, kpos_ref, *refs):
    mixed_ref, lse_ref, tile_buf, top, total, accum = refs[6:]
    step = pl.program_id(0)

    @pl.when(step == 0)
    def _():
        top[...] = jnp.full(top.shape, neg_big, f32)
        total[...] = jnp.zeros(total.shape, f32)
        accum[...] = jnp.zeros(accum.shape, f32)

    @pl.when(active[step] != 0)
    def _():
        load_tile(step // 4, tile_buf, *refs[:6])
        allowed = allowed_mask(pos_ref[...], start_ref[...], kpos_ref[0])
        both = [
            times_transposed(q_ref[:, head * HEAD_SIZE : (head + 1) * HEAD_SIZE], tile_buf[:, :HEAD_SIZE])
            for head in range(2)
        ]
        for head in range(2):
            scores = jnp.where(allowed, both[head], neg_big)
            top_old = top[head]
            top_new = jnp.maximum(top_old, jnp.max(scores, axis=-1, keepdims=True))
            weights_p = jnp.exp(scores - top_new)
            damping = jnp.exp(top_old - top_new)
            total[head] = total[head] * damping + jnp.sum(weights_p, axis=-1, keepdims=True)
            accum[head] = accum[head] * damping + product(weights_p.astype(bf16), tile_buf[:, HEAD_SIZE:])
            top[head] = top_new

    @pl.when(step == 15)
    def _():
        for head in range(2):
            mixed_ref[:, head * HEAD_SIZE : (head + 1) * HEAD_SIZE] = accum[head] / total[head]
            lse_ref[head] = top[head] + jnp.log(total[head])


def attend_back_kernel(active, q_ref, pos_ref, start_ref, kpos_ref, *refs):
    mixed_ref, lse_ref, dout_ref, dq_ref, down_ref, dpartner_ref, dprev_ref, dprev_partner_ref = refs[6:14]
    tile_buf, delta, sums = refs[14:]
    step = pl.program_id(0)
    tile = step // 4

    @pl.when(step == 0)
    def _():
        dq_ref[...] = jnp.zeros(dq_ref.shape, f32)
        for head in range(2):
            cols = slice(head * HEAD_SIZE, (head + 1) * HEAD_SIZE)
            delta[head] = jnp.sum(dout_ref[:, cols].astype(f32) * mixed_ref[:, cols], axis=-1, keepdims=True)

    @pl.when(active[step] == 0)
    def _():
        sums[...] = jnp.zeros(sums.shape, bf16)

    @pl.when(active[step] != 0)
    def _():
        load_tile(tile, tile_buf, *refs[:6])
        allowed = allowed_mask(pos_ref[...], start_ref[...], kpos_ref[0])
        dk = jnp.zeros((GROUP, HEAD_SIZE), f32)
        dv = jnp.zeros((GROUP, HEAD_SIZE), f32)
        for head in range(2):
            cols = slice(head * HEAD_SIZE, (head + 1) * HEAD_SIZE)
            query, dout = q_ref[:, cols], dout_ref[:, cols]
            scores = times_transposed(query, tile_buf[:, :HEAD_SIZE])
            weights_p = jnp.where(allowed, jnp.exp(scores - lse_ref[head]), 0.0)
            dprobs = times_transposed(dout, tile_buf[:, HEAD_SIZE:])
            dscores = (weights_p * (dprobs - delta[head])).astype(bf16)
            dq_ref[:, cols] += product(dscores, tile_buf[:, :HEAD_SIZE])
            dk = dk + inner_rows(dscores, query)
            dv = dv + inner_rows(weights_p.astype(bf16), dout)
        sums[:, :HEAD_SIZE] = dk.astype(bf16)
        sums[:, HEAD_SIZE:] = dv.astype(bf16)

    for at, out_ref in enumerate((dprev_ref, dprev_partner_ref, down_ref, dpartner_ref)):

        @pl.when(tile == at)
        def _():
            out_ref[0] = sums[...]


def whole(shape):
    return pl.BlockSpec(shape, lambda *grid_and_refs: (0,) * len(shape))


def line_spec(tile):
    return pl.BlockSpec((1, GROUP, GROUP), lambda i, active: (jnp.clip(i - 4 * tile, 0, 3), 0, 0))


def active_spec(tile, table):
    return pl.BlockSpec(
        (1, GROUP, GROUP), lambda i, active: (active[16 * table + 4 * tile + jnp.clip(i - 4 * tile, 0, 3)], 0, 0)
    )


def step_tables(active, c):
    marks = active.reshape(4, 4)
    at = jnp.arange(4, dtype=jnp.int32)
    seen = jnp.where((marks[:, None, :] != 0) & (at[None, None, :] <= at[None, :, None]), at[None, None, :], -1)
    last = jnp.max(seen, axis=2)
    first = jnp.min(jnp.where(marks != 0, at[None, :], 3), axis=1, keepdims=True)
    blocks = jnp.where(last >= 0, last, first).reshape(16).astype(jnp.int32)
    return jnp.concatenate([active, blocks, jnp.where(c == 0, blocks, 0), jnp.where(c == 0, 0, blocks)])


def common_specs():
    return [
        whole((GROUP, GROUP)),
        whole((GROUP, 1)),
        whole((GROUP, 1)),
        pl.BlockSpec((1, 1, GROUP), lambda i, active: (i, 0, 0)),
    ] + [active_spec(tile, table) for tile, table in ((2, 1), (3, 1), (0, 2), (1, 2), (0, 3), (1, 3))]


def attend(active, *operands):
    return pl.pallas_call(
        attend_kernel,
        grid_spec=pltpu.PrefetchScalarGridSpec(
            num_scalar_prefetch=1,
            grid=(16,),
            in_specs=common_specs(),
            out_specs=[whole((GROUP, GROUP)), whole((2, GROUP, 1))],
            scratch_shapes=[
                pltpu.VMEM((GROUP, GROUP), bf16),
                pltpu.VMEM((2, GROUP, 1), f32),
                pltpu.VMEM((2, GROUP, 1), f32),
                pltpu.VMEM((2, GROUP, HEAD_SIZE), f32),
            ],
        ),
        out_shape=[
            jax.ShapeDtypeStruct((GROUP, GROUP), f32),
            jax.ShapeDtypeStruct((2, GROUP, 1), f32),
        ],
        compiler_params=pltpu.CompilerParams(vmem_limit_bytes=48 << 20),
        cost_estimate=pl.CostEstimate(flops=6 << 30, bytes_accessed=10 << 20, transcendentals=8 << 20),
        name="attend",
    )(active, *operands)


def attend_back(active, *operands):
    return pl.pallas_call(
        attend_back_kernel,
        grid_spec=pltpu.PrefetchScalarGridSpec(
            num_scalar_prefetch=1,
            grid=(16,),
            in_specs=common_specs() + [whole((GROUP, GROUP)), whole((2, GROUP, 1)), whole((GROUP, GROUP))],
            out_specs=[whole((GROUP, GROUP))] + [line_spec(tile) for tile in (2, 3, 0, 1)],
            scratch_shapes=[
                pltpu.VMEM((GROUP, GROUP), bf16),
                pltpu.VMEM((2, GROUP, 1), f32),
                pltpu.VMEM((GROUP, GROUP), bf16),
            ],
        ),
        out_shape=[jax.ShapeDtypeStruct((GROUP, GROUP), f32)]
        + [jax.ShapeDtypeStruct((4, GROUP, GROUP), bf16)] * 4,
        compiler_params=pltpu.CompilerParams(vmem_limit_bytes=48 << 20),
        cost_estimate=pl.CostEstimate(flops=12 << 30, bytes_accessed=20 << 20, transcendentals=8 << 20),
        name="attend_back",
    )(active, *operands)


UNITS = 1024
CHUNK = 256


def ffn_kernel(
    at,
    nm_ref,
    cot_ref,
    lgu_ref,
    gld_ref,
    wg_ref,
    wu_ref,
    wd_ref,
    ge_ref,
    ue_ref,
    ds_ref,
    perm_ref,
    pick_ref,
    result_ref,
    back_ref,
    units_ref,
    nmp,
    result,
    grad,
    low,
):
    step = pl.program_id(0)
    rank = ds_ref.shape[1]

    @pl.when(step == 0)
    def _():
        for zone in range(4):
            cols = slice(zone * GROUP, (zone + 1) * GROUP)
            nmp[:, cols] = product(nm_ref[:, cols], perm_ref[...]).astype(bf16)
        result[...] = jnp.zeros(result.shape, f32)
        grad[...] = jnp.zeros(grad.shape, f32)
        low[...] = jnp.zeros(low.shape, f32)

    wg, wu = wg_ref[...].reshape(2048, CHUNK), wu_ref[...].reshape(2048, CHUNK)
    wd = wd_ref[...].reshape(CHUNK, 2048)
    ge, ue = product(ge_ref[...], pick_ref[0]).astype(bf16), product(ue_ref[...], pick_ref[0]).astype(bf16)
    ds = inner_rows(pick_ref[0], ds_ref[...]).astype(bf16)
    low_gate, low_up = lgu_ref[:, :rank], lgu_ref[:, rank:]
    gate_pre = product(nmp[...], wg) + product(low_gate, ge)
    up_pre = product(nmp[...], wu) + product(low_up, ue)
    sigmoid_g = jax.nn.sigmoid(gate_pre)
    silu_gate = gate_pre * sigmoid_g
    active_units = (silu_gate * up_pre).astype(bf16)
    grad_active = times_transposed(cot_ref[...], wd) + times_transposed(gld_ref[...], ds)
    grad_gate = (grad_active * up_pre * sigmoid_g * (1.0 + gate_pre * (1.0 - sigmoid_g))).astype(bf16)
    grad_up = (grad_active * silu_gate).astype(bf16)
    result[...] += product(active_units, wd)
    grad[...] += times_transposed(grad_gate, wg) + times_transposed(grad_up, wu)
    low[:, :rank] += times_transposed(grad_gate, ge)
    low[:, rank : 2 * rank] += times_transposed(grad_up, ue)
    low[:, 2 * rank :] += product(active_units, ds)
    units_ref[0, :, 0, :64] = inner_rows(grad_gate, low_gate).reshape(4, 64, rank)
    units_ref[0, :, 0, 64:128] = inner_rows(grad_up, low_up).reshape(4, 64, rank)
    units_ref[0, :, 0, 128:] = inner_rows(active_units, gld_ref[...]).reshape(4, 64, rank)

    @pl.when(step == 2 * UNITS // CHUNK - 1)
    def _():
        result_ref[...] = result[...].astype(bf16)
        for zone in range(4):
            cols = slice(zone * GROUP, (zone + 1) * GROUP)
            back_ref[:, cols] = product(grad[:, cols].astype(bf16), perm_ref[...]).astype(bf16)
        back_ref[:, 2048:] = low[...].astype(bf16)


def feed_forward(at, normed_mid, cot, low_gu, grad_low_down, weights, expands, perm, picks):
    rank = low_gu.shape[1] // 2
    steps = UNITS // CHUNK
    unit_spec = pl.BlockSpec((1, 4, 1, 192, rank), lambda i, at: (i % steps, 0, i // steps, 0, 0))
    return pl.pallas_call(
        ffn_kernel,
        grid_spec=pltpu.PrefetchScalarGridSpec(
            num_scalar_prefetch=1,
            grid=(2 * steps,),
            in_specs=[
                whole((GROUP, 2048)),
                whole((GROUP, 2048)),
                whole((GROUP, 2 * rank)),
                whole((GROUP, rank)),
                pl.BlockSpec((16, 1, 128, CHUNK), lambda i, at: (0, i // steps, 0, i % steps)),
                pl.BlockSpec((16, 1, 128, CHUNK), lambda i, at: (0, i // steps, 0, steps + i % steps)),
                pl.BlockSpec((4, 1, 64, 2048), lambda i, at: (i % steps, i // steps, 2, 0)),
                pl.BlockSpec((rank, 2 * CHUNK), lambda i, at: (0, 4 * (i % steps) + at[0])),
                pl.BlockSpec((rank, 2 * CHUNK), lambda i, at: (0, 4 * (i % steps) + at[0])),
                pl.BlockSpec((2 * CHUNK, rank), lambda i, at: (4 * (i % steps) + at[0], 0)),
                whole((GROUP, GROUP)),
                pl.BlockSpec((1, 2 * CHUNK, CHUNK), lambda i, at: (i // steps, 0, 0)),
            ],
            out_specs=[whole((GROUP, 2048)), whole((GROUP, 2048 + 3 * rank)), unit_spec],
            scratch_shapes=[
                pltpu.VMEM((GROUP, 2048), bf16),
                pltpu.VMEM((GROUP, 2048), f32),
                pltpu.VMEM((GROUP, 2048), f32),
                pltpu.VMEM((GROUP, 3 * rank), f32),
            ],
        ),
        out_shape=[
            jax.ShapeDtypeStruct((GROUP, 2048), bf16),
            jax.ShapeDtypeStruct((GROUP, 2048 + 3 * rank), bf16),
            jax.ShapeDtypeStruct((4, 4, 2, 192, rank), f32),
        ],
        compiler_params=pltpu.CompilerParams(vmem_limit_bytes=60 << 20),
        cost_estimate=pl.CostEstimate(flops=28 << 30, bytes_accessed=40 << 20, transcendentals=2 << 20),
        name="feed_forward",
    )(at, normed_mid, cot, low_gu, grad_low_down, weights, weights, weights, *expands, perm, picks)


EARLY = (64, 64, 64, 16, 16, 16, 16, 16)
LATE = (16, 8, 8, 16, 16, 16)


def cut(array, sizes):
    found, at = [], 0
    for size in sizes:
        found.append(array[..., at : at + size, :])
        at += size
    return found


def turned(array):
    at = lax.broadcasted_iota(jnp.int32, (128, 128), 0), lax.broadcasted_iota(jnp.int32, (128, 128), 1)
    return times_transposed((at[0] == at[1]).astype(f32).astype(bf16), array)


def early_kernel(all_ref, gate_ref, up_ref, down_ref, oshrink_ref, oexpand_ref, dexpand_ref, gateup_ref):
    pieces = [piece.reshape(-1, 128) for piece in cut(all_ref[...], EARLY)]
    gate_ref[...] = turned(pieces[0])
    up_ref[...] = turned(pieces[1])
    down_ref[...] = pieces[2].astype(f32)
    oshrink_ref[...] = pieces[3].astype(f32)
    oexpand_ref[...] = turned(pieces[4])
    dexpand_ref[...] = turned(pieces[5])
    gateup_ref[:, :128] = pieces[6].astype(f32)
    gateup_ref[:, 128:] = pieces[7].astype(f32)


def unpack_early(everyone):
    return pl.pallas_call(
        early_kernel,
        grid=(16,),
        in_specs=[pl.BlockSpec((8, sum(EARLY), 128), lambda i: (i, 0, 0))],
        out_specs=[
            pl.BlockSpec((128, 512), lambda i: (0, i)),
            pl.BlockSpec((128, 512), lambda i: (0, i)),
            pl.BlockSpec((512, 128), lambda i: (i, 0)),
            pl.BlockSpec((128, 128), lambda i: (i, 0)),
            pl.BlockSpec((128, 128), lambda i: (0, i)),
            pl.BlockSpec((128, 128), lambda i: (0, i)),
            pl.BlockSpec((128, 256), lambda i: (i, 0)),
        ],
        out_shape=[
            jax.ShapeDtypeStruct(shape, f32)
            for shape in ((128, 8192), (128, 8192), (8192, 128), (2048, 128), (128, 2048), (128, 2048), (2048, 256))
        ],
        cost_estimate=pl.CostEstimate(flops=1 << 20, bytes_accessed=27 << 20, transcendentals=0),
        name="unpack_early",
    )(everyone)


def late_kernel(core, mine_ref, other_ref, q_ref, k_ref, v_ref, low_ref):
    mine, other = mine_ref[0].astype(f32), other_ref[0].astype(f32)
    first, second = jnp.where(core[0] == 0, mine, other), jnp.where(core[0] == 0, other, mine)
    pieces = [
        jnp.stack(pair, axis=1).reshape(-1, 128) for pair in zip(cut(first, LATE), cut(second, LATE))
    ]
    q_ref[...] = turned(pieces[0].astype(bf16))
    k_ref[...] = turned(pieces[1].astype(bf16))
    v_ref[...] = turned(pieces[2].astype(bf16))
    for at in range(3):
        low_ref[:, at * 128 : (at + 1) * 128] = pieces[3 + at]


def unpack_late(core, mine, other):
    half = pl.BlockSpec((1, 8, sum(LATE), 128), lambda i, core: (i // 2, i % 2, 0, 0))
    return pl.pallas_call(
        late_kernel,
        grid_spec=pltpu.PrefetchScalarGridSpec(
            num_scalar_prefetch=1,
            grid=(8,),
            in_specs=[half, half],
            out_specs=[
                pl.BlockSpec((128, 256), lambda i, core: (0, i)),
                pl.BlockSpec((128, 128), lambda i, core: (0, i)),
                pl.BlockSpec((128, 128), lambda i, core: (0, i)),
                pl.BlockSpec((256, 384), lambda i, core: (i, 0)),
            ],
        ),
        out_shape=[
            jax.ShapeDtypeStruct(shape, f32) for shape in ((128, 2048), (128, 1024), (128, 1024), (2048, 384))
        ],
        cost_estimate=pl.CostEstimate(flops=1 << 20, bytes_accessed=8 << 20, transcendentals=0),
        name="unpack_late",
    )(core, mine, other)


def local(
    hidden_in,
    gain_attn,
    gain_ffn,
    w_query,
    w_key,
    w_value,
    w_out,
    w_gate,
    w_up,
    w_down,
    qkv_shrink,
    query_expand,
    key_expand,
    value_expand,
    out_shrink,
    out_expand,
    gateup_shrink,
    gate_expand,
    up_expand,
    down_shrink,
    down_expand,
    lengths,
    adapter,
    packed_pos,
    cotangent,
):
    zh, zl, x, y, c = (lax.axis_index(name) for name in ALL)
    row = 2 * zh + c
    factor = HEAD_SIZE ** (-0.5)
    rank = out_shrink.shape[1]

    def to_rows(value):
        own = lax.dynamic_slice_in_dim(value, c * HALF, HALF, 0)
        sent = lax.dynamic_slice_in_dim(value, (1 - c) * HALF, HALF, 0)
        return jnp.concatenate([own, swap_cores(sent)], axis=0)

    def from_rows(value):
        own, got = value[:HALF], swap_cores(value[HALF:])
        return jnp.where(c == 0, jnp.concatenate([own, got], 0), jnp.concatenate([got, own], 0))

    hidden = to_rows(hidden_in)
    cot = to_rows(cotangent)

    def roll(array, by, axis):
        return lax.dynamic_slice_in_dim(jnp.concatenate([array, array], axis), by, array.shape[axis], axis)

    spread = packed_pos.reshape(2, 2, 4, 4, 2, 2, HALF)
    spread = jnp.transpose(spread, (0, 5, 1, 2, 3, 4, 6))
    rows_pos = jnp.stack([spread[:, 0], spread[:, 1, :, :, :, ::-1]], axis=1).reshape(4, 2, 4, 4, 128)
    rows_pos = roll(roll(roll(rows_pos, zl, 1), x, 2), y, 3).reshape(4, 8, GROUP)
    own_row = lax.dynamic_index_in_dim(rows_pos, row, 0, keepdims=False)
    prev_row = lax.dynamic_index_in_dim(rows_pos, jnp.maximum(row - 1, 0), 0, keepdims=False)
    prev_row = jnp.where(row == 0, far, prev_row)
    tiles_pos = jnp.concatenate([prev_row, own_row])
    group_pos = own_row[0]
    seq_ends = jnp.cumsum(lengths)
    starts = seq_ends - lengths
    member = (group_pos[:, None] >= starts[None, :]) & (group_pos[:, None] < seq_ends[None, :])
    member_int = member.astype(jnp.int32)
    group_start = jnp.sum(member_int * starts[None, :], axis=1)

    def selected(pos):
        inside = (pos[:, None] >= starts[None, :]) & (pos[:, None] < seq_ends[None, :])
        owner = jnp.sum(inside.astype(jnp.int32) * adapter[None, :], axis=1)
        return (owner[:, None] == (jnp.arange(rank, dtype=jnp.int32) // RANK)[None, :]).astype(f32)

    key_runs, pos_runs, start_runs = tiles_pos.reshape(64, 128), group_pos.reshape(4, 128), group_start.reshape(4, 128)
    key_low, key_high = jnp.min(key_runs, axis=1)[:, None], jnp.max(key_runs, axis=1)[:, None]
    seen = (key_low <= jnp.max(pos_runs, axis=1)[None, :]) & (key_high >= jnp.min(start_runs, axis=1)[None, :])
    active = jnp.max(seen.astype(jnp.int32).reshape(16, 16), axis=1)
    active = step_tables(active, c)
    select_y = selected(group_pos)
    select_x = selected(own_row.reshape(2, 4, 4, 128)[0, :, 0].reshape(GROUP))
    select = select_y[:128]
    cos_table, sin_table = rope_tables(group_pos - group_start, HEAD_SIZE)

    def column_slices(weight):
        parts = weight.reshape(16, 4, 4, 4, 2, 64)
        return jnp.transpose(parts, (2, 4, 0, 1, 3, 5)).reshape(8, 16, 1024)

    heads_q = w_query.reshape(16, 4, 512)
    heads_kv = jnp.concatenate([w_key.reshape(16, 4, 256), w_value.reshape(16, 4, 256)], axis=2)
    qkv_parts = jnp.transpose(jnp.stack([heads_q, heads_kv], axis=2), (1, 2, 0, 3)).reshape(8, 16, 512)
    qkv_parts = lax.all_to_all(qkv_parts, ("y", "c"), split_axis=0, concat_axis=0, tiled=True).reshape(128, 512)
    gate_up = jnp.concatenate([column_slices(w_gate), column_slices(w_up)], axis=2)
    def columns_of(array, width):
        return lax.dynamic_slice_in_dim(array, y * width, width, 1)

    inputs = hidden.astype(f32)
    scale_in = row_scale(inputs)
    normed = (inputs * scale_in * gain_attn).astype(bf16)
    normed, cot, qkv_parts = lax.optimization_barrier((normed, cot, qkv_parts))
    normed_g = gather_near(normed, "y")
    cot_g = gather_near(cot, "x")
    qkv_parts = after(qkv_parts, normed_g, cot_g)
    qkv_mine = gather_ring(gather_ring(qkv_parts, "x"), "z").reshape(2048, 512)
    qkv_other = swap_cores(qkv_mine)
    wo = lax.all_gather(w_out + zero_of(qkv_mine).astype(bf16), ALL, axis=0, tiled=True)
    q_expand = columns_of(query_expand, 512)
    k_expand = columns_of(key_expand, 256)
    v_expand = columns_of(value_expand, 256)
    low_qkv = (product(normed_g, qkv_shrink) * jnp.tile(select_y, (1, 3))).astype(bf16)
    lin_mine, lin_other = product(normed_g, qkv_mine), product(normed_g, qkv_other)
    query_lin = jnp.where(c == 0, lin_mine, lin_other) + product(low_qkv[:, :rank], q_expand)
    kv_lin = jnp.where(c == 0, lin_other, lin_mine)
    key_lin = kv_lin[:, :256] + product(low_qkv[:, rank : 2 * rank], k_expand)
    value_lin = kv_lin[:, 256:] + product(low_qkv[:, 2 * rank :], v_expand)
    query_heads = query_lin.reshape(GROUP, 2, HEAD_SIZE)
    key_heads = key_lin.reshape(GROUP, 1, HEAD_SIZE)
    query = (query_heads * cos_table + rotate(query_heads) * sin_table).astype(bf16)
    query = (query * bf16(factor)).reshape(GROUP, 512)
    key = (key_heads * cos_table + rotate(key_heads) * sin_table).astype(bf16).reshape(GROUP, 256)

    lines = gather_row(jnp.concatenate([key, value_lin.astype(bf16)], axis=1))
    gate_up = gate_up + zero_of(lines[0]).astype(bf16)
    gate_up = lax.all_to_all(gate_up, ("x", "c"), split_axis=0, concat_axis=0, tiled=True).reshape(128, 2048)
    waited = zero_of(lines[1]) + zero_of(lines[2]) + zero_of(lines[3]) + zero_of(lines[4]) + zero_of(wo)
    ffn = jnp.concatenate([gate_up, w_down], axis=0) + waited.astype(bf16)
    ffn = lax.all_gather(ffn, OVER_X, axis=0, tiled=False).reshape(16, 2, 192, 2048)
    attended = (query, group_pos[:, None], group_start[:, None], tiles_pos.reshape(16, 1, GROUP)) + lines
    mixed_f, lse = attend(active, *attended)
    mixed = mixed_f.astype(bf16)

    heads = jnp.zeros((4, 128, 512), bf16)
    heads = lax.dynamic_update_index_in_dim(heads, mixed[:128], y, 0)
    for step in (1, 2, 3):
        got = shift(mixed[step * 128 : (step + 1) * 128], "y", step)
        heads = lax.dynamic_update_index_in_dim(heads, got, (y - step) % 4, 0)
    mixed_tok = jnp.transpose(heads, (1, 0, 2)).reshape(128, 2048)
    low_out = (product(mixed_tok, out_shrink) * select).astype(bf16)
    middle = inputs + product(mixed_tok, wo) + product(low_out, out_expand)
    scale_mid = row_scale(middle)
    normed_mid = (middle * scale_mid * gain_ffn).astype(bf16)
    normed_mid_g = gather_near(normed_mid, "x")

    select_two = jnp.tile(select_x, (1, 2))
    low_gu = (product(normed_mid_g, gateup_shrink) * select_two).astype(bf16)
    grad_low_down = (times_transposed(cot_g, down_expand) * select_x).astype(bf16)
    place = jnp.arange(GROUP, dtype=jnp.int32)
    turned = (place // 32 % 4) * 128 + (place // 128) * 32 + place % 32
    perm = (turned[:, None] == place[None, :]).astype(bf16)
    wide, narrow = jnp.arange(2 * CHUNK, dtype=jnp.int32), jnp.arange(CHUNK, dtype=jnp.int32)
    picks = jnp.stack(
        [(wide[:, None] == (narrow // 64 * 128 + core * 64 + narrow % 64)[None, :]).astype(bf16) for core in (0, 1)]
    )
    result, back_part, unit_grads = feed_forward(
        x.reshape(1).astype(jnp.int32),
        normed_mid_g,
        cot_g,
        low_gu,
        grad_low_down,
        ffn,
        (gate_expand, up_expand, down_shrink),
        perm,
        picks,
    )

    def sum_tokens(part, ring):
        sent = part.astype(bf16)
        return sum_near([sent[i * 128 : (i + 1) * 128] for i in range(4)], ring)

    back = sum_tokens(back_part, "x")
    back, back_low, low_down_sum = back[:, :2048], back[:, 2048 : 2048 + 2 * rank], back[:, 2048 + 2 * rank :]

    low_down = (low_down_sum * select).astype(bf16)
    grad_low_gu = (back_low * jnp.tile(select, (1, 2))).astype(bf16)
    grad_normed_mid = back + times_transposed(grad_low_gu, gateup_shrink)
    cot_f = cot.astype(f32)
    grad_middle = cot_f + norm_back(middle, scale_mid, gain_ffn, grad_normed_mid)
    grad_attn_out = grad_middle.astype(bf16)
    grad_low_out = (times_transposed(grad_attn_out, out_expand) * select).astype(bf16)
    grad_mixed = (times_transposed(grad_attn_out, wo) + times_transposed(grad_low_out, out_shrink)).astype(bf16)

    def slices_near(array):
        def columns_at(step):
            return lax.dynamic_slice_in_dim(array, ((y + step) % 4) * 512, 512, 1)

        return jnp.concatenate([columns_at(0)] + [shift(columns_at(4 - step), "y", -step) for step in (1, 2, 3)])

    dout = slices_near(grad_mixed)
    dq, *terms = attend_back(active, *attended, mixed_f, lse, dout)
    unit_sum = lax.psum_scatter(
        unit_grads.reshape(32, 192, rank), OVER_X, scatter_dimension=0, tiled=False
    )
    aheads = []

    def beside(start):
        aheads.append(sum_tokens(result + start.astype(bf16), "x"))
        return zero_of(aheads[0]) + zero_of(unit_sum)

    dkv = sum_row(*terms, beside)
    dk, dv = dkv[:, :HEAD_SIZE], dkv[:, HEAD_SIZE:]
    query_back = (dq * factor).astype(bf16).astype(f32).reshape(GROUP, 2, HEAD_SIZE)
    key_back = dk.astype(bf16).astype(f32).reshape(GROUP, 1, HEAD_SIZE)
    grad_value = dv.astype(bf16)
    grad_query = (query_back * cos_table - rotate(query_back * sin_table)).astype(bf16).reshape(GROUP, 512)
    grad_key = (key_back * cos_table - rotate(key_back * sin_table)).astype(bf16).reshape(GROUP, 256)
    grad_kv = jnp.concatenate([grad_key, grad_value], axis=1)

    grad_low_part = jnp.concatenate(
        [
            times_transposed(grad_query, q_expand),
            times_transposed(grad_key, k_expand),
            times_transposed(grad_value, v_expand),
        ],
        axis=1,
    )
    grad_low_qkv = (sum_tokens(grad_low_part, "y") * jnp.tile(select, (1, 3))).astype(bf16)
    for_mine = jnp.where(c == 0, grad_query, grad_kv)
    for_other = jnp.where(c == 0, grad_kv, grad_query)
    grad_normed_part = times_transposed(for_mine, qkv_mine) + times_transposed(for_other, qkv_other)
    grad_normed = sum_tokens(grad_normed_part, "y") + times_transposed(grad_low_qkv, qkv_shrink)
    output = (middle + aheads[0] + product(low_down, down_expand)).astype(bf16)
    grad_input = (grad_middle + norm_back(inputs, scale_in, gain_attn, grad_normed)).astype(bf16)

    def features(array, at):
        return lax.dynamic_slice_in_dim(array, at * 512, 512, 1)

    def by_cores(arrays):
        parts = jnp.concatenate([array.reshape(16, 2, array.shape[0] // 32, rank) for array in arrays], axis=2)
        kept = lax.dynamic_index_in_dim(parts, c, 1, keepdims=False)
        return kept, lax.dynamic_index_in_dim(parts, 1 - c, 1, keepdims=False)

    def sum_plane(kept, given, ring):
        terms = kept + swap_cores(given.astype(bf16)).astype(f32)
        return sum_ring(sum_ring(terms.reshape(4, 4, -1, rank), "z"), ring)

    row_terms = [
        inner_rows(mixed_tok, grad_low_out),
        inner_rows(grad_attn_out, low_out),
        inner_rows(cot, low_down),
        inner_rows(normed_mid, grad_low_gu[:, :rank]),
        inner_rows(normed_mid, grad_low_gu[:, rank:]),
    ]
    row_terms = jnp.concatenate([array.reshape(128, 16, rank) for array in row_terms], axis=1)
    row_terms = jnp.swapaxes(row_terms.reshape(4, 4, 8, 80, rank), 1, 2).reshape(32, 320, rank)
    row_sum = lax.psum_scatter(row_terms, OVER_X, scatter_dimension=0, tiled=False)
    row_sum = sum_ring((row_sum + zero_of(dkv)).reshape(4, 80, rank), "x")
    early_sum = jnp.concatenate([unit_sum, row_sum], axis=0).astype(bf16)
    early_all = lax.all_gather(early_sum, ALL, axis=0, tiled=False)

    grad_qkv = inner_rows(features(normed_g, y), gather_near(grad_low_qkv, "y"))
    kept, other = by_cores(
        [
            inner_rows(grad_query, low_qkv[:, :rank]),
            inner_rows(grad_key, low_qkv[:, rank : 2 * rank]),
            inner_rows(grad_value, low_qkv[:, 2 * rank :]),
            grad_qkv[:, :rank],
            grad_qkv[:, rank : 2 * rank],
            grad_qkv[:, 2 * rank :],
        ]
    )
    g_gate, g_up, g_down_shrink, g_out_shrink, g_out_expand, g_down_expand, g_gateup = unpack_early(early_all)
    late_sum = sum_plane(kept, other, "x").astype(bf16)
    late_all = gather_ring(gather_ring(late_sum, "x"), "z")
    late_all = gather_ring(late_all, "y", zero_of(g_gateup).astype(bf16))
    late_all = late_all.reshape(4, 16, -1, rank)
    late_other = swap_cores(late_all)
    g_q, g_k, g_v, g_qkv = unpack_late(c.reshape(1).astype(jnp.int32), late_all, late_other)
    return (
        from_rows(output),
        from_rows(grad_input),
        g_qkv,
        g_q,
        g_k,
        g_v,
        g_out_shrink,
        g_out_expand,
        g_gateup,
        g_gate,
        g_up,
        g_down_shrink,
        g_down_expand,
    )


def solution(mesh):
    fine = Mesh(mesh.devices.reshape(2, 2, 4, 4, 2), ALL)
    split = P(ALL, None)
    placed = (split, P(), P()) + (split,) * 7 + (P(),) * 14 + (split,)
    return jax.shard_map(
        local,
        mesh=fine,
        in_specs=placed,
        out_specs=(split, split) + (P(),) * 11,
        check_vma=False,
    )
```

```python
from functools import partial

import jax
import jax.numpy as jnp
from jax import lax
from jax.experimental import pallas as pl
from jax.experimental.pallas import tpu as pltpu
from jax.sharding import Mesh, PartitionSpec as P

HEAD_SIZE = 256
RANK = 16
HALF = 64
GROUP = 512

ALL = ("zh", "zl", "x", "y", "c")

norm_eps = 1e-06
rope_theta = 1000042.0
neg_big = -1e30
far = 1 << 30

f32 = jnp.float32
bf16 = jnp.bfloat16


def product(left, right):
    return jnp.dot(left, right, preferred_element_type=f32)


def times_transposed(left, right):
    return lax.dot_general(left, right, (((1,), (1,)), ((), ())), preferred_element_type=f32)


def inner_rows(left, right):
    return lax.dot_general(left, right, (((0,), (0,)), ((), ())), preferred_element_type=f32)


def row_scale(value_matrix):
    return lax.rsqrt(jnp.mean(value_matrix * value_matrix, axis=-1, keepdims=True) + norm_eps)


def norm_back(value_matrix, scale, gain, grad):
    scaled = gain * grad
    return scale * scaled - value_matrix * (scale * scale * scale) * jnp.mean(
        value_matrix * scaled, axis=-1, keepdims=True
    )


def rotate(value_matrix):
    middle = value_matrix.shape[-1] // 2
    return jnp.concatenate([-value_matrix[..., middle:], value_matrix[..., :middle]], axis=-1)


def rope_tables(positions, width):
    middle = width // 2
    inverse = rope_theta ** (-(jnp.arange(middle, dtype=f32) * 2.0) / width)
    angles = positions.astype(f32)[:, None] * inverse[None, :]
    cos_half, sin_half = jnp.cos(angles), jnp.sin(angles)
    cos_table = jnp.concatenate([cos_half, cos_half], axis=-1)[:, None, :]
    sin_table = jnp.concatenate([sin_half, sin_half], axis=-1)[:, None, :]
    return (cos_table, sin_table)


OVER_X = ("zh", "zl", "y", "c")
RING = {"x": ("x",), "y": ("y",), "z": ("zh", "zl")}


def swap_cores(value):
    return lax.ppermute(value, "c", [(0, 1), (1, 0)])


def shift(value, ring, step):
    return lax.ppermute(value, RING[ring], [(i, (i + step) % 4) for i in range(4)])


def place_in(ring):
    return lax.axis_index(RING[ring])


def gather_near(value, ring, axis=0):
    return jnp.concatenate([value] + [shift(value, ring, -step) for step in (1, 2, 3)], axis=axis)


def gather_ring(value, ring, base=0.0):
    at = place_in(ring)
    whole_ring = jnp.full((4,) + value.shape, base, value.dtype)
    whole_ring = lax.dynamic_update_index_in_dim(whole_ring, value, at, 0)
    for step in (1, 2, 3):
        got = shift(value, ring, -step)
        whole_ring = lax.dynamic_update_index_in_dim(whole_ring, got, (at + step) % 4, 0)
    return whole_ring


def sum_near(blocks, ring, base=0.0):
    got = [shift(blocks[step], ring, step) for step in (2, 1, 3)]
    total = blocks[0].astype(f32) + base
    for term in got:
        total = total + term.astype(f32)
    return total


def sum_ring(terms, ring):
    at = place_in(ring)
    got = [
        shift(lax.dynamic_index_in_dim(terms, (at + step) % 4, 0, keepdims=False).astype(bf16), ring, step)
        for step in (1, 2, 3)
    ]
    total = lax.dynamic_index_in_dim(terms, at, 0, keepdims=False)
    for term in got:
        total = total + term.astype(f32)
    return total


CORNER = ("zh", "zl", "c")
PARTNER = [(4 * zh + 2 * zl + c, 4 * zh + 2 * (1 - zl) + c) for zh in (0, 1) for zl in (0, 1) for c in (0, 1)]
LATER = [[(2 * zl + 1, 4 + 2 * (zl ^ flip)) for zl in (0, 1)] for flip in (0, 1)]
EARLIER = [[(to, came) for came, to in pairs] for pairs in LATER]
def after(value, *others):
    return lax.optimization_barrier((value,) + others)[0]


def zero_of(value):
    return value[(slice(0, 1),) * value.ndim].reshape(()).astype(f32) * 0.0


def gather_row(key_value):
    line = jnp.stack([key_value] + [shift(key_value, "x", -step) for step in (1, 2, 3)])
    ahead = [lax.ppermute(line, CORNER, pairs) for pairs in LATER]
    partner = lax.ppermute(line, CORNER, PARTNER)
    beside = [lax.ppermute(value, "c", [(0, 1)]) for value in (line, partner)]
    return line, partner, ahead[0], ahead[1], beside[0], beside[1]


def sum_row(own, own_partner, prev, prev_partner, beside):
    got = [lax.ppermute(value, "c", [(1, 0)]) for value in (prev_partner, prev)]
    terms = [lax.ppermute(value, CORNER, pairs) for value, pairs in zip((prev, prev_partner), EARLIER)]
    sent = (own_partner.astype(f32) + got[0].astype(f32)).astype(bf16)
    terms = [got[1], lax.ppermute(sent, CORNER, PARTNER)] + terms
    start = zero_of(sent)
    line = own.astype(f32)
    for term in terms:
        line = line + term.astype(f32)
    sent = (line + beside(start)).astype(bf16)
    total = line[0]
    for step in (2, 1, 3):
        total = total + shift(sent[step], "x", step).astype(f32)
    return total


def allowed_mask(own_pos, own_start, key_pos):
    return (key_pos <= own_pos) & (key_pos >= own_start)


def load_tile(tile, tile_buf, own_ref, partner_ref, ahead_ref, ahead_partner_ref, beside_ref, beside_partner_ref):
    @pl.when(tile == 0)
    def _():
        tile_buf[...] = ahead_ref[0] + beside_ref[0]

    @pl.when(tile == 1)
    def _():
        tile_buf[...] = ahead_partner_ref[0] + beside_partner_ref[0]

    @pl.when(tile == 2)
    def _():
        tile_buf[...] = own_ref[0]

    @pl.when(tile == 3)
    def _():
        tile_buf[...] = partner_ref[0]


def attend_kernel(active, q_ref, pos_ref, start_ref, kpos_ref, *refs):
    mixed_ref, lse_ref, tile_buf, top, total, accum = refs[6:]
    step = pl.program_id(0)

    @pl.when(step == 0)
    def _():
        top[...] = jnp.full(top.shape, neg_big, f32)
        total[...] = jnp.zeros(total.shape, f32)
        accum[...] = jnp.zeros(accum.shape, f32)

    @pl.when(active[step] != 0)
    def _():
        load_tile(step // 4, tile_buf, *refs[:6])
        allowed = allowed_mask(pos_ref[...], start_ref[...], kpos_ref[0])
        both = [
            times_transposed(q_ref[:, head * HEAD_SIZE : (head + 1) * HEAD_SIZE], tile_buf[:, :HEAD_SIZE])
            for head in range(2)
        ]
        for head in range(2):
            scores = jnp.where(allowed, both[head], neg_big)
            top_old = top[head]
            top_new = jnp.maximum(top_old, jnp.max(scores, axis=-1, keepdims=True))
            weights_p = jnp.exp(scores - top_new)
            damping = jnp.exp(top_old - top_new)
            total[head] = total[head] * damping + jnp.sum(weights_p, axis=-1, keepdims=True)
            accum[head] = accum[head] * damping + product(weights_p.astype(bf16), tile_buf[:, HEAD_SIZE:])
            top[head] = top_new

    @pl.when(step == 15)
    def _():
        for head in range(2):
            mixed_ref[:, head * HEAD_SIZE : (head + 1) * HEAD_SIZE] = accum[head] / total[head]
            lse_ref[head] = top[head] + jnp.log(total[head])


def attend_back_kernel(active, q_ref, pos_ref, start_ref, kpos_ref, *refs):
    mixed_ref, lse_ref, dout_ref, dq_ref, down_ref, dpartner_ref, dprev_ref, dprev_partner_ref = refs[6:14]
    tile_buf, delta, sums = refs[14:]
    step = pl.program_id(0)
    tile = step // 4

    @pl.when(step == 0)
    def _():
        dq_ref[...] = jnp.zeros(dq_ref.shape, f32)
        for head in range(2):
            cols = slice(head * HEAD_SIZE, (head + 1) * HEAD_SIZE)
            delta[head] = jnp.sum(dout_ref[:, cols].astype(f32) * mixed_ref[:, cols], axis=-1, keepdims=True)

    @pl.when(active[step] == 0)
    def _():
        sums[...] = jnp.zeros(sums.shape, bf16)

    @pl.when(active[step] != 0)
    def _():
        load_tile(tile, tile_buf, *refs[:6])
        allowed = allowed_mask(pos_ref[...], start_ref[...], kpos_ref[0])
        dk = jnp.zeros((GROUP, HEAD_SIZE), f32)
        dv = jnp.zeros((GROUP, HEAD_SIZE), f32)
        for head in range(2):
            cols = slice(head * HEAD_SIZE, (head + 1) * HEAD_SIZE)
            query, dout = q_ref[:, cols], dout_ref[:, cols]
            scores = times_transposed(query, tile_buf[:, :HEAD_SIZE])
            weights_p = jnp.where(allowed, jnp.exp(scores - lse_ref[head]), 0.0)
            dprobs = times_transposed(dout, tile_buf[:, HEAD_SIZE:])
            dscores = (weights_p * (dprobs - delta[head])).astype(bf16)
            dq_ref[:, cols] += product(dscores, tile_buf[:, :HEAD_SIZE])
            dk = dk + inner_rows(dscores, query)
            dv = dv + inner_rows(weights_p.astype(bf16), dout)
        sums[:, :HEAD_SIZE] = dk.astype(bf16)
        sums[:, HEAD_SIZE:] = dv.astype(bf16)

    for at, out_ref in enumerate((dprev_ref, dprev_partner_ref, down_ref, dpartner_ref)):

        @pl.when(tile == at)
        def _():
            out_ref[0] = sums[...]


def whole(shape):
    return pl.BlockSpec(shape, lambda *grid_and_refs: (0,) * len(shape))


def line_spec(tile):
    return pl.BlockSpec((1, GROUP, GROUP), lambda i, active: (jnp.clip(i - 4 * tile, 0, 3), 0, 0))


def active_spec(tile, table):
    return pl.BlockSpec(
        (1, GROUP, GROUP), lambda i, active: (active[16 * table + 4 * tile + jnp.clip(i - 4 * tile, 0, 3)], 0, 0)
    )


def step_tables(active, c):
    marks = active.reshape(4, 4)
    at = jnp.arange(4, dtype=jnp.int32)
    seen = jnp.where((marks[:, None, :] != 0) & (at[None, None, :] <= at[None, :, None]), at[None, None, :], -1)
    last = jnp.max(seen, axis=2)
    first = jnp.min(jnp.where(marks != 0, at[None, :], 3), axis=1, keepdims=True)
    blocks = jnp.where(last >= 0, last, first).reshape(16).astype(jnp.int32)
    return jnp.concatenate([active, blocks, jnp.where(c == 0, blocks, 0), jnp.where(c == 0, 0, blocks)])


def common_specs():
    return [
        whole((GROUP, GROUP)),
        whole((GROUP, 1)),
        whole((GROUP, 1)),
        pl.BlockSpec((1, 1, GROUP), lambda i, active: (i, 0, 0)),
    ] + [active_spec(tile, table) for tile, table in ((2, 1), (3, 1), (0, 2), (1, 2), (0, 3), (1, 3))]


def attend(active, *operands):
    return pl.pallas_call(
        attend_kernel,
        grid_spec=pltpu.PrefetchScalarGridSpec(
            num_scalar_prefetch=1,
            grid=(16,),
            in_specs=common_specs(),
            out_specs=[whole((GROUP, GROUP)), whole((2, GROUP, 1))],
            scratch_shapes=[
                pltpu.VMEM((GROUP, GROUP), bf16),
                pltpu.VMEM((2, GROUP, 1), f32),
                pltpu.VMEM((2, GROUP, 1), f32),
                pltpu.VMEM((2, GROUP, HEAD_SIZE), f32),
            ],
        ),
        out_shape=[
            jax.ShapeDtypeStruct((GROUP, GROUP), f32),
            jax.ShapeDtypeStruct((2, GROUP, 1), f32),
        ],
        compiler_params=pltpu.CompilerParams(vmem_limit_bytes=48 << 20),
        cost_estimate=pl.CostEstimate(flops=6 << 30, bytes_accessed=10 << 20, transcendentals=8 << 20),
        name="attend",
    )(active, *operands)


def attend_back(active, *operands):
    return pl.pallas_call(
        attend_back_kernel,
        grid_spec=pltpu.PrefetchScalarGridSpec(
            num_scalar_prefetch=1,
            grid=(16,),
            in_specs=common_specs() + [whole((GROUP, GROUP)), whole((2, GROUP, 1)), whole((GROUP, GROUP))],
            out_specs=[whole((GROUP, GROUP))] + [line_spec(tile) for tile in (2, 3, 0, 1)],
            scratch_shapes=[
                pltpu.VMEM((GROUP, GROUP), bf16),
                pltpu.VMEM((2, GROUP, 1), f32),
                pltpu.VMEM((GROUP, GROUP), bf16),
            ],
        ),
        out_shape=[jax.ShapeDtypeStruct((GROUP, GROUP), f32)]
        + [jax.ShapeDtypeStruct((4, GROUP, GROUP), bf16)] * 4,
        compiler_params=pltpu.CompilerParams(vmem_limit_bytes=48 << 20),
        cost_estimate=pl.CostEstimate(flops=12 << 30, bytes_accessed=20 << 20, transcendentals=8 << 20),
        name="attend_back",
    )(active, *operands)


UNITS = 1024
CHUNK = 256


def ffn_kernel(
    at,
    nm_ref,
    cot_ref,
    lgu_ref,
    gld_ref,
    wg_ref,
    wu_ref,
    wd_ref,
    ge_ref,
    ue_ref,
    ds_ref,
    perm_ref,
    pick_ref,
    result_ref,
    back_ref,
    units_ref,
    nmp,
    result,
    grad,
    low,
):
    step = pl.program_id(0)
    rank = ds_ref.shape[1]

    @pl.when(step == 0)
    def _():
        for zone in range(4):
            cols = slice(zone * GROUP, (zone + 1) * GROUP)
            nmp[:, cols] = product(nm_ref[:, cols], perm_ref[...]).astype(bf16)
        result[...] = jnp.zeros(result.shape, f32)
        grad[...] = jnp.zeros(grad.shape, f32)
        low[...] = jnp.zeros(low.shape, f32)

    wg, wu = wg_ref[...].reshape(2048, CHUNK), wu_ref[...].reshape(2048, CHUNK)
    wd = wd_ref[...].reshape(CHUNK, 2048)
    ge, ue = product(ge_ref[...], pick_ref[0]).astype(bf16), product(ue_ref[...], pick_ref[0]).astype(bf16)
    ds = inner_rows(pick_ref[0], ds_ref[...]).astype(bf16)
    low_gate, low_up = lgu_ref[:, :rank], lgu_ref[:, rank:]
    gate_pre = product(nmp[...], wg) + product(low_gate, ge)
    up_pre = product(nmp[...], wu) + product(low_up, ue)
    sigmoid_g = jax.nn.sigmoid(gate_pre)
    silu_gate = gate_pre * sigmoid_g
    active_units = (silu_gate * up_pre).astype(bf16)
    grad_active = times_transposed(cot_ref[...], wd) + times_transposed(gld_ref[...], ds)
    grad_gate = (grad_active * up_pre * sigmoid_g * (1.0 + gate_pre * (1.0 - sigmoid_g))).astype(bf16)
    grad_up = (grad_active * silu_gate).astype(bf16)
    result[...] += product(active_units, wd)
    grad[...] += times_transposed(grad_gate, wg) + times_transposed(grad_up, wu)
    low[:, :rank] += times_transposed(grad_gate, ge)
    low[:, rank : 2 * rank] += times_transposed(grad_up, ue)
    low[:, 2 * rank :] += product(active_units, ds)
    units_ref[0, :, 0, :64] = inner_rows(grad_gate, low_gate).reshape(4, 64, rank)
    units_ref[0, :, 0, 64:128] = inner_rows(grad_up, low_up).reshape(4, 64, rank)
    units_ref[0, :, 0, 128:] = inner_rows(active_units, gld_ref[...]).reshape(4, 64, rank)

    @pl.when(step == 2 * UNITS // CHUNK - 1)
    def _():
        result_ref[...] = result[...].astype(bf16)
        for zone in range(4):
            cols = slice(zone * GROUP, (zone + 1) * GROUP)
            back_ref[:, cols] = product(grad[:, cols].astype(bf16), perm_ref[...]).astype(bf16)
        back_ref[:, 2048:] = low[...].astype(bf16)


def feed_forward(at, normed_mid, cot, low_gu, grad_low_down, weights, expands, perm, picks):
    rank = low_gu.shape[1] // 2
    steps = UNITS // CHUNK
    unit_spec = pl.BlockSpec((1, 4, 1, 192, rank), lambda i, at: (i % steps, 0, i // steps, 0, 0))
    return pl.pallas_call(
        ffn_kernel,
        grid_spec=pltpu.PrefetchScalarGridSpec(
            num_scalar_prefetch=1,
            grid=(2 * steps,),
            in_specs=[
                whole((GROUP, 2048)),
                whole((GROUP, 2048)),
                whole((GROUP, 2 * rank)),
                whole((GROUP, rank)),
                pl.BlockSpec((16, 1, 128, CHUNK), lambda i, at: (0, i // steps, 0, i % steps)),
                pl.BlockSpec((16, 1, 128, CHUNK), lambda i, at: (0, i // steps, 0, steps + i % steps)),
                pl.BlockSpec((4, 1, 64, 2048), lambda i, at: (i % steps, i // steps, 2, 0)),
                pl.BlockSpec((rank, 2 * CHUNK), lambda i, at: (0, 4 * (i % steps) + at[0])),
                pl.BlockSpec((rank, 2 * CHUNK), lambda i, at: (0, 4 * (i % steps) + at[0])),
                pl.BlockSpec((2 * CHUNK, rank), lambda i, at: (4 * (i % steps) + at[0], 0)),
                whole((GROUP, GROUP)),
                pl.BlockSpec((1, 2 * CHUNK, CHUNK), lambda i, at: (i // steps, 0, 0)),
            ],
            out_specs=[whole((GROUP, 2048)), whole((GROUP, 2048 + 3 * rank)), unit_spec],
            scratch_shapes=[
                pltpu.VMEM((GROUP, 2048), bf16),
                pltpu.VMEM((GROUP, 2048), f32),
                pltpu.VMEM((GROUP, 2048), f32),
                pltpu.VMEM((GROUP, 3 * rank), f32),
            ],
        ),
        out_shape=[
            jax.ShapeDtypeStruct((GROUP, 2048), bf16),
            jax.ShapeDtypeStruct((GROUP, 2048 + 3 * rank), bf16),
            jax.ShapeDtypeStruct((4, 4, 2, 192, rank), f32),
        ],
        compiler_params=pltpu.CompilerParams(vmem_limit_bytes=60 << 20),
        cost_estimate=pl.CostEstimate(flops=28 << 30, bytes_accessed=40 << 20, transcendentals=2 << 20),
        name="feed_forward",
    )(at, normed_mid, cot, low_gu, grad_low_down, weights, weights, weights, *expands, perm, picks)


EARLY = (64, 64, 64, 16, 16, 16, 16, 16)
LATE = (16, 8, 8, 16, 16, 16)


def cut(array, sizes):
    found, at = [], 0
    for size in sizes:
        found.append(array[..., at : at + size, :])
        at += size
    return found


def turned(array):
    at = lax.broadcasted_iota(jnp.int32, (128, 128), 0), lax.broadcasted_iota(jnp.int32, (128, 128), 1)
    return times_transposed((at[0] == at[1]).astype(f32).astype(bf16), array)


def early_kernel(all_ref, gate_ref, up_ref, down_ref, oshrink_ref, oexpand_ref, dexpand_ref, gateup_ref):
    pieces = [piece.reshape(-1, 128) for piece in cut(all_ref[...], EARLY)]
    gate_ref[...] = turned(pieces[0])
    up_ref[...] = turned(pieces[1])
    down_ref[...] = pieces[2].astype(f32)
    oshrink_ref[...] = pieces[3].astype(f32)
    oexpand_ref[...] = turned(pieces[4])
    dexpand_ref[...] = turned(pieces[5])
    gateup_ref[:, :128] = pieces[6].astype(f32)
    gateup_ref[:, 128:] = pieces[7].astype(f32)


def unpack_early(everyone):
    return pl.pallas_call(
        early_kernel,
        grid=(16,),
        in_specs=[pl.BlockSpec((8, sum(EARLY), 128), lambda i: (i, 0, 0))],
        out_specs=[
            pl.BlockSpec((128, 512), lambda i: (0, i)),
            pl.BlockSpec((128, 512), lambda i: (0, i)),
            pl.BlockSpec((512, 128), lambda i: (i, 0)),
            pl.BlockSpec((128, 128), lambda i: (i, 0)),
            pl.BlockSpec((128, 128), lambda i: (0, i)),
            pl.BlockSpec((128, 128), lambda i: (0, i)),
            pl.BlockSpec((128, 256), lambda i: (i, 0)),
        ],
        out_shape=[
            jax.ShapeDtypeStruct(shape, f32)
            for shape in ((128, 8192), (128, 8192), (8192, 128), (2048, 128), (128, 2048), (128, 2048), (2048, 256))
        ],
        cost_estimate=pl.CostEstimate(flops=1 << 20, bytes_accessed=27 << 20, transcendentals=0),
        name="unpack_early",
    )(everyone)


def late_kernel(core, mine_ref, other_ref, q_ref, k_ref, v_ref, low_ref):
    mine, other = mine_ref[0].astype(f32), other_ref[0].astype(f32)
    first, second = jnp.where(core[0] == 0, mine, other), jnp.where(core[0] == 0, other, mine)
    pieces = [
        jnp.stack(pair, axis=1).reshape(-1, 128) for pair in zip(cut(first, LATE), cut(second, LATE))
    ]
    q_ref[...] = turned(pieces[0].astype(bf16))
    k_ref[...] = turned(pieces[1].astype(bf16))
    v_ref[...] = turned(pieces[2].astype(bf16))
    for at in range(3):
        low_ref[:, at * 128 : (at + 1) * 128] = pieces[3 + at]


def unpack_late(core, mine, other):
    half = pl.BlockSpec((1, 8, sum(LATE), 128), lambda i, core: (i // 2, i % 2, 0, 0))
    return pl.pallas_call(
        late_kernel,
        grid_spec=pltpu.PrefetchScalarGridSpec(
            num_scalar_prefetch=1,
            grid=(8,),
            in_specs=[half, half],
            out_specs=[
                pl.BlockSpec((128, 256), lambda i, core: (0, i)),
                pl.BlockSpec((128, 128), lambda i, core: (0, i)),
                pl.BlockSpec((128, 128), lambda i, core: (0, i)),
                pl.BlockSpec((256, 384), lambda i, core: (i, 0)),
            ],
        ),
        out_shape=[
            jax.ShapeDtypeStruct(shape, f32) for shape in ((128, 2048), (128, 1024), (128, 1024), (2048, 384))
        ],
        cost_estimate=pl.CostEstimate(flops=1 << 20, bytes_accessed=8 << 20, transcendentals=0),
        name="unpack_late",
    )(core, mine, other)


def local(
    hidden_in,
    gain_attn,
    gain_ffn,
    w_query,
    w_key,
    w_value,
    w_out,
    w_gate,
    w_up,
    w_down,
    qkv_shrink,
    query_expand,
    key_expand,
    value_expand,
    out_shrink,
    out_expand,
    gateup_shrink,
    gate_expand,
    up_expand,
    down_shrink,
    down_expand,
    lengths,
    adapter,
    packed_pos,
    cotangent,
):
    zh, zl, x, y, c = (lax.axis_index(name) for name in ALL)
    row = 2 * zh + c
    factor = HEAD_SIZE ** (-0.5)
    rank = out_shrink.shape[1]

    def to_rows(value):
        own = lax.dynamic_slice_in_dim(value, c * HALF, HALF, 0)
        sent = lax.dynamic_slice_in_dim(value, (1 - c) * HALF, HALF, 0)
        return jnp.concatenate([own, swap_cores(sent)], axis=0)

    def from_rows(value):
        own, got = value[:HALF], swap_cores(value[HALF:])
        return jnp.where(c == 0, jnp.concatenate([own, got], 0), jnp.concatenate([got, own], 0))

    hidden = to_rows(hidden_in)
    cot = to_rows(cotangent)

    def roll(array, by, axis):
        return lax.dynamic_slice_in_dim(jnp.concatenate([array, array], axis), by, array.shape[axis], axis)

    spread = packed_pos.reshape(2, 2, 4, 4, 2, 2, HALF)
    spread = jnp.transpose(spread, (0, 5, 1, 2, 3, 4, 6))
    rows_pos = jnp.stack([spread[:, 0], spread[:, 1, :, :, :, ::-1]], axis=1).reshape(4, 2, 4, 4, 128)
    rows_pos = roll(roll(roll(rows_pos, zl, 1), x, 2), y, 3).reshape(4, 8, GROUP)
    own_row = lax.dynamic_index_in_dim(rows_pos, row, 0, keepdims=False)
    prev_row = lax.dynamic_index_in_dim(rows_pos, jnp.maximum(row - 1, 0), 0, keepdims=False)
    prev_row = jnp.where(row == 0, far, prev_row)
    tiles_pos = jnp.concatenate([prev_row, own_row])
    group_pos = own_row[0]
    seq_ends = jnp.cumsum(lengths)
    starts = seq_ends - lengths
    member = (group_pos[:, None] >= starts[None, :]) & (group_pos[:, None] < seq_ends[None, :])
    member_int = member.astype(jnp.int32)
    group_start = jnp.sum(member_int * starts[None, :], axis=1)

    def selected(pos):
        inside = (pos[:, None] >= starts[None, :]) & (pos[:, None] < seq_ends[None, :])
        owner = jnp.sum(inside.astype(jnp.int32) * adapter[None, :], axis=1)
        return (owner[:, None] == (jnp.arange(rank, dtype=jnp.int32) // RANK)[None, :]).astype(f32)

    key_runs, pos_runs, start_runs = tiles_pos.reshape(64, 128), group_pos.reshape(4, 128), group_start.reshape(4, 128)
    key_low, key_high = jnp.min(key_runs, axis=1)[:, None], jnp.max(key_runs, axis=1)[:, None]
    seen = (key_low <= jnp.max(pos_runs, axis=1)[None, :]) & (key_high >= jnp.min(start_runs, axis=1)[None, :])
    active = jnp.max(seen.astype(jnp.int32).reshape(16, 16), axis=1)
    active = step_tables(active, c)
    select_y = selected(group_pos)
    select_x = selected(own_row.reshape(2, 4, 4, 128)[0, :, 0].reshape(GROUP))
    select = select_y[:128]
    cos_table, sin_table = rope_tables(group_pos - group_start, HEAD_SIZE)

    def column_slices(weight):
        parts = weight.reshape(16, 4, 4, 4, 2, 64)
        return jnp.transpose(parts, (2, 4, 0, 1, 3, 5)).reshape(8, 16, 1024)

    heads_q = w_query.reshape(16, 4, 512)
    heads_kv = jnp.concatenate([w_key.reshape(16, 4, 256), w_value.reshape(16, 4, 256)], axis=2)
    qkv_parts = jnp.transpose(jnp.stack([heads_q, heads_kv], axis=2), (1, 2, 0, 3)).reshape(8, 16, 512)
    qkv_parts = lax.all_to_all(qkv_parts, ("y", "c"), split_axis=0, concat_axis=0, tiled=True).reshape(128, 512)
    gate_up = jnp.concatenate([column_slices(w_gate), column_slices(w_up)], axis=2)
    def columns_of(array, width):
        return lax.dynamic_slice_in_dim(array, y * width, width, 1)

    inputs = hidden.astype(f32)
    scale_in = row_scale(inputs)
    normed = (inputs * scale_in * gain_attn).astype(bf16)
    normed, cot, qkv_parts = lax.optimization_barrier((normed, cot, qkv_parts))
    normed_g = gather_near(normed, "y")
    cot_g = gather_near(cot, "x")
    qkv_parts = after(qkv_parts, normed_g, cot_g)
    qkv_mine = gather_ring(gather_ring(qkv_parts, "x"), "z").reshape(2048, 512)
    qkv_other = swap_cores(qkv_mine)
    wo = lax.all_gather(w_out, ALL, axis=0, tiled=True)
    q_expand = columns_of(query_expand, 512)
    k_expand = columns_of(key_expand, 256)
    v_expand = columns_of(value_expand, 256)
    low_qkv = (product(normed_g, qkv_shrink) * jnp.tile(select_y, (1, 3))).astype(bf16)
    lin_mine, lin_other = product(normed_g, qkv_mine), product(normed_g, qkv_other)
    query_lin = jnp.where(c == 0, lin_mine, lin_other) + product(low_qkv[:, :rank], q_expand)
    kv_lin = jnp.where(c == 0, lin_other, lin_mine)
    key_lin = kv_lin[:, :256] + product(low_qkv[:, rank : 2 * rank], k_expand)
    value_lin = kv_lin[:, 256:] + product(low_qkv[:, 2 * rank :], v_expand)
    query_heads = query_lin.reshape(GROUP, 2, HEAD_SIZE)
    key_heads = key_lin.reshape(GROUP, 1, HEAD_SIZE)
    query = (query_heads * cos_table + rotate(query_heads) * sin_table).astype(bf16)
    query = (query * bf16(factor)).reshape(GROUP, 512)
    key = (key_heads * cos_table + rotate(key_heads) * sin_table).astype(bf16).reshape(GROUP, 256)

    lines = gather_row(jnp.concatenate([key, value_lin.astype(bf16)], axis=1))
    gate_up = gate_up + zero_of(lines[0]).astype(bf16)
    gate_up = lax.all_to_all(gate_up, ("x", "c"), split_axis=0, concat_axis=0, tiled=True).reshape(128, 2048)
    waited = zero_of(lines[1]) + zero_of(lines[2]) + zero_of(lines[3]) + zero_of(lines[4]) + zero_of(wo)
    ffn = jnp.concatenate([gate_up, w_down], axis=0) + waited.astype(bf16)
    ffn = lax.all_gather(ffn, OVER_X, axis=0, tiled=False).reshape(16, 2, 192, 2048)
    attended = (query, group_pos[:, None], group_start[:, None], tiles_pos.reshape(16, 1, GROUP)) + lines
    mixed_f, lse = attend(active, *attended)
    mixed = mixed_f.astype(bf16)

    heads = jnp.zeros((4, 128, 512), bf16)
    heads = lax.dynamic_update_index_in_dim(heads, mixed[:128], y, 0)
    for step in (1, 2, 3):
        got = shift(mixed[step * 128 : (step + 1) * 128], "y", step)
        heads = lax.dynamic_update_index_in_dim(heads, got, (y - step) % 4, 0)
    mixed_tok = jnp.transpose(heads, (1, 0, 2)).reshape(128, 2048)
    low_out = (product(mixed_tok, out_shrink) * select).astype(bf16)
    middle = inputs + product(mixed_tok, wo) + product(low_out, out_expand)
    scale_mid = row_scale(middle)
    normed_mid = (middle * scale_mid * gain_ffn).astype(bf16)
    normed_mid_g = gather_near(normed_mid, "x")

    select_two = jnp.tile(select_x, (1, 2))
    low_gu = (product(normed_mid_g, gateup_shrink) * select_two).astype(bf16)
    grad_low_down = (times_transposed(cot_g, down_expand) * select_x).astype(bf16)
    place = jnp.arange(GROUP, dtype=jnp.int32)
    turned = (place // 32 % 4) * 128 + (place // 128) * 32 + place % 32
    perm = (turned[:, None] == place[None, :]).astype(bf16)
    wide, narrow = jnp.arange(2 * CHUNK, dtype=jnp.int32), jnp.arange(CHUNK, dtype=jnp.int32)
    picks = jnp.stack(
        [(wide[:, None] == (narrow // 64 * 128 + core * 64 + narrow % 64)[None, :]).astype(bf16) for core in (0, 1)]
    )
    result, back_part, unit_grads = feed_forward(
        x.reshape(1).astype(jnp.int32),
        normed_mid_g,
        cot_g,
        low_gu,
        grad_low_down,
        ffn,
        (gate_expand, up_expand, down_shrink),
        perm,
        picks,
    )

    def sum_tokens(part, ring, base=0.0):
        sent = part.astype(bf16)
        return sum_near([sent[i * 128 : (i + 1) * 128] for i in range(4)], ring, base)

    back = sum_tokens(back_part, "x")
    back, back_low, low_down_sum = back[:, :2048], back[:, 2048 : 2048 + 2 * rank], back[:, 2048 + 2 * rank :]

    low_down = (low_down_sum * select).astype(bf16)
    grad_low_gu = (back_low * jnp.tile(select, (1, 2))).astype(bf16)
    grad_normed_mid = back + times_transposed(grad_low_gu, gateup_shrink)
    cot_f = cot.astype(f32)
    grad_middle = cot_f + norm_back(middle, scale_mid, gain_ffn, grad_normed_mid)
    grad_attn_out = grad_middle.astype(bf16)
    grad_low_out = (times_transposed(grad_attn_out, out_expand) * select).astype(bf16)
    grad_mixed = (times_transposed(grad_attn_out, wo) + times_transposed(grad_low_out, out_shrink)).astype(bf16)

    def slices_near(array):
        def columns_at(step):
            return lax.dynamic_slice_in_dim(array, ((y + step) % 4) * 512, 512, 1)

        return jnp.concatenate([columns_at(0)] + [shift(columns_at(4 - step), "y", -step) for step in (1, 2, 3)])

    dout = slices_near(grad_mixed)
    dq, *terms = attend_back(active, *attended, mixed_f, lse, dout)
    unit_sum = lax.psum_scatter(
        unit_grads.reshape(32, 192, rank), OVER_X, scatter_dimension=0, tiled=False
    )
    aheads = []

    def beside(start):
        aheads.append(sum_tokens(result + start.astype(bf16), "x"))
        return zero_of(aheads[0]) + zero_of(unit_sum)

    dkv = sum_row(*terms, beside)
    dk, dv = dkv[:, :HEAD_SIZE], dkv[:, HEAD_SIZE:]
    query_back = (dq * factor).astype(bf16).astype(f32).reshape(GROUP, 2, HEAD_SIZE)
    key_back = dk.astype(bf16).astype(f32).reshape(GROUP, 1, HEAD_SIZE)
    grad_value = dv.astype(bf16)
    grad_query = (query_back * cos_table - rotate(query_back * sin_table)).astype(bf16).reshape(GROUP, 512)
    grad_key = (key_back * cos_table - rotate(key_back * sin_table)).astype(bf16).reshape(GROUP, 256)
    grad_kv = jnp.concatenate([grad_key, grad_value], axis=1)

    grad_low_part = jnp.concatenate(
        [
            times_transposed(grad_query, q_expand),
            times_transposed(grad_key, k_expand),
            times_transposed(grad_value, v_expand),
        ],
        axis=1,
    )
    grad_low_qkv = (sum_tokens(grad_low_part, "y") * jnp.tile(select, (1, 3))).astype(bf16)
    for_mine = jnp.where(c == 0, grad_query, grad_kv)
    for_other = jnp.where(c == 0, grad_kv, grad_query)
    grad_normed_part = times_transposed(for_mine, qkv_mine) + times_transposed(for_other, qkv_other)
    def features(array, at):
        return lax.dynamic_slice_in_dim(array, at * 512, 512, 1)

    def by_cores(arrays):
        parts = jnp.concatenate([array.reshape(16, 2, array.shape[0] // 32, rank) for array in arrays], axis=2)
        kept = lax.dynamic_index_in_dim(parts, c, 1, keepdims=False)
        return kept, lax.dynamic_index_in_dim(parts, 1 - c, 1, keepdims=False)

    def sum_plane(kept, given, ring):
        terms = kept + swap_cores(given.astype(bf16)).astype(f32)
        return sum_ring(sum_ring(terms.reshape(4, 4, -1, rank), "z"), ring)

    row_terms = [
        inner_rows(mixed_tok, grad_low_out),
        inner_rows(grad_attn_out, low_out),
        inner_rows(cot, low_down),
        inner_rows(normed_mid, grad_low_gu[:, :rank]),
        inner_rows(normed_mid, grad_low_gu[:, rank:]),
    ]
    row_terms = jnp.concatenate([array.reshape(128, 16, rank) for array in row_terms], axis=1)
    row_terms = jnp.swapaxes(row_terms.reshape(4, 4, 8, 80, rank), 1, 2).reshape(32, 320, rank)
    row_sum = lax.psum_scatter(row_terms, OVER_X, scatter_dimension=0, tiled=False)
    row_sum = sum_ring((row_sum + zero_of(dkv)).reshape(4, 80, rank), "x")
    early_sum = jnp.concatenate([unit_sum, row_sum], axis=0).astype(bf16)
    early_all = lax.all_gather(early_sum, ALL, axis=0, tiled=False)

    grad_qkv = inner_rows(features(normed_g, y), gather_near(grad_low_qkv, "y"))
    kept, other = by_cores(
        [
            inner_rows(grad_query, low_qkv[:, :rank]),
            inner_rows(grad_key, low_qkv[:, rank : 2 * rank]),
            inner_rows(grad_value, low_qkv[:, 2 * rank :]),
            grad_qkv[:, :rank],
            grad_qkv[:, rank : 2 * rank],
            grad_qkv[:, 2 * rank :],
        ]
    )
    g_gate, g_up, g_down_shrink, g_out_shrink, g_out_expand, g_down_expand, g_gateup = unpack_early(early_all)
    late_sum = sum_plane(kept, other, "x").astype(bf16)
    late_all = gather_ring(gather_ring(late_sum, "x"), "z")
    grad_normed = sum_tokens(grad_normed_part, "y", zero_of(late_all)) + times_transposed(grad_low_qkv, qkv_shrink)
    output = (middle + aheads[0] + product(low_down, down_expand)).astype(bf16)
    grad_input = (grad_middle + norm_back(inputs, scale_in, gain_attn, grad_normed)).astype(bf16)
    late_all = gather_ring(late_all, "y", zero_of(g_gateup).astype(bf16))
    late_all = late_all.reshape(4, 16, -1, rank)
    late_other = swap_cores(late_all)
    g_q, g_k, g_v, g_qkv = unpack_late(c.reshape(1).astype(jnp.int32), late_all, late_other)
    return (
        from_rows(output),
        from_rows(grad_input),
        g_qkv,
        g_q,
        g_k,
        g_v,
        g_out_shrink,
        g_out_expand,
        g_gateup,
        g_gate,
        g_up,
        g_down_shrink,
        g_down_expand,
    )


def solution(mesh):
    fine = Mesh(mesh.devices.reshape(2, 2, 4, 4, 2), ALL)
    split = P(ALL, None)
    placed = (split, P(), P()) + (split,) * 7 + (P(),) * 14 + (split,)
    return jax.shard_map(
        local,
        mesh=fine,
        in_specs=placed,
        out_specs=(split, split) + (P(),) * 11,
        check_vma=False,
    )
```

```python
from functools import partial

import jax
import jax.numpy as jnp
from jax import lax
from jax.experimental import pallas as pl
from jax.experimental.pallas import tpu as pltpu
from jax.sharding import Mesh, PartitionSpec as P

HEAD_SIZE = 256
RANK = 16
HALF = 64
GROUP = 512

ALL = ("zh", "zl", "x", "y", "c")

norm_eps = 1e-06
rope_theta = 1000042.0
neg_big = -1e30
far = 1 << 30

f32 = jnp.float32
bf16 = jnp.bfloat16


def product(left, right):
    return jnp.dot(left, right, preferred_element_type=f32)


def times_transposed(left, right):
    return lax.dot_general(left, right, (((1,), (1,)), ((), ())), preferred_element_type=f32)


def inner_rows(left, right):
    return lax.dot_general(left, right, (((0,), (0,)), ((), ())), preferred_element_type=f32)


def row_scale(value_matrix):
    return lax.rsqrt(jnp.mean(value_matrix * value_matrix, axis=-1, keepdims=True) + norm_eps)


def norm_back(value_matrix, scale, gain, grad):
    scaled = gain * grad
    return scale * scaled - value_matrix * (scale * scale * scale) * jnp.mean(
        value_matrix * scaled, axis=-1, keepdims=True
    )


def rotate(value_matrix):
    middle = value_matrix.shape[-1] // 2
    return jnp.concatenate([-value_matrix[..., middle:], value_matrix[..., :middle]], axis=-1)


def rope_tables(positions, width):
    middle = width // 2
    inverse = rope_theta ** (-(jnp.arange(middle, dtype=f32) * 2.0) / width)
    angles = positions.astype(f32)[:, None] * inverse[None, :]
    cos_half, sin_half = jnp.cos(angles), jnp.sin(angles)
    cos_table = jnp.concatenate([cos_half, cos_half], axis=-1)[:, None, :]
    sin_table = jnp.concatenate([sin_half, sin_half], axis=-1)[:, None, :]
    return (cos_table, sin_table)


OVER_X = ("zh", "zl", "y", "c")
RING = {"x": ("x",), "y": ("y",), "z": ("zh", "zl")}


def swap_cores(value):
    return lax.ppermute(value, "c", [(0, 1), (1, 0)])


def shift(value, ring, step):
    return lax.ppermute(value, RING[ring], [(i, (i + step) % 4) for i in range(4)])


def place_in(ring):
    return lax.axis_index(RING[ring])


def gather_near(value, ring, axis=0):
    return jnp.concatenate([value] + [shift(value, ring, -step) for step in (1, 2, 3)], axis=axis)


def gather_ring(value, ring, base=0.0):
    at = place_in(ring)
    whole_ring = jnp.full((4,) + value.shape, base, value.dtype)
    whole_ring = lax.dynamic_update_index_in_dim(whole_ring, value, at, 0)
    for step in (1, 2, 3):
        got = shift(value, ring, -step)
        whole_ring = lax.dynamic_update_index_in_dim(whole_ring, got, (at + step) % 4, 0)
    return whole_ring


def sum_near(blocks, ring, base=0.0):
    got = [shift(blocks[step], ring, step) for step in (2, 1, 3)]
    total = blocks[0].astype(f32) + base
    for term in got:
        total = total + term.astype(f32)
    return total


def sum_ring(terms, ring):
    at = place_in(ring)
    got = [
        shift(lax.dynamic_index_in_dim(terms, (at + step) % 4, 0, keepdims=False).astype(bf16), ring, step)
        for step in (1, 2, 3)
    ]
    total = lax.dynamic_index_in_dim(terms, at, 0, keepdims=False)
    for term in got:
        total = total + term.astype(f32)
    return total


CORNER = ("zh", "zl", "c")
PARTNER = [(4 * zh + 2 * zl + c, 4 * zh + 2 * (1 - zl) + c) for zh in (0, 1) for zl in (0, 1) for c in (0, 1)]
LATER = [[(2 * zl + 1, 4 + 2 * (zl ^ flip)) for zl in (0, 1)] for flip in (0, 1)]
EARLIER = [[(to, came) for came, to in pairs] for pairs in LATER]
def after(value, *others):
    return lax.optimization_barrier((value,) + others)[0]


def zero_of(value):
    return value[(slice(0, 1),) * value.ndim].reshape(()).astype(f32) * 0.0


def gather_row(key_value):
    line = jnp.stack([key_value] + [shift(key_value, "x", -step) for step in (1, 2, 3)])
    ahead = [lax.ppermute(line, CORNER, pairs) for pairs in LATER]
    partner = lax.ppermute(line, CORNER, PARTNER)
    beside = [lax.ppermute(value, "c", [(0, 1)]) for value in (line, partner)]
    return line, partner, ahead[0], ahead[1], beside[0], beside[1]


def sum_row(own, own_partner, prev, prev_partner, beside):
    got = [lax.ppermute(value, "c", [(1, 0)]) for value in (prev_partner, prev)]
    terms = [lax.ppermute(value, CORNER, pairs) for value, pairs in zip((prev, prev_partner), EARLIER)]
    sent = (own_partner.astype(f32) + got[0].astype(f32)).astype(bf16)
    terms = [got[1], lax.ppermute(sent, CORNER, PARTNER)] + terms
    start = zero_of(sent)
    line = own.astype(f32)
    for term in terms:
        line = line + term.astype(f32)
    sent = (line + beside(start)).astype(bf16)
    total = line[0]
    for step in (2, 1, 3):
        total = total + shift(sent[step], "x", step).astype(f32)
    return total


def allowed_mask(own_pos, own_start, key_pos):
    return (key_pos <= own_pos) & (key_pos >= own_start)


def load_tile(tile, tile_buf, own_ref, partner_ref, ahead_ref, ahead_partner_ref, beside_ref, beside_partner_ref):
    @pl.when(tile == 0)
    def _():
        tile_buf[...] = ahead_ref[0] + beside_ref[0]

    @pl.when(tile == 1)
    def _():
        tile_buf[...] = ahead_partner_ref[0] + beside_partner_ref[0]

    @pl.when(tile == 2)
    def _():
        tile_buf[...] = own_ref[0]

    @pl.when(tile == 3)
    def _():
        tile_buf[...] = partner_ref[0]


def attend_kernel(active, q_ref, pos_ref, start_ref, kpos_ref, *refs):
    mixed_ref, lse_ref, tile_buf, top, total, accum = refs[6:]
    step = pl.program_id(0)

    @pl.when(step == 0)
    def _():
        top[...] = jnp.full(top.shape, neg_big, f32)
        total[...] = jnp.zeros(total.shape, f32)
        accum[...] = jnp.zeros(accum.shape, f32)

    @pl.when(active[step] != 0)
    def _():
        load_tile(step // 4, tile_buf, *refs[:6])
        allowed = allowed_mask(pos_ref[...], start_ref[...], kpos_ref[0])
        both = [
            times_transposed(q_ref[:, head * HEAD_SIZE : (head + 1) * HEAD_SIZE], tile_buf[:, :HEAD_SIZE])
            for head in range(2)
        ]
        for head in range(2):
            scores = jnp.where(allowed, both[head], neg_big)
            top_old = top[head]
            top_new = jnp.maximum(top_old, jnp.max(scores, axis=-1, keepdims=True))
            weights_p = jnp.exp(scores - top_new)
            damping = jnp.exp(top_old - top_new)
            total[head] = total[head] * damping + jnp.sum(weights_p, axis=-1, keepdims=True)
            accum[head] = accum[head] * damping + product(weights_p.astype(bf16), tile_buf[:, HEAD_SIZE:])
            top[head] = top_new

    @pl.when(step == 15)
    def _():
        for head in range(2):
            mixed_ref[:, head * HEAD_SIZE : (head + 1) * HEAD_SIZE] = accum[head] / total[head]
            lse_ref[head] = top[head] + jnp.log(total[head])


def attend_back_kernel(active, q_ref, pos_ref, start_ref, kpos_ref, *refs):
    mixed_ref, lse_ref, dout_ref, dq_ref, down_ref, dpartner_ref, dprev_ref, dprev_partner_ref = refs[6:14]
    tile_buf, delta, sums = refs[14:]
    step = pl.program_id(0)
    tile = step // 4

    @pl.when(step == 0)
    def _():
        dq_ref[...] = jnp.zeros(dq_ref.shape, f32)
        for head in range(2):
            cols = slice(head * HEAD_SIZE, (head + 1) * HEAD_SIZE)
            delta[head] = jnp.sum(dout_ref[:, cols].astype(f32) * mixed_ref[:, cols], axis=-1, keepdims=True)

    @pl.when(active[step] == 0)
    def _():
        sums[...] = jnp.zeros(sums.shape, bf16)

    @pl.when(active[step] != 0)
    def _():
        load_tile(tile, tile_buf, *refs[:6])
        allowed = allowed_mask(pos_ref[...], start_ref[...], kpos_ref[0])
        dk = jnp.zeros((GROUP, HEAD_SIZE), f32)
        dv = jnp.zeros((GROUP, HEAD_SIZE), f32)
        for head in range(2):
            cols = slice(head * HEAD_SIZE, (head + 1) * HEAD_SIZE)
            query, dout = q_ref[:, cols], dout_ref[:, cols]
            scores = times_transposed(query, tile_buf[:, :HEAD_SIZE])
            weights_p = jnp.where(allowed, jnp.exp(scores - lse_ref[head]), 0.0)
            dprobs = times_transposed(dout, tile_buf[:, HEAD_SIZE:])
            dscores = (weights_p * (dprobs - delta[head])).astype(bf16)
            dq_ref[:, cols] += product(dscores, tile_buf[:, :HEAD_SIZE])
            dk = dk + inner_rows(dscores, query)
            dv = dv + inner_rows(weights_p.astype(bf16), dout)
        sums[:, :HEAD_SIZE] = dk.astype(bf16)
        sums[:, HEAD_SIZE:] = dv.astype(bf16)

    for at, out_ref in enumerate((dprev_ref, dprev_partner_ref, down_ref, dpartner_ref)):

        @pl.when(tile == at)
        def _():
            out_ref[0] = sums[...]


def whole(shape):
    return pl.BlockSpec(shape, lambda *grid_and_refs: (0,) * len(shape))


def line_spec(tile):
    return pl.BlockSpec((1, GROUP, GROUP), lambda i, active: (jnp.clip(i - 4 * tile, 0, 3), 0, 0))


def active_spec(tile, table):
    return pl.BlockSpec(
        (1, GROUP, GROUP), lambda i, active: (active[16 * table + 4 * tile + jnp.clip(i - 4 * tile, 0, 3)], 0, 0)
    )


def step_tables(active, c):
    marks = active.reshape(4, 4)
    at = jnp.arange(4, dtype=jnp.int32)
    seen = jnp.where((marks[:, None, :] != 0) & (at[None, None, :] <= at[None, :, None]), at[None, None, :], -1)
    last = jnp.max(seen, axis=2)
    first = jnp.min(jnp.where(marks != 0, at[None, :], 3), axis=1, keepdims=True)
    blocks = jnp.where(last >= 0, last, first).reshape(16).astype(jnp.int32)
    return jnp.concatenate([active, blocks, jnp.where(c == 0, blocks, 0), jnp.where(c == 0, 0, blocks)])


def common_specs():
    return [
        whole((GROUP, GROUP)),
        whole((GROUP, 1)),
        whole((GROUP, 1)),
        pl.BlockSpec((1, 1, GROUP), lambda i, active: (i, 0, 0)),
    ] + [active_spec(tile, table) for tile, table in ((2, 1), (3, 1), (0, 2), (1, 2), (0, 3), (1, 3))]


def attend(active, *operands):
    return pl.pallas_call(
        attend_kernel,
        grid_spec=pltpu.PrefetchScalarGridSpec(
            num_scalar_prefetch=1,
            grid=(16,),
            in_specs=common_specs(),
            out_specs=[whole((GROUP, GROUP)), whole((2, GROUP, 1))],
            scratch_shapes=[
                pltpu.VMEM((GROUP, GROUP), bf16),
                pltpu.VMEM((2, GROUP, 1), f32),
                pltpu.VMEM((2, GROUP, 1), f32),
                pltpu.VMEM((2, GROUP, HEAD_SIZE), f32),
            ],
        ),
        out_shape=[
            jax.ShapeDtypeStruct((GROUP, GROUP), f32),
            jax.ShapeDtypeStruct((2, GROUP, 1), f32),
        ],
        compiler_params=pltpu.CompilerParams(vmem_limit_bytes=48 << 20),
        cost_estimate=pl.CostEstimate(flops=6 << 30, bytes_accessed=10 << 20, transcendentals=8 << 20),
        name="attend",
    )(active, *operands)


def attend_back(active, *operands):
    return pl.pallas_call(
        attend_back_kernel,
        grid_spec=pltpu.PrefetchScalarGridSpec(
            num_scalar_prefetch=1,
            grid=(16,),
            in_specs=common_specs() + [whole((GROUP, GROUP)), whole((2, GROUP, 1)), whole((GROUP, GROUP))],
            out_specs=[whole((GROUP, GROUP))] + [line_spec(tile) for tile in (2, 3, 0, 1)],
            scratch_shapes=[
                pltpu.VMEM((GROUP, GROUP), bf16),
                pltpu.VMEM((2, GROUP, 1), f32),
                pltpu.VMEM((GROUP, GROUP), bf16),
            ],
        ),
        out_shape=[jax.ShapeDtypeStruct((GROUP, GROUP), f32)]
        + [jax.ShapeDtypeStruct((4, GROUP, GROUP), bf16)] * 4,
        compiler_params=pltpu.CompilerParams(vmem_limit_bytes=48 << 20),
        cost_estimate=pl.CostEstimate(flops=12 << 30, bytes_accessed=20 << 20, transcendentals=8 << 20),
        name="attend_back",
    )(active, *operands)


UNITS = 1024
CHUNK = 256


def ffn_kernel(
    at,
    nm_ref,
    cot_ref,
    lgu_ref,
    gld_ref,
    wg_ref,
    wu_ref,
    wd_ref,
    ge_ref,
    ue_ref,
    ds_ref,
    perm_ref,
    pick_ref,
    result_ref,
    back_ref,
    units_ref,
    nmp,
    result,
    grad,
    low,
):
    step = pl.program_id(0)
    rank = ds_ref.shape[1]

    @pl.when(step == 0)
    def _():
        for zone in range(4):
            cols = slice(zone * GROUP, (zone + 1) * GROUP)
            nmp[:, cols] = product(nm_ref[:, cols], perm_ref[...]).astype(bf16)
        result[...] = jnp.zeros(result.shape, f32)
        grad[...] = jnp.zeros(grad.shape, f32)
        low[...] = jnp.zeros(low.shape, f32)

    wg, wu = wg_ref[...].reshape(2048, CHUNK), wu_ref[...].reshape(2048, CHUNK)
    wd = wd_ref[...].reshape(CHUNK, 2048)
    ge, ue = product(ge_ref[...], pick_ref[0]).astype(bf16), product(ue_ref[...], pick_ref[0]).astype(bf16)
    ds = inner_rows(pick_ref[0], ds_ref[...]).astype(bf16)
    low_gate, low_up = lgu_ref[:, :rank], lgu_ref[:, rank:]
    gate_pre = product(nmp[...], wg) + product(low_gate, ge)
    up_pre = product(nmp[...], wu) + product(low_up, ue)
    sigmoid_g = jax.nn.sigmoid(gate_pre)
    silu_gate = gate_pre * sigmoid_g
    active_units = (silu_gate * up_pre).astype(bf16)
    grad_active = times_transposed(cot_ref[...], wd) + times_transposed(gld_ref[...], ds)
    grad_gate = (grad_active * up_pre * sigmoid_g * (1.0 + gate_pre * (1.0 - sigmoid_g))).astype(bf16)
    grad_up = (grad_active * silu_gate).astype(bf16)
    result[...] += product(active_units, wd)
    grad[...] += times_transposed(grad_gate, wg) + times_transposed(grad_up, wu)
    low[:, :rank] += times_transposed(grad_gate, ge)
    low[:, rank : 2 * rank] += times_transposed(grad_up, ue)
    low[:, 2 * rank :] += product(active_units, ds)
    units_ref[0, :, 0, :64] = inner_rows(grad_gate, low_gate).reshape(4, 64, rank)
    units_ref[0, :, 0, 64:128] = inner_rows(grad_up, low_up).reshape(4, 64, rank)
    units_ref[0, :, 0, 128:] = inner_rows(active_units, gld_ref[...]).reshape(4, 64, rank)

    @pl.when(step == 2 * UNITS // CHUNK - 1)
    def _():
        result_ref[...] = result[...].astype(bf16)
        for zone in range(4):
            cols = slice(zone * GROUP, (zone + 1) * GROUP)
            back_ref[:, cols] = product(grad[:, cols].astype(bf16), perm_ref[...]).astype(bf16)
        back_ref[:, 2048:] = low[...].astype(bf16)


def feed_forward(at, normed_mid, cot, low_gu, grad_low_down, weights, expands, perm, picks):
    rank = low_gu.shape[1] // 2
    steps = UNITS // CHUNK
    unit_spec = pl.BlockSpec((1, 4, 1, 192, rank), lambda i, at: (i % steps, 0, i // steps, 0, 0))
    return pl.pallas_call(
        ffn_kernel,
        grid_spec=pltpu.PrefetchScalarGridSpec(
            num_scalar_prefetch=1,
            grid=(2 * steps,),
            in_specs=[
                whole((GROUP, 2048)),
                whole((GROUP, 2048)),
                whole((GROUP, 2 * rank)),
                whole((GROUP, rank)),
                pl.BlockSpec((16, 1, 128, CHUNK), lambda i, at: (0, i // steps, 0, i % steps)),
                pl.BlockSpec((16, 1, 128, CHUNK), lambda i, at: (0, i // steps, 0, steps + i % steps)),
                pl.BlockSpec((4, 1, 64, 2048), lambda i, at: (i % steps, i // steps, 2, 0)),
                pl.BlockSpec((rank, 2 * CHUNK), lambda i, at: (0, 4 * (i % steps) + at[0])),
                pl.BlockSpec((rank, 2 * CHUNK), lambda i, at: (0, 4 * (i % steps) + at[0])),
                pl.BlockSpec((2 * CHUNK, rank), lambda i, at: (4 * (i % steps) + at[0], 0)),
                whole((GROUP, GROUP)),
                pl.BlockSpec((1, 2 * CHUNK, CHUNK), lambda i, at: (i // steps, 0, 0)),
            ],
            out_specs=[whole((GROUP, 2048)), whole((GROUP, 2048 + 3 * rank)), unit_spec],
            scratch_shapes=[
                pltpu.VMEM((GROUP, 2048), bf16),
                pltpu.VMEM((GROUP, 2048), f32),
                pltpu.VMEM((GROUP, 2048), f32),
                pltpu.VMEM((GROUP, 3 * rank), f32),
            ],
        ),
        out_shape=[
            jax.ShapeDtypeStruct((GROUP, 2048), bf16),
            jax.ShapeDtypeStruct((GROUP, 2048 + 3 * rank), bf16),
            jax.ShapeDtypeStruct((4, 4, 2, 192, rank), f32),
        ],
        compiler_params=pltpu.CompilerParams(vmem_limit_bytes=60 << 20),
        cost_estimate=pl.CostEstimate(flops=28 << 30, bytes_accessed=40 << 20, transcendentals=2 << 20),
        name="feed_forward",
    )(at, normed_mid, cot, low_gu, grad_low_down, weights, weights, weights, *expands, perm, picks)


EARLY = (64, 64, 64, 16, 16, 16, 16, 16)
LATE = (16, 8, 8, 16, 16, 16)


def cut(array, sizes):
    found, at = [], 0
    for size in sizes:
        found.append(array[..., at : at + size, :])
        at += size
    return found


def turned(array):
    at = lax.broadcasted_iota(jnp.int32, (128, 128), 0), lax.broadcasted_iota(jnp.int32, (128, 128), 1)
    return times_transposed((at[0] == at[1]).astype(f32).astype(bf16), array)


def early_kernel(all_ref, gate_ref, up_ref, down_ref, oshrink_ref, oexpand_ref, dexpand_ref, gateup_ref):
    pieces = [piece.reshape(-1, 128) for piece in cut(all_ref[...], EARLY)]
    gate_ref[...] = turned(pieces[0])
    up_ref[...] = turned(pieces[1])
    down_ref[...] = pieces[2].astype(f32)
    oshrink_ref[...] = pieces[3].astype(f32)
    oexpand_ref[...] = turned(pieces[4])
    dexpand_ref[...] = turned(pieces[5])
    gateup_ref[:, :128] = pieces[6].astype(f32)
    gateup_ref[:, 128:] = pieces[7].astype(f32)


def unpack_early(everyone):
    return pl.pallas_call(
        early_kernel,
        grid=(8,),
        in_specs=[pl.BlockSpec((16, sum(EARLY), 128), lambda i: (i, 0, 0))],
        out_specs=[
            pl.BlockSpec((128, 1024), lambda i: (0, i)),
            pl.BlockSpec((128, 1024), lambda i: (0, i)),
            pl.BlockSpec((1024, 128), lambda i: (i, 0)),
            pl.BlockSpec((256, 128), lambda i: (i, 0)),
            pl.BlockSpec((128, 256), lambda i: (0, i)),
            pl.BlockSpec((128, 256), lambda i: (0, i)),
            pl.BlockSpec((256, 256), lambda i: (i, 0)),
        ],
        out_shape=[
            jax.ShapeDtypeStruct(shape, f32)
            for shape in ((128, 8192), (128, 8192), (8192, 128), (2048, 128), (128, 2048), (128, 2048), (2048, 256))
        ],
        cost_estimate=pl.CostEstimate(flops=1 << 20, bytes_accessed=27 << 20, transcendentals=0),
        name="unpack_early",
    )(everyone)


def late_kernel(core, mine_ref, other_ref, q_ref, k_ref, v_ref, low_ref):
    mine, other = mine_ref[0].astype(f32), other_ref[0].astype(f32)
    first, second = jnp.where(core[0] == 0, mine, other), jnp.where(core[0] == 0, other, mine)
    pieces = [
        jnp.stack(pair, axis=1).reshape(-1, 128) for pair in zip(cut(first, LATE), cut(second, LATE))
    ]
    q_ref[...] = turned(pieces[0].astype(bf16))
    k_ref[...] = turned(pieces[1].astype(bf16))
    v_ref[...] = turned(pieces[2].astype(bf16))
    for at in range(3):
        low_ref[:, at * 128 : (at + 1) * 128] = pieces[3 + at]


def unpack_late(core, mine, other):
    half = pl.BlockSpec((1, 16, sum(LATE), 128), lambda i, core: (i, 0, 0, 0))
    return pl.pallas_call(
        late_kernel,
        grid_spec=pltpu.PrefetchScalarGridSpec(
            num_scalar_prefetch=1,
            grid=(4,),
            in_specs=[half, half],
            out_specs=[
                pl.BlockSpec((128, 512), lambda i, core: (0, i)),
                pl.BlockSpec((128, 256), lambda i, core: (0, i)),
                pl.BlockSpec((128, 256), lambda i, core: (0, i)),
                pl.BlockSpec((512, 384), lambda i, core: (i, 0)),
            ],
        ),
        out_shape=[
            jax.ShapeDtypeStruct(shape, f32) for shape in ((128, 2048), (128, 1024), (128, 1024), (2048, 384))
        ],
        cost_estimate=pl.CostEstimate(flops=1 << 20, bytes_accessed=8 << 20, transcendentals=0),
        name="unpack_late",
    )(core, mine, other)


def local(
    hidden_in,
    gain_attn,
    gain_ffn,
    w_query,
    w_key,
    w_value,
    w_out,
    w_gate,
    w_up,
    w_down,
    qkv_shrink,
    query_expand,
    key_expand,
    value_expand,
    out_shrink,
    out_expand,
    gateup_shrink,
    gate_expand,
    up_expand,
    down_shrink,
    down_expand,
    lengths,
    adapter,
    packed_pos,
    cotangent,
):
    zh, zl, x, y, c = (lax.axis_index(name) for name in ALL)
    row = 2 * zh + c
    factor = HEAD_SIZE ** (-0.5)
    rank = out_shrink.shape[1]

    def to_rows(value):
        own = lax.dynamic_slice_in_dim(value, c * HALF, HALF, 0)
        sent = lax.dynamic_slice_in_dim(value, (1 - c) * HALF, HALF, 0)
        return jnp.concatenate([own, swap_cores(sent)], axis=0)

    def from_rows(value):
        own, got = value[:HALF], swap_cores(value[HALF:])
        return jnp.where(c == 0, jnp.concatenate([own, got], 0), jnp.concatenate([got, own], 0))

    hidden = to_rows(hidden_in)
    cot = to_rows(cotangent)

    def roll(array, by, axis):
        return lax.dynamic_slice_in_dim(jnp.concatenate([array, array], axis), by, array.shape[axis], axis)

    spread = packed_pos.reshape(2, 2, 4, 4, 2, 2, HALF)
    spread = jnp.transpose(spread, (0, 5, 1, 2, 3, 4, 6))
    rows_pos = jnp.stack([spread[:, 0], spread[:, 1, :, :, :, ::-1]], axis=1).reshape(4, 2, 4, 4, 128)
    rows_pos = roll(roll(roll(rows_pos, zl, 1), x, 2), y, 3).reshape(4, 8, GROUP)
    own_row = lax.dynamic_index_in_dim(rows_pos, row, 0, keepdims=False)
    prev_row = lax.dynamic_index_in_dim(rows_pos, jnp.maximum(row - 1, 0), 0, keepdims=False)
    prev_row = jnp.where(row == 0, far, prev_row)
    tiles_pos = jnp.concatenate([prev_row, own_row])
    group_pos = own_row[0]
    seq_ends = jnp.cumsum(lengths)
    starts = seq_ends - lengths
    member = (group_pos[:, None] >= starts[None, :]) & (group_pos[:, None] < seq_ends[None, :])
    member_int = member.astype(jnp.int32)
    group_start = jnp.sum(member_int * starts[None, :], axis=1)

    def selected(pos):
        inside = (pos[:, None] >= starts[None, :]) & (pos[:, None] < seq_ends[None, :])
        owner = jnp.sum(inside.astype(jnp.int32) * adapter[None, :], axis=1)
        return (owner[:, None] == (jnp.arange(rank, dtype=jnp.int32) // RANK)[None, :]).astype(f32)

    key_runs, pos_runs, start_runs = tiles_pos.reshape(64, 128), group_pos.reshape(4, 128), group_start.reshape(4, 128)
    key_low, key_high = jnp.min(key_runs, axis=1)[:, None], jnp.max(key_runs, axis=1)[:, None]
    seen = (key_low <= jnp.max(pos_runs, axis=1)[None, :]) & (key_high >= jnp.min(start_runs, axis=1)[None, :])
    active = jnp.max(seen.astype(jnp.int32).reshape(16, 16), axis=1)
    active = step_tables(active, c)
    select_y = selected(group_pos)
    select_x = selected(own_row.reshape(2, 4, 4, 128)[0, :, 0].reshape(GROUP))
    select = select_y[:128]
    cos_table, sin_table = rope_tables(group_pos - group_start, HEAD_SIZE)

    def column_slices(weight):
        parts = weight.reshape(16, 4, 4, 4, 2, 64)
        return jnp.transpose(parts, (2, 4, 0, 1, 3, 5)).reshape(8, 16, 1024)

    heads_q = w_query.reshape(16, 4, 512)
    heads_kv = jnp.concatenate([w_key.reshape(16, 4, 256), w_value.reshape(16, 4, 256)], axis=2)
    qkv_parts = jnp.transpose(jnp.stack([heads_q, heads_kv], axis=2), (1, 2, 0, 3)).reshape(8, 16, 512)
    qkv_parts = lax.all_to_all(qkv_parts, ("y", "c"), split_axis=0, concat_axis=0, tiled=True).reshape(128, 512)
    gate_up = jnp.concatenate([column_slices(w_gate), column_slices(w_up)], axis=2)
    def columns_of(array, width):
        return lax.dynamic_slice_in_dim(array, y * width, width, 1)

    inputs = hidden.astype(f32)
    scale_in = row_scale(inputs)
    normed = (inputs * scale_in * gain_attn).astype(bf16)
    normed, cot, qkv_parts = lax.optimization_barrier((normed, cot, qkv_parts))
    normed_g = gather_near(normed, "y")
    cot_g = gather_near(cot, "x")
    qkv_parts = after(qkv_parts, normed_g, cot_g)
    qkv_mine = gather_ring(gather_ring(qkv_parts, "x"), "z").reshape(2048, 512)
    qkv_other = swap_cores(qkv_mine)
    wo = lax.all_gather(w_out, ALL, axis=0, tiled=True)
    q_expand = columns_of(query_expand, 512)
    k_expand = columns_of(key_expand, 256)
    v_expand = columns_of(value_expand, 256)
    low_qkv = (product(normed_g, qkv_shrink) * jnp.tile(select_y, (1, 3))).astype(bf16)
    lin_mine, lin_other = product(normed_g, qkv_mine), product(normed_g, qkv_other)
    query_lin = jnp.where(c == 0, lin_mine, lin_other) + product(low_qkv[:, :rank], q_expand)
    kv_lin = jnp.where(c == 0, lin_other, lin_mine)
    key_lin = kv_lin[:, :256] + product(low_qkv[:, rank : 2 * rank], k_expand)
    value_lin = kv_lin[:, 256:] + product(low_qkv[:, 2 * rank :], v_expand)
    query_heads = query_lin.reshape(GROUP, 2, HEAD_SIZE)
    key_heads = key_lin.reshape(GROUP, 1, HEAD_SIZE)
    query = (query_heads * cos_table + rotate(query_heads) * sin_table).astype(bf16)
    query = (query * bf16(factor)).reshape(GROUP, 512)
    key = (key_heads * cos_table + rotate(key_heads) * sin_table).astype(bf16).reshape(GROUP, 256)

    lines = gather_row(jnp.concatenate([key, value_lin.astype(bf16)], axis=1))
    gate_up = gate_up + zero_of(lines[0]).astype(bf16)
    gate_up = lax.all_to_all(gate_up, ("x", "c"), split_axis=0, concat_axis=0, tiled=True).reshape(128, 2048)
    waited = zero_of(lines[1]) + zero_of(lines[2]) + zero_of(lines[3]) + zero_of(lines[4]) + zero_of(wo)
    ffn = jnp.concatenate([gate_up, w_down], axis=0) + waited.astype(bf16)
    ffn = lax.all_gather(ffn, OVER_X, axis=0, tiled=False).reshape(16, 2, 192, 2048)
    attended = (query, group_pos[:, None], group_start[:, None], tiles_pos.reshape(16, 1, GROUP)) + lines
    mixed_f, lse = attend(active, *attended)
    mixed = mixed_f.astype(bf16)

    heads = jnp.zeros((4, 128, 512), bf16)
    heads = lax.dynamic_update_index_in_dim(heads, mixed[:128], y, 0)
    for step in (1, 2, 3):
        got = shift(mixed[step * 128 : (step + 1) * 128], "y", step)
        heads = lax.dynamic_update_index_in_dim(heads, got, (y - step) % 4, 0)
    mixed_tok = jnp.transpose(heads, (1, 0, 2)).reshape(128, 2048)
    low_out = (product(mixed_tok, out_shrink) * select).astype(bf16)
    middle = inputs + product(mixed_tok, wo) + product(low_out, out_expand)
    scale_mid = row_scale(middle)
    normed_mid = (middle * scale_mid * gain_ffn).astype(bf16)
    normed_mid_g = gather_near(normed_mid, "x")

    select_two = jnp.tile(select_x, (1, 2))
    low_gu = (product(normed_mid_g, gateup_shrink) * select_two).astype(bf16)
    grad_low_down = (times_transposed(cot_g, down_expand) * select_x).astype(bf16)
    place = jnp.arange(GROUP, dtype=jnp.int32)
    turned = (place // 32 % 4) * 128 + (place // 128) * 32 + place % 32
    perm = (turned[:, None] == place[None, :]).astype(bf16)
    wide, narrow = jnp.arange(2 * CHUNK, dtype=jnp.int32), jnp.arange(CHUNK, dtype=jnp.int32)
    picks = jnp.stack(
        [(wide[:, None] == (narrow // 64 * 128 + core * 64 + narrow % 64)[None, :]).astype(bf16) for core in (0, 1)]
    )
    result, back_part, unit_grads = feed_forward(
        x.reshape(1).astype(jnp.int32),
        normed_mid_g,
        cot_g,
        low_gu,
        grad_low_down,
        ffn,
        (gate_expand, up_expand, down_shrink),
        perm,
        picks,
    )

    def sum_tokens(part, ring, base=0.0):
        sent = part.astype(bf16)
        return sum_near([sent[i * 128 : (i + 1) * 128] for i in range(4)], ring, base)

    back = sum_tokens(back_part, "x")
    back, back_low, low_down_sum = back[:, :2048], back[:, 2048 : 2048 + 2 * rank], back[:, 2048 + 2 * rank :]

    low_down = (low_down_sum * select).astype(bf16)
    grad_low_gu = (back_low * jnp.tile(select, (1, 2))).astype(bf16)
    grad_normed_mid = back + times_transposed(grad_low_gu, gateup_shrink)
    cot_f = cot.astype(f32)
    grad_middle = cot_f + norm_back(middle, scale_mid, gain_ffn, grad_normed_mid)
    grad_attn_out = grad_middle.astype(bf16)
    grad_low_out = (times_transposed(grad_attn_out, out_expand) * select).astype(bf16)
    grad_mixed = (times_transposed(grad_attn_out, wo) + times_transposed(grad_low_out, out_shrink)).astype(bf16)

    def slices_near(array):
        def columns_at(step):
            return lax.dynamic_slice_in_dim(array, ((y + step) % 4) * 512, 512, 1)

        return jnp.concatenate([columns_at(0)] + [shift(columns_at(4 - step), "y", -step) for step in (1, 2, 3)])

    dout = slices_near(grad_mixed)
    dq, *terms = attend_back(active, *attended, mixed_f, lse, dout)
    unit_sum = lax.psum_scatter(
        unit_grads.reshape(32, 192, rank), OVER_X, scatter_dimension=0, tiled=False
    )
    aheads = []

    def beside(start):
        aheads.append(sum_tokens(result + start.astype(bf16), "x"))
        return zero_of(aheads[0]) + zero_of(unit_sum)

    dkv = sum_row(*terms, beside)
    dk, dv = dkv[:, :HEAD_SIZE], dkv[:, HEAD_SIZE:]
    query_back = (dq * factor).astype(bf16).astype(f32).reshape(GROUP, 2, HEAD_SIZE)
    key_back = dk.astype(bf16).astype(f32).reshape(GROUP, 1, HEAD_SIZE)
    grad_value = dv.astype(bf16)
    grad_query = (query_back * cos_table - rotate(query_back * sin_table)).astype(bf16).reshape(GROUP, 512)
    grad_key = (key_back * cos_table - rotate(key_back * sin_table)).astype(bf16).reshape(GROUP, 256)
    grad_kv = jnp.concatenate([grad_key, grad_value], axis=1)

    grad_low_part = jnp.concatenate(
        [
            times_transposed(grad_query, q_expand),
            times_transposed(grad_key, k_expand),
            times_transposed(grad_value, v_expand),
        ],
        axis=1,
    )
    grad_low_qkv = (sum_tokens(grad_low_part, "y") * jnp.tile(select, (1, 3))).astype(bf16)
    for_mine = jnp.where(c == 0, grad_query, grad_kv)
    for_other = jnp.where(c == 0, grad_kv, grad_query)
    grad_normed_part = times_transposed(for_mine, qkv_mine) + times_transposed(for_other, qkv_other)
    def features(array, at):
        return lax.dynamic_slice_in_dim(array, at * 512, 512, 1)

    def by_cores(arrays):
        parts = jnp.concatenate([array.reshape(16, 2, array.shape[0] // 32, rank) for array in arrays], axis=2)
        kept = lax.dynamic_index_in_dim(parts, c, 1, keepdims=False)
        return kept, lax.dynamic_index_in_dim(parts, 1 - c, 1, keepdims=False)

    def sum_plane(kept, given, ring):
        terms = kept + swap_cores(given.astype(bf16)).astype(f32)
        return sum_ring(sum_ring(terms.reshape(4, 4, -1, rank), "z"), ring)

    row_terms = [
        inner_rows(mixed_tok, grad_low_out),
        inner_rows(grad_attn_out, low_out),
        inner_rows(cot, low_down),
        inner_rows(normed_mid, grad_low_gu[:, :rank]),
        inner_rows(normed_mid, grad_low_gu[:, rank:]),
    ]
    row_terms = jnp.concatenate([array.reshape(128, 16, rank) for array in row_terms], axis=1)
    row_terms = jnp.swapaxes(row_terms.reshape(4, 4, 8, 80, rank), 1, 2).reshape(32, 320, rank)
    row_sum = lax.psum_scatter(row_terms, OVER_X, scatter_dimension=0, tiled=False)
    row_sum = sum_ring((row_sum + zero_of(dkv)).reshape(4, 80, rank), "x")
    early_sum = jnp.concatenate([unit_sum, row_sum], axis=0).astype(bf16)
    early_all = lax.all_gather(early_sum, ALL, axis=0, tiled=False)

    grad_qkv = inner_rows(features(normed_g, y), gather_near(grad_low_qkv, "y"))
    kept, other = by_cores(
        [
            inner_rows(grad_query, low_qkv[:, :rank]),
            inner_rows(grad_key, low_qkv[:, rank : 2 * rank]),
            inner_rows(grad_value, low_qkv[:, 2 * rank :]),
            grad_qkv[:, :rank],
            grad_qkv[:, rank : 2 * rank],
            grad_qkv[:, 2 * rank :],
        ]
    )
    g_gate, g_up, g_down_shrink, g_out_shrink, g_out_expand, g_down_expand, g_gateup = unpack_early(early_all)
    late_sum = sum_plane(kept, other, "x").astype(bf16)
    late_all = gather_ring(gather_ring(late_sum, "x"), "z")
    grad_normed = sum_tokens(grad_normed_part, "y", zero_of(late_all)) + times_transposed(grad_low_qkv, qkv_shrink)
    output = (middle + aheads[0] + product(low_down, down_expand)).astype(bf16)
    grad_input = (grad_middle + norm_back(inputs, scale_in, gain_attn, grad_normed)).astype(bf16)
    late_all = gather_ring(late_all, "y", zero_of(g_gateup).astype(bf16))
    late_all = late_all.reshape(4, 16, -1, rank)
    late_other = swap_cores(late_all)
    g_q, g_k, g_v, g_qkv = unpack_late(c.reshape(1).astype(jnp.int32), late_all, late_other)
    return (
        from_rows(output),
        from_rows(grad_input),
        g_qkv,
        g_q,
        g_k,
        g_v,
        g_out_shrink,
        g_out_expand,
        g_gateup,
        g_gate,
        g_up,
        g_down_shrink,
        g_down_expand,
    )


def solution(mesh):
    fine = Mesh(mesh.devices.reshape(2, 2, 4, 4, 2), ALL)
    split = P(ALL, None)
    placed = (split, P(), P()) + (split,) * 7 + (P(),) * 14 + (split,)
    return jax.shard_map(
        local,
        mesh=fine,
        in_specs=placed,
        out_specs=(split, split) + (P(),) * 11,
        check_vma=False,
    )
```

```python
from functools import partial

import jax
import jax.numpy as jnp
from jax import lax
from jax.experimental import pallas as pl
from jax.experimental.pallas import tpu as pltpu
from jax.sharding import Mesh, PartitionSpec as P

HEAD_SIZE = 256
RANK = 16
HALF = 64
GROUP = 512

ALL = ("zh", "zl", "x", "y", "c")

norm_eps = 1e-06
rope_theta = 1000042.0
neg_big = -1e30
far = 1 << 30

f32 = jnp.float32
bf16 = jnp.bfloat16


def product(left, right):
    return jnp.dot(left, right, preferred_element_type=f32)


def times_transposed(left, right):
    return lax.dot_general(left, right, (((1,), (1,)), ((), ())), preferred_element_type=f32)


def inner_rows(left, right):
    return lax.dot_general(left, right, (((0,), (0,)), ((), ())), preferred_element_type=f32)


def row_scale(value_matrix):
    return lax.rsqrt(jnp.mean(value_matrix * value_matrix, axis=-1, keepdims=True) + norm_eps)


def norm_back(value_matrix, scale, gain, grad):
    scaled = gain * grad
    return scale * scaled - value_matrix * (scale * scale * scale) * jnp.mean(
        value_matrix * scaled, axis=-1, keepdims=True
    )


def rotate(value_matrix):
    middle = value_matrix.shape[-1] // 2
    return jnp.concatenate([-value_matrix[..., middle:], value_matrix[..., :middle]], axis=-1)


def rope_tables(positions, width):
    middle = width // 2
    inverse = rope_theta ** (-(jnp.arange(middle, dtype=f32) * 2.0) / width)
    angles = positions.astype(f32)[:, None] * inverse[None, :]
    cos_half, sin_half = jnp.cos(angles), jnp.sin(angles)
    cos_table = jnp.concatenate([cos_half, cos_half], axis=-1)[:, None, :]
    sin_table = jnp.concatenate([sin_half, sin_half], axis=-1)[:, None, :]
    return (cos_table, sin_table)


OVER_X = ("zh", "zl", "y", "c")
RING = {"x": ("x",), "y": ("y",), "z": ("zh", "zl")}


def swap_cores(value):
    return lax.ppermute(value, "c", [(0, 1), (1, 0)])


def shift(value, ring, step):
    return lax.ppermute(value, RING[ring], [(i, (i + step) % 4) for i in range(4)])


def place_in(ring):
    return lax.axis_index(RING[ring])


def gather_near(value, ring, axis=0):
    return jnp.concatenate([value] + [shift(value, ring, -step) for step in (1, 2, 3)], axis=axis)


def gather_ring(value, ring, base=0.0):
    at = place_in(ring)
    whole_ring = jnp.full((4,) + value.shape, base, value.dtype)
    whole_ring = lax.dynamic_update_index_in_dim(whole_ring, value, at, 0)
    for step in (1, 2, 3):
        got = shift(value, ring, -step)
        whole_ring = lax.dynamic_update_index_in_dim(whole_ring, got, (at + step) % 4, 0)
    return whole_ring


def sum_near(blocks, ring, base=0.0):
    got = [shift(blocks[step], ring, step) for step in (2, 1, 3)]
    total = blocks[0].astype(f32) + base
    for term in got:
        total = total + term.astype(f32)
    return total


def sum_ring(terms, ring):
    at = place_in(ring)
    got = [
        shift(lax.dynamic_index_in_dim(terms, (at + step) % 4, 0, keepdims=False).astype(bf16), ring, step)
        for step in (1, 2, 3)
    ]
    total = lax.dynamic_index_in_dim(terms, at, 0, keepdims=False)
    for term in got:
        total = total + term.astype(f32)
    return total


CORNER = ("zh", "zl", "c")
PARTNER = [(4 * zh + 2 * zl + c, 4 * zh + 2 * (1 - zl) + c) for zh in (0, 1) for zl in (0, 1) for c in (0, 1)]
LATER = [[(2 * zl + 1, 4 + 2 * (zl ^ flip)) for zl in (0, 1)] for flip in (0, 1)]
EARLIER = [[(to, came) for came, to in pairs] for pairs in LATER]
def after(value, *others):
    return lax.optimization_barrier((value,) + others)[0]


def zero_of(value):
    return value[(slice(0, 1),) * value.ndim].reshape(()).astype(f32) * 0.0


def gather_row(key_value):
    line = jnp.stack([key_value] + [shift(key_value, "x", -step) for step in (1, 2, 3)])
    ahead = [lax.ppermute(line, CORNER, pairs) for pairs in LATER]
    partner = lax.ppermute(line, CORNER, PARTNER)
    beside = [lax.ppermute(value, "c", [(0, 1)]) for value in (line, partner)]
    return line, partner, ahead[0], ahead[1], beside[0], beside[1]


def sum_row(own, own_partner, prev, prev_partner, beside):
    got = [lax.ppermute(value, "c", [(1, 0)]) for value in (prev_partner, prev)]
    terms = [lax.ppermute(value, CORNER, pairs) for value, pairs in zip((prev, prev_partner), EARLIER)]
    sent = (own_partner.astype(f32) + got[0].astype(f32)).astype(bf16)
    terms = [got[1], lax.ppermute(sent, CORNER, PARTNER)] + terms
    start = zero_of(sent)
    line = own.astype(f32)
    for term in terms:
        line = line + term.astype(f32)
    sent = (line + beside(start)).astype(bf16)
    total = line[0]
    for step in (2, 1, 3):
        total = total + shift(sent[step], "x", step).astype(f32)
    return total


def allowed_mask(own_pos, own_start, key_pos):
    return (key_pos <= own_pos) & (key_pos >= own_start)


def load_tile(tile, tile_buf, own_ref, partner_ref, ahead_ref, ahead_partner_ref, beside_ref, beside_partner_ref):
    @pl.when(tile == 0)
    def _():
        tile_buf[...] = ahead_ref[0] + beside_ref[0]

    @pl.when(tile == 1)
    def _():
        tile_buf[...] = ahead_partner_ref[0] + beside_partner_ref[0]

    @pl.when(tile == 2)
    def _():
        tile_buf[...] = own_ref[0]

    @pl.when(tile == 3)
    def _():
        tile_buf[...] = partner_ref[0]


def attend_kernel(active, q_ref, pos_ref, start_ref, kpos_ref, *refs):
    mixed_ref, lse_ref, tile_buf, top, total, accum = refs[6:]
    step = pl.program_id(0)

    @pl.when(step == 0)
    def _():
        top[...] = jnp.full(top.shape, neg_big, f32)
        total[...] = jnp.zeros(total.shape, f32)
        accum[...] = jnp.zeros(accum.shape, f32)

    @pl.when(active[step] != 0)
    def _():
        load_tile(step // 4, tile_buf, *refs[:6])
        allowed = allowed_mask(pos_ref[...], start_ref[...], kpos_ref[0])
        both = [
            times_transposed(q_ref[:, head * HEAD_SIZE : (head + 1) * HEAD_SIZE], tile_buf[:, :HEAD_SIZE])
            for head in range(2)
        ]
        for head in range(2):
            scores = jnp.where(allowed, both[head], neg_big)
            top_old = top[head]
            top_new = jnp.maximum(top_old, jnp.max(scores, axis=-1, keepdims=True))
            weights_p = jnp.exp(scores - top_new)
            damping = jnp.exp(top_old - top_new)
            total[head] = total[head] * damping + jnp.sum(weights_p, axis=-1, keepdims=True)
            accum[head] = accum[head] * damping + product(weights_p.astype(bf16), tile_buf[:, HEAD_SIZE:])
            top[head] = top_new

    @pl.when(step == 15)
    def _():
        for head in range(2):
            mixed_ref[:, head * HEAD_SIZE : (head + 1) * HEAD_SIZE] = accum[head] / total[head]
            lse_ref[head] = top[head] + jnp.log(total[head])


def attend_back_kernel(active, q_ref, pos_ref, start_ref, kpos_ref, *refs):
    mixed_ref, lse_ref, dout_ref, dq_ref, down_ref, dpartner_ref, dprev_ref, dprev_partner_ref = refs[6:14]
    tile_buf, delta, sums = refs[14:]
    step = pl.program_id(0)
    tile = step // 4

    @pl.when(step == 0)
    def _():
        dq_ref[...] = jnp.zeros(dq_ref.shape, f32)
        for head in range(2):
            cols = slice(head * HEAD_SIZE, (head + 1) * HEAD_SIZE)
            delta[head] = jnp.sum(dout_ref[:, cols].astype(f32) * mixed_ref[:, cols], axis=-1, keepdims=True)

    @pl.when(active[step] == 0)
    def _():
        sums[...] = jnp.zeros(sums.shape, bf16)

    @pl.when(active[step] != 0)
    def _():
        load_tile(tile, tile_buf, *refs[:6])
        allowed = allowed_mask(pos_ref[...], start_ref[...], kpos_ref[0])
        dk = jnp.zeros((GROUP, HEAD_SIZE), f32)
        dv = jnp.zeros((GROUP, HEAD_SIZE), f32)
        both = [
            times_transposed(q_ref[:, head * HEAD_SIZE : (head + 1) * HEAD_SIZE], tile_buf[:, :HEAD_SIZE])
            for head in range(2)
        ]
        for head in range(2):
            cols = slice(head * HEAD_SIZE, (head + 1) * HEAD_SIZE)
            query, dout = q_ref[:, cols], dout_ref[:, cols]
            weights_p = jnp.where(allowed, jnp.exp(both[head] - lse_ref[head]), 0.0)
            dprobs = times_transposed(dout, tile_buf[:, HEAD_SIZE:])
            dscores = (weights_p * (dprobs - delta[head])).astype(bf16)
            dq_ref[:, cols] += product(dscores, tile_buf[:, :HEAD_SIZE])
            dk = dk + inner_rows(dscores, query)
            dv = dv + inner_rows(weights_p.astype(bf16), dout)
        sums[:, :HEAD_SIZE] = dk.astype(bf16)
        sums[:, HEAD_SIZE:] = dv.astype(bf16)

    for at, out_ref in enumerate((dprev_ref, dprev_partner_ref, down_ref, dpartner_ref)):

        @pl.when(tile == at)
        def _():
            out_ref[0] = sums[...]


def whole(shape):
    return pl.BlockSpec(shape, lambda *grid_and_refs: (0,) * len(shape))


def line_spec(tile):
    return pl.BlockSpec((1, GROUP, GROUP), lambda i, active: (jnp.clip(i - 4 * tile, 0, 3), 0, 0))


def active_spec(tile, table):
    return pl.BlockSpec(
        (1, GROUP, GROUP), lambda i, active: (active[16 * table + 4 * tile + jnp.clip(i - 4 * tile, 0, 3)], 0, 0)
    )


def step_tables(active, c):
    marks = active.reshape(4, 4)
    at = jnp.arange(4, dtype=jnp.int32)
    seen = jnp.where((marks[:, None, :] != 0) & (at[None, None, :] <= at[None, :, None]), at[None, None, :], -1)
    last = jnp.max(seen, axis=2)
    first = jnp.min(jnp.where(marks != 0, at[None, :], 3), axis=1, keepdims=True)
    blocks = jnp.where(last >= 0, last, first).reshape(16).astype(jnp.int32)
    return jnp.concatenate([active, blocks, jnp.where(c == 0, blocks, 0), jnp.where(c == 0, 0, blocks)])


def common_specs():
    return [
        whole((GROUP, GROUP)),
        whole((GROUP, 1)),
        whole((GROUP, 1)),
        pl.BlockSpec((1, 1, GROUP), lambda i, active: (i, 0, 0)),
    ] + [active_spec(tile, table) for tile, table in ((2, 1), (3, 1), (0, 2), (1, 2), (0, 3), (1, 3))]


def attend(active, *operands):
    return pl.pallas_call(
        attend_kernel,
        grid_spec=pltpu.PrefetchScalarGridSpec(
            num_scalar_prefetch=1,
            grid=(16,),
            in_specs=common_specs(),
            out_specs=[whole((GROUP, GROUP)), whole((2, GROUP, 1))],
            scratch_shapes=[
                pltpu.VMEM((GROUP, GROUP), bf16),
                pltpu.VMEM((2, GROUP, 1), f32),
                pltpu.VMEM((2, GROUP, 1), f32),
                pltpu.VMEM((2, GROUP, HEAD_SIZE), f32),
            ],
        ),
        out_shape=[
            jax.ShapeDtypeStruct((GROUP, GROUP), f32),
            jax.ShapeDtypeStruct((2, GROUP, 1), f32),
        ],
        compiler_params=pltpu.CompilerParams(vmem_limit_bytes=48 << 20),
        cost_estimate=pl.CostEstimate(flops=6 << 30, bytes_accessed=10 << 20, transcendentals=8 << 20),
        name="attend",
    )(active, *operands)


def attend_back(active, *operands):
    return pl.pallas_call(
        attend_back_kernel,
        grid_spec=pltpu.PrefetchScalarGridSpec(
            num_scalar_prefetch=1,
            grid=(16,),
            in_specs=common_specs() + [whole((GROUP, GROUP)), whole((2, GROUP, 1)), whole((GROUP, GROUP))],
            out_specs=[whole((GROUP, GROUP))] + [line_spec(tile) for tile in (2, 3, 0, 1)],
            scratch_shapes=[
                pltpu.VMEM((GROUP, GROUP), bf16),
                pltpu.VMEM((2, GROUP, 1), f32),
                pltpu.VMEM((GROUP, GROUP), bf16),
            ],
        ),
        out_shape=[jax.ShapeDtypeStruct((GROUP, GROUP), f32)]
        + [jax.ShapeDtypeStruct((4, GROUP, GROUP), bf16)] * 4,
        compiler_params=pltpu.CompilerParams(vmem_limit_bytes=48 << 20),
        cost_estimate=pl.CostEstimate(flops=12 << 30, bytes_accessed=20 << 20, transcendentals=8 << 20),
        name="attend_back",
    )(active, *operands)


UNITS = 1024
CHUNK = 256


def ffn_kernel(
    at,
    nm_ref,
    cot_ref,
    lgu_ref,
    gld_ref,
    wg_ref,
    wu_ref,
    wd_ref,
    ge_ref,
    ue_ref,
    ds_ref,
    perm_ref,
    pick_ref,
    result_ref,
    back_ref,
    units_ref,
    nmp,
    result,
    grad,
    low,
):
    step = pl.program_id(0)
    rank = ds_ref.shape[1]

    @pl.when(step == 0)
    def _():
        for zone in range(4):
            cols = slice(zone * GROUP, (zone + 1) * GROUP)
            nmp[:, cols] = product(nm_ref[:, cols], perm_ref[...]).astype(bf16)
        result[...] = jnp.zeros(result.shape, f32)
        grad[...] = jnp.zeros(grad.shape, f32)
        low[...] = jnp.zeros(low.shape, f32)

    wg, wu = wg_ref[...].reshape(2048, CHUNK), wu_ref[...].reshape(2048, CHUNK)
    wd = wd_ref[...].reshape(CHUNK, 2048)
    ge, ue = product(ge_ref[...], pick_ref[0]).astype(bf16), product(ue_ref[...], pick_ref[0]).astype(bf16)
    ds = inner_rows(pick_ref[0], ds_ref[...]).astype(bf16)
    low_gate, low_up = lgu_ref[:, :rank], lgu_ref[:, rank:]
    gate_pre = product(nmp[...], wg) + product(low_gate, ge)
    up_pre = product(nmp[...], wu) + product(low_up, ue)
    sigmoid_g = jax.nn.sigmoid(gate_pre)
    silu_gate = gate_pre * sigmoid_g
    active_units = (silu_gate * up_pre).astype(bf16)
    grad_active = times_transposed(cot_ref[...], wd) + times_transposed(gld_ref[...], ds)
    grad_gate = (grad_active * up_pre * sigmoid_g * (1.0 + gate_pre * (1.0 - sigmoid_g))).astype(bf16)
    grad_up = (grad_active * silu_gate).astype(bf16)
    result[...] += product(active_units, wd)
    grad[...] += times_transposed(grad_gate, wg) + times_transposed(grad_up, wu)
    low[:, :rank] += times_transposed(grad_gate, ge)
    low[:, rank : 2 * rank] += times_transposed(grad_up, ue)
    low[:, 2 * rank :] += product(active_units, ds)
    units_ref[0, :, 0, :64] = inner_rows(grad_gate, low_gate).reshape(4, 64, rank)
    units_ref[0, :, 0, 64:128] = inner_rows(grad_up, low_up).reshape(4, 64, rank)
    units_ref[0, :, 0, 128:] = inner_rows(active_units, gld_ref[...]).reshape(4, 64, rank)

    @pl.when(step == 2 * UNITS // CHUNK - 1)
    def _():
        result_ref[...] = result[...].astype(bf16)
        for zone in range(4):
            cols = slice(zone * GROUP, (zone + 1) * GROUP)
            back_ref[:, cols] = product(grad[:, cols].astype(bf16), perm_ref[...]).astype(bf16)
        back_ref[:, 2048:] = low[...].astype(bf16)


def feed_forward(at, normed_mid, cot, low_gu, grad_low_down, weights, expands, perm, picks):
    rank = low_gu.shape[1] // 2
    steps = UNITS // CHUNK
    unit_spec = pl.BlockSpec((1, 4, 1, 192, rank), lambda i, at: (i % steps, 0, i // steps, 0, 0))
    return pl.pallas_call(
        ffn_kernel,
        grid_spec=pltpu.PrefetchScalarGridSpec(
            num_scalar_prefetch=1,
            grid=(2 * steps,),
            in_specs=[
                whole((GROUP, 2048)),
                whole((GROUP, 2048)),
                whole((GROUP, 2 * rank)),
                whole((GROUP, rank)),
                pl.BlockSpec((16, 1, 128, CHUNK), lambda i, at: (0, i // steps, 0, i % steps)),
                pl.BlockSpec((16, 1, 128, CHUNK), lambda i, at: (0, i // steps, 0, steps + i % steps)),
                pl.BlockSpec((4, 1, 64, 2048), lambda i, at: (i % steps, i // steps, 2, 0)),
                pl.BlockSpec((rank, 2 * CHUNK), lambda i, at: (0, 4 * (i % steps) + at[0])),
                pl.BlockSpec((rank, 2 * CHUNK), lambda i, at: (0, 4 * (i % steps) + at[0])),
                pl.BlockSpec((2 * CHUNK, rank), lambda i, at: (4 * (i % steps) + at[0], 0)),
                whole((GROUP, GROUP)),
                pl.BlockSpec((1, 2 * CHUNK, CHUNK), lambda i, at: (i // steps, 0, 0)),
            ],
            out_specs=[whole((GROUP, 2048)), whole((GROUP, 2048 + 3 * rank)), unit_spec],
            scratch_shapes=[
                pltpu.VMEM((GROUP, 2048), bf16),
                pltpu.VMEM((GROUP, 2048), f32),
                pltpu.VMEM((GROUP, 2048), f32),
                pltpu.VMEM((GROUP, 3 * rank), f32),
            ],
        ),
        out_shape=[
            jax.ShapeDtypeStruct((GROUP, 2048), bf16),
            jax.ShapeDtypeStruct((GROUP, 2048 + 3 * rank), bf16),
            jax.ShapeDtypeStruct((4, 4, 2, 192, rank), f32),
        ],
        compiler_params=pltpu.CompilerParams(vmem_limit_bytes=60 << 20),
        cost_estimate=pl.CostEstimate(flops=28 << 30, bytes_accessed=40 << 20, transcendentals=2 << 20),
        name="feed_forward",
    )(at, normed_mid, cot, low_gu, grad_low_down, weights, weights, weights, *expands, perm, picks)


EARLY = (64, 64, 64, 16, 16, 16, 16, 16)
LATE = (16, 8, 8, 16, 16, 16)


def cut(array, sizes):
    found, at = [], 0
    for size in sizes:
        found.append(array[..., at : at + size, :])
        at += size
    return found


def turned(array):
    at = lax.broadcasted_iota(jnp.int32, (128, 128), 0), lax.broadcasted_iota(jnp.int32, (128, 128), 1)
    return times_transposed((at[0] == at[1]).astype(f32).astype(bf16), array)


def early_kernel(all_ref, gate_ref, up_ref, down_ref, oshrink_ref, oexpand_ref, dexpand_ref, gateup_ref):
    pieces = [piece.reshape(-1, 128) for piece in cut(all_ref[...], EARLY)]
    gate_ref[...] = turned(pieces[0])
    up_ref[...] = turned(pieces[1])
    down_ref[...] = pieces[2].astype(f32)
    oshrink_ref[...] = pieces[3].astype(f32)
    oexpand_ref[...] = turned(pieces[4])
    dexpand_ref[...] = turned(pieces[5])
    gateup_ref[:, :128] = pieces[6].astype(f32)
    gateup_ref[:, 128:] = pieces[7].astype(f32)


def unpack_early(everyone):
    return pl.pallas_call(
        early_kernel,
        grid=(8,),
        in_specs=[pl.BlockSpec((16, sum(EARLY), 128), lambda i: (i, 0, 0))],
        out_specs=[
            pl.BlockSpec((128, 1024), lambda i: (0, i)),
            pl.BlockSpec((128, 1024), lambda i: (0, i)),
            pl.BlockSpec((1024, 128), lambda i: (i, 0)),
            pl.BlockSpec((256, 128), lambda i: (i, 0)),
            pl.BlockSpec((128, 256), lambda i: (0, i)),
            pl.BlockSpec((128, 256), lambda i: (0, i)),
            pl.BlockSpec((256, 256), lambda i: (i, 0)),
        ],
        out_shape=[
            jax.ShapeDtypeStruct(shape, f32)
            for shape in ((128, 8192), (128, 8192), (8192, 128), (2048, 128), (128, 2048), (128, 2048), (2048, 256))
        ],
        cost_estimate=pl.CostEstimate(flops=1 << 20, bytes_accessed=27 << 20, transcendentals=0),
        name="unpack_early",
    )(everyone)


def late_kernel(core, mine_ref, other_ref, q_ref, k_ref, v_ref, low_ref):
    mine, other = mine_ref[0].astype(f32), other_ref[0].astype(f32)
    first, second = jnp.where(core[0] == 0, mine, other), jnp.where(core[0] == 0, other, mine)
    pieces = [
        jnp.stack(pair, axis=1).reshape(-1, 128) for pair in zip(cut(first, LATE), cut(second, LATE))
    ]
    q_ref[...] = turned(pieces[0].astype(bf16))
    k_ref[...] = turned(pieces[1].astype(bf16))
    v_ref[...] = turned(pieces[2].astype(bf16))
    for at in range(3):
        low_ref[:, at * 128 : (at + 1) * 128] = pieces[3 + at]


def unpack_late(core, mine, other):
    half = pl.BlockSpec((1, 16, sum(LATE), 128), lambda i, core: (i, 0, 0, 0))
    return pl.pallas_call(
        late_kernel,
        grid_spec=pltpu.PrefetchScalarGridSpec(
            num_scalar_prefetch=1,
            grid=(4,),
            in_specs=[half, half],
            out_specs=[
                pl.BlockSpec((128, 512), lambda i, core: (0, i)),
                pl.BlockSpec((128, 256), lambda i, core: (0, i)),
                pl.BlockSpec((128, 256), lambda i, core: (0, i)),
                pl.BlockSpec((512, 384), lambda i, core: (i, 0)),
            ],
        ),
        out_shape=[
            jax.ShapeDtypeStruct(shape, f32) for shape in ((128, 2048), (128, 1024), (128, 1024), (2048, 384))
        ],
        cost_estimate=pl.CostEstimate(flops=1 << 20, bytes_accessed=8 << 20, transcendentals=0),
        name="unpack_late",
    )(core, mine, other)


def local(
    hidden_in,
    gain_attn,
    gain_ffn,
    w_query,
    w_key,
    w_value,
    w_out,
    w_gate,
    w_up,
    w_down,
    qkv_shrink,
    query_expand,
    key_expand,
    value_expand,
    out_shrink,
    out_expand,
    gateup_shrink,
    gate_expand,
    up_expand,
    down_shrink,
    down_expand,
    lengths,
    adapter,
    packed_pos,
    cotangent,
):
    zh, zl, x, y, c = (lax.axis_index(name) for name in ALL)
    row = 2 * zh + c
    factor = HEAD_SIZE ** (-0.5)
    rank = out_shrink.shape[1]

    def to_rows(value):
        own = lax.dynamic_slice_in_dim(value, c * HALF, HALF, 0)
        sent = lax.dynamic_slice_in_dim(value, (1 - c) * HALF, HALF, 0)
        return jnp.concatenate([own, swap_cores(sent)], axis=0)

    def from_rows(value):
        own, got = value[:HALF], swap_cores(value[HALF:])
        return jnp.where(c == 0, jnp.concatenate([own, got], 0), jnp.concatenate([got, own], 0))

    hidden = to_rows(hidden_in)
    cot = to_rows(cotangent)

    def roll(array, by, axis):
        return lax.dynamic_slice_in_dim(jnp.concatenate([array, array], axis), by, array.shape[axis], axis)

    spread = packed_pos.reshape(2, 2, 4, 4, 2, 2, HALF)
    spread = jnp.transpose(spread, (0, 5, 1, 2, 3, 4, 6))
    rows_pos = jnp.stack([spread[:, 0], spread[:, 1, :, :, :, ::-1]], axis=1).reshape(4, 2, 4, 4, 128)
    rows_pos = roll(roll(roll(rows_pos, zl, 1), x, 2), y, 3).reshape(4, 8, GROUP)
    own_row = lax.dynamic_index_in_dim(rows_pos, row, 0, keepdims=False)
    prev_row = lax.dynamic_index_in_dim(rows_pos, jnp.maximum(row - 1, 0), 0, keepdims=False)
    prev_row = jnp.where(row == 0, far, prev_row)
    tiles_pos = jnp.concatenate([prev_row, own_row])
    group_pos = own_row[0]
    seq_ends = jnp.cumsum(lengths)
    starts = seq_ends - lengths
    member = (group_pos[:, None] >= starts[None, :]) & (group_pos[:, None] < seq_ends[None, :])
    member_int = member.astype(jnp.int32)
    group_start = jnp.sum(member_int * starts[None, :], axis=1)

    def selected(pos):
        inside = (pos[:, None] >= starts[None, :]) & (pos[:, None] < seq_ends[None, :])
        owner = jnp.sum(inside.astype(jnp.int32) * adapter[None, :], axis=1)
        return (owner[:, None] == (jnp.arange(rank, dtype=jnp.int32) // RANK)[None, :]).astype(f32)

    key_runs, pos_runs, start_runs = tiles_pos.reshape(64, 128), group_pos.reshape(4, 128), group_start.reshape(4, 128)
    key_low, key_high = jnp.min(key_runs, axis=1)[:, None], jnp.max(key_runs, axis=1)[:, None]
    seen = (key_low <= jnp.max(pos_runs, axis=1)[None, :]) & (key_high >= jnp.min(start_runs, axis=1)[None, :])
    active = jnp.max(seen.astype(jnp.int32).reshape(16, 16), axis=1)
    active = step_tables(active, c)
    select_y = selected(group_pos)
    select_x = selected(own_row.reshape(2, 4, 4, 128)[0, :, 0].reshape(GROUP))
    select = select_y[:128]
    cos_table, sin_table = rope_tables(group_pos - group_start, HEAD_SIZE)

    def column_slices(weight):
        parts = weight.reshape(16, 4, 4, 4, 2, 64)
        return jnp.transpose(parts, (2, 4, 0, 1, 3, 5)).reshape(8, 16, 1024)

    heads_q = w_query.reshape(16, 4, 512)
    heads_kv = jnp.concatenate([w_key.reshape(16, 4, 256), w_value.reshape(16, 4, 256)], axis=2)
    qkv_parts = jnp.transpose(jnp.stack([heads_q, heads_kv], axis=2), (1, 2, 0, 3)).reshape(8, 16, 512)
    qkv_parts = lax.all_to_all(qkv_parts, ("y", "c"), split_axis=0, concat_axis=0, tiled=True).reshape(128, 512)
    gate_up = jnp.concatenate([column_slices(w_gate), column_slices(w_up)], axis=2)
    def columns_of(array, width):
        return lax.dynamic_slice_in_dim(array, y * width, width, 1)

    inputs = hidden.astype(f32)
    scale_in = row_scale(inputs)
    normed = (inputs * scale_in * gain_attn).astype(bf16)
    normed, cot, qkv_parts = lax.optimization_barrier((normed, cot, qkv_parts))
    normed_g = gather_near(normed, "y")
    cot_g = gather_near(cot, "x")
    qkv_parts = after(qkv_parts, normed_g, cot_g)
    qkv_mine = gather_ring(gather_ring(qkv_parts, "x"), "z").reshape(2048, 512)
    qkv_other = swap_cores(qkv_mine)
    wo = lax.all_gather(w_out, ALL, axis=0, tiled=True)
    q_expand = columns_of(query_expand, 512)
    k_expand = columns_of(key_expand, 256)
    v_expand = columns_of(value_expand, 256)
    low_qkv = (product(normed_g, qkv_shrink) * jnp.tile(select_y, (1, 3))).astype(bf16)
    lin_mine, lin_other = product(normed_g, qkv_mine), product(normed_g, qkv_other)
    query_lin = jnp.where(c == 0, lin_mine, lin_other) + product(low_qkv[:, :rank], q_expand)
    kv_lin = jnp.where(c == 0, lin_other, lin_mine)
    key_lin = kv_lin[:, :256] + product(low_qkv[:, rank : 2 * rank], k_expand)
    value_lin = kv_lin[:, 256:] + product(low_qkv[:, 2 * rank :], v_expand)
    query_heads = query_lin.reshape(GROUP, 2, HEAD_SIZE)
    key_heads = key_lin.reshape(GROUP, 1, HEAD_SIZE)
    query = (query_heads * cos_table + rotate(query_heads) * sin_table).astype(bf16)
    query = (query * bf16(factor)).reshape(GROUP, 512)
    key = (key_heads * cos_table + rotate(key_heads) * sin_table).astype(bf16).reshape(GROUP, 256)

    lines = gather_row(jnp.concatenate([key, value_lin.astype(bf16)], axis=1))
    gate_up = gate_up + zero_of(lines[0]).astype(bf16)
    gate_up = lax.all_to_all(gate_up, ("x", "c"), split_axis=0, concat_axis=0, tiled=True).reshape(128, 2048)
    waited = zero_of(lines[1]) + zero_of(lines[2]) + zero_of(lines[3]) + zero_of(lines[4]) + zero_of(wo)
    ffn = jnp.concatenate([gate_up, w_down], axis=0) + waited.astype(bf16)
    ffn = lax.all_gather(ffn, OVER_X, axis=0, tiled=False).reshape(16, 2, 192, 2048)
    attended = (query, group_pos[:, None], group_start[:, None], tiles_pos.reshape(16, 1, GROUP)) + lines
    mixed_f, lse = attend(active, *attended)
    mixed = mixed_f.astype(bf16)

    heads = jnp.zeros((4, 128, 512), bf16)
    heads = lax.dynamic_update_index_in_dim(heads, mixed[:128], y, 0)
    for step in (1, 2, 3):
        got = shift(mixed[step * 128 : (step + 1) * 128], "y", step)
        heads = lax.dynamic_update_index_in_dim(heads, got, (y - step) % 4, 0)
    mixed_tok = jnp.transpose(heads, (1, 0, 2)).reshape(128, 2048)
    low_out = (product(mixed_tok, out_shrink) * select).astype(bf16)
    middle = inputs + product(mixed_tok, wo) + product(low_out, out_expand)
    scale_mid = row_scale(middle)
    normed_mid = (middle * scale_mid * gain_ffn).astype(bf16)
    normed_mid_g = gather_near(normed_mid, "x")

    select_two = jnp.tile(select_x, (1, 2))
    low_gu = (product(normed_mid_g, gateup_shrink) * select_two).astype(bf16)
    grad_low_down = (times_transposed(cot_g, down_expand) * select_x).astype(bf16)
    place = jnp.arange(GROUP, dtype=jnp.int32)
    turned = (place // 32 % 4) * 128 + (place // 128) * 32 + place % 32
    perm = (turned[:, None] == place[None, :]).astype(bf16)
    wide, narrow = jnp.arange(2 * CHUNK, dtype=jnp.int32), jnp.arange(CHUNK, dtype=jnp.int32)
    picks = jnp.stack(
        [(wide[:, None] == (narrow // 64 * 128 + core * 64 + narrow % 64)[None, :]).astype(bf16) for core in (0, 1)]
    )
    result, back_part, unit_grads = feed_forward(
        x.reshape(1).astype(jnp.int32),
        normed_mid_g,
        cot_g,
        low_gu,
        grad_low_down,
        ffn,
        (gate_expand, up_expand, down_shrink),
        perm,
        picks,
    )

    def sum_tokens(part, ring, base=0.0):
        sent = part.astype(bf16)
        return sum_near([sent[i * 128 : (i + 1) * 128] for i in range(4)], ring, base)

    back = sum_tokens(back_part, "x")
    back, back_low, low_down_sum = back[:, :2048], back[:, 2048 : 2048 + 2 * rank], back[:, 2048 + 2 * rank :]

    low_down = (low_down_sum * select).astype(bf16)
    grad_low_gu = (back_low * jnp.tile(select, (1, 2))).astype(bf16)
    grad_normed_mid = back + times_transposed(grad_low_gu, gateup_shrink)
    cot_f = cot.astype(f32)
    grad_middle = cot_f + norm_back(middle, scale_mid, gain_ffn, grad_normed_mid)
    grad_attn_out = grad_middle.astype(bf16)
    grad_low_out = (times_transposed(grad_attn_out, out_expand) * select).astype(bf16)
    grad_mixed = (times_transposed(grad_attn_out, wo) + times_transposed(grad_low_out, out_shrink)).astype(bf16)

    def slices_near(array):
        def columns_at(step):
            return lax.dynamic_slice_in_dim(array, ((y + step) % 4) * 512, 512, 1)

        return jnp.concatenate([columns_at(0)] + [shift(columns_at(4 - step), "y", -step) for step in (1, 2, 3)])

    dout = slices_near(grad_mixed)
    dq, *terms = attend_back(active, *attended, mixed_f, lse, dout)
    unit_sum = lax.psum_scatter(
        unit_grads.reshape(32, 192, rank), OVER_X, scatter_dimension=0, tiled=False
    )
    aheads = []

    def beside(start):
        aheads.append(sum_tokens(result + start.astype(bf16), "x"))
        return zero_of(aheads[0]) + zero_of(unit_sum)

    dkv = sum_row(*terms, beside)
    dk, dv = dkv[:, :HEAD_SIZE], dkv[:, HEAD_SIZE:]
    query_back = (dq * factor).astype(bf16).astype(f32).reshape(GROUP, 2, HEAD_SIZE)
    key_back = dk.astype(bf16).astype(f32).reshape(GROUP, 1, HEAD_SIZE)
    grad_value = dv.astype(bf16)
    grad_query = (query_back * cos_table - rotate(query_back * sin_table)).astype(bf16).reshape(GROUP, 512)
    grad_key = (key_back * cos_table - rotate(key_back * sin_table)).astype(bf16).reshape(GROUP, 256)
    grad_kv = jnp.concatenate([grad_key, grad_value], axis=1)

    grad_low_part = jnp.concatenate(
        [
            times_transposed(grad_query, q_expand),
            times_transposed(grad_key, k_expand),
            times_transposed(grad_value, v_expand),
        ],
        axis=1,
    )
    grad_low_qkv = (sum_tokens(grad_low_part, "y") * jnp.tile(select, (1, 3))).astype(bf16)
    for_mine = jnp.where(c == 0, grad_query, grad_kv)
    for_other = jnp.where(c == 0, grad_kv, grad_query)
    grad_normed_part = times_transposed(for_mine, qkv_mine) + times_transposed(for_other, qkv_other)
    def features(array, at):
        return lax.dynamic_slice_in_dim(array, at * 512, 512, 1)

    def by_cores(arrays):
        parts = jnp.concatenate([array.reshape(16, 2, array.shape[0] // 32, rank) for array in arrays], axis=2)
        kept = lax.dynamic_index_in_dim(parts, c, 1, keepdims=False)
        return kept, lax.dynamic_index_in_dim(parts, 1 - c, 1, keepdims=False)

    def sum_plane(kept, given, ring):
        terms = kept + swap_cores(given.astype(bf16)).astype(f32)
        return sum_ring(sum_ring(terms.reshape(4, 4, -1, rank), "z"), ring)

    row_terms = [
        inner_rows(mixed_tok, grad_low_out),
        inner_rows(grad_attn_out, low_out),
        inner_rows(cot, low_down),
        inner_rows(normed_mid, grad_low_gu[:, :rank]),
        inner_rows(normed_mid, grad_low_gu[:, rank:]),
    ]
    row_terms = jnp.concatenate([array.reshape(128, 16, rank) for array in row_terms], axis=1)
    row_terms = jnp.swapaxes(row_terms.reshape(4, 4, 8, 80, rank), 1, 2).reshape(32, 320, rank)
    row_sum = lax.psum_scatter(row_terms, OVER_X, scatter_dimension=0, tiled=False)
    row_sum = sum_ring((row_sum + zero_of(dkv)).reshape(4, 80, rank), "x")
    early_sum = jnp.concatenate([unit_sum, row_sum], axis=0).astype(bf16)
    early_all = lax.all_gather(early_sum, ALL, axis=0, tiled=False)

    grad_qkv = inner_rows(features(normed_g, y), gather_near(grad_low_qkv, "y"))
    kept, other = by_cores(
        [
            inner_rows(grad_query, low_qkv[:, :rank]),
            inner_rows(grad_key, low_qkv[:, rank : 2 * rank]),
            inner_rows(grad_value, low_qkv[:, 2 * rank :]),
            grad_qkv[:, :rank],
            grad_qkv[:, rank : 2 * rank],
            grad_qkv[:, 2 * rank :],
        ]
    )
    g_gate, g_up, g_down_shrink, g_out_shrink, g_out_expand, g_down_expand, g_gateup = unpack_early(early_all)
    late_sum = sum_plane(kept, other, "x").astype(bf16)
    late_all = gather_ring(gather_ring(late_sum, "x"), "z")
    grad_normed = sum_tokens(grad_normed_part, "y", zero_of(late_all)) + times_transposed(grad_low_qkv, qkv_shrink)
    output = (middle + aheads[0] + product(low_down, down_expand)).astype(bf16)
    grad_input = (grad_middle + norm_back(inputs, scale_in, gain_attn, grad_normed)).astype(bf16)
    late_all = gather_ring(late_all, "y", zero_of(g_gateup).astype(bf16))
    late_all = late_all.reshape(4, 16, -1, rank)
    late_other = swap_cores(late_all)
    g_q, g_k, g_v, g_qkv = unpack_late(c.reshape(1).astype(jnp.int32), late_all, late_other)
    return (
        from_rows(output),
        from_rows(grad_input),
        g_qkv,
        g_q,
        g_k,
        g_v,
        g_out_shrink,
        g_out_expand,
        g_gateup,
        g_gate,
        g_up,
        g_down_shrink,
        g_down_expand,
    )


def solution(mesh):
    fine = Mesh(mesh.devices.reshape(2, 2, 4, 4, 2), ALL)
    split = P(ALL, None)
    placed = (split, P(), P()) + (split,) * 7 + (P(),) * 14 + (split,)
    return jax.shard_map(
        local,
        mesh=fine,
        in_specs=placed,
        out_specs=(split, split) + (P(),) * 11,
        check_vma=False,
    )
```
